32 devices in a mesh: ctx: 8 (over y, x, core), shard: 4 (over z).
Axes of the slice: x: 2, y: 2, z: 4, core: 2. Of those that a mesh axis runs over, the one named last changes fastest.
Arguments:
- tokens: bfloat16 [4, 1024, 2048], P('shard', 'ctx'), may hold values from -6 to 6
- lengths: int32 [4, 9], P('shard'), may hold values from 1 to 512, as said below
- cotangent: bfloat16 [4, 1024, 2048], P('shard', 'ctx'), may hold values from -6 to 6
- w_qkv: bfloat16 [2048, 3072], P(('ctx', 'shard')), may hold values from -0.5 to 0.5
- w_out: bfloat16 [2048, 2048], P(('ctx', 'shard')), may hold values from -2 to 2
- w_gate_up: bfloat16 [2048, 16384], P(('ctx', 'shard')), may hold values from -0.125 to 0.125
- w_down: bfloat16 [8192, 2048], P(('ctx', 'shard')), may hold values from -0.25 to 0.25
- gain_attn: bfloat16 [2048], P(('ctx', 'shard')), may hold values from 0.5 to 1.5
- gain_mlp: bfloat16 [2048], P(('ctx', 'shard')), may hold values from 0.5 to 1.5
Outputs:
- mixed: bfloat16 [4, 1024, 2048], P('shard', 'ctx')
- grad_tokens: float32 [4, 1024, 2048], P('shard', 'ctx')
- grad_qkv: float32 [2048, 3072], P(('ctx', 'shard'))
- grad_out: float32 [2048, 2048], P(('ctx', 'shard'))
- grad_gate_up: float32 [2048, 16384], P(('ctx', 'shard'))
- grad_down: float32 [8192, 2048], P(('ctx', 'shard'))
- grad_gain_attn: float32 [2048], P(('ctx', 'shard'))
- grad_gain_mlp: float32 [2048], P(('ctx', 'shard'))
- clip: float32 [32], replicated
The draws below stay inside these ranges and needn't reach their ends.
Inputs may be any that keep to these rules, and one draw needn't show every extreme that they name: Each row is the prompt's length 512, then the lengths of 8 continuations that fill the rest of the group.
All inputs are finite; a program needn't handle non-finite values.
Results may differ from the reference program's by a relative error of at most 0.02.
Values may be sent and summed in bfloat16 or wider, within the bound.
A program may use at most 448 MiB of HBM per device.

```python
import math
from functools import partial
import jax
import jax.numpy as jnp
from jax import lax

D = 2048
HEADS = 32
KV_HEADS = 8
HEAD_DIM = 64
FF = 8192
CONTS = 8
GROUP_TOK = 1024
GROUPS = 4


def draw_lengths(key, part):
    key = jax.random.fold_in(key, 11)
    rest = GROUP_TOK - GROUP_TOK // 2
    weights = jax.random.randint(key, (GROUPS, CONTS), 1, 5)
    scaled = rest * weights // jnp.sum(weights, axis=1, keepdims=True)
    head = scaled[:, :CONTS - 1]
    last = rest - jnp.sum(head, axis=1, keepdims=True)
    prompt = jnp.full((GROUPS, 1), GROUP_TOK // 2, jnp.int32)
    return jnp.concatenate([prompt, head, last], axis=1).astype(jnp.int32)


def level_of(key, extent, pieces, smallest, top_value):
    level, own = 1.0, jax.random.fold_in(key, 6)
    for axis_at, shards_of in pieces:
        steps = jnp.exp(jax.random.uniform(jax.random.fold_in(own, axis_at), (shards_of,), jnp.float32, smallest / len(pieces), top_value / len(pieces)))
        level = level * jnp.repeat(steps, extent[axis_at] // shards_of).reshape([-1 if axis == axis_at else 1 for axis in range(len(extent))])
    return level


def centred(key, shape, scale, most, split=(), kind=jnp.bfloat16):
    drawn = scale * jax.random.normal(key, shape, jnp.float32)
    if split:
        drawn = drawn * level_of(key, shape, split, -0.22, 0.18)
    return jnp.clip(drawn, -most, most).astype(kind)


def setup_inputs(seed: int = 0) -> dict:
    seeds = jax.random.split(jax.random.key(seed), 10)
    return {
        "tokens": centred(seeds[0], (GROUPS, GROUP_TOK, D), 1.0, 6.0, ((0, 4), (1, 8))),
        "lengths": draw_lengths(jax.random.fold_in(seeds[9], 71), 0),
        "cotangent": centred(seeds[2], (GROUPS, GROUP_TOK, D), 1.0, 6.0, ((0, 4), (1, 8))),
        "w_qkv": centred(seeds[3], (D, (HEADS + 2 * KV_HEADS) * HEAD_DIM), (D // 16) ** -0.5, 0.5, ((0, 32),)),
        "w_out": centred(seeds[4], (HEADS * HEAD_DIM, D), 8 ** -0.5, 2.0, ((0, 32),)),
        "w_gate_up": centred(seeds[5], (D, 2 * FF), D ** -0.5, 0.125, ((0, 32),)),
        "w_down": centred(seeds[6], (FF, D), (FF // 16) ** -0.5, 0.25, ((0, 32),)),
        "gain_attn": jnp.clip(1.0 + 0.1 * jax.random.normal(seeds[7], (D,), jnp.float32), 0.5, 1.5).astype(jnp.bfloat16),
        "gain_mlp": jnp.clip(1.0 + 0.1 * jax.random.normal(seeds[8], (D,), jnp.float32), 0.5, 1.5).astype(jnp.bfloat16),
    }


SCALE = 0.015625
BRANCH = 0.22
EPSILON = 1e-05
CLIP_TARGET = 4.0
NEGATIVE = -1e+30
HIGHEST = lax.Precision.HIGHEST

@jax.custom_vjp
def low(v):
    return lax.optimization_barrier(v.astype(jnp.bfloat16)).astype(jnp.float32)

@jax.custom_vjp
def low_back(v):
    return v

def low_keep(v):
    return (low(v), None)

def low_pass(kept, grad):
    return (grad,)

def back_keep(v):
    return (v, None)

def back_low(kept, grad):
    return (low(grad),)
low.defvjp(low_keep, low_pass)
low_back.defvjp(back_keep, back_low)

def segment_ids(positions, lengths_row):
    bounds = jnp.cumsum(lengths_row)[:-1]
    return lax.optimization_barrier(jnp.sum((positions[:, None] >= bounds[None, :]).astype(jnp.int32), axis=1))

def visible(q_pos, q_seg, k_pos, k_seg):
    earlier = k_pos[None, :] <= q_pos[:, None]
    shared = (k_seg[None, :] == 0) | (k_seg[None, :] == q_seg[:, None])
    return earlier & shared

def rms_norm(rows, gain):
    return rows * lax.rsqrt(lax.optimization_barrier(jnp.mean(rows * rows, axis=-1, keepdims=True)) + EPSILON) * gain

def block_attention(keys_four, values_four, k_pos, k_seg, lengths_row, item):
    q_block, q_pos = item
    q_seg = segment_ids(q_pos, lengths_row)
    live = visible(q_pos, q_seg, k_pos, k_seg)[:, None, None, :]
    scores = low_back(SCALE * jnp.einsum('tgrd,kgd->tgrk', q_block, keys_four, precision=HIGHEST))
    masked = jnp.where(live, scores, NEGATIVE)
    top = lax.optimization_barrier(jnp.max(masked, axis=-1, keepdims=True))
    expo = jnp.where(live, jnp.exp(masked - top), 0.0)
    probs = low(expo / lax.optimization_barrier(jnp.sum(expo, axis=-1, keepdims=True)))
    out = jnp.einsum('tgrk,kgd->tgrd', probs, values_four, precision=HIGHEST)
    return (out.reshape(out.shape[0], HEADS * HEAD_DIM), lax.optimization_barrier(jnp.max(top[..., 0], axis=0)))

def group_attention(item):
    queries, keys, values, lengths_row = item
    size = queries.shape[0]
    block = math.gcd(size, 512)
    repeat = HEADS // KV_HEADS
    positions = jnp.arange(size, dtype=jnp.int32)
    k_seg = segment_ids(positions, lengths_row)
    keys_four = keys.reshape(size, KV_HEADS, HEAD_DIM)
    values_four = values.reshape(size, KV_HEADS, HEAD_DIM)
    q_blocks = queries.reshape(size // block, block, KV_HEADS, repeat, HEAD_DIM)
    work = jax.checkpoint(partial(block_attention, keys_four, values_four, positions, k_seg, lengths_row))
    outs, tops = lax.map(work, (q_blocks, positions.reshape(size // block, block)))
    return (outs.reshape(size, HEADS * HEAD_DIM), lax.optimization_barrier(jnp.max(tops, axis=0)))

def reference(tokens, lengths, cotangent, w_qkv, w_out, w_gate_up, w_down, gain_attn, gain_mlp):
    groups, size, width = tokens.shape
    q_width = HEADS * HEAD_DIM
    kv_width = KV_HEADS * HEAD_DIM

    def forward(rows, wq, wo, wg, wd, ga, gm):
        flat = rows.reshape(groups * size, width)
        normed_one = low(rms_norm(flat, ga))
        projected = jnp.dot(normed_one, wq, precision=HIGHEST, preferred_element_type=jnp.float32)
        queries = low_back(low(projected[:, :q_width]))
        keys = low_back(low(projected[:, q_width:q_width + kv_width]))
        values = low_back(low(projected[:, q_width + kv_width:]))
        heads_out, tops = lax.map(group_attention, (queries.reshape(groups, size, q_width), keys.reshape(groups, size, kv_width), values.reshape(groups, size, kv_width), lengths))
        attn_out = low_back(low(heads_out.reshape(groups * size, q_width)))
        attn_proj = low_back(jnp.dot(attn_out, wo, precision=HIGHEST, preferred_element_type=jnp.float32))
        mid = flat + BRANCH * attn_proj
        normed_two = low(rms_norm(mid, gm))
        gate_up = low_back(jnp.dot(normed_two, wg, precision=HIGHEST, preferred_element_type=jnp.float32))
        gate = gate_up[:, :FF]
        up = gate_up[:, FF:]
        hidden = low(gate * jax.nn.sigmoid(gate) * up)
        mlp_proj = low_back(jnp.dot(hidden, wd, precision=HIGHEST, preferred_element_type=jnp.float32))
        result = mid + BRANCH * mlp_proj
        return (result.reshape(groups, size, width), lax.optimization_barrier(jnp.max(tops, axis=0)).reshape(HEADS))
    inputs = tuple((a.astype(jnp.float32) for a in (tokens, w_qkv, w_out, w_gate_up, w_down, gain_attn, gain_mlp)))
    result, pull, top = jax.vjp(forward, *inputs, has_aux=True)
    grads = pull(cotangent.astype(jnp.float32))
    clip = CLIP_TARGET / jnp.maximum(top, CLIP_TARGET)
    return (result.astype(jnp.bfloat16), grads[0], grads[1], grads[2], grads[3], grads[4], grads[5], grads[6], clip)
```

```python
import functools
import math

import jax
import jax.numpy as jnp
from jax import lax
from jax.experimental import pallas as pl
from jax.experimental.pallas import tpu as pltpu
from jax.sharding import PartitionSpec as P

HEADS = 32
KV_HEADS = 8
HEAD_DIM = 64


SCALE = 0.015625
BRANCH = 0.22
EPSILON = 1e-05
CLIP_TARGET = 4.0
NEGATIVE = -1e30
MIB = 1024 * 1024
EVERY = ("ctx", "shard")


def segment_ids(positions, lengths_row):
    bounds = jnp.cumsum(lengths_row)[:-1]
    return jnp.sum((positions[:, None] >= bounds[None, :]).astype(jnp.int32), axis=1)


def rms_scale(rows):
    return lax.rsqrt(jnp.mean(rows * rows, axis=-1, keepdims=True) + EPSILON)


def norm_backward(d_normed, rows, scale, gain):
    unit = rows * scale
    d_unit = d_normed * gain
    gain_term = jnp.sum(d_normed * unit, axis=0)
    d_rows = scale * (d_unit - unit * jnp.mean(d_unit * unit, axis=-1, keepdims=True))
    return (d_rows, gain_term)


def dot(left, right, dims):
    return lax.dot_general(left, right, ((dims[0], dims[1]), ((), ())), preferred_element_type=jnp.float32)


def seen_mask(row0, rows, cols, q_seg, k_seg):
    q_pos = row0 + lax.broadcasted_iota(jnp.int32, (rows, cols), 0)
    k_pos = lax.broadcasted_iota(jnp.int32, (rows, cols), 1)
    return (k_pos <= q_pos) & ((k_seg == 0) | (k_seg == q_seg))


def attend_kernel(heads, block, q_ref, k_ref, v_ref, q_seg_ref, k_seg_ref, o_ref, lse_ref, top_ref):
    size = q_ref.shape[0]
    tops = [jnp.full((1, 1), NEGATIVE, jnp.float32)] * heads
    for i in range(size // block):
        rows, cols = pl.ds(i * block, block), (i + 1) * block
        live = seen_mask(i * block, block, cols, q_seg_ref[rows, :], k_seg_ref[:, :cols])
        keys, values = k_ref[:cols, :], v_ref[:cols, :]
        for h in range(heads):
            span = slice(h * HEAD_DIM, (h + 1) * HEAD_DIM)
            scores = dot(q_ref[rows, span], keys, ((1,), (1,))) * SCALE
            scores = jnp.where(live, scores, NEGATIVE)
            peak = jnp.max(scores, axis=-1, keepdims=True)
            weights = jnp.exp(scores - peak)
            total = jnp.sum(weights, axis=-1, keepdims=True)
            out = dot(weights.astype(jnp.bfloat16), values, ((1,), (0,)))
            o_ref[rows, span] = (out / total).astype(jnp.bfloat16)
            lse_ref[rows, h : h + 1] = peak + jnp.log(total)
            tops[h] = jnp.maximum(tops[h], jnp.max(peak, axis=0, keepdims=True))
    for h in range(heads):
        top_ref[:, h : h + 1] = tops[h]


def attend(queries, keys, values, q_seg, k_seg):
    size, width = queries.shape
    heads = width // HEAD_DIM
    return pl.pallas_call(
        functools.partial(attend_kernel, heads, math.gcd(size, 256)),
        out_shape=(
            jax.ShapeDtypeStruct((size, width), jnp.bfloat16),
            jax.ShapeDtypeStruct((size, heads), jnp.float32),
            jax.ShapeDtypeStruct((1, heads), jnp.float32),
        ),
        compiler_params=pltpu.CompilerParams(vmem_limit_bytes=48 * MIB),
    )(queries, keys, values, q_seg, k_seg)


def attend_back_kernel(
    heads, block, q_ref, k_ref, v_ref, o_ref, do_ref, lse_ref, q_seg_ref, k_seg_ref, dq_ref, dk_ref, dv_ref, dk_sum, dv_sum
):
    size = q_ref.shape[0]
    dk_sum[...] = jnp.zeros_like(dk_sum)
    dv_sum[...] = jnp.zeros_like(dv_sum)
    for i in range(size // block):
        rows, cols = pl.ds(i * block, block), (i + 1) * block
        live = seen_mask(i * block, block, cols, q_seg_ref[rows, :], k_seg_ref[:, :cols])
        keys, values = k_ref[:cols, :], v_ref[:cols, :]
        for h in range(heads):
            span = slice(h * HEAD_DIM, (h + 1) * HEAD_DIM)
            queries, d_out = q_ref[rows, span], do_ref[rows, span]
            delta = jnp.sum(d_out.astype(jnp.float32) * o_ref[rows, span].astype(jnp.float32), axis=-1, keepdims=True)
            scores = dot(queries, keys, ((1,), (1,))) * SCALE
            probs = jnp.where(live, jnp.exp(scores - lse_ref[rows, h : h + 1]), 0.0)
            d_probs = dot(d_out, values, ((1,), (1,)))
            d_scores = (probs * (d_probs - delta)).astype(jnp.bfloat16)
            dq_ref[rows, span] = (dot(d_scores, keys, ((1,), (0,))) * SCALE).astype(jnp.bfloat16)
            dk_sum[:cols, :] += dot(d_scores, queries, ((0,), (0,)))
            dv_sum[:cols, :] += dot(probs.astype(jnp.bfloat16), d_out, ((0,), (0,)))
    dk_ref[...] = (dk_sum[...] * SCALE).astype(jnp.bfloat16)
    dv_ref[...] = dv_sum[...].astype(jnp.bfloat16)


def attend_back(queries, keys, values, out, d_out, lse, q_seg, k_seg):
    size, width = queries.shape
    heads = width // HEAD_DIM
    like_kv = jax.ShapeDtypeStruct((size, HEAD_DIM), jnp.bfloat16)
    return pl.pallas_call(
        functools.partial(attend_back_kernel, heads, math.gcd(size, 256)),
        out_shape=(jax.ShapeDtypeStruct((size, width), jnp.bfloat16), like_kv, like_kv),
        scratch_shapes=[pltpu.VMEM((size, HEAD_DIM), jnp.float32)] * 2,
        compiler_params=pltpu.CompilerParams(vmem_limit_bytes=48 * MIB),
    )(queries, keys, values, out, d_out, lse, q_seg, k_seg)


def split_heads(w, parts):
    rows = w.shape[0]
    q_width, kv_width = HEADS * HEAD_DIM, KV_HEADS * HEAD_DIM
    copies = max(1, parts // KV_HEADS)
    q = w[:, :q_width].reshape(rows, parts, q_width // parts)
    k = w[:, q_width : q_width + kv_width].reshape(rows, parts // copies, 1, -1)
    v = w[:, q_width + kv_width :].reshape(rows, parts // copies, 1, -1)
    k, v = (jnp.broadcast_to(a, (rows, parts // copies, copies, a.shape[3])).reshape(rows, parts, -1) for a in (k, v))
    return jnp.concatenate([q, k, v], axis=2)


def join_heads(grads, parts):
    rows = grads.shape[0]
    copies = max(1, parts // KV_HEADS)
    q_part = HEADS * HEAD_DIM // parts
    kv_part = (grads.shape[2] - q_part) // 2
    q = grads[:, :, :q_part].reshape(rows, -1)
    k, v = (
        jnp.sum(grads[:, :, at : at + kv_part].reshape(rows, parts // copies, copies, kv_part), axis=2).reshape(rows, -1)
        for at in (q_part, q_part + kv_part)
    )
    return jnp.concatenate([q, k, v], axis=1)


def per_device(n_ctx, n_shard, tokens, lengths, cotangent, w_qkv, w_out, w_gate_up, w_down, gain_attn, gain_mlp):
    count, width = tokens.shape[1:]
    n = n_ctx * n_shard
    w_rows = w_qkv.shape[0]
    ff_part = w_down.shape[0]
    q_part = HEADS * HEAD_DIM // n_ctx
    rows = tokens.reshape(count, width).astype(jnp.float32)
    grad_rows = cotangent.reshape(count, width).astype(jnp.float32)
    size = count * n_ctx
    positions = jnp.arange(size, dtype=jnp.int32)
    seg = segment_ids(positions, lengths[0])
    q_seg, k_seg = seg.reshape(size, 1), seg.reshape(1, size)

    gains = lax.all_gather(jnp.stack([gain_attn, gain_mlp]), EVERY, axis=1, tiled=True).astype(jnp.float32)
    gain_one, gain_two = gains[0], gains[1]

    qkv_cols = lax.all_to_all(split_heads(w_qkv, n_ctx), "ctx", split_axis=1, concat_axis=1, tiled=True)
    qkv_cols = qkv_cols.reshape(w_rows, n_ctx, -1).transpose(1, 0, 2)
    qkv_mine = lax.all_gather(qkv_cols, "shard", axis=1, tiled=True).reshape(width, -1)
    out_mine = lax.all_gather(w_out, "shard", axis=0, tiled=True)
    gate_up_mine = lax.all_to_all(w_gate_up.reshape(w_rows, 2, n, ff_part), EVERY, split_axis=2, concat_axis=0, tiled=True)
    gate_up_mine = gate_up_mine.reshape(width, 2 * ff_part)

    scale_one = rms_scale(rows)
    normed_one = lax.all_gather((rows * scale_one * gain_one).astype(jnp.bfloat16), "ctx", axis=0, tiled=True)
    projected = dot(normed_one, qkv_mine, ((1,), (0,))).astype(jnp.bfloat16)
    kv_part = (projected.shape[1] - q_part) // 2
    queries, keys, values = (
        projected[:, :q_part],
        projected[:, q_part : q_part + kv_part],
        projected[:, q_part + kv_part :],
    )
    attn_out, lse, tops = attend(queries, keys, values, q_seg, k_seg)
    out_term = dot(attn_out, out_mine, ((1,), (0,))).astype(jnp.bfloat16)
    attn_proj = lax.psum_scatter(out_term, "ctx", scatter_dimension=0, tiled=True)
    mid = rows + BRANCH * attn_proj.astype(jnp.float32)
    head_top = lax.all_gather(lax.pmax(tops, "shard"), "ctx", axis=1, tiled=True).reshape(HEADS)
    clip = CLIP_TARGET / jnp.maximum(head_top, CLIP_TARGET)

    scale_two = rms_scale(mid)
    d_mlp = lax.all_gather((BRANCH * grad_rows).astype(jnp.bfloat16), EVERY, axis=0, tiled=True)
    normed_two = lax.all_gather((mid * scale_two * gain_two).astype(jnp.bfloat16), EVERY, axis=0, tiled=True)
    gate_up = dot(normed_two, gate_up_mine, ((1,), (0,)))
    gate, up = gate_up[:, :ff_part], gate_up[:, ff_part:]
    sigma = jax.nn.sigmoid(gate)
    active = gate * sigma
    hidden = (active * up).astype(jnp.bfloat16)
    down_term = dot(hidden, w_down, ((1,), (0,))).astype(jnp.bfloat16)
    d_hidden = dot(d_mlp, w_down, ((1,), (1,)))
    d_gate = d_hidden * up * sigma * (1.0 + gate * (1.0 - sigma))
    d_up = d_hidden * active
    d_gate_up = jnp.concatenate([d_gate, d_up], axis=1).astype(jnp.bfloat16)
    normed_term = dot(d_gate_up, gate_up_mine, ((1,), (1,))).astype(jnp.bfloat16)
    grad_down = dot(hidden, d_mlp, ((0,), (0,)))
    gate_up_grad = dot(normed_two, d_gate_up, ((0,), (0,))).astype(jnp.bfloat16)
    mlp_proj = lax.psum_scatter(down_term, EVERY, scatter_dimension=0, tiled=True)
    mixed = (mid + BRANCH * mlp_proj.astype(jnp.float32)).astype(jnp.bfloat16).reshape(1, count, width)
    d_normed_two = lax.psum_scatter(normed_term, EVERY, scatter_dimension=0, tiled=True).astype(jnp.float32)
    grad_gate_up = lax.all_to_all(gate_up_grad.reshape(n * w_rows, 2, 1, ff_part), EVERY, split_axis=0, concat_axis=2, tiled=True)
    grad_gate_up = grad_gate_up.reshape(w_rows, 2 * n * ff_part).astype(jnp.float32)
    d_mid_norm, gain_two_term = norm_backward(d_normed_two, mid, scale_two, gain_two)
    d_mid = grad_rows + d_mid_norm

    d_attn = lax.all_gather((BRANCH * d_mid).astype(jnp.bfloat16), "ctx", axis=0, tiled=True)
    grad_out = lax.psum_scatter(dot(attn_out, d_attn, ((0,), (0,))), "shard", scatter_dimension=0, tiled=True)
    d_heads = dot(d_attn, out_mine, ((1,), (1,))).astype(jnp.bfloat16)
    d_q, d_k, d_v = attend_back(queries, keys, values, attn_out, d_heads, lse, q_seg, k_seg)
    d_qkv = jnp.concatenate([d_q, d_k, d_v], axis=1)
    qkv_term = dot(d_qkv, qkv_mine, ((1,), (1,))).astype(jnp.bfloat16)
    d_normed_one = lax.psum_scatter(qkv_term, "ctx", scatter_dimension=0, tiled=True).astype(jnp.float32)
    qkv_grad = dot(normed_one, d_qkv, ((0,), (0,))).reshape(n_ctx, n_shard * w_rows, -1)
    qkv_grad = lax.psum_scatter(qkv_grad, "shard", scatter_dimension=1, tiled=True)
    qkv_grad = lax.all_to_all(qkv_grad, "ctx", split_axis=0, concat_axis=0, tiled=True)
    grad_qkv = join_heads(qkv_grad.transpose(1, 0, 2), n_ctx)
    d_rows_norm, gain_one_term = norm_backward(d_normed_one, rows, scale_one, gain_one)
    grad_tokens = (d_mid + d_rows_norm).reshape(1, count, width)
    gain_terms = lax.psum_scatter(jnp.stack([gain_one_term, gain_two_term]), EVERY, scatter_dimension=1, tiled=True)
    return (mixed, grad_tokens, grad_qkv, grad_out, grad_gate_up, grad_down, gain_terms[0], gain_terms[1], clip)


def solution(mesh):
    by_token, by_row = P("shard", "ctx", None), P(EVERY, None)
    return jax.shard_map(
        functools.partial(per_device, mesh.shape["ctx"], mesh.shape["shard"]),
        mesh=mesh,
        in_specs=(by_token, P("shard", None), by_token, by_row, by_row, by_row, by_row, P(EVERY), P(EVERY)),
        out_specs=(by_token, by_token, by_row, by_row, by_row, by_row, P(EVERY), P(EVERY), P()),
        check_vma=False,
    )
```

```python
import functools
import math

import jax
import jax.numpy as jnp
from jax import lax
from jax.experimental import pallas as pl
from jax.experimental.pallas import tpu as pltpu
from jax.sharding import PartitionSpec as P

HEADS = 32
KV_HEADS = 8
HEAD_DIM = 64


SCALE = 0.015625
BRANCH = 0.22
EPSILON = 1e-05
CLIP_TARGET = 4.0
NEGATIVE = -1e30
MIB = 1024 * 1024
EVERY = ("ctx", "shard")


def segment_ids(positions, lengths_row):
    bounds = jnp.cumsum(lengths_row)[:-1]
    return jnp.sum((positions[:, None] >= bounds[None, :]).astype(jnp.int32), axis=1)


def rms_scale(rows):
    return lax.rsqrt(jnp.mean(rows * rows, axis=-1, keepdims=True) + EPSILON)


def norm_backward(d_normed, rows, scale, gain):
    unit = rows * scale
    d_unit = d_normed * gain
    gain_term = jnp.sum(d_normed * unit, axis=0)
    d_rows = scale * (d_unit - unit * jnp.mean(d_unit * unit, axis=-1, keepdims=True))
    return (d_rows, gain_term)


def dot(left, right, dims):
    return lax.dot_general(left, right, ((dims[0], dims[1]), ((), ())), preferred_element_type=jnp.float32)


def seen_mask(row0, rows, cols, q_seg, k_seg):
    q_pos = row0 + lax.broadcasted_iota(jnp.int32, (rows, cols), 0)
    k_pos = lax.broadcasted_iota(jnp.int32, (rows, cols), 1)
    return (k_pos <= q_pos) & ((k_seg == 0) | (k_seg == q_seg))


def attend_kernel(heads, block, q_ref, k_ref, v_ref, q_seg_ref, k_seg_ref, o_ref, lse_ref, top_ref):
    size = q_ref.shape[0]
    tops = [jnp.full((1, 1), NEGATIVE, jnp.float32)] * heads
    for i in range(size // block):
        rows, cols = pl.ds(i * block, block), (i + 1) * block
        live = seen_mask(i * block, block, cols, q_seg_ref[rows, :], k_seg_ref[:, :cols])
        keys, values = k_ref[:cols, :], v_ref[:cols, :]
        for h in range(heads):
            span = slice(h * HEAD_DIM, (h + 1) * HEAD_DIM)
            scores = dot(q_ref[rows, span], keys, ((1,), (1,))) * SCALE
            scores = jnp.where(live, scores, NEGATIVE)
            peak = jnp.max(scores, axis=-1, keepdims=True)
            weights = jnp.exp(scores - peak)
            total = jnp.sum(weights, axis=-1, keepdims=True)
            out = dot(weights.astype(jnp.bfloat16), values, ((1,), (0,)))
            o_ref[rows, span] = (out / total).astype(jnp.bfloat16)
            lse_ref[rows, h : h + 1] = peak + jnp.log(total)
            tops[h] = jnp.maximum(tops[h], jnp.max(peak, axis=0, keepdims=True))
    for h in range(heads):
        top_ref[:, h : h + 1] = tops[h]


def attend(queries, keys, values, q_seg, k_seg):
    size, width = queries.shape
    heads = width // HEAD_DIM
    return pl.pallas_call(
        functools.partial(attend_kernel, heads, math.gcd(size, 256)),
        out_shape=(
            jax.ShapeDtypeStruct((size, width), jnp.bfloat16),
            jax.ShapeDtypeStruct((size, heads), jnp.float32),
            jax.ShapeDtypeStruct((1, heads), jnp.float32),
        ),
        compiler_params=pltpu.CompilerParams(vmem_limit_bytes=48 * MIB),
    )(queries, keys, values, q_seg, k_seg)


def attend_back_kernel(
    heads, block, q_ref, k_ref, v_ref, o_ref, do_ref, lse_ref, q_seg_ref, k_seg_ref, dq_ref, dk_ref, dv_ref, dk_sum, dv_sum
):
    size = q_ref.shape[0]
    dk_sum[...] = jnp.zeros_like(dk_sum)
    dv_sum[...] = jnp.zeros_like(dv_sum)
    for i in range(size // block):
        rows, cols = pl.ds(i * block, block), (i + 1) * block
        live = seen_mask(i * block, block, cols, q_seg_ref[rows, :], k_seg_ref[:, :cols])
        keys, values = k_ref[:cols, :], v_ref[:cols, :]
        for h in range(heads):
            span = slice(h * HEAD_DIM, (h + 1) * HEAD_DIM)
            queries, d_out = q_ref[rows, span], do_ref[rows, span]
            delta = jnp.sum(d_out.astype(jnp.float32) * o_ref[rows, span].astype(jnp.float32), axis=-1, keepdims=True)
            scores = dot(queries, keys, ((1,), (1,))) * SCALE
            probs = jnp.where(live, jnp.exp(scores - lse_ref[rows, h : h + 1]), 0.0)
            d_probs = dot(d_out, values, ((1,), (1,)))
            d_scores = (probs * (d_probs - delta)).astype(jnp.bfloat16)
            dq_ref[rows, span] = (dot(d_scores, keys, ((1,), (0,))) * SCALE).astype(jnp.bfloat16)
            dk_sum[:cols, :] += dot(d_scores, queries, ((0,), (0,)))
            dv_sum[:cols, :] += dot(probs.astype(jnp.bfloat16), d_out, ((0,), (0,)))
    dk_ref[...] = (dk_sum[...] * SCALE).astype(jnp.bfloat16)
    dv_ref[...] = dv_sum[...].astype(jnp.bfloat16)


def attend_back(queries, keys, values, out, d_out, lse, q_seg, k_seg):
    size, width = queries.shape
    heads = width // HEAD_DIM
    like_kv = jax.ShapeDtypeStruct((size, HEAD_DIM), jnp.bfloat16)
    return pl.pallas_call(
        functools.partial(attend_back_kernel, heads, math.gcd(size, 256)),
        out_shape=(jax.ShapeDtypeStruct((size, width), jnp.bfloat16), like_kv, like_kv),
        scratch_shapes=[pltpu.VMEM((size, HEAD_DIM), jnp.float32)] * 2,
        compiler_params=pltpu.CompilerParams(vmem_limit_bytes=48 * MIB),
    )(queries, keys, values, out, d_out, lse, q_seg, k_seg)


def remote(src, dst, send_sem, recv_sem, device):
    return pltpu.make_async_remote_copy(
        src_ref=src, dst_ref=dst, send_sem=send_sem, recv_sem=recv_sem, device_id=device, device_id_type=pl.DeviceIdType.MESH
    )


def greet(devices, extra):
    barrier = pltpu.get_barrier_semaphore()
    count = len(devices)
    for device in devices:
        pl.semaphore_signal(barrier, inc=1, device_id=device, device_id_type=pl.DeviceIdType.MESH)
    for condition, device in extra:

        @pl.when(condition)
        def _():
            pl.semaphore_signal(barrier, inc=1, device_id=device, device_id_type=pl.DeviceIdType.MESH)

        count = count + condition.astype(jnp.int32)
    pl.semaphore_wait(barrier, count)


def add_rows(target, sources, rows, keep=None, step=32):
    @pl.loop(0, rows // step)
    def _(i):
        part = pl.ds(pl.multiple_of(i * step, step), step)
        total = target[part, :].astype(jnp.float32)
        for source in sources:
            total = total + source[part, :].astype(jnp.float32)
        if keep is None:
            target[part, :] = total.astype(jnp.bfloat16)
        else:
            keep[part, :] = total


def mlp_kernel(
    line, blk, part, normed_ref, d_mlp_ref, gate_up_ref, down_ref,
    mlp_ref, d_normed_ref, gate_up_grad_ref, down_grad_ref,
    act, land, line_land, w_gu, w_down, acc_gu, acc_down, hid, d_gu, sib_gu, sib_down,
    z_send, z_recv, p_send, p_recv, f_send, f_recv, r2_send, r2_recv, r3_send, r3_recv, r4_send, r4_recv,
    w_send, w_recv, g_send, g_recv, own_sem, out_sem,
):
    c, z = lax.axis_index("ctx"), lax.axis_index("shard")
    q, core = c // 2, c % 2
    half = blk // 2
    width = w_down.shape[1]
    slot_rows = 4 * blk
    cx, cy, sibling = (c + 2 - 4 * (q % 2), z), (c + 4 - 8 * (q // 2), z), (c + 1 - 2 * core, z)
    qx, qy = q + 1 - 2 * (q % 2), q + 2 - 4 * (q // 2)
    qd = 3 - q
    up, down = (c, z + 1), (c, z - 1)
    has_up, has_down = z < line - 1, z > 0

    def source(k):
        if line == 1:
            return z * 0
        mirrored = z >= line // 2
        near = jnp.where(mirrored, line - 1 - z, z)
        turn = (k + 1) // 2
        both = near - turn if k % 2 == 1 else near + turn
        at = jnp.where(k <= 2 * near, both, k)
        return jnp.where(mirrored, line - 1 - at, at)

    def block(at, chip):
        return pl.multiple_of((at * 4 + chip) * blk, blk)

    def rows(tensor, at, chip, first=0, count=blk):
        return act.at[tensor, pl.ds(pl.multiple_of(block(at, chip) + first, half), count), :]

    greet([cx, cy, sibling], [(has_up, up), (has_down, down)])

    own = [
        pltpu.make_async_copy(normed_ref, rows(0, z, q), own_sem.at[0]),
        pltpu.make_async_copy(d_mlp_ref, rows(1, z, q), own_sem.at[1]),
    ]
    mine = [pl.ds(pl.multiple_of(core * part + extra, part), part) for extra in (0, 2 * part)]
    own_weights = [
        pltpu.make_async_copy(gate_up_ref.at[:, :part], w_gu.at[:, mine[0]], own_sem.at[2]),
        pltpu.make_async_copy(gate_up_ref.at[:, part:], w_gu.at[:, mine[1]], own_sem.at[3]),
        pltpu.make_async_copy(down_ref, w_down.at[mine[0], :], own_sem.at[4]),
    ]
    to_sibling = [
        remote(gate_up_ref.at[:, :part], w_gu.at[:, mine[0]], w_send.at[0], w_recv.at[0], sibling),
        remote(gate_up_ref.at[:, part:], w_gu.at[:, mine[1]], w_send.at[1], w_recv.at[1], sibling),
        remote(down_ref, w_down.at[mine[0], :], w_send.at[2], w_recv.at[2], sibling),
    ]
    theirs = [pl.ds(pl.multiple_of((1 - core) * part + extra, part), part) for extra in (0, 2 * part)]
    from_sibling = [
        remote(gate_up_ref.at[:, :part], w_gu.at[:, theirs[0]], w_send.at[0], w_recv.at[0], sibling),
        remote(gate_up_ref.at[:, part:], w_gu.at[:, theirs[1]], w_send.at[1], w_recv.at[1], sibling),
        remote(down_ref, w_down.at[theirs[0], :], w_send.at[2], w_recv.at[2], sibling),
    ]

    def line_copy(tensor, at, way):
        ref = rows(tensor, at, q)
        return remote(ref, ref, z_send.at[tensor, at, way], z_recv.at[tensor, at], (up, down)[way])

    def plane_copies(tensor, at):
        copies = []
        for i, (device, first) in enumerate(((cx, 0), (cy, half), (cx, half), (cy, 0))):
            ref = rows(tensor, at, q, first, half)
            copies.append(remote(ref, ref, p_send.at[tensor, at, i], p_recv.at[tensor, at, i], device))
        return copies

    def plane_arrivals(tensor, at):
        arrivals = []
        for i, (device, chip, first) in enumerate(((cx, qx, 0), (cy, qy, half), (cx, qx, half), (cy, qy, 0))):
            ref = rows(tensor, at, chip, first, half)
            arrivals.append(remote(ref, ref, p_send.at[tensor, at, i], p_recv.at[tensor, at, i], device))
        return arrivals

    def onward_copies(tensor, at):
        first, second = rows(tensor, at, qx, 0, half), rows(tensor, at, qy, half, half)
        return [
            remote(first, first, f_send.at[tensor, at, 0], f_recv.at[tensor, at, 0], cy),
            remote(second, second, f_send.at[tensor, at, 1], f_recv.at[tensor, at, 1], cx),
        ]

    def onward_arrivals(tensor, at):
        first, second = rows(tensor, at, qd, 0, half), rows(tensor, at, qd, half, half)
        return [
            remote(first, first, f_send.at[tensor, at, 0], f_recv.at[tensor, at, 0], cy),
            remote(second, second, f_send.at[tensor, at, 1], f_recv.at[tensor, at, 1], cx),
        ]

    def send_line(tensor, at, condition, way):
        @pl.when(condition)
        def _():
            line_copy(tensor, at, way).start()

    def wait_line(tensor, at, condition, way):
        @pl.when(condition)
        def _():
            line_copy(tensor, at, way).wait_send()

    def step_a(k):
        at = source(k)
        for tensor in (0, 1):
            if k > 0:
                line_copy(tensor, at, 0).wait_recv()
                send_line(tensor, at, (at < z) & has_up, 0)
                send_line(tensor, at, (at > z) & has_down, 1)
            for copy in plane_copies(tensor, at):
                copy.start()

    def step_b(k):
        at = source(k)
        for tensor in (0, 1):
            arrivals = plane_arrivals(tensor, at)
            onward = onward_copies(tensor, at)
            for i in (0, 1):
                arrivals[i].wait_recv()
                onward[i].start()

    def step_c(k):
        at = source(k)
        for tensor in (0, 1):
            for copy in plane_arrivals(tensor, at)[2:] + onward_arrivals(tensor, at):
                copy.wait_recv()
            for copy in plane_copies(tensor, at) + onward_copies(tensor, at):
                copy.wait_send()
            wait_line(tensor, at, (at <= z) & has_up, 0)
            wait_line(tensor, at, (at >= z) & has_down, 1)

    def compute(k):
        slot = pl.ds(pl.multiple_of(source(k) * slot_rows, slot_rows), slot_rows)
        tile = 256 if part % 256 == 0 else part

        @pl.loop(0, 2 * part // tile)
        def _(j):
            span = pl.ds(pl.multiple_of(j * tile, tile), tile)
            upper = pl.ds(pl.multiple_of(j * tile + 2 * part, tile), tile)
            gate = dot(act[0, slot, :], w_gu[:, span], ((1,), (0,)))
            above = dot(act[0, slot, :], w_gu[:, upper], ((1,), (0,)))
            d_hidden = dot(act[1, slot, :], w_down[span, :], ((1,), (1,)))
            sigma = jax.nn.sigmoid(gate)
            active = gate * sigma
            hid[:, span] = (active * above).astype(jnp.bfloat16)
            d_gu[:, span] = (d_hidden * above * sigma * (1.0 + gate * (1.0 - sigma))).astype(jnp.bfloat16)
            d_gu[:, upper] = (d_hidden * active).astype(jnp.bfloat16)

        @pl.loop(0, width // 256)
        def _(j):
            span = pl.ds(pl.multiple_of(j * 256, 256), 256)
            down_term = dot(hid[...], act[1, slot, span], ((0,), (0,)))
            gate_up_term = dot(act[0, slot, span], d_gu[...], ((0,), (0,)))
            if k > 0:
                down_term = down_term + acc_down[:, span]
                gate_up_term = gate_up_term + acc_gu[span, :]
            acc_down[:, span] = down_term
            acc_gu[span, :] = gate_up_term
            act[1, slot, span] = dot(hid[...], w_down[:, span], ((1,), (0,))).astype(jnp.bfloat16)
            act[0, slot, span] = dot(d_gu[...], w_gu[span, :], ((1,), (1,))).astype(jnp.bfloat16)

    def landing(tensor, at, first, count):
        return land.at[tensor, at, pl.ds(first, count), :]

    def second_copies(tensor, at):
        return [
            remote(rows(tensor, at, qd, 0, half), landing(tensor, at, 2 * blk, half), r2_send.at[tensor, at, 0], r2_recv.at[tensor, at, 0], cy),
            remote(rows(tensor, at, qd, half, half), landing(tensor, at, 2 * blk + half, half), r2_send.at[tensor, at, 1], r2_recv.at[tensor, at, 1], cx),
        ]

    def third_copies(tensor, at):
        copies = []
        for i, (device, chip, first, lands) in enumerate(((cx, qx, 0, 0), (cy, qy, half, blk + half), (cx, qx, half, half), (cy, qy, 0, blk))):
            copies.append(
                remote(rows(tensor, at, chip, first, half), landing(tensor, at, lands, half), r3_send.at[tensor, at, i], r3_recv.at[tensor, at, i], device)
            )
        return copies

    def reduce_a(k):
        at = source(k)
        for tensor in (1, 0):
            for copy in second_copies(tensor, at) + third_copies(tensor, at)[2:]:
                copy.start()

    def reduce_b(k):
        at = source(k)
        for tensor in (1, 0):
            for i, (chip, first) in enumerate(((qx, 0), (qy, half))):
                second_copies(tensor, at)[i].wait_recv()
                add_rows(rows(tensor, at, chip, first, half), [landing(tensor, at, 2 * blk + first, half)], half)
                third_copies(tensor, at)[i].start()

    def sum_copy(tensor, at, way):
        place = jnp.where((way == 1) & (at == z - 1), line, at)
        return remote(rows(tensor, at, q), line_land.at[tensor, place], r4_send.at[tensor, at], r4_recv.at[tensor, place], (up, down)[way])

    def reduce_c(k):
        at = source(k)
        results = (d_normed_ref, mlp_ref)
        for tensor in (1, 0):
            for copy in third_copies(tensor, at):
                copy.wait_recv()
            mine_rows = rows(tensor, at, q)
            plane = [landing(tensor, at, 0, blk), landing(tensor, at, blk, blk)]
            if k > 0:
                joined = ((at > z) & has_down) | ((at < z) & has_up)

                @pl.when(joined)
                def _():
                    arrival = remote(mine_rows, line_land.at[tensor, at], r4_send.at[tensor, at], r4_recv.at[tensor, at], sibling)
                    arrival.wait_recv()
                    add_rows(mine_rows, plane + [line_land.at[tensor, at]], blk)

                @pl.when(jnp.logical_not(joined))
                def _():
                    add_rows(mine_rows, plane, blk)

                @pl.when(at > z)
                def _():
                    sum_copy(tensor, at, 0).start()

                @pl.when(at < z)
                def _():
                    sum_copy(tensor, at, 1).start()

            else:
                add_rows(mine_rows, plane, blk, results[tensor])
                for condition, place in ((has_down, at), (has_up, line)):

                    @pl.when(condition)
                    def _():
                        remote(mine_rows, line_land.at[tensor, place], r4_send.at[tensor, at], r4_recv.at[tensor, place], sibling).wait_recv()
                        add_rows(results[tensor], [line_land.at[tensor, place]], blk, results[tensor])

    def reduce_end(k):
        at = source(k)
        for tensor in (1, 0):
            for copy in second_copies(tensor, at) + third_copies(tensor, at):
                copy.wait_send()
            if k > 0:
                sum_copy(tensor, at, 0).wait_send()

    def exchange_grads():
        gate_half, up_half = theirs[0], theirs[1]

        @pl.loop(0, width // 256)
        def _(j):
            span = pl.ds(pl.multiple_of(j * 256, 256), 256)
            w_gu[span, :part] = acc_gu[span, gate_half].astype(jnp.bfloat16)
            w_gu[span, part : 2 * part] = acc_gu[span, up_half].astype(jnp.bfloat16)

        w_down[:part, :] = acc_down[theirs[0], :].astype(jnp.bfloat16)
        for copy in grad_copies:
            copy.start()

    grad_copies = [
        remote(w_gu.at[:, : 2 * part], sib_gu, g_send.at[0], g_recv.at[0], sibling),
        remote(w_down.at[:part, :], sib_down, g_send.at[1], g_recv.at[1], sibling),
    ]
    grad_outs = [
        pltpu.make_async_copy(w_gu.at[:, 2 * part :], gate_up_grad_ref, out_sem.at[0]),
        pltpu.make_async_copy(acc_down.at[mine[0], :], down_grad_ref, out_sem.at[1]),
    ]

    def finish_grads():
        for copy in grad_copies:
            copy.wait_recv()

        @pl.loop(0, width // 256)
        def _(j):
            span = pl.ds(pl.multiple_of(j * 256, 256), 256)
            for i in (0, 1):
                cols = slice(i * part, (i + 1) * part)
                w_gu[span, 2 * part + i * part : 2 * part + (i + 1) * part] = (
                    acc_gu[span, mine[i]] + sib_gu[span, cols].astype(jnp.float32)
                ).astype(jnp.bfloat16)

        acc_down[mine[0], :] = acc_down[mine[0], :] + sib_down[...].astype(jnp.float32)
        for copy in grad_outs:
            copy.start()

    for copy in own:
        copy.start()
    for copy in own:
        copy.wait()
    for tensor in (0, 1):
        send_line(tensor, z, has_up, 0)
        send_line(tensor, z, has_down, 1)
    step_a(0)
    for copy in to_sibling + own_weights:
        copy.start()
    for k in range(line):
        if k + 1 < line:
            step_a(k + 1)
        step_b(k)
        if k == 0:
            for copy in own_weights:
                copy.wait()
            for copy in from_sibling:
                copy.wait_recv()
            for copy in to_sibling:
                copy.wait_send()
        else:
            step_c(k - 1)
            compute(k - 1)
            reduce_a(k - 1)
    step_c(line - 1)
    compute(line - 1)
    reduce_a(line - 1)
    exchange_grads()
    backwards = range(line - 1, -1, -1)
    for k in backwards:
        reduce_b(k)
    finish_grads()
    for k in backwards:
        reduce_c(k)
    for k in backwards:
        reduce_end(k)
    for copy in grad_copies:
        copy.wait_send()
    for copy in grad_outs:
        copy.wait()


def mlp_exchange(line, normed, d_mlp, gate_up, down):
    blk, width = normed.shape
    part = down.shape[0]
    any_spec, vmem_spec = pl.BlockSpec(memory_space=pl.ANY), pl.BlockSpec(memory_space=pltpu.VMEM)
    bf16, f32, dma = jnp.bfloat16, jnp.float32, pltpu.SemaphoreType.DMA
    return pl.pallas_call(
        functools.partial(mlp_kernel, line, blk, part),
        out_shape=(
            jax.ShapeDtypeStruct((blk, width), f32),
            jax.ShapeDtypeStruct((blk, width), f32),
            jax.ShapeDtypeStruct((width, 2 * part), bf16),
            jax.ShapeDtypeStruct((part, width), f32),
        ),
        in_specs=[any_spec] * 4,
        out_specs=(vmem_spec, vmem_spec, any_spec, any_spec),
        scratch_shapes=[
            pltpu.VMEM((2, line * 4 * blk, width), bf16),
            pltpu.VMEM((2, line, 3 * blk, width), bf16),
            pltpu.VMEM((2, line + 1, blk, width), bf16),
            pltpu.VMEM((width, 4 * part), bf16),
            pltpu.VMEM((2 * part, width), bf16),
            pltpu.VMEM((width, 4 * part), f32),
            pltpu.VMEM((2 * part, width), f32),
            pltpu.VMEM((4 * blk, 2 * part), bf16),
            pltpu.VMEM((4 * blk, 4 * part), bf16),
            pltpu.VMEM((width, 2 * part), bf16),
            pltpu.VMEM((part, width), bf16),
            dma((2, line, 2)),
            dma((2, line)),
            dma((2, line, 4)),
            dma((2, line, 4)),
            dma((2, line, 2)),
            dma((2, line, 2)),
            dma((2, line, 2)),
            dma((2, line, 2)),
            dma((2, line, 4)),
            dma((2, line, 4)),
            dma((2, line)),
            dma((2, line + 1)),
            dma((3,)),
            dma((3,)),
            dma((2,)),
            dma((2,)),
            dma((5,)),
            dma((2,)),
        ],
        compiler_params=pltpu.CompilerParams(collective_id=0, has_side_effects=True, vmem_limit_bytes=63 * MIB),
    )(normed, d_mlp, gate_up, down)


def mlp_lax(normed_two, d_mlp, gate_up_mine, w_down):
    ff_part = w_down.shape[0]
    d_mlp = lax.all_gather(d_mlp, EVERY, axis=0, tiled=True)
    normed_two = lax.all_gather(normed_two, EVERY, axis=0, tiled=True)
    gate_up = dot(normed_two, gate_up_mine, ((1,), (0,)))
    gate, up = gate_up[:, :ff_part], gate_up[:, ff_part:]
    sigma = jax.nn.sigmoid(gate)
    active = gate * sigma
    hidden = (active * up).astype(jnp.bfloat16)
    down_term = dot(hidden, w_down, ((1,), (0,))).astype(jnp.bfloat16)
    d_hidden = dot(d_mlp, w_down, ((1,), (1,)))
    d_gate = d_hidden * up * sigma * (1.0 + gate * (1.0 - sigma))
    d_up = d_hidden * active
    d_gate_up = jnp.concatenate([d_gate, d_up], axis=1).astype(jnp.bfloat16)
    normed_term = dot(d_gate_up, gate_up_mine, ((1,), (1,))).astype(jnp.bfloat16)
    grad_down = dot(hidden, d_mlp, ((0,), (0,)))
    gate_up_grad = dot(normed_two, d_gate_up, ((0,), (0,))).astype(jnp.bfloat16)
    mlp_proj = lax.psum_scatter(down_term, EVERY, scatter_dimension=0, tiled=True).astype(jnp.float32)
    d_normed_two = lax.psum_scatter(normed_term, EVERY, scatter_dimension=0, tiled=True).astype(jnp.float32)
    return (mlp_proj, d_normed_two, gate_up_grad, grad_down)


def split_heads(w, parts):
    rows = w.shape[0]
    q_width, kv_width = HEADS * HEAD_DIM, KV_HEADS * HEAD_DIM
    copies = max(1, parts // KV_HEADS)
    q = w[:, :q_width].reshape(rows, parts, q_width // parts)
    k = w[:, q_width : q_width + kv_width].reshape(rows, parts // copies, 1, -1)
    v = w[:, q_width + kv_width :].reshape(rows, parts // copies, 1, -1)
    k, v = (jnp.broadcast_to(a, (rows, parts // copies, copies, a.shape[3])).reshape(rows, parts, -1) for a in (k, v))
    return jnp.concatenate([q, k, v], axis=2)


def join_heads(grads, parts):
    rows = grads.shape[0]
    copies = max(1, parts // KV_HEADS)
    q_part = HEADS * HEAD_DIM // parts
    kv_part = (grads.shape[2] - q_part) // 2
    q = grads[:, :, :q_part].reshape(rows, -1)
    k, v = (
        jnp.sum(grads[:, :, at : at + kv_part].reshape(rows, parts // copies, copies, kv_part), axis=2).reshape(rows, -1)
        for at in (q_part, q_part + kv_part)
    )
    return jnp.concatenate([q, k, v], axis=1)


def per_device(n_ctx, n_shard, tokens, lengths, cotangent, w_qkv, w_out, w_gate_up, w_down, gain_attn, gain_mlp):
    count, width = tokens.shape[1:]
    n = n_ctx * n_shard
    w_rows = w_qkv.shape[0]
    ff_part = w_down.shape[0]
    q_part = HEADS * HEAD_DIM // n_ctx
    rows = tokens.reshape(count, width).astype(jnp.float32)
    grad_rows = cotangent.reshape(count, width).astype(jnp.float32)
    size = count * n_ctx
    positions = jnp.arange(size, dtype=jnp.int32)
    seg = segment_ids(positions, lengths[0])
    q_seg, k_seg = seg.reshape(size, 1), seg.reshape(1, size)

    gains = lax.all_gather(jnp.stack([gain_attn, gain_mlp]), EVERY, axis=1, tiled=True).astype(jnp.float32)
    gain_one, gain_two = gains[0], gains[1]

    qkv_cols = lax.all_to_all(split_heads(w_qkv, n_ctx), "ctx", split_axis=1, concat_axis=1, tiled=True)
    qkv_cols = qkv_cols.reshape(w_rows, n_ctx, -1).transpose(1, 0, 2)
    qkv_mine = lax.all_gather(qkv_cols, "shard", axis=1, tiled=True).reshape(width, -1)
    out_mine = lax.all_gather(w_out, "shard", axis=0, tiled=True)
    gate_up_mine = lax.all_to_all(w_gate_up.reshape(w_rows, 2, n, ff_part), EVERY, split_axis=2, concat_axis=0, tiled=True)
    gate_up_mine = gate_up_mine.reshape(width, 2 * ff_part)

    scale_one = rms_scale(rows)
    normed_one = lax.all_gather((rows * scale_one * gain_one).astype(jnp.bfloat16), "ctx", axis=0, tiled=True)
    projected = dot(normed_one, qkv_mine, ((1,), (0,))).astype(jnp.bfloat16)
    kv_part = (projected.shape[1] - q_part) // 2
    queries, keys, values = (
        projected[:, :q_part],
        projected[:, q_part : q_part + kv_part],
        projected[:, q_part + kv_part :],
    )
    attn_out, lse, tops = attend(queries, keys, values, q_seg, k_seg)
    out_term = dot(attn_out, out_mine, ((1,), (0,))).astype(jnp.bfloat16)
    attn_proj = lax.psum_scatter(out_term, "ctx", scatter_dimension=0, tiled=True)
    mid = rows + BRANCH * attn_proj.astype(jnp.float32)
    head_top = lax.all_gather(lax.pmax(tops, "shard"), "ctx", axis=1, tiled=True).reshape(HEADS)
    clip = CLIP_TARGET / jnp.maximum(head_top, CLIP_TARGET)

    scale_two = rms_scale(mid)
    d_mlp = (BRANCH * grad_rows).astype(jnp.bfloat16)
    normed_two = (mid * scale_two * gain_two).astype(jnp.bfloat16)
    mlp = functools.partial(mlp_exchange, n_shard) if n_ctx == 8 else mlp_lax
    mlp_proj, d_normed_two, gate_up_grad, grad_down = mlp(normed_two, d_mlp, gate_up_mine, w_down)
    mixed = (mid + BRANCH * mlp_proj).astype(jnp.bfloat16).reshape(1, count, width)
    grad_gate_up = lax.all_to_all(gate_up_grad.reshape(n * w_rows, 2, 1, ff_part), EVERY, split_axis=0, concat_axis=2, tiled=True)
    grad_gate_up = grad_gate_up.reshape(w_rows, 2 * n * ff_part).astype(jnp.float32)
    d_mid_norm, gain_two_term = norm_backward(d_normed_two, mid, scale_two, gain_two)
    d_mid = grad_rows + d_mid_norm

    d_attn = lax.all_gather((BRANCH * d_mid).astype(jnp.bfloat16), "ctx", axis=0, tiled=True)
    grad_out = lax.psum_scatter(dot(attn_out, d_attn, ((0,), (0,))), "shard", scatter_dimension=0, tiled=True)
    d_heads = dot(d_attn, out_mine, ((1,), (1,))).astype(jnp.bfloat16)
    d_q, d_k, d_v = attend_back(queries, keys, values, attn_out, d_heads, lse, q_seg, k_seg)
    d_qkv = jnp.concatenate([d_q, d_k, d_v], axis=1)
    qkv_term = dot(d_qkv, qkv_mine, ((1,), (1,))).astype(jnp.bfloat16)
    d_normed_one = lax.psum_scatter(qkv_term, "ctx", scatter_dimension=0, tiled=True).astype(jnp.float32)
    qkv_grad = dot(normed_one, d_qkv, ((0,), (0,))).reshape(n_ctx, n_shard * w_rows, -1)
    qkv_grad = lax.psum_scatter(qkv_grad, "shard", scatter_dimension=1, tiled=True)
    qkv_grad = lax.all_to_all(qkv_grad, "ctx", split_axis=0, concat_axis=0, tiled=True)
    grad_qkv = join_heads(qkv_grad.transpose(1, 0, 2), n_ctx)
    d_rows_norm, gain_one_term = norm_backward(d_normed_one, rows, scale_one, gain_one)
    grad_tokens = (d_mid + d_rows_norm).reshape(1, count, width)
    gain_terms = lax.psum_scatter(jnp.stack([gain_one_term, gain_two_term]), EVERY, scatter_dimension=1, tiled=True)
    return (mixed, grad_tokens, grad_qkv, grad_out, grad_gate_up, grad_down, gain_terms[0], gain_terms[1], clip)


def solution(mesh):
    by_token, by_row = P("shard", "ctx", None), P(EVERY, None)
    return jax.shard_map(
        functools.partial(per_device, mesh.shape["ctx"], mesh.shape["shard"]),
        mesh=mesh,
        in_specs=(by_token, P("shard", None), by_token, by_row, by_row, by_row, by_row, P(EVERY), P(EVERY)),
        out_specs=(by_token, by_token, by_row, by_row, by_row, by_row, P(EVERY), P(EVERY), P()),
        check_vma=False,
    )
```

```python
import functools
import math

import jax
import jax.numpy as jnp
from jax import lax
from jax.experimental import pallas as pl
from jax.experimental.pallas import tpu as pltpu
from jax.sharding import PartitionSpec as P

HEADS = 32
KV_HEADS = 8
HEAD_DIM = 64


SCALE = 0.015625
BRANCH = 0.22
EPSILON = 1e-05
CLIP_TARGET = 4.0
NEGATIVE = -1e30
MIB = 1024 * 1024
EVERY = ("ctx", "shard")


def segment_ids(positions, lengths_row):
    bounds = jnp.cumsum(lengths_row)[:-1]
    return jnp.sum((positions[:, None] >= bounds[None, :]).astype(jnp.int32), axis=1)


def rms_scale(rows):
    return lax.rsqrt(jnp.mean(rows * rows, axis=-1, keepdims=True) + EPSILON)


def norm_backward(d_normed, rows, scale, gain):
    unit = rows * scale
    d_unit = d_normed * gain
    gain_term = jnp.sum(d_normed * unit, axis=0)
    d_rows = scale * (d_unit - unit * jnp.mean(d_unit * unit, axis=-1, keepdims=True))
    return (d_rows, gain_term)


def dot(left, right, dims):
    return lax.dot_general(left, right, ((dims[0], dims[1]), ((), ())), preferred_element_type=jnp.float32)


def seen_mask(row0, rows, cols, q_seg, k_seg):
    q_pos = row0 + lax.broadcasted_iota(jnp.int32, (rows, cols), 0)
    k_pos = lax.broadcasted_iota(jnp.int32, (rows, cols), 1)
    return (k_pos <= q_pos) & ((k_seg == 0) | (k_seg == q_seg))


def attend_kernel(heads, block, q_ref, k_ref, v_ref, q_seg_ref, k_seg_ref, o_ref, lse_ref, top_ref):
    size = q_ref.shape[0]
    tops = [jnp.full((1, 1), NEGATIVE, jnp.float32)] * heads
    for i in range(size // block):
        rows, cols = pl.ds(i * block, block), (i + 1) * block
        live = seen_mask(i * block, block, cols, q_seg_ref[rows, :], k_seg_ref[:, :cols])
        keys, values = k_ref[:cols, :], v_ref[:cols, :]
        for h in range(heads):
            span = slice(h * HEAD_DIM, (h + 1) * HEAD_DIM)
            scores = dot(q_ref[rows, span], keys, ((1,), (1,))) * SCALE
            scores = jnp.where(live, scores, NEGATIVE)
            peak = jnp.max(scores, axis=-1, keepdims=True)
            weights = jnp.exp(scores - peak)
            total = jnp.sum(weights, axis=-1, keepdims=True)
            out = dot(weights.astype(jnp.bfloat16), values, ((1,), (0,)))
            o_ref[rows, span] = (out / total).astype(jnp.bfloat16)
            lse_ref[rows, h : h + 1] = peak + jnp.log(total)
            tops[h] = jnp.maximum(tops[h], jnp.max(peak, axis=0, keepdims=True))
    for h in range(heads):
        top_ref[:, h : h + 1] = tops[h]


def attend(queries, keys, values, q_seg, k_seg):
    size, width = queries.shape
    heads = width // HEAD_DIM
    return pl.pallas_call(
        functools.partial(attend_kernel, heads, math.gcd(size, 256)),
        out_shape=(
            jax.ShapeDtypeStruct((size, width), jnp.bfloat16),
            jax.ShapeDtypeStruct((size, heads), jnp.float32),
            jax.ShapeDtypeStruct((1, heads), jnp.float32),
        ),
        compiler_params=pltpu.CompilerParams(vmem_limit_bytes=48 * MIB),
    )(queries, keys, values, q_seg, k_seg)


def attend_back_kernel(
    heads, block, q_ref, k_ref, v_ref, o_ref, do_ref, lse_ref, q_seg_ref, k_seg_ref, dq_ref, dk_ref, dv_ref, dk_sum, dv_sum
):
    size = q_ref.shape[0]
    dk_sum[...] = jnp.zeros_like(dk_sum)
    dv_sum[...] = jnp.zeros_like(dv_sum)
    for i in range(size // block):
        rows, cols = pl.ds(i * block, block), (i + 1) * block
        live = seen_mask(i * block, block, cols, q_seg_ref[rows, :], k_seg_ref[:, :cols])
        keys, values = k_ref[:cols, :], v_ref[:cols, :]
        for h in range(heads):
            span = slice(h * HEAD_DIM, (h + 1) * HEAD_DIM)
            queries, d_out = q_ref[rows, span], do_ref[rows, span]
            delta = jnp.sum(d_out.astype(jnp.float32) * o_ref[rows, span].astype(jnp.float32), axis=-1, keepdims=True)
            scores = dot(queries, keys, ((1,), (1,))) * SCALE
            probs = jnp.where(live, jnp.exp(scores - lse_ref[rows, h : h + 1]), 0.0)
            d_probs = dot(d_out, values, ((1,), (1,)))
            d_scores = (probs * (d_probs - delta)).astype(jnp.bfloat16)
            dq_ref[rows, span] = (dot(d_scores, keys, ((1,), (0,))) * SCALE).astype(jnp.bfloat16)
            dk_sum[:cols, :] += dot(d_scores, queries, ((0,), (0,)))
            dv_sum[:cols, :] += dot(probs.astype(jnp.bfloat16), d_out, ((0,), (0,)))
    dk_ref[...] = (dk_sum[...] * SCALE).astype(jnp.bfloat16)
    dv_ref[...] = dv_sum[...].astype(jnp.bfloat16)


def attend_back(queries, keys, values, out, d_out, lse, q_seg, k_seg):
    size, width = queries.shape
    heads = width // HEAD_DIM
    like_kv = jax.ShapeDtypeStruct((size, HEAD_DIM), jnp.bfloat16)
    return pl.pallas_call(
        functools.partial(attend_back_kernel, heads, math.gcd(size, 256)),
        out_shape=(jax.ShapeDtypeStruct((size, width), jnp.bfloat16), like_kv, like_kv),
        scratch_shapes=[pltpu.VMEM((size, HEAD_DIM), jnp.float32)] * 2,
        compiler_params=pltpu.CompilerParams(vmem_limit_bytes=48 * MIB),
    )(queries, keys, values, out, d_out, lse, q_seg, k_seg)


def remote(src, dst, send_sem, recv_sem, device):
    return pltpu.make_async_remote_copy(
        src_ref=src, dst_ref=dst, send_sem=send_sem, recv_sem=recv_sem, device_id=device, device_id_type=pl.DeviceIdType.MESH
    )


def greet(devices, extra):
    barrier = pltpu.get_barrier_semaphore()
    count = len(devices)
    for device in devices:
        pl.semaphore_signal(barrier, inc=1, device_id=device, device_id_type=pl.DeviceIdType.MESH)
    for condition, device in extra:

        @pl.when(condition)
        def _():
            pl.semaphore_signal(barrier, inc=1, device_id=device, device_id_type=pl.DeviceIdType.MESH)

        count = count + condition.astype(jnp.int32)
    pl.semaphore_wait(barrier, count)


def add_rows(target, sources, rows, keep=None, step=32):
    @pl.loop(0, rows // step)
    def _(i):
        part = pl.ds(pl.multiple_of(i * step, step), step)
        total = target[part, :].astype(jnp.float32)
        for source in sources:
            total = total + source[part, :].astype(jnp.float32)
        if keep is None:
            target[part, :] = total.astype(jnp.bfloat16)
        else:
            keep[part, :] = total


def mlp_kernel(
    line, blk, part, normed_ref, d_mlp_ref, gate_up_ref, down_ref,
    mlp_ref, d_normed_ref, gate_up_grad_ref, down_grad_ref,
    act, land, line_land, w_gu, w_down, acc_gu, acc_down, hid, d_gu, sib_gu, sib_down,
    z_send, z_recv, p_send, p_recv, f_send, f_recv, r2_send, r2_recv, r3_send, r3_recv, r4_send, r4_recv,
    w_send, w_recv, g_send, g_recv, own_sem, out_sem,
):
    c, z = lax.axis_index("ctx"), lax.axis_index("shard")
    q, core = c // 2, c % 2
    half = blk // 2
    width = w_down.shape[1]
    slot_rows = 4 * blk
    cx, cy, sibling = (c + 2 - 4 * (q % 2), z), (c + 4 - 8 * (q // 2), z), (c + 1 - 2 * core, z)
    qx, qy = q + 1 - 2 * (q % 2), q + 2 - 4 * (q // 2)
    qd = 3 - q
    up, down = (c, z + 1), (c, z - 1)
    has_up, has_down = z < line - 1, z > 0

    def source(k):
        if line == 1:
            return z * 0
        mirrored = z >= line // 2
        near = jnp.where(mirrored, line - 1 - z, z)
        turn = (k + 1) // 2
        both = near - turn if k % 2 == 1 else near + turn
        at = jnp.where(k <= 2 * near, both, k)
        return jnp.where(mirrored, line - 1 - at, at)

    def block(at, chip):
        return pl.multiple_of((at * 4 + chip) * blk, blk)

    def rows(tensor, at, chip, first=0, count=blk):
        return act.at[tensor, pl.ds(pl.multiple_of(block(at, chip) + first, half), count), :]

    greet([cx, cy, sibling], [(has_up, up), (has_down, down)])

    own = [
        pltpu.make_async_copy(normed_ref, rows(0, z, q), own_sem.at[0]),
        pltpu.make_async_copy(d_mlp_ref, rows(1, z, q), own_sem.at[1]),
    ]
    mine = [pl.ds(pl.multiple_of(core * part + extra, part), part) for extra in (0, 2 * part)]
    own_weights = [
        pltpu.make_async_copy(gate_up_ref.at[:, :part], w_gu.at[:, mine[0]], own_sem.at[2]),
        pltpu.make_async_copy(gate_up_ref.at[:, part:], w_gu.at[:, mine[1]], own_sem.at[3]),
        pltpu.make_async_copy(down_ref, w_down.at[mine[0], :], own_sem.at[4]),
    ]
    to_sibling = [
        remote(gate_up_ref.at[:, :part], w_gu.at[:, mine[0]], w_send.at[0], w_recv.at[0], sibling),
        remote(gate_up_ref.at[:, part:], w_gu.at[:, mine[1]], w_send.at[1], w_recv.at[1], sibling),
        remote(down_ref, w_down.at[mine[0], :], w_send.at[2], w_recv.at[2], sibling),
    ]
    theirs = [pl.ds(pl.multiple_of((1 - core) * part + extra, part), part) for extra in (0, 2 * part)]
    from_sibling = [
        remote(gate_up_ref.at[:, :part], w_gu.at[:, theirs[0]], w_send.at[0], w_recv.at[0], sibling),
        remote(gate_up_ref.at[:, part:], w_gu.at[:, theirs[1]], w_send.at[1], w_recv.at[1], sibling),
        remote(down_ref, w_down.at[theirs[0], :], w_send.at[2], w_recv.at[2], sibling),
    ]

    def line_copy(tensor, at, way):
        ref = rows(tensor, at, q)
        return remote(ref, ref, z_send.at[tensor, at, way], z_recv.at[tensor, at], (up, down)[way])

    def plane_copies(tensor, at):
        copies = []
        for i, (device, first) in enumerate(((cx, 0), (cy, half), (cx, half), (cy, 0))):
            ref = rows(tensor, at, q, first, half)
            copies.append(remote(ref, ref, p_send.at[tensor, at, i], p_recv.at[tensor, at, i], device))
        return copies

    def plane_arrivals(tensor, at):
        arrivals = []
        for i, (device, chip, first) in enumerate(((cx, qx, 0), (cy, qy, half), (cx, qx, half), (cy, qy, 0))):
            ref = rows(tensor, at, chip, first, half)
            arrivals.append(remote(ref, ref, p_send.at[tensor, at, i], p_recv.at[tensor, at, i], device))
        return arrivals

    def onward_copies(tensor, at):
        first, second = rows(tensor, at, qx, 0, half), rows(tensor, at, qy, half, half)
        return [
            remote(first, first, f_send.at[tensor, at, 0], f_recv.at[tensor, at, 0], cy),
            remote(second, second, f_send.at[tensor, at, 1], f_recv.at[tensor, at, 1], cx),
        ]

    def onward_arrivals(tensor, at):
        first, second = rows(tensor, at, qd, 0, half), rows(tensor, at, qd, half, half)
        return [
            remote(first, first, f_send.at[tensor, at, 0], f_recv.at[tensor, at, 0], cy),
            remote(second, second, f_send.at[tensor, at, 1], f_recv.at[tensor, at, 1], cx),
        ]

    def send_line(tensor, at, condition, way):
        @pl.when(condition)
        def _():
            line_copy(tensor, at, way).start()

    def wait_line(tensor, at, condition, way):
        @pl.when(condition)
        def _():
            line_copy(tensor, at, way).wait_send()

    def step_a(k):
        at = source(k)
        for tensor in (0, 1):
            if k > 0:
                line_copy(tensor, at, 0).wait_recv()
                send_line(tensor, at, (at < z) & has_up, 0)
                send_line(tensor, at, (at > z) & has_down, 1)
            for copy in plane_copies(tensor, at):
                copy.start()

    def step_b(k):
        at = source(k)
        for tensor in (0, 1):
            arrivals = plane_arrivals(tensor, at)
            onward = onward_copies(tensor, at)
            for i in (0, 1):
                arrivals[i].wait_recv()
                onward[i].start()

    def step_c(k):
        at = source(k)
        for tensor in (0, 1):
            for copy in plane_arrivals(tensor, at)[2:] + onward_arrivals(tensor, at):
                copy.wait_recv()
            for copy in plane_copies(tensor, at) + onward_copies(tensor, at):
                copy.wait_send()
            wait_line(tensor, at, (at <= z) & has_up, 0)
            wait_line(tensor, at, (at >= z) & has_down, 1)

    def compute(k):
        slot = pl.ds(pl.multiple_of(source(k) * slot_rows, slot_rows), slot_rows)
        tile = 256 if part % 256 == 0 else part

        @pl.loop(0, 2 * part // tile)
        def _(j):
            span = pl.ds(pl.multiple_of(j * tile, tile), tile)
            upper = pl.ds(pl.multiple_of(j * tile + 2 * part, tile), tile)
            gate = dot(act[0, slot, :], w_gu[:, span], ((1,), (0,)))
            above = dot(act[0, slot, :], w_gu[:, upper], ((1,), (0,)))
            d_hidden = dot(act[1, slot, :], w_down[span, :], ((1,), (1,)))
            sigma = jax.nn.sigmoid(gate)
            active = gate * sigma
            hid[:, span] = (active * above).astype(jnp.bfloat16)
            d_gu[:, span] = (d_hidden * above * sigma * (1.0 + gate * (1.0 - sigma))).astype(jnp.bfloat16)
            d_gu[:, upper] = (d_hidden * active).astype(jnp.bfloat16)

        @pl.loop(0, width // 256)
        def _(j):
            span = pl.ds(pl.multiple_of(j * 256, 256), 256)
            down_term = dot(hid[...], act[1, slot, span], ((0,), (0,)))
            gate_up_term = dot(act[0, slot, span], d_gu[...], ((0,), (0,)))
            if k > 0:
                down_term = down_term + acc_down[:, span]
                gate_up_term = gate_up_term + acc_gu[span, :]
            acc_down[:, span] = down_term
            acc_gu[span, :] = gate_up_term
            act[1, slot, span] = dot(hid[...], w_down[:, span], ((1,), (0,))).astype(jnp.bfloat16)
            act[0, slot, span] = dot(d_gu[...], w_gu[span, :], ((1,), (1,))).astype(jnp.bfloat16)

    def landing(tensor, at, first, count):
        return land.at[tensor, at, pl.ds(first, count), :]

    def second_copies(tensor, at):
        return [
            remote(rows(tensor, at, qd, 0, half), landing(tensor, at, 2 * blk, half), r2_send.at[tensor, at, 0], r2_recv.at[tensor, at, 0], cy),
            remote(rows(tensor, at, qd, half, half), landing(tensor, at, 2 * blk + half, half), r2_send.at[tensor, at, 1], r2_recv.at[tensor, at, 1], cx),
        ]

    def third_copies(tensor, at):
        copies = []
        for i, (device, chip, first, lands) in enumerate(((cx, qx, 0, 0), (cy, qy, half, blk + half), (cx, qx, half, half), (cy, qy, 0, blk))):
            copies.append(
                remote(rows(tensor, at, chip, first, half), landing(tensor, at, lands, half), r3_send.at[tensor, at, i], r3_recv.at[tensor, at, i], device)
            )
        return copies

    def reduce_a(k):
        at = source(k)
        for tensor in (1, 0):
            for copy in second_copies(tensor, at) + third_copies(tensor, at)[2:]:
                copy.start()

    def reduce_b(k):
        at = source(k)
        for tensor in (1, 0):
            for i, (chip, first) in enumerate(((qx, 0), (qy, half))):
                second_copies(tensor, at)[i].wait_recv()
                add_rows(rows(tensor, at, chip, first, half), [landing(tensor, at, 2 * blk + first, half)], half)
                third_copies(tensor, at)[i].start()

    def sum_copy(tensor, at, way):
        place = jnp.where((way == 1) & (at == z - 1), line, at)
        return remote(rows(tensor, at, q), line_land.at[tensor, place], r4_send.at[tensor, at], r4_recv.at[tensor, place], (up, down)[way])

    def reduce_c(k):
        at = source(k)
        results = (d_normed_ref, mlp_ref)
        for tensor in (1, 0):
            for copy in third_copies(tensor, at):
                copy.wait_recv()
            mine_rows = rows(tensor, at, q)
            plane = [landing(tensor, at, 0, blk), landing(tensor, at, blk, blk)]
            if k > 0:
                joined = ((at > z) & has_down) | ((at < z) & has_up)

                @pl.when(joined)
                def _():
                    arrival = remote(mine_rows, line_land.at[tensor, at], r4_send.at[tensor, at], r4_recv.at[tensor, at], sibling)
                    arrival.wait_recv()
                    add_rows(mine_rows, plane + [line_land.at[tensor, at]], blk)

                @pl.when(jnp.logical_not(joined))
                def _():
                    add_rows(mine_rows, plane, blk)

                @pl.when(at > z)
                def _():
                    sum_copy(tensor, at, 0).start()

                @pl.when(at < z)
                def _():
                    sum_copy(tensor, at, 1).start()

            else:
                add_rows(mine_rows, plane, blk, results[tensor])
                for condition, place in ((has_down, at), (has_up, line)):

                    @pl.when(condition)
                    def _():
                        remote(mine_rows, line_land.at[tensor, place], r4_send.at[tensor, at], r4_recv.at[tensor, place], sibling).wait_recv()
                        add_rows(results[tensor], [line_land.at[tensor, place]], blk, results[tensor])

    def reduce_end(k):
        at = source(k)
        for tensor in (1, 0):
            for copy in second_copies(tensor, at) + third_copies(tensor, at):
                copy.wait_send()
            if k > 0:
                sum_copy(tensor, at, 0).wait_send()

    def exchange_grads():
        gate_half, up_half = theirs[0], theirs[1]

        @pl.loop(0, width // 256)
        def _(j):
            span = pl.ds(pl.multiple_of(j * 256, 256), 256)
            w_gu[span, :part] = acc_gu[span, gate_half].astype(jnp.bfloat16)
            w_gu[span, part : 2 * part] = acc_gu[span, up_half].astype(jnp.bfloat16)

        w_down[:part, :] = acc_down[theirs[0], :].astype(jnp.bfloat16)
        for copy in grad_copies:
            copy.start()

    grad_copies = [
        remote(w_gu.at[:, : 2 * part], sib_gu, g_send.at[0], g_recv.at[0], sibling),
        remote(w_down.at[:part, :], sib_down, g_send.at[1], g_recv.at[1], sibling),
    ]
    grad_outs = [
        pltpu.make_async_copy(w_gu.at[:, 2 * part :], gate_up_grad_ref, out_sem.at[0]),
        pltpu.make_async_copy(acc_down.at[mine[0], :], down_grad_ref, out_sem.at[1]),
    ]

    def finish_grads():
        for copy in grad_copies:
            copy.wait_recv()

        @pl.loop(0, width // 256)
        def _(j):
            span = pl.ds(pl.multiple_of(j * 256, 256), 256)
            for i in (0, 1):
                cols = slice(i * part, (i + 1) * part)
                w_gu[span, 2 * part + i * part : 2 * part + (i + 1) * part] = (
                    acc_gu[span, mine[i]] + sib_gu[span, cols].astype(jnp.float32)
                ).astype(jnp.bfloat16)

        acc_down[mine[0], :] = acc_down[mine[0], :] + sib_down[...].astype(jnp.float32)
        for copy in grad_outs:
            copy.start()

    for copy in own:
        copy.start()
    for copy in own:
        copy.wait()
    for tensor in (0, 1):
        send_line(tensor, z, has_up, 0)
        send_line(tensor, z, has_down, 1)
    step_a(0)
    for copy in to_sibling + own_weights:
        copy.start()
    for k in range(line):
        if k + 1 < line:
            step_a(k + 1)
        step_b(k)
        if k == 0:
            for copy in own_weights:
                copy.wait()
            for copy in from_sibling:
                copy.wait_recv()
            for copy in to_sibling:
                copy.wait_send()
        else:
            step_c(k - 1)
            compute(k - 1)
            reduce_a(k - 1)
    step_c(line - 1)
    compute(line - 1)
    reduce_a(line - 1)
    exchange_grads()
    backwards = range(line - 1, -1, -1)
    for k in backwards:
        reduce_b(k)
    finish_grads()
    for k in backwards:
        reduce_c(k)
    for k in backwards:
        reduce_end(k)
    for copy in grad_copies:
        copy.wait_send()
    for copy in grad_outs:
        copy.wait()


def mlp_exchange(line, normed, d_mlp, gate_up, down):
    blk, width = normed.shape
    part = down.shape[0]
    any_spec, vmem_spec = pl.BlockSpec(memory_space=pl.ANY), pl.BlockSpec(memory_space=pltpu.VMEM)
    bf16, f32, dma = jnp.bfloat16, jnp.float32, pltpu.SemaphoreType.DMA
    return pl.pallas_call(
        functools.partial(mlp_kernel, line, blk, part),
        out_shape=(
            jax.ShapeDtypeStruct((blk, width), f32),
            jax.ShapeDtypeStruct((blk, width), f32),
            jax.ShapeDtypeStruct((width, 2 * part), bf16),
            jax.ShapeDtypeStruct((part, width), f32),
        ),
        in_specs=[any_spec] * 4,
        out_specs=(vmem_spec, vmem_spec, any_spec, any_spec),
        scratch_shapes=[
            pltpu.VMEM((2, line * 4 * blk, width), bf16),
            pltpu.VMEM((2, line, 3 * blk, width), bf16),
            pltpu.VMEM((2, line + 1, blk, width), bf16),
            pltpu.VMEM((width, 4 * part), bf16),
            pltpu.VMEM((2 * part, width), bf16),
            pltpu.VMEM((width, 4 * part), f32),
            pltpu.VMEM((2 * part, width), f32),
            pltpu.VMEM((4 * blk, 2 * part), bf16),
            pltpu.VMEM((4 * blk, 4 * part), bf16),
            pltpu.VMEM((width, 2 * part), bf16),
            pltpu.VMEM((part, width), bf16),
            dma((2, line, 2)),
            dma((2, line)),
            dma((2, line, 4)),
            dma((2, line, 4)),
            dma((2, line, 2)),
            dma((2, line, 2)),
            dma((2, line, 2)),
            dma((2, line, 2)),
            dma((2, line, 4)),
            dma((2, line, 4)),
            dma((2, line)),
            dma((2, line + 1)),
            dma((3,)),
            dma((3,)),
            dma((2,)),
            dma((2,)),
            dma((5,)),
            dma((2,)),
        ],
        compiler_params=pltpu.CompilerParams(collective_id=0, has_side_effects=True, vmem_limit_bytes=63 * MIB),
    )(normed, d_mlp, gate_up, down)


class Place:
    def __init__(self, line):
        self.line = line
        self.c, self.z = lax.axis_index("ctx"), lax.axis_index("shard")
        self.q, self.core = self.c // 2, self.c % 2
        self.me = self.c * line + self.z
        self.every = 8 * line
        self.cx, self.cy = (self.c + 2 - 4 * (self.q % 2), self.z), (self.c + 4 - 8 * (self.q // 2), self.z)
        self.sibling = (self.c + 1 - 2 * self.core, self.z)
        self.qx, self.qy, self.qd = self.q + 1 - 2 * (self.q % 2), self.q + 2 - 4 * (self.q // 2), 3 - self.q

    def peer(self, i):
        other = lax.rem(self.me + i, self.every)
        return other, (other // self.line, other % self.line)

    def greet_all(self):
        barrier = pltpu.get_barrier_semaphore()

        @pl.loop(1, self.every)
        def _(i):
            pl.semaphore_signal(barrier, inc=1, device_id=self.peer(i)[1], device_id_type=pl.DeviceIdType.MESH)

        pl.semaphore_wait(barrier, self.every - 1)

    def push_all(self, source, target, send_sems, recv_sems):
        @pl.loop(1, self.every)
        def _(i):
            other, device = self.peer(i)
            remote(source(other), target(self.me), send_sems.at[other], recv_sems.at[self.me], device).start()

    def wait_all(self, source, target, send_sems, recv_sems, sent=True):
        @pl.loop(1, self.every)
        def _(i):
            other, device = self.peer(i)
            copy = remote(source(other), target(other), send_sems.at[other], recv_sems.at[other], device)
            if sent:
                copy.wait_send()
            else:
                copy.wait_recv()


def plane_gather(at, buf, blk, sems):
    p_send, p_recv, f_send, f_recv, s_send, s_recv = sems
    half = blk // 2

    def rows(chip, core, first=0, count=half):
        return buf.at[pl.ds(pl.multiple_of((2 * chip + core) * blk + first, half), count), :]

    def same(ref, send, recv, device):
        return remote(ref, ref, send, recv, device)

    way = ((at.cx, at.qx, 0), (at.cy, at.qy, half), (at.cx, at.qx, half), (at.cy, at.qy, 0))

    def sent(i):
        return same(rows(at.q, at.core, way[i][2]), p_send.at[i], p_recv.at[i], way[i][0])

    def arriving(i):
        return same(rows(way[i][1], at.core, way[i][2]), p_send.at[i], p_recv.at[i], way[i][0])

    def onward(i):
        chip, first, device = ((at.qx, 0, at.cy), (at.qy, half, at.cx))[i]
        return same(rows(chip, at.core, first), f_send.at[i], f_recv.at[i], device)

    def passed(i):
        first, device = ((0, at.cy), (half, at.cx))[i]
        return same(rows(at.qd, at.core, first), f_send.at[i], f_recv.at[i], device)

    def across(i, core):
        if i == 0:
            ref = rows(at.q, core, 0, blk)
        elif i < 5:
            ref = rows(way[i - 1][1], core, way[i - 1][2])
        else:
            ref = rows(at.qd, core, (i - 5) * half)
        return same(ref, s_send.at[i], s_recv.at[i], at.sibling)

    def start():
        for i in range(4):
            sent(i).start()
        across(0, at.core).start()

    def finish():
        for i in (0, 1):
            arriving(i).wait_recv()
            onward(i).start()
            across(i + 1, at.core).start()
        for i in (2, 3):
            arriving(i).wait_recv()
            across(i + 1, at.core).start()
        for i in (0, 1):
            passed(i).wait_recv()
            across(i + 5, at.core).start()
        for i in range(7):
            across(i, 1 - at.core).wait_recv()

    def end():
        for i in range(4):
            sent(i).wait_send()
        for i in (0, 1):
            onward(i).wait_send()
        for i in range(7):
            across(i, at.core).wait_send()

    return start, finish, end


GATHER_SEMS = (4, 4, 2, 2, 7, 7)
REDUCE_SEMS = (4, 4, 2, 2, 4, 4)


def plane_reduce(at, term, core_land, land, blk, sems):
    s_send, s_recv, r2_send, r2_recv, r3_send, r3_recv = sems
    half = blk // 2
    chips = (at.qd, at.qx, at.qy, at.q)

    def rows(chip, core, first=0, count=half):
        return term.at[pl.ds(pl.multiple_of((2 * chip + core) * blk + first, half), count), :]

    def landed(first, count):
        return land.at[pl.ds(first, count), :]

    def across(i):
        return remote(rows(chips[i], 1 - at.core, 0, blk), core_land.at[i], s_send.at[i], s_recv.at[i], at.sibling)

    def second(i):
        first, device = ((0, at.cy), (half, at.cx))[i]
        return remote(rows(at.qd, at.core, first), landed(2 * blk + first, half), r2_send.at[i], r2_recv.at[i], device)

    def third(i):
        device, chip, first, lands = (
            (at.cx, at.qx, 0, 0), (at.cy, at.qy, half, blk + half), (at.cx, at.qx, half, half), (at.cy, at.qy, 0, blk)
        )[i]
        return remote(rows(chip, at.core, first), landed(lands, half), r3_send.at[i], r3_recv.at[i], device)

    def add_core(i):
        across(i).wait_recv()
        add_rows(rows(chips[i], at.core, 0, blk), [core_land.at[i]], blk)

    def give(i):
        across(i).start()

    def take(result):
        add_core(0)
        second(0).start()
        second(1).start()
        add_core(1)
        third(2).start()
        add_core(2)
        third(3).start()
        for i, (chip, first) in enumerate(((at.qx, 0), (at.qy, half))):
            second(i).wait_recv()
            add_rows(rows(chip, at.core, first), [landed(2 * blk + first, half)], half)
            third(i).start()
        add_core(3)
        for i in range(4):
            third(i).wait_recv()
        add_rows(rows(at.q, at.core, 0, blk), [landed(0, blk), landed(blk, blk)], blk, result)

    def end():
        for i in range(4):
            across(i).wait_send()
            third(i).wait_send()
        for i in (0, 1):
            second(i).wait_send()

    return give, take, end


def front_kernel(
    line, blk, q_part, kv_part,
    tokens_ref, gains_ref, w_qkv_ref, w_out_ref, q_seg_ref, k_seg_ref,
    mid_ref, normed_two_ref, qkv_ref, attn_ref, lse_ref, tops_ref, gain_ref, normed_ref, w_qkv_all_ref, w_out_all_ref,
    buf, term, core_land, land, w_qkv, w_out, gain_land, top_land, proj,
    *sems,
):
    at = Place(line)
    gather = plane_gather(at, buf, blk, sems[:6])
    reduce = plane_reduce(at, term, core_land, land, blk, sems[6:12])
    qkv_send, qkv_recv, gain_send, gain_recv, top_send, top_recv, out_send, out_recv, own_sem, write_sem = sems[12:]
    w_rows, width = w_out_ref.shape
    size = 8 * blk
    mine = pl.ds(pl.multiple_of(at.c * blk, blk), blk)

    own = [
        pltpu.make_async_copy(tokens_ref, buf.at[mine, :], own_sem.at[0]),
        pltpu.make_async_copy(gains_ref, gain_land.at[at.me], own_sem.at[1]),
        pltpu.make_async_copy(w_qkv_ref.at[at.c], w_qkv.at[at.me], own_sem.at[2]),
        pltpu.make_async_copy(w_out_ref, w_out.at[at.z], own_sem.at[3]),
    ]
    for copy in own:
        copy.start()
    at.greet_all()
    qkv_push = (lambda other: w_qkv_ref.at[other // line], lambda slot: w_qkv.at[slot], qkv_send, qkv_recv)
    gain_push = (lambda other: gains_ref, lambda slot: gain_land.at[slot], gain_send, gain_recv)
    top_push = (lambda other: top_land.at[at.me], lambda slot: top_land.at[slot], top_send, top_recv)
    at.push_all(*gain_push)
    own[0].wait()
    gather[0]()
    at.push_all(*qkv_push)

    def out_copy(i, slot):
        z = lax.rem(at.z + i, line)
        return z, remote(w_out_ref, w_out.at[slot(z)], out_send.at[z], out_recv.at[slot(z)], (at.c, z))

    for i in range(1, line):
        out_copy(i, lambda z: at.z)[1].start()
    gather[1]()
    for copy in own[1:]:
        copy.wait()
    at.wait_all(*gain_push, sent=False)
    for i in range(at.every // 2):
        pair = gain_land[2 * i].astype(jnp.float32) + gain_land[2 * i + 1].astype(jnp.float32)
        gain_ref[:, i * 128 : (i + 1) * 128] = pair[:8, :]
    gather[2]()
    at.wait_all(*gain_push)

    @pl.loop(0, size // 32)
    def _(i):
        part = pl.ds(pl.multiple_of(i * 32, 32), 32)
        rows = buf[part, :].astype(jnp.float32)
        buf[part, :] = (rows * rms_scale(rows) * gain_ref[0:1, :]).astype(jnp.bfloat16)

    writes = [
        pltpu.make_async_copy(buf, normed_ref, write_sem.at[0]),
        pltpu.make_async_copy(w_qkv, w_qkv_all_ref, write_sem.at[1]),
        pltpu.make_async_copy(w_out, w_out_all_ref, write_sem.at[2]),
    ]
    writes[0].start()
    at.wait_all(*qkv_push, sent=False)
    writes[1].start()

    @pl.loop(0, size // 256)
    def _(i):
        part = pl.ds(pl.multiple_of(i * 256, 256), 256)
        qkv_ref[part, :] = dot(buf[part, :], w_qkv[...].reshape(width, q_part + 2 * kv_part), ((1,), (0,))).astype(jnp.bfloat16)

    heads = q_part // HEAD_DIM
    block = math.gcd(size, 256)
    tops = [jnp.full((1, 1), NEGATIVE, jnp.float32)] * heads
    for i in range(size // block):
        rows, cols = pl.ds(i * block, block), (i + 1) * block
        live = seen_mask(i * block, block, cols, q_seg_ref[rows, :], k_seg_ref[:, :cols])
        keys, values = qkv_ref[:cols, q_part : q_part + kv_part], qkv_ref[:cols, q_part + kv_part :]
        for h in range(heads):
            span = slice(h * HEAD_DIM, (h + 1) * HEAD_DIM)
            scores = dot(qkv_ref[rows, span], keys, ((1,), (1,))) * SCALE
            scores = jnp.where(live, scores, NEGATIVE)
            peak = jnp.max(scores, axis=-1, keepdims=True)
            weights = jnp.exp(scores - peak)
            total = jnp.sum(weights, axis=-1, keepdims=True)
            out = dot(weights.astype(jnp.bfloat16), values, ((1,), (0,)))
            attn_ref[rows, span] = (out / total).astype(jnp.bfloat16)
            lse_ref[rows, h : h + 1] = peak + jnp.log(total)
            tops[h] = jnp.maximum(tops[h], jnp.max(peak, axis=0, keepdims=True))
    lanes = lax.broadcasted_iota(jnp.int32, (8, 128), 1)
    tile = jnp.full((8, 128), NEGATIVE, jnp.float32)
    for h in range(heads):
        tile = jnp.where(lanes == h, tops[h], tile)
    top_land[at.me] = tile
    at.push_all(*top_push)

    for i in range(1, line):
        out_copy(i, lambda z: z)[1].wait_recv()
    writes[2].start()
    for i, chip in enumerate((at.qd, at.qx, at.qy, at.q)):
        for core in (1 - at.core, at.core):
            part = pl.ds(pl.multiple_of((2 * chip + core) * blk, blk), blk)

            @pl.loop(0, width // 512)
            def _(j):
                span = pl.ds(pl.multiple_of(j * 512, 512), 512)
                matrix = w_out[:, :, span].reshape(line * w_rows, 512)
                term[part, span] = dot(attn_ref[part, :], matrix, ((1,), (0,))).astype(jnp.bfloat16)

        reduce[0](i)
    reduce[1](proj)

    own_again = pltpu.make_async_copy(tokens_ref, land.at[pl.ds(0, blk), :], own_sem.at[0])
    own_again.start()
    own_again.wait()

    @pl.loop(0, blk // 32)
    def _(i):
        part = pl.ds(pl.multiple_of(i * 32, 32), 32)
        rows = land[part, :].astype(jnp.float32) + BRANCH * proj[part, :]
        mid_ref[part, :] = rows
        normed_two_ref[part, :] = (rows * rms_scale(rows) * gain_ref[1:2, :]).astype(jnp.bfloat16)

    at.wait_all(*top_push, sent=False)
    tops_ref[...] = top_land[...]
    reduce[2]()
    at.wait_all(*qkv_push)
    at.wait_all(*top_push)
    for i in range(1, line):
        out_copy(i, lambda z: at.z)[1].wait_send()
    for copy in writes:
        copy.wait()


def front(line, tokens, gains, w_qkv, w_out, q_seg, k_seg):
    blk, width = tokens.shape
    w_rows, cols = w_out.shape[0], w_qkv.shape[2]
    size, every = 8 * blk, 8 * line
    q_part = HEADS * HEAD_DIM // 8
    kv_part = (cols - q_part) // 2
    heads = q_part // HEAD_DIM
    any_spec, vmem_spec = pl.BlockSpec(memory_space=pl.ANY), pl.BlockSpec(memory_space=pltpu.VMEM)
    bf16, f32, dma, out = jnp.bfloat16, jnp.float32, pltpu.SemaphoreType.DMA, jax.ShapeDtypeStruct
    return pl.pallas_call(
        functools.partial(front_kernel, line, blk, q_part, kv_part),
        out_shape=(
            out((blk, width), f32),
            out((blk, width), bf16),
            out((size, cols), bf16),
            out((size, q_part), bf16),
            out((size, heads), f32),
            out((every, 8, 128), f32),
            out((8, width), f32),
            out((size, width), bf16),
            out((every, w_rows, cols), bf16),
            out((line, w_rows, width), bf16),
        ),
        in_specs=[any_spec] * 4 + [vmem_spec] * 2,
        out_specs=(vmem_spec,) * 7 + (any_spec,) * 3,
        scratch_shapes=[
            pltpu.VMEM((size, width), bf16),
            pltpu.VMEM((size, width), bf16),
            pltpu.VMEM((4, blk, width), bf16),
            pltpu.VMEM((3 * blk, width), bf16),
            pltpu.VMEM((every, w_rows, cols), bf16),
            pltpu.VMEM((line, w_rows, width), bf16),
            pltpu.VMEM((every, 16, 128), bf16),
            pltpu.VMEM((every, 8, 128), f32),
            pltpu.VMEM((blk, width), f32),
            *[dma((n,)) for n in GATHER_SEMS + REDUCE_SEMS + (every,) * 6 + (line, line, 4, 3)],
        ],
        compiler_params=pltpu.CompilerParams(collective_id=1, has_side_effects=True, vmem_limit_bytes=60 * MIB),
    )(tokens, gains, w_qkv, w_out, q_seg, k_seg)


def back_kernel(
    line, blk, q_part, kv_part,
    d_attn_ref, tokens_ref, d_mid_ref, qkv_ref, attn_ref, lse_ref, gain_ref, gain_term_ref, q_seg_ref, k_seg_ref, normed_ref, w_qkv_ref, w_out_ref,
    grad_tokens_ref, grad_qkv_ref, grad_out_ref, gain_sum_ref,
    buf, term, core_land, land, w_qkv, w_out, normed, d_heads, d_qkv, dk_sum, dv_sum, stage_qkv, stage_out, qkv_land, out_land, gain_stage, gain_land, d_normed,
    *sems,
):
    at = Place(line)
    gather = plane_gather(at, buf, blk, sems[:6])
    reduce = plane_reduce(at, term, core_land, land, blk, sems[6:12])
    qkv_send, qkv_recv, gain_send, gain_recv, out_send, out_recv, own_sem = sems[12:]
    width = buf.shape[1]
    w_rows = w_out.shape[1]
    size = 8 * blk
    mine = pl.ds(pl.multiple_of(at.c * blk, blk), blk)
    own = [
        pltpu.make_async_copy(d_attn_ref, buf.at[mine, :], own_sem.at[0]),
        pltpu.make_async_copy(w_out_ref, w_out, own_sem.at[1]),
        pltpu.make_async_copy(w_qkv_ref, w_qkv, own_sem.at[2]),
        pltpu.make_async_copy(normed_ref, normed, own_sem.at[3]),
    ]
    for copy in own:
        copy.start()
    at.greet_all()
    own[0].wait()
    gather[0]()
    gather[1]()
    for copy in own[1:]:
        copy.wait()

    @pl.loop(0, size // 256)
    def _(i):
        part = pl.ds(pl.multiple_of(i * 256, 256), 256)
        d_heads[part, :] = dot(buf[part, :], w_out[...].reshape(line * w_rows, width), ((1,), (1,))).astype(jnp.bfloat16)

    @pl.loop(0, width // 256)
    def _(i):
        span = pl.ds(pl.multiple_of(i * 256, 256), 256)
        stage_out[:, :, span] = dot(attn_ref[...], buf[:, span], ((0,), (0,))).astype(jnp.bfloat16).reshape(line, w_rows, 256)

    def out_copy(i):
        z = lax.rem(at.z + i, line)
        return remote(stage_out.at[z], out_land.at[at.z], out_send.at[z], out_recv.at[at.z], (at.c, z))

    def out_arrival(i):
        z = lax.rem(at.z + i, line)
        return remote(stage_out.at[z], out_land.at[z], out_send.at[z], out_recv.at[z], (at.c, z))

    for i in range(1, line):
        out_copy(i).start()

    heads = q_part // HEAD_DIM
    block = math.gcd(size, 256)
    dk_sum[...] = jnp.zeros_like(dk_sum)
    dv_sum[...] = jnp.zeros_like(dv_sum)
    for i in range(size // block):
        rows, cols = pl.ds(i * block, block), (i + 1) * block
        live = seen_mask(i * block, block, cols, q_seg_ref[rows, :], k_seg_ref[:, :cols])
        keys, values = qkv_ref[:cols, q_part : q_part + kv_part], qkv_ref[:cols, q_part + kv_part :]
        for h in range(heads):
            span = slice(h * HEAD_DIM, (h + 1) * HEAD_DIM)
            queries, d_out = qkv_ref[rows, span], d_heads[rows, span]
            delta = jnp.sum(d_out.astype(jnp.float32) * attn_ref[rows, span].astype(jnp.float32), axis=-1, keepdims=True)
            scores = dot(queries, keys, ((1,), (1,))) * SCALE
            probs = jnp.where(live, jnp.exp(scores - lse_ref[rows, h : h + 1]), 0.0)
            d_probs = dot(d_out, values, ((1,), (1,)))
            d_scores = (probs * (d_probs - delta)).astype(jnp.bfloat16)
            d_qkv[rows, span] = (dot(d_scores, keys, ((1,), (0,))) * SCALE).astype(jnp.bfloat16)
            dk_sum[:cols, :] += dot(d_scores, queries, ((0,), (0,)))
            dv_sum[:cols, :] += dot(probs.astype(jnp.bfloat16), d_out, ((0,), (0,)))
    d_qkv[:, q_part : q_part + kv_part] = (dk_sum[...] * SCALE).astype(jnp.bfloat16)
    d_qkv[:, q_part + kv_part :] = dv_sum[...].astype(jnp.bfloat16)

    for i, chip in enumerate((at.qd, at.qx, at.qy, at.q)):
        for core in (1 - at.core, at.core):
            part = pl.ds(pl.multiple_of((2 * chip + core) * blk, blk), blk)

            @pl.loop(0, width // 512)
            def _(j):
                span = pl.ds(pl.multiple_of(j * 512, 512), 512)
                matrix = w_qkv[pl.ds(pl.multiple_of(j * (512 // w_rows), 512 // w_rows), 512 // w_rows)].reshape(512, q_part + 2 * kv_part)
                term[part, span] = dot(d_qkv[part, :], matrix, ((1,), (1,))).astype(jnp.bfloat16)

        reduce[0](i)

    @pl.loop(0, width // 256)
    def _(i):
        span = pl.ds(pl.multiple_of(i * 256, 256), 256)
        blocks = pl.ds(pl.multiple_of(i * (256 // w_rows), 256 // w_rows), 256 // w_rows)
        grads = dot(normed[:, span], d_qkv[...], ((0,), (0,))).astype(jnp.bfloat16)
        stage_qkv[blocks] = grads.reshape(256 // w_rows, w_rows, q_part + 2 * kv_part)

    qkv_push = (lambda other: stage_qkv.at[other], lambda slot: qkv_land.at[slot], qkv_send, qkv_recv)
    at.push_all(*qkv_push)
    qkv_land[at.me] = stage_qkv[at.me]
    out_land[at.z] = stage_out[at.z]
    reduce[1](d_normed)

    gain_stage[...] = jnp.zeros_like(gain_stage)
    gain_stage[1:2, :] = gain_term_ref[...]

    @pl.loop(0, blk // 32)
    def _(i):
        part = pl.ds(pl.multiple_of(i * 32, 32), 32)
        rows = tokens_ref[part, :].astype(jnp.float32)
        d_rows, gain_term = norm_backward(d_normed[part, :], rows, rms_scale(rows), gain_ref[0:1, :])
        grad_tokens_ref[part, :] = d_mid_ref[part, :] + d_rows
        gain_stage[0:1, :] += gain_term.reshape(1, width)

    def gain_tile(other):
        return gain_stage.at[:, pl.ds(pl.multiple_of((other // 2) * 128, 128), 128)]

    gain_push = (gain_tile, lambda slot: gain_land.at[slot], gain_send, gain_recv)
    at.push_all(*gain_push)
    gain_land[at.me] = gain_stage[:, pl.ds(pl.multiple_of((at.me // 2) * 128, 128), 128)]

    for i in range(1, line):
        out_arrival(i).wait_recv()
    total = out_land[0].astype(jnp.float32)
    for i in range(1, line):
        total = total + out_land[i].astype(jnp.float32)
    grad_out_ref[...] = total
    at.wait_all(*qkv_push, sent=False)

    @pl.loop(0, 8)
    def _(i):
        total = qkv_land[i * line].astype(jnp.float32)
        for j in range(1, line):
            total = total + qkv_land[i * line + j].astype(jnp.float32)
        grad_qkv_ref[i] = total

    at.wait_all(*gain_push, sent=False)
    gain_sum_ref[...] = jnp.sum(gain_land[...], axis=0)
    gather[2]()
    reduce[2]()
    at.wait_all(*qkv_push)
    at.wait_all(*gain_push)
    for i in range(1, line):
        out_copy(i).wait_send()


def back(line, d_attn, tokens, d_mid, qkv, attn_out, lse, gain, gain_term, q_seg, k_seg, normed, w_qkv, w_out):
    blk, width = tokens.shape
    w_rows, cols = w_out.shape[1], w_qkv.shape[2]
    size, every = 8 * blk, 8 * line
    q_part = HEADS * HEAD_DIM // 8
    kv_part = (cols - q_part) // 2
    any_spec, vmem_spec = pl.BlockSpec(memory_space=pl.ANY), pl.BlockSpec(memory_space=pltpu.VMEM)
    bf16, f32, dma, out = jnp.bfloat16, jnp.float32, pltpu.SemaphoreType.DMA, jax.ShapeDtypeStruct
    return pl.pallas_call(
        functools.partial(back_kernel, line, blk, q_part, kv_part),
        out_shape=(out((blk, width), f32), out((8, w_rows, cols), f32), out((w_rows, width), f32), out((8, 128), f32)),
        in_specs=[any_spec] + [vmem_spec] * 9 + [any_spec] * 3,
        out_specs=(vmem_spec,) * 4,
        scratch_shapes=[
            pltpu.VMEM((size, width), bf16),
            pltpu.VMEM((size, width), bf16),
            pltpu.VMEM((4, blk, width), bf16),
            pltpu.VMEM((3 * blk, width), bf16),
            pltpu.VMEM((every, w_rows, cols), bf16),
            pltpu.VMEM((line, w_rows, width), bf16),
            pltpu.VMEM((size, width), bf16),
            pltpu.VMEM((size, q_part), bf16),
            pltpu.VMEM((size, cols), bf16),
            pltpu.VMEM((size, kv_part), f32),
            pltpu.VMEM((size, kv_part), f32),
            pltpu.VMEM((every, w_rows, cols), bf16),
            pltpu.VMEM((line, w_rows, width), bf16),
            pltpu.VMEM((every, w_rows, cols), bf16),
            pltpu.VMEM((line, w_rows, width), bf16),
            pltpu.VMEM((8, width), f32),
            pltpu.VMEM((every, 8, 128), f32),
            pltpu.VMEM((blk, width), f32),
            *[dma((n,)) for n in GATHER_SEMS + REDUCE_SEMS + (every,) * 4 + (line, line, 4)],
        ],
        compiler_params=pltpu.CompilerParams(collective_id=2, has_side_effects=True, vmem_limit_bytes=60 * MIB),
    )(d_attn, tokens, d_mid, qkv, attn_out, lse, gain, gain_term, q_seg, k_seg, normed, w_qkv, w_out)


def split_heads(w, parts):
    rows = w.shape[0]
    q_width, kv_width = HEADS * HEAD_DIM, KV_HEADS * HEAD_DIM
    copies = max(1, parts // KV_HEADS)
    q = w[:, :q_width].reshape(rows, parts, q_width // parts)
    k = w[:, q_width : q_width + kv_width].reshape(rows, parts // copies, 1, -1)
    v = w[:, q_width + kv_width :].reshape(rows, parts // copies, 1, -1)
    k, v = (jnp.broadcast_to(a, (rows, parts // copies, copies, a.shape[3])).reshape(rows, parts, -1) for a in (k, v))
    return jnp.concatenate([q, k, v], axis=2)


def join_heads(grads, parts):
    rows = grads.shape[0]
    copies = max(1, parts // KV_HEADS)
    q_part = HEADS * HEAD_DIM // parts
    kv_part = (grads.shape[2] - q_part) // 2
    q = grads[:, :, :q_part].reshape(rows, -1)
    k, v = (
        jnp.sum(grads[:, :, at : at + kv_part].reshape(rows, parts // copies, copies, kv_part), axis=2).reshape(rows, -1)
        for at in (q_part, q_part + kv_part)
    )
    return jnp.concatenate([q, k, v], axis=1)


def per_device(n_ctx, n_shard, tokens, lengths, cotangent, w_qkv, w_out, w_gate_up, w_down, gain_attn, gain_mlp):
    count, width = tokens.shape[1:]
    n = n_ctx * n_shard
    w_rows = w_qkv.shape[0]
    ff_part = w_down.shape[0]
    q_part = HEADS * HEAD_DIM // n_ctx
    rows = tokens.reshape(count, width).astype(jnp.float32)
    grad_rows = cotangent.reshape(count, width).astype(jnp.float32)
    size = count * n_ctx
    positions = jnp.arange(size, dtype=jnp.int32)
    seg = segment_ids(positions, lengths[0])
    q_seg, k_seg = seg.reshape(size, 1), seg.reshape(1, size)

    gains = lax.all_gather(jnp.stack([gain_attn, gain_mlp]), EVERY, axis=1, tiled=True).astype(jnp.float32)
    gain_one, gain_two = gains[0], gains[1]

    qkv_cols = lax.all_to_all(split_heads(w_qkv, n_ctx), "ctx", split_axis=1, concat_axis=1, tiled=True)
    qkv_cols = qkv_cols.reshape(w_rows, n_ctx, -1).transpose(1, 0, 2)
    qkv_mine = lax.all_gather(qkv_cols, "shard", axis=1, tiled=True).reshape(width, -1)
    out_mine = lax.all_gather(w_out, "shard", axis=0, tiled=True)
    gate_up_mine = lax.all_to_all(w_gate_up.reshape(w_rows, 2, n, ff_part), EVERY, split_axis=2, concat_axis=0, tiled=True)
    gate_up_mine = gate_up_mine.reshape(width, 2 * ff_part)

    scale_one = rms_scale(rows)
    normed_one = lax.all_gather((rows * scale_one * gain_one).astype(jnp.bfloat16), "ctx", axis=0, tiled=True)
    projected = dot(normed_one, qkv_mine, ((1,), (0,))).astype(jnp.bfloat16)
    kv_part = (projected.shape[1] - q_part) // 2
    queries, keys, values = (
        projected[:, :q_part],
        projected[:, q_part : q_part + kv_part],
        projected[:, q_part + kv_part :],
    )
    attn_out, lse, tops = attend(queries, keys, values, q_seg, k_seg)
    out_term = dot(attn_out, out_mine, ((1,), (0,))).astype(jnp.bfloat16)
    attn_proj = lax.psum_scatter(out_term, "ctx", scatter_dimension=0, tiled=True)
    mid = rows + BRANCH * attn_proj.astype(jnp.float32)
    head_top = lax.all_gather(lax.pmax(tops, "shard"), "ctx", axis=1, tiled=True).reshape(HEADS)
    clip = CLIP_TARGET / jnp.maximum(head_top, CLIP_TARGET)

    scale_two = rms_scale(mid)
    d_mlp = lax.all_gather((BRANCH * grad_rows).astype(jnp.bfloat16), EVERY, axis=0, tiled=True)
    normed_two = lax.all_gather((mid * scale_two * gain_two).astype(jnp.bfloat16), EVERY, axis=0, tiled=True)
    gate_up = dot(normed_two, gate_up_mine, ((1,), (0,)))
    gate, up = gate_up[:, :ff_part], gate_up[:, ff_part:]
    sigma = jax.nn.sigmoid(gate)
    active = gate * sigma
    hidden = (active * up).astype(jnp.bfloat16)
    down_term = dot(hidden, w_down, ((1,), (0,))).astype(jnp.bfloat16)
    d_hidden = dot(d_mlp, w_down, ((1,), (1,)))
    d_gate = d_hidden * up * sigma * (1.0 + gate * (1.0 - sigma))
    d_up = d_hidden * active
    d_gate_up = jnp.concatenate([d_gate, d_up], axis=1).astype(jnp.bfloat16)
    normed_term = dot(d_gate_up, gate_up_mine, ((1,), (1,))).astype(jnp.bfloat16)
    grad_down = dot(hidden, d_mlp, ((0,), (0,)))
    gate_up_grad = dot(normed_two, d_gate_up, ((0,), (0,))).astype(jnp.bfloat16)
    mlp_proj = lax.psum_scatter(down_term, EVERY, scatter_dimension=0, tiled=True)
    mixed = (mid + BRANCH * mlp_proj.astype(jnp.float32)).astype(jnp.bfloat16).reshape(1, count, width)
    d_normed_two = lax.psum_scatter(normed_term, EVERY, scatter_dimension=0, tiled=True).astype(jnp.float32)
    grad_gate_up = lax.all_to_all(gate_up_grad.reshape(n * w_rows, 2, 1, ff_part), EVERY, split_axis=0, concat_axis=2, tiled=True)
    grad_gate_up = grad_gate_up.reshape(w_rows, 2 * n * ff_part).astype(jnp.float32)
    d_mid_norm, gain_two_term = norm_backward(d_normed_two, mid, scale_two, gain_two)
    d_mid = grad_rows + d_mid_norm

    d_attn = lax.all_gather((BRANCH * d_mid).astype(jnp.bfloat16), "ctx", axis=0, tiled=True)
    grad_out = lax.psum_scatter(dot(attn_out, d_attn, ((0,), (0,))), "shard", scatter_dimension=0, tiled=True)
    d_heads = dot(d_attn, out_mine, ((1,), (1,))).astype(jnp.bfloat16)
    d_q, d_k, d_v = attend_back(queries, keys, values, attn_out, d_heads, lse, q_seg, k_seg)
    d_qkv = jnp.concatenate([d_q, d_k, d_v], axis=1)
    qkv_term = dot(d_qkv, qkv_mine, ((1,), (1,))).astype(jnp.bfloat16)
    d_normed_one = lax.psum_scatter(qkv_term, "ctx", scatter_dimension=0, tiled=True).astype(jnp.float32)
    qkv_grad = dot(normed_one, d_qkv, ((0,), (0,))).reshape(n_ctx, n_shard * w_rows, -1)
    qkv_grad = lax.psum_scatter(qkv_grad, "shard", scatter_dimension=1, tiled=True)
    qkv_grad = lax.all_to_all(qkv_grad, "ctx", split_axis=0, concat_axis=0, tiled=True)
    grad_qkv = join_heads(qkv_grad.transpose(1, 0, 2), n_ctx)
    d_rows_norm, gain_one_term = norm_backward(d_normed_one, rows, scale_one, gain_one)
    grad_tokens = (d_mid + d_rows_norm).reshape(1, count, width)
    gain_terms = lax.psum_scatter(jnp.stack([gain_one_term, gain_two_term]), EVERY, scatter_dimension=1, tiled=True)
    return (mixed, grad_tokens, grad_qkv, grad_out, grad_gate_up, grad_down, gain_terms[0], gain_terms[1], clip)


def on_planes(n_shard, tokens, lengths, cotangent, w_qkv, w_out, w_gate_up, w_down, gain_attn, gain_mlp):
    count, width = tokens.shape[1:]
    n = 8 * n_shard
    w_rows = w_qkv.shape[0]
    ff_part = w_down.shape[0]
    rows = tokens.reshape(count, width)
    grad_rows = cotangent.reshape(count, width).astype(jnp.float32)
    size = count * 8
    seg = segment_ids(jnp.arange(size, dtype=jnp.int32), lengths[0])
    q_seg, k_seg = seg.reshape(size, 1), seg.reshape(1, size)
    side = lax.rem(lax.axis_index("ctx") * n_shard + lax.axis_index("shard"), 2)

    gains = jnp.stack([gain_attn, gain_mlp])
    none = jnp.zeros_like(gains)
    gains = jnp.where(side == 0, jnp.concatenate([gains, none], axis=1), jnp.concatenate([none, gains], axis=1))
    gains = jnp.pad(gains, ((0, 14), (0, 0)))
    mid, normed_two, qkv, attn_out, lse, tops, gain, normed_one, qkv_mine, out_mine = front(
        n_shard, rows, gains, split_heads(w_qkv, 8).transpose(1, 0, 2), w_out, q_seg, k_seg
    )
    heads = HEADS // 8
    head_top = jnp.max(tops[:, 0, :heads].reshape(8, n_shard, heads), axis=1).reshape(HEADS)
    clip = CLIP_TARGET / jnp.maximum(head_top, CLIP_TARGET)

    gate_up_mine = lax.all_to_all(w_gate_up.reshape(w_rows, 2, n, ff_part), EVERY, split_axis=2, concat_axis=0, tiled=True)
    gate_up_mine = gate_up_mine.reshape(width, 2 * ff_part)
    d_mlp = (BRANCH * grad_rows).astype(jnp.bfloat16)
    mlp_proj, d_normed_two, gate_up_grad, grad_down = mlp_exchange(n_shard, normed_two, d_mlp, gate_up_mine, w_down)
    mixed = (mid + BRANCH * mlp_proj).astype(jnp.bfloat16).reshape(1, count, width)
    grad_gate_up = lax.all_to_all(gate_up_grad.reshape(n * w_rows, 2, 1, ff_part), EVERY, split_axis=0, concat_axis=2, tiled=True)
    grad_gate_up = grad_gate_up.reshape(w_rows, 2 * n * ff_part).astype(jnp.float32)
    d_mid_norm, gain_two_term = norm_backward(d_normed_two, mid, rms_scale(mid), gain[1:2])
    d_mid = grad_rows + d_mid_norm

    d_attn = (BRANCH * d_mid).astype(jnp.bfloat16)
    grad_tokens, qkv_grad, grad_out, gain_sum = back(
        n_shard, d_attn, rows, d_mid, qkv, attn_out, lse, gain, gain_two_term.reshape(1, width), q_seg, k_seg, normed_one, qkv_mine, out_mine
    )
    grad_qkv = join_heads(qkv_grad.transpose(1, 0, 2), 8)
    gain_grads = jnp.where(side == 0, gain_sum[:2, :w_rows], gain_sum[:2, w_rows : 2 * w_rows])
    return (mixed, grad_tokens.reshape(1, count, width), grad_qkv, grad_out, grad_gate_up, grad_down, gain_grads[0], gain_grads[1], clip)


def solution(mesh):
    by_token, by_row = P("shard", "ctx", None), P(EVERY, None)
    n_ctx, n_shard = mesh.shape["ctx"], mesh.shape["shard"]
    program = functools.partial(on_planes, n_shard) if n_ctx == 8 else functools.partial(per_device, n_ctx, n_shard)
    return jax.shard_map(
        program,
        mesh=mesh,
        in_specs=(by_token, P("shard", None), by_token, by_row, by_row, by_row, by_row, P(EVERY), P(EVERY)),
        out_specs=(by_token, by_token, by_row, by_row, by_row, by_row, P(EVERY), P(EVERY), P()),
        check_vma=False,
    )
```

```python
import functools
import math

import jax
import jax.numpy as jnp
from jax import lax
from jax.experimental import pallas as pl
from jax.experimental.pallas import tpu as pltpu
from jax.sharding import PartitionSpec as P

HEADS = 32
KV_HEADS = 8
HEAD_DIM = 64


SCALE = 0.015625
BRANCH = 0.22
EPSILON = 1e-05
CLIP_TARGET = 4.0
NEGATIVE = -1e30
MIB = 1024 * 1024
EVERY = ("ctx", "shard")


def segment_ids(positions, lengths_row):
    bounds = jnp.cumsum(lengths_row)[:-1]
    return jnp.sum((positions[:, None] >= bounds[None, :]).astype(jnp.int32), axis=1)


def rms_scale(rows):
    return lax.rsqrt(jnp.mean(rows * rows, axis=-1, keepdims=True) + EPSILON)


def norm_backward(d_normed, rows, scale, gain):
    unit = rows * scale
    d_unit = d_normed * gain
    gain_term = jnp.sum(d_normed * unit, axis=0)
    d_rows = scale * (d_unit - unit * jnp.mean(d_unit * unit, axis=-1, keepdims=True))
    return (d_rows, gain_term)


def dot(left, right, dims):
    return lax.dot_general(left, right, ((dims[0], dims[1]), ((), ())), preferred_element_type=jnp.float32)


def seen_mask(row0, rows, cols, q_seg, k_seg):
    q_pos = row0 + lax.broadcasted_iota(jnp.int32, (rows, cols), 0)
    k_pos = lax.broadcasted_iota(jnp.int32, (rows, cols), 1)
    return (k_pos <= q_pos) & ((k_seg == 0) | (k_seg == q_seg))


def attend_kernel(heads, block, q_ref, k_ref, v_ref, q_seg_ref, k_seg_ref, o_ref, lse_ref, top_ref):
    size = q_ref.shape[0]
    tops = [jnp.full((1, 1), NEGATIVE, jnp.float32)] * heads
    for i in range(size // block):
        rows, cols = pl.ds(i * block, block), (i + 1) * block
        live = seen_mask(i * block, block, cols, q_seg_ref[rows, :], k_seg_ref[:, :cols])
        keys, values = k_ref[:cols, :], v_ref[:cols, :]
        for h in range(heads):
            span = slice(h * HEAD_DIM, (h + 1) * HEAD_DIM)
            scores = dot(q_ref[rows, span], keys, ((1,), (1,))) * SCALE
            scores = jnp.where(live, scores, NEGATIVE)
            peak = jnp.max(scores, axis=-1, keepdims=True)
            weights = jnp.exp(scores - peak)
            total = jnp.sum(weights, axis=-1, keepdims=True)
            out = dot(weights.astype(jnp.bfloat16), values, ((1,), (0,)))
            o_ref[rows, span] = (out / total).astype(jnp.bfloat16)
            lse_ref[rows, h : h + 1] = peak + jnp.log(total)
            tops[h] = jnp.maximum(tops[h], jnp.max(peak, axis=0, keepdims=True))
    for h in range(heads):
        top_ref[:, h : h + 1] = tops[h]


def attend(queries, keys, values, q_seg, k_seg):
    size, width = queries.shape
    heads = width // HEAD_DIM
    return pl.pallas_call(
        functools.partial(attend_kernel, heads, math.gcd(size, 256)),
        out_shape=(
            jax.ShapeDtypeStruct((size, width), jnp.bfloat16),
            jax.ShapeDtypeStruct((size, heads), jnp.float32),
            jax.ShapeDtypeStruct((1, heads), jnp.float32),
        ),
        compiler_params=pltpu.CompilerParams(vmem_limit_bytes=48 * MIB),
    )(queries, keys, values, q_seg, k_seg)


def attend_back_kernel(
    heads, block, q_ref, k_ref, v_ref, o_ref, do_ref, lse_ref, q_seg_ref, k_seg_ref, dq_ref, dk_ref, dv_ref, dk_sum, dv_sum
):
    size = q_ref.shape[0]
    dk_sum[...] = jnp.zeros_like(dk_sum)
    dv_sum[...] = jnp.zeros_like(dv_sum)
    for i in range(size // block):
        rows, cols = pl.ds(i * block, block), (i + 1) * block
        live = seen_mask(i * block, block, cols, q_seg_ref[rows, :], k_seg_ref[:, :cols])
        keys, values = k_ref[:cols, :], v_ref[:cols, :]
        for h in range(heads):
            span = slice(h * HEAD_DIM, (h + 1) * HEAD_DIM)
            queries, d_out = q_ref[rows, span], do_ref[rows, span]
            delta = jnp.sum(d_out.astype(jnp.float32) * o_ref[rows, span].astype(jnp.float32), axis=-1, keepdims=True)
            scores = dot(queries, keys, ((1,), (1,))) * SCALE
            probs = jnp.where(live, jnp.exp(scores - lse_ref[rows, h : h + 1]), 0.0)
            d_probs = dot(d_out, values, ((1,), (1,)))
            d_scores = (probs * (d_probs - delta)).astype(jnp.bfloat16)
            dq_ref[rows, span] = (dot(d_scores, keys, ((1,), (0,))) * SCALE).astype(jnp.bfloat16)
            dk_sum[:cols, :] += dot(d_scores, queries, ((0,), (0,)))
            dv_sum[:cols, :] += dot(probs.astype(jnp.bfloat16), d_out, ((0,), (0,)))
    dk_ref[...] = (dk_sum[...] * SCALE).astype(jnp.bfloat16)
    dv_ref[...] = dv_sum[...].astype(jnp.bfloat16)


def attend_back(queries, keys, values, out, d_out, lse, q_seg, k_seg):
    size, width = queries.shape
    heads = width // HEAD_DIM
    like_kv = jax.ShapeDtypeStruct((size, HEAD_DIM), jnp.bfloat16)
    return pl.pallas_call(
        functools.partial(attend_back_kernel, heads, math.gcd(size, 256)),
        out_shape=(jax.ShapeDtypeStruct((size, width), jnp.bfloat16), like_kv, like_kv),
        scratch_shapes=[pltpu.VMEM((size, HEAD_DIM), jnp.float32)] * 2,
        compiler_params=pltpu.CompilerParams(vmem_limit_bytes=48 * MIB),
    )(queries, keys, values, out, d_out, lse, q_seg, k_seg)


def remote(src, dst, send_sem, recv_sem, device):
    return pltpu.make_async_remote_copy(
        src_ref=src, dst_ref=dst, send_sem=send_sem, recv_sem=recv_sem, device_id=device, device_id_type=pl.DeviceIdType.MESH
    )


def greet(devices, extra):
    barrier = pltpu.get_barrier_semaphore()
    count = len(devices)
    for device in devices:
        pl.semaphore_signal(barrier, inc=1, device_id=device, device_id_type=pl.DeviceIdType.MESH)
    for condition, device in extra:

        @pl.when(condition)
        def _():
            pl.semaphore_signal(barrier, inc=1, device_id=device, device_id_type=pl.DeviceIdType.MESH)

        count = count + condition.astype(jnp.int32)
    pl.semaphore_wait(barrier, count)


def add_rows(target, sources, rows, keep=None, step=32):
    @pl.loop(0, rows // step)
    def _(i):
        part = pl.ds(pl.multiple_of(i * step, step), step)
        total = target[part, :].astype(jnp.float32)
        for source in sources:
            total = total + source[part, :].astype(jnp.float32)
        if keep is None:
            target[part, :] = total.astype(jnp.bfloat16)
        else:
            keep[part, :] = total


class Place:
    def __init__(self, line):
        self.line = line
        self.c, self.z = lax.axis_index("ctx"), lax.axis_index("shard")
        self.q, self.core = self.c // 2, self.c % 2
        self.me = self.c * line + self.z
        self.every = 8 * line
        self.cx, self.cy = (self.c + 2 - 4 * (self.q % 2), self.z), (self.c + 4 - 8 * (self.q // 2), self.z)
        self.sibling = (self.c + 1 - 2 * self.core, self.z)
        self.qx, self.qy, self.qd = self.q + 1 - 2 * (self.q % 2), self.q + 2 - 4 * (self.q // 2), 3 - self.q

    def source(self, k):
        if self.line == 1:
            return self.z * 0
        mirrored = self.z >= self.line // 2
        near = jnp.where(mirrored, self.line - 1 - self.z, self.z)
        turn = (k + 1) // 2
        both = near - turn if k % 2 == 1 else near + turn
        at = jnp.where(k <= 2 * near, both, k)
        return jnp.where(mirrored, self.line - 1 - at, at)

    def line_spread(self, copy, k):
        at = self.source(k)
        if k > 0:
            copy(at, 0).wait_recv()
        for way, condition in enumerate(self.line_ways(at)):

            @pl.when(condition)
            def _():
                copy(at, way).start()

    def line_sent(self, copy, k):
        at = self.source(k)
        for way, condition in enumerate(self.line_ways(at)):

            @pl.when(condition)
            def _():
                copy(at, way).wait_send()

    def line_ways(self, at):
        return ((at <= self.z) & (self.z < self.line - 1), (at >= self.z) & (self.z > 0))

    def peer(self, i):
        other = lax.rem(self.me + i, self.every)
        return other, (other // self.line, other % self.line)

    def greet_all(self):
        barrier = pltpu.get_barrier_semaphore()

        @pl.loop(1, self.every)
        def _(i):
            pl.semaphore_signal(barrier, inc=1, device_id=self.peer(i)[1], device_id_type=pl.DeviceIdType.MESH)

        pl.semaphore_wait(barrier, self.every - 1)

    def push_all(self, source, target, send_sems, recv_sems):
        @pl.loop(1, self.every)
        def _(i):
            other, device = self.peer(i)
            remote(source(other), target(self.me), send_sems.at[other], recv_sems.at[self.me], device).start()

    def wait_all(self, source, target, send_sems, recv_sems, sent=True):
        @pl.loop(1, self.every)
        def _(i):
            other, device = self.peer(i)
            copy = remote(source(other), target(other), send_sems.at[other], recv_sems.at[other], device)
            if sent:
                copy.wait_send()
            else:
                copy.wait_recv()


class SliceGather:
    def __init__(self, place, rows, blk, sems):
        self.place, self.rows, self.half = place, rows, blk // 2
        self.z_send, self.z_recv, self.p_send, self.p_recv, self.f_send, self.f_recv = sems
        p, half = place, blk // 2
        self.ways = ((p.cx, p.qx, 0), (p.cy, p.qy, half), (p.cx, p.qx, half), (p.cy, p.qy, 0))
        self.turns = ((p.qx, 0, p.cy), (p.qy, half, p.cx))

    def line_copy(self, at, way):
        ref = self.rows(at, self.place.q, 0, 2 * self.half)
        return remote(ref, ref, self.z_send.at[at, way], self.z_recv.at[at], (self.place.c, self.place.z + 1 - 2 * way))

    def plane_copy(self, at, i, arriving=False):
        device, chip, first = self.ways[i]
        ref = self.rows(at, chip if arriving else self.place.q, first, self.half)
        return remote(ref, ref, self.p_send.at[at, i], self.p_recv.at[at, i], device)

    def onward_copy(self, at, i, arriving=False):
        chip, first, device = self.turns[i]
        ref = self.rows(at, self.place.qd if arriving else chip, first, self.half)
        return remote(ref, ref, self.f_send.at[at, i], self.f_recv.at[at, i], device)

    def a(self, k):
        self.place.line_spread(self.line_copy, k)
        for i in range(4):
            self.plane_copy(self.place.source(k), i).start()

    def b(self, k):
        at = self.place.source(k)
        for i in (0, 1):
            self.plane_copy(at, i, True).wait_recv()
            self.onward_copy(at, i).start()

    def c(self, k):
        at = self.place.source(k)
        for i in (2, 3):
            self.plane_copy(at, i, True).wait_recv()
        for i in (0, 1):
            self.onward_copy(at, i, True).wait_recv()
        for i in range(4):
            self.plane_copy(at, i).wait_send()
        for i in (0, 1):
            self.onward_copy(at, i).wait_send()
        self.place.line_sent(self.line_copy, k)


def slice_gather_sems(line):
    return [pltpu.SemaphoreType.DMA(shape) for shape in ((line, 2), (line,), (line, 4), (line, 4), (line, 2), (line, 2))]


class SliceReduce:
    def __init__(self, place, rows, blk, land, line_land, result, sems):
        self.place, self.rows, self.blk, self.half = place, rows, blk, blk // 2
        self.land, self.line_land, self.result = land, line_land, result
        self.r2_send, self.r2_recv, self.r3_send, self.r3_recv, self.r4_send, self.r4_recv = sems
        p, half = place, blk // 2
        self.seconds = ((0, p.cy), (half, p.cx))
        self.thirds = ((p.cx, p.qx, 0, 0), (p.cy, p.qy, half, blk + half), (p.cx, p.qx, half, half), (p.cy, p.qy, 0, blk))

    def landing(self, at, first, count):
        return self.land.at[at, pl.ds(first, count), :]

    def second(self, at, i):
        first, device = self.seconds[i]
        return remote(
            self.rows(at, self.place.qd, first, self.half), self.landing(at, 2 * self.blk + first, self.half), self.r2_send.at[at, i], self.r2_recv.at[at, i], device
        )

    def third(self, at, i):
        device, chip, first, lands = self.thirds[i]
        return remote(
            self.rows(at, chip, first, self.half), self.landing(at, lands, self.half), self.r3_send.at[at, i], self.r3_recv.at[at, i], device
        )

    def line_copy(self, at, way):
        p = self.place
        slot = jnp.where((way == 1) & (at == p.z - 1), p.line, at)
        return remote(
            self.rows(at, p.q, 0, self.blk), self.line_land.at[slot], self.r4_send.at[at], self.r4_recv.at[slot], (p.c, p.z + 1 - 2 * way)
        )

    def line_arrival(self, at, slot):
        return remote(self.rows(at, self.place.q, 0, self.blk), self.line_land.at[slot], self.r4_send.at[at], self.r4_recv.at[slot], self.place.sibling)

    def a(self, k):
        at = self.place.source(k)
        for i in (0, 1):
            self.second(at, i).start()
        for i in (2, 3):
            self.third(at, i).start()

    def b(self, k):
        at = self.place.source(k)
        for i in (0, 1):
            chip, first = self.thirds[i][1:3]
            self.second(at, i).wait_recv()
            add_rows(self.rows(at, chip, first, self.half), [self.landing(at, 2 * self.blk + first, self.half)], self.half)
            self.third(at, i).start()

    def c(self, k):
        p, blk = self.place, self.blk
        at = p.source(k)
        has_up, has_down = p.z < p.line - 1, p.z > 0
        for i in range(4):
            self.third(at, i).wait_recv()
        mine = self.rows(at, p.q, 0, blk)
        plane = [self.landing(at, 0, blk), self.landing(at, blk, blk)]
        if k > 0:
            joined = ((at > p.z) & has_down) | ((at < p.z) & has_up)

            @pl.when(joined)
            def _():
                self.line_arrival(at, at).wait_recv()
                add_rows(mine, plane + [self.line_land.at[at]], blk)

            @pl.when(jnp.logical_not(joined))
            def _():
                add_rows(mine, plane, blk)

            for way, condition in enumerate((at > p.z, at < p.z)):

                @pl.when(condition)
                def _():
                    self.line_copy(at, way).start()

        else:
            add_rows(mine, plane, blk, self.result)
            for condition, slot in ((has_down, at), (has_up, p.line)):

                @pl.when(condition)
                def _():
                    self.line_arrival(at, slot).wait_recv()
                    add_rows(self.result, [self.line_land.at[slot]], blk, self.result)

    def end(self, k):
        at = self.place.source(k)
        for i in (0, 1):
            self.second(at, i).wait_send()
        for i in range(4):
            self.third(at, i).wait_send()
        if k > 0:
            self.line_copy(at, 0).wait_send()


def slice_reduce_sems(line):
    return [pltpu.SemaphoreType.DMA(shape) for shape in ((line, 2), (line, 2), (line, 4), (line, 4), (line,), (line + 1,))]


def slice_rows(ref, blk):
    def rows(at, chip, first, count):
        return ref.at[pl.ds(pl.multiple_of((at * 4 + chip) * blk + first, blk // 2), count), :]

    return rows


def mlp_kernel(
    line, blk, part, normed_ref, d_mlp_ref, w_gate_up_ref, down_ref,
    mlp_term_ref, d_normed_ref, gate_up_grad_ref, down_grad_ref,
    act, land, line_land, w_gu, w_down, acc_gu, acc_down, hid, d_gu, sib_gu, sib_down, grad_land,
    w_send, w_recv, g_send, g_recv, c_send, c_recv, d_send, d_recv, own_sem, out_sem, *sems,
):
    place = Place(line)
    core, me, sibling = place.core, place.me, place.sibling
    width = w_down.shape[1]
    w_rows = w_gate_up_ref.shape[0]
    slot_rows = 4 * blk
    rows = slice_rows(act.at[0], blk)
    gather = SliceGather(place, rows, blk, sems[:6])
    reduce = SliceReduce(place, rows, blk, land, line_land, d_normed_ref, sems[6:])

    def slot_of(k):
        return pl.ds(pl.multiple_of(place.source(k) * slot_rows, slot_rows), slot_rows)

    own = pltpu.make_async_copy(normed_ref, rows(place.z, place.q, 0, blk), own_sem.at[0])
    d_mlp_in = pltpu.make_async_copy(d_mlp_ref, act.at[1], own_sem.at[1])
    mine = pl.ds(pl.multiple_of(core * 2 * part, 2 * part), 2 * part)
    theirs = pl.ds(pl.multiple_of((1 - core) * 2 * part, 2 * part), 2 * part)
    mine_rows = pl.ds(pl.multiple_of(core * part, part), part)
    their_rows = pl.ds(pl.multiple_of((1 - core) * part, part), part)

    def columns(other, i):
        return w_gate_up_ref.at[:, pl.ds(pl.multiple_of((i * place.every + other) * part, part), part)]

    def column_place(other, slot, i):
        first = ((other // line) % 2) * 2 * part + i * part
        return w_gu.at[pl.ds(pl.multiple_of(slot * w_rows, w_rows), w_rows), pl.ds(pl.multiple_of(first, part), part)]

    def send_columns():
        @pl.loop(1, place.every)
        def _(i):
            other, device = place.peer(i)
            for j in (0, 1):
                remote(columns(other, j), column_place(other, me, j), c_send.at[j, other], c_recv.at[j, me], device).start()

    def wait_columns(sent):
        @pl.loop(1, place.every)
        def _(i):
            other, device = place.peer(i)
            for j in (0, 1):
                copy = remote(columns(other, j), column_place(me, other, j), c_send.at[j, other], c_recv.at[j, other], device)
                if sent:
                    copy.wait_send()
                else:
                    copy.wait_recv()

    own_weights = [pltpu.make_async_copy(columns(me, j), column_place(me, me, j), own_sem.at[2 + j]) for j in (0, 1)]
    own_weights.append(pltpu.make_async_copy(down_ref, w_down.at[mine_rows, :], own_sem.at[4]))
    down_to = remote(down_ref, w_down.at[mine_rows, :], w_send.at[0], w_recv.at[0], sibling)
    down_from = remote(down_ref, w_down.at[their_rows, :], w_send.at[0], w_recv.at[0], sibling)
    columns_to = remote(w_gu.at[:, mine], w_gu.at[:, mine], w_send.at[1], w_recv.at[1], sibling)
    columns_from = remote(w_gu.at[:, theirs], w_gu.at[:, theirs], w_send.at[1], w_recv.at[1], sibling)

    def compute(k):
        slot = slot_of(k)

        @pl.loop(0, 2)
        def _(j):
            span = pl.ds(pl.multiple_of(j * part, part), part)
            lower = pl.ds(pl.multiple_of(j * 2 * part, part), part)
            upper = pl.ds(pl.multiple_of(j * 2 * part + part, part), part)
            gate = dot(act[0, slot, :], w_gu[:, lower], ((1,), (0,)))
            above = dot(act[0, slot, :], w_gu[:, upper], ((1,), (0,)))
            d_hidden = dot(act[1, slot, :], w_down[span, :], ((1,), (1,)))
            sigma = jax.nn.sigmoid(gate)
            active = gate * sigma
            hid[:, span] = (active * above).astype(jnp.bfloat16)
            d_gu[:, lower] = (d_hidden * above * sigma * (1.0 + gate * (1.0 - sigma))).astype(jnp.bfloat16)
            d_gu[:, upper] = (d_hidden * active).astype(jnp.bfloat16)

        @pl.loop(0, width // 256)
        def _(j):
            span = pl.ds(pl.multiple_of(j * 256, 256), 256)
            down_term = dot(hid[...], act[1, slot, span], ((0,), (0,)))
            gate_up_term = dot(act[0, slot, span], d_gu[...], ((0,), (0,)))
            if k > 0:
                down_term = down_term + acc_down[:, span]
                gate_up_term = gate_up_term + acc_gu[span, :]
            acc_down[:, span] = down_term
            acc_gu[span, :] = gate_up_term
            act[1, slot, span] = dot(hid[...], w_down[:, span], ((1,), (0,))).astype(jnp.bfloat16)
            act[0, slot, span] = dot(d_gu[...], w_gu[span, :], ((1,), (1,))).astype(jnp.bfloat16)

    def term_out(k):
        return pltpu.make_async_copy(act.at[1, slot_of(k), :], mlp_term_ref.at[slot_of(k), :], out_sem.at[2 + k])

    half_gu, whole_gu = pl.ds(0, 2 * part), pl.ds(2 * part, 2 * part)
    grad_copies = [
        remote(w_gu.at[:, half_gu], sib_gu, g_send.at[0], g_recv.at[0], sibling),
        remote(w_down.at[:part, :], sib_down, g_send.at[1], g_recv.at[1], sibling),
    ]
    down_out = pltpu.make_async_copy(acc_down.at[mine_rows, :], down_grad_ref, out_sem.at[0])

    def exchange_grads():
        @pl.loop(0, width // 256)
        def _(j):
            span = pl.ds(pl.multiple_of(j * 256, 256), 256)
            w_gu[span, half_gu] = acc_gu[span, theirs].astype(jnp.bfloat16)

        w_down[:part, :] = acc_down[their_rows, :].astype(jnp.bfloat16)
        for copy in grad_copies:
            copy.start()

    grad_push = (
        lambda other: w_gu.at[pl.ds(pl.multiple_of(other * w_rows, w_rows), w_rows), whole_gu],
        lambda slot: grad_land.at[slot],
        d_send,
        d_recv,
    )

    def finish_grads():
        for copy in grad_copies:
            copy.wait_recv()

        @pl.loop(0, width // 256)
        def _(j):
            span = pl.ds(pl.multiple_of(j * 256, 256), 256)
            w_gu[span, whole_gu] = (acc_gu[span, mine] + sib_gu[span, :].astype(jnp.float32)).astype(jnp.bfloat16)

        place.push_all(*grad_push)
        grad_land[me] = w_gu[pl.ds(pl.multiple_of(me * w_rows, w_rows), w_rows), whole_gu]
        acc_down[mine_rows, :] = acc_down[mine_rows, :] + sib_down[...].astype(jnp.float32)
        down_out.start()

    def write_grads():
        place.wait_all(*grad_push, sent=False)

        @pl.loop(0, place.every)
        def _(j):
            span = pl.ds(pl.multiple_of(j * w_rows, w_rows), w_rows)
            acc_gu[span, half_gu] = grad_land[j].astype(jnp.float32)
            for i in (0, 1):
                target = gate_up_grad_ref.at[:, pl.ds(pl.multiple_of((i * place.every + j) * part, part), part)]
                pltpu.make_async_copy(acc_gu.at[span, pl.ds(i * part, part)], target, out_sem.at[1]).start()

    for copy in [own, d_mlp_in] + own_weights:
        copy.start()
    place.greet_all()
    own.wait()
    gather.a(0)
    down_to.start()
    send_columns()
    for k in range(1, line):
        gather.a(k)
        gather.b(k - 1)
    for copy in [d_mlp_in] + own_weights:
        copy.wait()
    wait_columns(False)
    columns_to.start()
    down_from.wait_recv()
    columns_from.wait_recv()
    down_to.wait_send()
    columns_to.wait_send()
    wait_columns(True)
    for k in range(line):
        gather.c(k)
        compute(k)
        reduce.a(k)
        term_out(k).start()
        if k == 0:
            gather.b(line - 1)
    exchange_grads()
    backwards = range(line - 1, -1, -1)
    for k in backwards:
        reduce.b(k)
    finish_grads()
    for k in backwards:
        reduce.c(k)
    write_grads()
    for k in backwards:
        reduce.end(k)
        term_out(k).wait()
    for copy in grad_copies:
        copy.wait_send()
    place.wait_all(*grad_push)
    down_out.wait()
    pltpu.make_async_copy(gate_up_grad_ref, gate_up_grad_ref, out_sem.at[1]).wait()


def mlp_exchange(line, normed, d_mlp, gate_up, down):
    blk, width = normed.shape
    part = down.shape[0]
    any_spec, vmem_spec = pl.BlockSpec(memory_space=pl.ANY), pl.BlockSpec(memory_space=pltpu.VMEM)
    bf16, f32, dma = jnp.bfloat16, jnp.float32, pltpu.SemaphoreType.DMA
    return pl.pallas_call(
        functools.partial(mlp_kernel, line, blk, part),
        out_shape=(
            jax.ShapeDtypeStruct(d_mlp.shape, bf16),
            jax.ShapeDtypeStruct((blk, width), f32),
            jax.ShapeDtypeStruct(gate_up.shape, f32),
            jax.ShapeDtypeStruct((part, width), f32),
        ),
        in_specs=[any_spec] * 4,
        out_specs=(any_spec, vmem_spec, any_spec, any_spec),
        scratch_shapes=[
            pltpu.VMEM((2, line * 4 * blk, width), bf16),
            pltpu.VMEM((line, 3 * blk, width), bf16),
            pltpu.VMEM((line + 1, blk, width), bf16),
            pltpu.VMEM((width, 4 * part), bf16),
            pltpu.VMEM((2 * part, width), bf16),
            pltpu.VMEM((width, 4 * part), f32),
            pltpu.VMEM((2 * part, width), f32),
            pltpu.VMEM((4 * blk, 2 * part), bf16),
            pltpu.VMEM((4 * blk, 4 * part), bf16),
            pltpu.VMEM((width, 2 * part), bf16),
            pltpu.VMEM((part, width), bf16),
            pltpu.VMEM((8 * line, gate_up.shape[0], 2 * part), bf16),
            dma((2,)),
            dma((2,)),
            dma((2,)),
            dma((2,)),
            dma((2, 8 * line)),
            dma((2, 8 * line)),
            dma((8 * line,)),
            dma((8 * line,)),
            dma((5,)),
            dma((2 + line,)),
            *slice_gather_sems(line),
            *slice_reduce_sems(line),
        ],
        compiler_params=pltpu.CompilerParams(collective_id=0, has_side_effects=True, vmem_limit_bytes=63 * MIB),
    )(normed, d_mlp, gate_up, down)


def plane_gather(at, buf, blk, sems):
    p_send, p_recv, f_send, f_recv, s_send, s_recv = sems
    half = blk // 2

    def rows(chip, core, first=0, count=half):
        return buf.at[pl.ds(pl.multiple_of((2 * chip + core) * blk + first, half), count), :]

    def same(ref, send, recv, device):
        return remote(ref, ref, send, recv, device)

    way = ((at.cx, at.qx, 0), (at.cy, at.qy, half), (at.cx, at.qx, half), (at.cy, at.qy, 0))

    def sent(i):
        return same(rows(at.q, at.core, way[i][2]), p_send.at[i], p_recv.at[i], way[i][0])

    def arriving(i):
        return same(rows(way[i][1], at.core, way[i][2]), p_send.at[i], p_recv.at[i], way[i][0])

    def onward(i):
        chip, first, device = ((at.qx, 0, at.cy), (at.qy, half, at.cx))[i]
        return same(rows(chip, at.core, first), f_send.at[i], f_recv.at[i], device)

    def passed(i):
        first, device = ((0, at.cy), (half, at.cx))[i]
        return same(rows(at.qd, at.core, first), f_send.at[i], f_recv.at[i], device)

    def across(i, core):
        if i == 0:
            ref = rows(at.q, core, 0, blk)
        elif i < 5:
            ref = rows(way[i - 1][1], core, way[i - 1][2])
        else:
            ref = rows(at.qd, core, (i - 5) * half)
        return same(ref, s_send.at[i], s_recv.at[i], at.sibling)

    def start():
        for i in range(4):
            sent(i).start()
        across(0, at.core).start()

    def turn():
        for i in (0, 1):
            arriving(i).wait_recv()
            onward(i).start()
            across(i + 1, at.core).start()

    def rest():
        for i in (2, 3):
            arriving(i).wait_recv()
            across(i + 1, at.core).start()
        for i in (0, 1):
            passed(i).wait_recv()
            across(i + 5, at.core).start()

    def whole():
        for i in range(7):
            across(i, 1 - at.core).wait_recv()

    def end():
        for i in range(4):
            sent(i).wait_send()
        for i in (0, 1):
            onward(i).wait_send()
        for i in range(7):
            across(i, at.core).wait_send()

    return start, turn, rest, whole, end


GATHER_SEMS = (4, 4, 2, 2, 7, 7)
REDUCE_SEMS = (4, 4, 2, 2, 4, 4)


def plane_reduce(at, term, core_land, land, blk, sems):
    s_send, s_recv, r2_send, r2_recv, r3_send, r3_recv = sems
    half = blk // 2
    chips = (at.qd, at.qx, at.qy, at.q)

    def rows(chip, core, first=0, count=half):
        return term.at[pl.ds(pl.multiple_of((2 * chip + core) * blk + first, half), count), :]

    def landed(first, count):
        return land.at[pl.ds(first, count), :]

    def across(i):
        return remote(rows(chips[i], 1 - at.core, 0, blk), core_land.at[i], s_send.at[i], s_recv.at[i], at.sibling)

    def second(i):
        first, device = ((0, at.cy), (half, at.cx))[i]
        return remote(rows(at.qd, at.core, first), landed(2 * blk + first, half), r2_send.at[i], r2_recv.at[i], device)

    def third(i):
        device, chip, first, lands = (
            (at.cx, at.qx, 0, 0), (at.cy, at.qy, half, blk + half), (at.cx, at.qx, half, half), (at.cy, at.qy, 0, blk)
        )[i]
        return remote(rows(chip, at.core, first), landed(lands, half), r3_send.at[i], r3_recv.at[i], device)

    def add_core(i):
        across(i).wait_recv()
        add_rows(rows(chips[i], at.core, 0, blk), [core_land.at[i]], blk)

    def give(i):
        across(i).start()

    def take(result):
        add_core(0)
        second(0).start()
        second(1).start()
        add_core(1)
        third(2).start()
        add_core(2)
        third(3).start()
        for i, (chip, first) in enumerate(((at.qx, 0), (at.qy, half))):
            second(i).wait_recv()
            add_rows(rows(chip, at.core, first), [landed(2 * blk + first, half)], half)
            third(i).start()
        add_core(3)
        for i in range(4):
            third(i).wait_recv()
        add_rows(rows(at.q, at.core, 0, blk), [landed(0, blk), landed(blk, blk)], blk, result)

    def end():
        for i in range(4):
            across(i).wait_send()
            third(i).wait_send()
        for i in (0, 1):
            second(i).wait_send()

    return give, take, end


def front_kernel(
    line, blk, q_part, kv_part,
    tokens_ref, d_mlp_ref, gains_ref, w_qkv_ref, w_out_ref, q_seg_ref, k_seg_ref,
    mid_ref, normed_two_ref, qkv_ref, attn_ref, lse_ref, tops_ref, gain_ref, normed_ref, w_qkv_all_ref, w_out_all_ref, d_mlp_all_ref,
    buf, term, core_land, land, w_qkv, w_line, w_out, gain_land, top_land, proj,
    *sems,
):
    at = Place(line)
    gather = plane_gather(at, buf, blk, sems[:6])
    reduce = plane_reduce(at, term, core_land, land, blk, sems[6:12])
    line_send, line_recv, qkv_send, qkv_recv, gain_send, gain_recv, top_send, top_recv, out_send, out_recv, own_sem, write_sem = sems[12:24]
    d_mlp_rows = slice_rows(d_mlp_all_ref, blk)
    beside = SliceGather(at, d_mlp_rows, blk, sems[24:])
    w_rows, width = w_out_ref.shape
    size = 8 * blk
    mine = pl.ds(pl.multiple_of(at.c * blk, blk), blk)

    own = [
        pltpu.make_async_copy(tokens_ref, buf.at[mine, :], own_sem.at[0]),
        pltpu.make_async_copy(gains_ref, gain_land.at[at.me], own_sem.at[1]),
        pltpu.make_async_copy(w_qkv_ref, w_line.at[at.z], own_sem.at[2]),
        pltpu.make_async_copy(w_out_ref, w_out.at[at.z], own_sem.at[3]),
        pltpu.make_async_copy(d_mlp_ref, d_mlp_rows(at.z, at.q, 0, blk), own_sem.at[4]),
    ]
    for copy in own:
        copy.start()
    at.greet_all()
    gain_push = (lambda other: gains_ref, lambda slot: gain_land.at[slot], gain_send, gain_recv)
    top_push = (lambda other: top_land.at[at.me], lambda slot: top_land.at[slot], top_send, top_recv)

    def qkv_line(place, way):
        return remote(w_line.at[place], w_line.at[place], line_send.at[place, way], line_recv.at[place], (at.c, at.z + 1 - 2 * way))

    def out_line(place, way):
        return remote(w_out.at[place], w_out.at[place], out_send.at[place, way], out_recv.at[place], (at.c, at.z + 1 - 2 * way))

    def qkv_copy(i, place, arriving=False):
        other = lax.rem(at.c + i, 8)
        slot = (other if arriving else at.c) * line + place
        return remote(w_line.at[place, other], w_qkv.at[slot], qkv_send.at[place, other], qkv_recv.at[slot], (other, at.z))

    def qkv_step(k):
        at.line_spread(qkv_line, k)

        @pl.loop(1, 8)
        def _(i):
            qkv_copy(i, at.source(k)).start()

        w_qkv[at.c * line + at.source(k)] = w_line[at.source(k), at.c]

    start, turn, rest, whole, end = gather
    own[0].wait()
    start()
    own[2].wait()
    qkv_step(0)
    at.push_all(*gain_push)
    turn()
    qkv_step(1)
    rest()
    for k in range(2, line - 1):
        qkv_step(k)
    own[1].wait()
    at.wait_all(*gain_push, sent=False)
    for i in range(at.every // 2):
        pair = gain_land[2 * i].astype(jnp.float32) + gain_land[2 * i + 1].astype(jnp.float32)
        gain_ref[:, i * 128 : (i + 1) * 128] = pair[:8, :]
    own[4].wait()
    beside.a(0)
    whole()
    end()
    at.wait_all(*gain_push)

    @pl.loop(0, size // 32)
    def _(i):
        part = pl.ds(pl.multiple_of(i * 32, 32), 32)
        rows = buf[part, :].astype(jnp.float32)
        buf[part, :] = (rows * rms_scale(rows) * gain_ref[0:1, :]).astype(jnp.bfloat16)

    writes = [
        pltpu.make_async_copy(buf, normed_ref, write_sem.at[0]),
        pltpu.make_async_copy(w_qkv, w_qkv_all_ref, write_sem.at[1]),
        pltpu.make_async_copy(w_out, w_out_all_ref, write_sem.at[2]),
    ]
    writes[0].start()
    qkv_step(line - 1)
    own[3].wait()
    at.line_spread(out_line, 0)
    beside.b(0)
    for k in range(line):

        @pl.loop(1, 8)
        def _(i):
            qkv_copy(i, at.source(k), True).wait_recv()

    writes[1].start()

    @pl.loop(0, size // 256)
    def _(i):
        part = pl.ds(pl.multiple_of(i * 256, 256), 256)
        qkv_ref[part, :] = dot(buf[part, :], w_qkv[...].reshape(width, q_part + 2 * kv_part), ((1,), (0,))).astype(jnp.bfloat16)

    at.line_spread(out_line, 1)
    beside.a(1)
    heads = q_part // HEAD_DIM
    block = math.gcd(size, 256)
    tops = [jnp.full((1, 1), NEGATIVE, jnp.float32)] * heads
    for i in range(size // block):
        if i > 0 and i + 1 < line:
            at.line_spread(out_line, i + 1)
        rows, cols = pl.ds(i * block, block), (i + 1) * block
        live = seen_mask(i * block, block, cols, q_seg_ref[rows, :], k_seg_ref[:, :cols])
        keys, values = qkv_ref[:cols, q_part : q_part + kv_part], qkv_ref[:cols, q_part + kv_part :]
        for h in range(heads):
            span = slice(h * HEAD_DIM, (h + 1) * HEAD_DIM)
            scores = dot(qkv_ref[rows, span], keys, ((1,), (1,))) * SCALE
            scores = jnp.where(live, scores, NEGATIVE)
            peak = jnp.max(scores, axis=-1, keepdims=True)
            weights = jnp.exp(scores - peak)
            total = jnp.sum(weights, axis=-1, keepdims=True)
            out = dot(weights.astype(jnp.bfloat16), values, ((1,), (0,)))
            attn_ref[rows, span] = (out / total).astype(jnp.bfloat16)
            lse_ref[rows, h : h + 1] = peak + jnp.log(total)
            tops[h] = jnp.maximum(tops[h], jnp.max(peak, axis=0, keepdims=True))
    lanes = lax.broadcasted_iota(jnp.int32, (8, 128), 1)
    tile = jnp.full((8, 128), NEGATIVE, jnp.float32)
    for h in range(heads):
        tile = jnp.where(lanes == h, tops[h], tile)
    top_land[at.me] = tile
    at.push_all(*top_push)

    for k in range(size // block + 1, line):
        at.line_spread(out_line, k)
    beside.b(1)
    beside.a(2)
    writes[2].start()
    for i, chip in enumerate((at.qd, at.qx, at.qy, at.q)):
        for core in (1 - at.core, at.core):
            part = pl.ds(pl.multiple_of((2 * chip + core) * blk, blk), blk)

            @pl.loop(0, width // 512)
            def _(j):
                span = pl.ds(pl.multiple_of(j * 512, 512), 512)
                matrix = w_out[:, :, span].reshape(line * w_rows, 512)
                term[part, span] = dot(attn_ref[part, :], matrix, ((1,), (0,))).astype(jnp.bfloat16)

        reduce[0](i)
    reduce[1](proj)
    beside.b(2)
    for k in range(3, line):
        beside.a(k)
        beside.b(k)

    own_again = pltpu.make_async_copy(tokens_ref, land.at[pl.ds(0, blk), :], own_sem.at[0])
    own_again.start()
    own_again.wait()

    @pl.loop(0, blk // 32)
    def _(i):
        part = pl.ds(pl.multiple_of(i * 32, 32), 32)
        rows = land[part, :].astype(jnp.float32) + BRANCH * proj[part, :]
        mid_ref[part, :] = rows
        normed_two_ref[part, :] = (rows * rms_scale(rows) * gain_ref[1:2, :]).astype(jnp.bfloat16)

    at.wait_all(*top_push, sent=False)
    tops_ref[...] = top_land[...]
    reduce[2]()
    at.wait_all(*top_push)
    for k in range(line):
        at.line_sent(qkv_line, k)
        at.line_sent(out_line, k)

        @pl.loop(1, 8)
        def _(i):
            qkv_copy(i, at.source(k)).wait_send()

    for k in range(line):
        beside.c(k)
    for copy in writes:
        copy.wait()


def front(line, tokens, d_mlp, gains, w_qkv, w_out, q_seg, k_seg):
    blk, width = tokens.shape
    w_rows, cols = w_out.shape[0], w_qkv.shape[2]
    size, every = 8 * blk, 8 * line
    q_part = HEADS * HEAD_DIM // 8
    kv_part = (cols - q_part) // 2
    heads = q_part // HEAD_DIM
    any_spec, vmem_spec = pl.BlockSpec(memory_space=pl.ANY), pl.BlockSpec(memory_space=pltpu.VMEM)
    bf16, f32, dma, out = jnp.bfloat16, jnp.float32, pltpu.SemaphoreType.DMA, jax.ShapeDtypeStruct
    return pl.pallas_call(
        functools.partial(front_kernel, line, blk, q_part, kv_part),
        out_shape=(
            out((blk, width), f32),
            out((blk, width), bf16),
            out((size, cols), bf16),
            out((size, q_part), bf16),
            out((size, heads), f32),
            out((every, 8, 128), f32),
            out((8, width), f32),
            out((size, width), bf16),
            out((every, w_rows, cols), bf16),
            out((line, w_rows, width), bf16),
            out((line * 4 * blk, width), bf16),
        ),
        in_specs=[any_spec] * 5 + [vmem_spec] * 2,
        out_specs=(vmem_spec,) * 7 + (any_spec,) * 4,
        scratch_shapes=[
            pltpu.VMEM((size, width), bf16),
            pltpu.VMEM((size, width), bf16),
            pltpu.VMEM((4, blk, width), bf16),
            pltpu.VMEM((3 * blk, width), bf16),
            pltpu.VMEM((every, w_rows, cols), bf16),
            pltpu.VMEM((line, 8, w_rows, cols), bf16),
            pltpu.VMEM((line, w_rows, width), bf16),
            pltpu.VMEM((every, 16, 128), bf16),
            pltpu.VMEM((every, 8, 128), f32),
            pltpu.VMEM((blk, width), f32),
            *[dma((n,)) for n in GATHER_SEMS + REDUCE_SEMS],
            dma((line, 2)),
            dma((line,)),
            dma((line, 8)),
            *[dma((every,))] * 5,
            dma((line, 2)),
            dma((line,)),
            dma((5,)),
            dma((3,)),
            *slice_gather_sems(line),
        ],
        compiler_params=pltpu.CompilerParams(collective_id=1, has_side_effects=True, vmem_limit_bytes=60 * MIB),
    )(tokens, d_mlp, gains, w_qkv, w_out, q_seg, k_seg)


def back_kernel(
    line, blk, q_part, kv_part,
    d_attn_ref, tokens_ref, mid_ref, d_mid_ref, qkv_ref, attn_ref, lse_ref, gain_ref, gain_term_ref, q_seg_ref, k_seg_ref, normed_ref, w_qkv_ref, w_out_ref, mlp_term_ref,
    mixed_ref, grad_tokens_ref, grad_qkv_ref, grad_out_ref, gain_sum_ref,
    buf, term, core_land, land, w_qkv, w_out, normed, d_heads, d_qkv, dk_sum, dv_sum, stage_qkv, stage_out, qkv_land, out_land, gain_stage, gain_land, d_normed, mlp_term, mlp_land, mlp_line_land, mlp_sum,
    *sems,
):
    at = Place(line)
    gather = plane_gather(at, buf, blk, sems[:6])
    reduce = plane_reduce(at, term, core_land, land, blk, sems[6:12])
    qkv_send, qkv_recv, gain_send, gain_recv, out_send, out_recv, own_sem = sems[12:19]
    beside = SliceReduce(at, slice_rows(mlp_term, blk), blk, mlp_land, mlp_line_land, mlp_sum, sems[19:])
    width = buf.shape[1]
    w_rows = w_out.shape[1]
    size = 8 * blk
    mine = pl.ds(pl.multiple_of(at.c * blk, blk), blk)
    own = [
        pltpu.make_async_copy(d_attn_ref, buf.at[mine, :], own_sem.at[0]),
        pltpu.make_async_copy(w_out_ref, w_out, own_sem.at[1]),
        pltpu.make_async_copy(w_qkv_ref, w_qkv, own_sem.at[2]),
        pltpu.make_async_copy(normed_ref, normed, own_sem.at[3]),
        pltpu.make_async_copy(mlp_term_ref, mlp_term, own_sem.at[4]),
    ]
    for copy in own:
        copy.start()
    at.greet_all()
    own[0].wait()
    start, turn, rest, whole, end = gather
    start()
    turn()
    rest()
    for copy in own[1:]:
        copy.wait()
    beside.a(line - 1)
    whole()

    @pl.loop(0, size // 256)
    def _(i):
        part = pl.ds(pl.multiple_of(i * 256, 256), 256)
        d_heads[part, :] = dot(buf[part, :], w_out[...].reshape(line * w_rows, width), ((1,), (1,))).astype(jnp.bfloat16)

    if line > 1:
        beside.a(line - 2)

    @pl.loop(0, width // 256)
    def _(i):
        span = pl.ds(pl.multiple_of(i * 256, 256), 256)
        stage_out[:, :, span] = dot(attn_ref[...], buf[:, span], ((0,), (0,))).astype(jnp.bfloat16).reshape(line, w_rows, 256)

    def out_copy(i):
        z = lax.rem(at.z + i, line)
        return remote(stage_out.at[z], out_land.at[at.z], out_send.at[z], out_recv.at[at.z], (at.c, z))

    def out_arrival(i):
        z = lax.rem(at.z + i, line)
        return remote(stage_out.at[z], out_land.at[z], out_send.at[z], out_recv.at[z], (at.c, z))

    for i in range(1, line):
        out_copy(i).start()

    heads = q_part // HEAD_DIM
    block = math.gcd(size, 256)
    dk_sum[...] = jnp.zeros_like(dk_sum)
    dv_sum[...] = jnp.zeros_like(dv_sum)
    for i in range(size // block):
        rows, cols = pl.ds(i * block, block), (i + 1) * block
        live = seen_mask(i * block, block, cols, q_seg_ref[rows, :], k_seg_ref[:, :cols])
        keys, values = qkv_ref[:cols, q_part : q_part + kv_part], qkv_ref[:cols, q_part + kv_part :]
        for h in range(heads):
            span = slice(h * HEAD_DIM, (h + 1) * HEAD_DIM)
            queries, d_out = qkv_ref[rows, span], d_heads[rows, span]
            delta = jnp.sum(d_out.astype(jnp.float32) * attn_ref[rows, span].astype(jnp.float32), axis=-1, keepdims=True)
            scores = dot(queries, keys, ((1,), (1,))) * SCALE
            probs = jnp.where(live, jnp.exp(scores - lse_ref[rows, h : h + 1]), 0.0)
            d_probs = dot(d_out, values, ((1,), (1,)))
            d_scores = (probs * (d_probs - delta)).astype(jnp.bfloat16)
            d_qkv[rows, span] = (dot(d_scores, keys, ((1,), (0,))) * SCALE).astype(jnp.bfloat16)
            dk_sum[:cols, :] += dot(d_scores, queries, ((0,), (0,)))
            dv_sum[:cols, :] += dot(probs.astype(jnp.bfloat16), d_out, ((0,), (0,)))
    d_qkv[:, q_part : q_part + kv_part] = (dk_sum[...] * SCALE).astype(jnp.bfloat16)
    d_qkv[:, q_part + kv_part :] = dv_sum[...].astype(jnp.bfloat16)
    beside.b(line - 1)
    for k in range(line - 3, 0, -1):
        beside.a(k)

    for i, chip in enumerate((at.qd, at.qx, at.qy, at.q)):
        for core in (1 - at.core, at.core):
            part = pl.ds(pl.multiple_of((2 * chip + core) * blk, blk), blk)

            @pl.loop(0, width // 512)
            def _(j):
                span = pl.ds(pl.multiple_of(j * 512, 512), 512)
                matrix = w_qkv[pl.ds(pl.multiple_of(j * (512 // w_rows), 512 // w_rows), 512 // w_rows)].reshape(512, q_part + 2 * kv_part)
                term[part, span] = dot(d_qkv[part, :], matrix, ((1,), (1,))).astype(jnp.bfloat16)

        reduce[0](i)

    @pl.loop(0, width // 256)
    def _(i):
        span = pl.ds(pl.multiple_of(i * 256, 256), 256)
        blocks = pl.ds(pl.multiple_of(i * (256 // w_rows), 256 // w_rows), 256 // w_rows)
        grads = dot(normed[:, span], d_qkv[...], ((0,), (0,))).astype(jnp.bfloat16)
        stage_qkv[blocks] = grads.reshape(256 // w_rows, w_rows, q_part + 2 * kv_part)

    qkv_push = (lambda other: stage_qkv.at[other], lambda slot: qkv_land.at[slot], qkv_send, qkv_recv)
    at.push_all(*qkv_push)
    qkv_land[at.me] = stage_qkv[at.me]
    out_land[at.z] = stage_out[at.z]
    reduce[1](d_normed)
    if line > 2:
        beside.a(0)
    for k in range(line - 2, -1, -1):
        beside.b(k)

    gain_stage[...] = jnp.zeros_like(gain_stage)
    gain_stage[1:2, :] = gain_term_ref[...]

    @pl.loop(0, blk // 32)
    def _(i):
        part = pl.ds(pl.multiple_of(i * 32, 32), 32)
        rows = tokens_ref[part, :].astype(jnp.float32)
        d_rows, gain_term = norm_backward(d_normed[part, :], rows, rms_scale(rows), gain_ref[0:1, :])
        grad_tokens_ref[part, :] = d_mid_ref[part, :] + d_rows
        gain_stage[0:1, :] += gain_term.reshape(1, width)

    def gain_tile(other):
        return gain_stage.at[:, pl.ds(pl.multiple_of((other // 2) * 128, 128), 128)]

    gain_push = (gain_tile, lambda slot: gain_land.at[slot], gain_send, gain_recv)
    at.push_all(*gain_push)
    gain_land[at.me] = gain_stage[:, pl.ds(pl.multiple_of((at.me // 2) * 128, 128), 128)]

    for k in range(line - 1, -1, -1):
        beside.c(k)
    mixed_ref[...] = (mid_ref[...] + BRANCH * mlp_sum[...]).astype(jnp.bfloat16)
    for i in range(1, line):
        out_arrival(i).wait_recv()
    total = out_land[0].astype(jnp.float32)
    for i in range(1, line):
        total = total + out_land[i].astype(jnp.float32)
    grad_out_ref[...] = total
    at.wait_all(*qkv_push, sent=False)

    @pl.loop(0, 8)
    def _(i):
        total = qkv_land[i * line].astype(jnp.float32)
        for j in range(1, line):
            total = total + qkv_land[i * line + j].astype(jnp.float32)
        grad_qkv_ref[i] = total

    at.wait_all(*gain_push, sent=False)
    gain_sum_ref[...] = jnp.sum(gain_land[...], axis=0)
    end()
    reduce[2]()
    for k in range(line):
        beside.end(k)
    at.wait_all(*qkv_push)
    at.wait_all(*gain_push)
    for i in range(1, line):
        out_copy(i).wait_send()


def back(line, d_attn, tokens, mid, d_mid, qkv, attn_out, lse, gain, gain_term, q_seg, k_seg, normed, w_qkv, w_out, mlp_term):
    blk, width = tokens.shape
    w_rows, cols = w_out.shape[1], w_qkv.shape[2]
    size, every = 8 * blk, 8 * line
    q_part = HEADS * HEAD_DIM // 8
    kv_part = (cols - q_part) // 2
    any_spec, vmem_spec = pl.BlockSpec(memory_space=pl.ANY), pl.BlockSpec(memory_space=pltpu.VMEM)
    bf16, f32, dma, out = jnp.bfloat16, jnp.float32, pltpu.SemaphoreType.DMA, jax.ShapeDtypeStruct
    return pl.pallas_call(
        functools.partial(back_kernel, line, blk, q_part, kv_part),
        out_shape=(out((blk, width), bf16), out((blk, width), f32), out((8, w_rows, cols), f32), out((w_rows, width), f32), out((8, 128), f32)),
        in_specs=[any_spec] + [vmem_spec] * 10 + [any_spec] * 4,
        out_specs=(vmem_spec,) * 5,
        scratch_shapes=[
            pltpu.VMEM((size, width), bf16),
            pltpu.VMEM((size, width), bf16),
            pltpu.VMEM((4, blk, width), bf16),
            pltpu.VMEM((3 * blk, width), bf16),
            pltpu.VMEM((every, w_rows, cols), bf16),
            pltpu.VMEM((line, w_rows, width), bf16),
            pltpu.VMEM((size, width), bf16),
            pltpu.VMEM((size, q_part), bf16),
            pltpu.VMEM((size, cols), bf16),
            pltpu.VMEM((size, kv_part), f32),
            pltpu.VMEM((size, kv_part), f32),
            pltpu.VMEM((every, w_rows, cols), bf16),
            pltpu.VMEM((line, w_rows, width), bf16),
            pltpu.VMEM((every, w_rows, cols), bf16),
            pltpu.VMEM((line, w_rows, width), bf16),
            pltpu.VMEM((8, width), f32),
            pltpu.VMEM((every, 8, 128), f32),
            pltpu.VMEM((blk, width), f32),
            pltpu.VMEM((line * 4 * blk, width), bf16),
            pltpu.VMEM((line, 3 * blk, width), bf16),
            pltpu.VMEM((line + 1, blk, width), bf16),
            pltpu.VMEM((blk, width), f32),
            *[dma((n,)) for n in GATHER_SEMS + REDUCE_SEMS + (every,) * 4 + (line, line, 5)],
            *slice_reduce_sems(line),
        ],
        compiler_params=pltpu.CompilerParams(collective_id=2, has_side_effects=True, vmem_limit_bytes=60 * MIB),
    )(d_attn, tokens, mid, d_mid, qkv, attn_out, lse, gain, gain_term, q_seg, k_seg, normed, w_qkv, w_out, mlp_term)


def split_heads(w, parts):
    rows = w.shape[0]
    q_width, kv_width = HEADS * HEAD_DIM, KV_HEADS * HEAD_DIM
    copies = max(1, parts // KV_HEADS)
    q = w[:, :q_width].reshape(rows, parts, q_width // parts)
    k = w[:, q_width : q_width + kv_width].reshape(rows, parts // copies, 1, -1)
    v = w[:, q_width + kv_width :].reshape(rows, parts // copies, 1, -1)
    k, v = (jnp.broadcast_to(a, (rows, parts // copies, copies, a.shape[3])).reshape(rows, parts, -1) for a in (k, v))
    return jnp.concatenate([q, k, v], axis=2)


def join_heads(grads, parts):
    rows = grads.shape[0]
    copies = max(1, parts // KV_HEADS)
    q_part = HEADS * HEAD_DIM // parts
    kv_part = (grads.shape[2] - q_part) // 2
    q = grads[:, :, :q_part].reshape(rows, -1)
    k, v = (
        jnp.sum(grads[:, :, at : at + kv_part].reshape(rows, parts // copies, copies, kv_part), axis=2).reshape(rows, -1)
        for at in (q_part, q_part + kv_part)
    )
    return jnp.concatenate([q, k, v], axis=1)


def per_device(n_ctx, n_shard, tokens, lengths, cotangent, w_qkv, w_out, w_gate_up, w_down, gain_attn, gain_mlp):
    count, width = tokens.shape[1:]
    n = n_ctx * n_shard
    w_rows = w_qkv.shape[0]
    ff_part = w_down.shape[0]
    q_part = HEADS * HEAD_DIM // n_ctx
    rows = tokens.reshape(count, width).astype(jnp.float32)
    grad_rows = cotangent.reshape(count, width).astype(jnp.float32)
    size = count * n_ctx
    positions = jnp.arange(size, dtype=jnp.int32)
    seg = segment_ids(positions, lengths[0])
    q_seg, k_seg = seg.reshape(size, 1), seg.reshape(1, size)

    gains = lax.all_gather(jnp.stack([gain_attn, gain_mlp]), EVERY, axis=1, tiled=True).astype(jnp.float32)
    gain_one, gain_two = gains[0], gains[1]

    qkv_cols = lax.all_to_all(split_heads(w_qkv, n_ctx), "ctx", split_axis=1, concat_axis=1, tiled=True)
    qkv_cols = qkv_cols.reshape(w_rows, n_ctx, -1).transpose(1, 0, 2)
    qkv_mine = lax.all_gather(qkv_cols, "shard", axis=1, tiled=True).reshape(width, -1)
    out_mine = lax.all_gather(w_out, "shard", axis=0, tiled=True)
    gate_up_mine = lax.all_to_all(w_gate_up.reshape(w_rows, 2, n, ff_part), EVERY, split_axis=2, concat_axis=0, tiled=True)
    gate_up_mine = gate_up_mine.reshape(width, 2 * ff_part)

    scale_one = rms_scale(rows)
    normed_one = lax.all_gather((rows * scale_one * gain_one).astype(jnp.bfloat16), "ctx", axis=0, tiled=True)
    projected = dot(normed_one, qkv_mine, ((1,), (0,))).astype(jnp.bfloat16)
    kv_part = (projected.shape[1] - q_part) // 2
    queries, keys, values = (
        projected[:, :q_part],
        projected[:, q_part : q_part + kv_part],
        projected[:, q_part + kv_part :],
    )
    attn_out, lse, tops = attend(queries, keys, values, q_seg, k_seg)
    out_term = dot(attn_out, out_mine, ((1,), (0,))).astype(jnp.bfloat16)
    attn_proj = lax.psum_scatter(out_term, "ctx", scatter_dimension=0, tiled=True)
    mid = rows + BRANCH * attn_proj.astype(jnp.float32)
    head_top = lax.all_gather(lax.pmax(tops, "shard"), "ctx", axis=1, tiled=True).reshape(HEADS)
    clip = CLIP_TARGET / jnp.maximum(head_top, CLIP_TARGET)

    scale_two = rms_scale(mid)
    d_mlp = lax.all_gather((BRANCH * grad_rows).astype(jnp.bfloat16), EVERY, axis=0, tiled=True)
    normed_two = lax.all_gather((mid * scale_two * gain_two).astype(jnp.bfloat16), EVERY, axis=0, tiled=True)
    gate_up = dot(normed_two, gate_up_mine, ((1,), (0,)))
    gate, up = gate_up[:, :ff_part], gate_up[:, ff_part:]
    sigma = jax.nn.sigmoid(gate)
    active = gate * sigma
    hidden = (active * up).astype(jnp.bfloat16)
    down_term = dot(hidden, w_down, ((1,), (0,))).astype(jnp.bfloat16)
    d_hidden = dot(d_mlp, w_down, ((1,), (1,)))
    d_gate = d_hidden * up * sigma * (1.0 + gate * (1.0 - sigma))
    d_up = d_hidden * active
    d_gate_up = jnp.concatenate([d_gate, d_up], axis=1).astype(jnp.bfloat16)
    normed_term = dot(d_gate_up, gate_up_mine, ((1,), (1,))).astype(jnp.bfloat16)
    grad_down = dot(hidden, d_mlp, ((0,), (0,)))
    gate_up_grad = dot(normed_two, d_gate_up, ((0,), (0,))).astype(jnp.bfloat16)
    mlp_proj = lax.psum_scatter(down_term, EVERY, scatter_dimension=0, tiled=True)
    mixed = (mid + BRANCH * mlp_proj.astype(jnp.float32)).astype(jnp.bfloat16).reshape(1, count, width)
    d_normed_two = lax.psum_scatter(normed_term, EVERY, scatter_dimension=0, tiled=True).astype(jnp.float32)
    grad_gate_up = lax.all_to_all(gate_up_grad.reshape(n * w_rows, 2, 1, ff_part), EVERY, split_axis=0, concat_axis=2, tiled=True)
    grad_gate_up = grad_gate_up.reshape(w_rows, 2 * n * ff_part).astype(jnp.float32)
    d_mid_norm, gain_two_term = norm_backward(d_normed_two, mid, scale_two, gain_two)
    d_mid = grad_rows + d_mid_norm

    d_attn = lax.all_gather((BRANCH * d_mid).astype(jnp.bfloat16), "ctx", axis=0, tiled=True)
    grad_out = lax.psum_scatter(dot(attn_out, d_attn, ((0,), (0,))), "shard", scatter_dimension=0, tiled=True)
    d_heads = dot(d_attn, out_mine, ((1,), (1,))).astype(jnp.bfloat16)
    d_q, d_k, d_v = attend_back(queries, keys, values, attn_out, d_heads, lse, q_seg, k_seg)
    d_qkv = jnp.concatenate([d_q, d_k, d_v], axis=1)
    qkv_term = dot(d_qkv, qkv_mine, ((1,), (1,))).astype(jnp.bfloat16)
    d_normed_one = lax.psum_scatter(qkv_term, "ctx", scatter_dimension=0, tiled=True).astype(jnp.float32)
    qkv_grad = dot(normed_one, d_qkv, ((0,), (0,))).reshape(n_ctx, n_shard * w_rows, -1)
    qkv_grad = lax.psum_scatter(qkv_grad, "shard", scatter_dimension=1, tiled=True)
    qkv_grad = lax.all_to_all(qkv_grad, "ctx", split_axis=0, concat_axis=0, tiled=True)
    grad_qkv = join_heads(qkv_grad.transpose(1, 0, 2), n_ctx)
    d_rows_norm, gain_one_term = norm_backward(d_normed_one, rows, scale_one, gain_one)
    grad_tokens = (d_mid + d_rows_norm).reshape(1, count, width)
    gain_terms = lax.psum_scatter(jnp.stack([gain_one_term, gain_two_term]), EVERY, scatter_dimension=1, tiled=True)
    return (mixed, grad_tokens, grad_qkv, grad_out, grad_gate_up, grad_down, gain_terms[0], gain_terms[1], clip)


def on_planes(n_shard, tokens, lengths, cotangent, w_qkv, w_out, w_gate_up, w_down, gain_attn, gain_mlp):
    count, width = tokens.shape[1:]
    w_rows = w_qkv.shape[0]
    rows = tokens.reshape(count, width)
    grad_rows = cotangent.reshape(count, width).astype(jnp.float32)
    size = count * 8
    seg = segment_ids(jnp.arange(size, dtype=jnp.int32), lengths[0])
    q_seg, k_seg = seg.reshape(size, 1), seg.reshape(1, size)
    side = lax.rem(lax.axis_index("ctx") * n_shard + lax.axis_index("shard"), 2)

    gains = jnp.stack([gain_attn, gain_mlp])
    none = jnp.zeros_like(gains)
    gains = jnp.where(side == 0, jnp.concatenate([gains, none], axis=1), jnp.concatenate([none, gains], axis=1))
    gains = jnp.pad(gains, ((0, 14), (0, 0)))
    mid, normed_two, qkv, attn_out, lse, tops, gain, normed_one, qkv_mine, out_mine, d_mlp = front(
        n_shard, rows, (BRANCH * grad_rows).astype(jnp.bfloat16), gains, split_heads(w_qkv, 8).transpose(1, 0, 2), w_out, q_seg, k_seg
    )
    heads = HEADS // 8
    head_top = jnp.max(tops[:, 0, :heads].reshape(8, n_shard, heads), axis=1).reshape(HEADS)
    clip = CLIP_TARGET / jnp.maximum(head_top, CLIP_TARGET)

    mlp_term, d_normed_two, grad_gate_up, grad_down = mlp_exchange(n_shard, normed_two, d_mlp, w_gate_up, w_down)
    d_mid_norm, gain_two_term = norm_backward(d_normed_two, mid, rms_scale(mid), gain[1:2])
    d_mid = grad_rows + d_mid_norm

    d_attn = (BRANCH * d_mid).astype(jnp.bfloat16)
    mixed, grad_tokens, qkv_grad, grad_out, gain_sum = back(
        n_shard, d_attn, rows, mid, d_mid, qkv, attn_out, lse, gain, gain_two_term.reshape(1, width), q_seg, k_seg, normed_one, qkv_mine, out_mine, mlp_term
    )
    grad_qkv = join_heads(qkv_grad.transpose(1, 0, 2), 8)
    gain_grads = jnp.where(side == 0, gain_sum[:2, :w_rows], gain_sum[:2, w_rows : 2 * w_rows])
    return (mixed.reshape(1, count, width), grad_tokens.reshape(1, count, width), grad_qkv, grad_out, grad_gate_up, grad_down, gain_grads[0], gain_grads[1], clip)


def solution(mesh):
    by_token, by_row = P("shard", "ctx", None), P(EVERY, None)
    n_ctx, n_shard = mesh.shape["ctx"], mesh.shape["shard"]
    program = functools.partial(on_planes, n_shard) if n_ctx == 8 else functools.partial(per_device, n_ctx, n_shard)
    return jax.shard_map(
        program,
        mesh=mesh,
        in_specs=(by_token, P("shard", None), by_token, by_row, by_row, by_row, by_row, P(EVERY), P(EVERY)),
        out_specs=(by_token, by_token, by_row, by_row, by_row, by_row, P(EVERY), P(EVERY), P()),
        check_vma=False,
    )
```

```python
import functools
import math

import jax
import jax.numpy as jnp
from jax import lax
from jax.experimental import pallas as pl
from jax.experimental.pallas import tpu as pltpu
from jax.sharding import PartitionSpec as P

HEADS = 32
KV_HEADS = 8
HEAD_DIM = 64


SCALE = 0.015625
BRANCH = 0.22
EPSILON = 1e-05
CLIP_TARGET = 4.0
NEGATIVE = -1e30
MIB = 1024 * 1024
EVERY = ("ctx", "shard")


def segment_ids(positions, lengths_row):
    bounds = jnp.cumsum(lengths_row)[:-1]
    return jnp.sum((positions[:, None] >= bounds[None, :]).astype(jnp.int32), axis=1)


def rms_scale(rows):
    return lax.rsqrt(jnp.mean(rows * rows, axis=-1, keepdims=True) + EPSILON)


def norm_backward(d_normed, rows, scale, gain):
    unit = rows * scale
    d_unit = d_normed * gain
    gain_term = jnp.sum(d_normed * unit, axis=0)
    d_rows = scale * (d_unit - unit * jnp.mean(d_unit * unit, axis=-1, keepdims=True))
    return (d_rows, gain_term)


def dot(left, right, dims):
    return lax.dot_general(left, right, ((dims[0], dims[1]), ((), ())), preferred_element_type=jnp.float32)


def seen_mask(row0, rows, cols, q_seg, k_seg):
    q_pos = row0 + lax.broadcasted_iota(jnp.int32, (rows, cols), 0)
    k_pos = lax.broadcasted_iota(jnp.int32, (rows, cols), 1)
    return (k_pos <= q_pos) & ((k_seg == 0) | (k_seg == q_seg))


def attend_kernel(heads, block, q_ref, k_ref, v_ref, q_seg_ref, k_seg_ref, o_ref, lse_ref, top_ref):
    size = q_ref.shape[0]
    tops = [jnp.full((1, 1), NEGATIVE, jnp.float32)] * heads
    for i in range(size // block):
        rows, cols = pl.ds(i * block, block), (i + 1) * block
        live = seen_mask(i * block, block, cols, q_seg_ref[rows, :], k_seg_ref[:, :cols])
        keys, values = k_ref[:cols, :], v_ref[:cols, :]
        for h in range(heads):
            span = slice(h * HEAD_DIM, (h + 1) * HEAD_DIM)
            scores = dot(q_ref[rows, span], keys, ((1,), (1,))) * SCALE
            scores = jnp.where(live, scores, NEGATIVE)
            peak = jnp.max(scores, axis=-1, keepdims=True)
            weights = jnp.exp(scores - peak)
            total = jnp.sum(weights, axis=-1, keepdims=True)
            out = dot(weights.astype(jnp.bfloat16), values, ((1,), (0,)))
            o_ref[rows, span] = (out / total).astype(jnp.bfloat16)
            lse_ref[rows, h : h + 1] = peak + jnp.log(total)
            tops[h] = jnp.maximum(tops[h], jnp.max(peak, axis=0, keepdims=True))
    for h in range(heads):
        top_ref[:, h : h + 1] = tops[h]


def attend(queries, keys, values, q_seg, k_seg):
    size, width = queries.shape
    heads = width // HEAD_DIM
    return pl.pallas_call(
        functools.partial(attend_kernel, heads, math.gcd(size, 256)),
        out_shape=(
            jax.ShapeDtypeStruct((size, width), jnp.bfloat16),
            jax.ShapeDtypeStruct((size, heads), jnp.float32),
            jax.ShapeDtypeStruct((1, heads), jnp.float32),
        ),
        compiler_params=pltpu.CompilerParams(vmem_limit_bytes=48 * MIB),
    )(queries, keys, values, q_seg, k_seg)


def attend_back_kernel(
    heads, block, q_ref, k_ref, v_ref, o_ref, do_ref, lse_ref, q_seg_ref, k_seg_ref, dq_ref, dk_ref, dv_ref, dk_sum, dv_sum
):
    size = q_ref.shape[0]
    dk_sum[...] = jnp.zeros_like(dk_sum)
    dv_sum[...] = jnp.zeros_like(dv_sum)
    for i in range(size // block):
        rows, cols = pl.ds(i * block, block), (i + 1) * block
        live = seen_mask(i * block, block, cols, q_seg_ref[rows, :], k_seg_ref[:, :cols])
        keys, values = k_ref[:cols, :], v_ref[:cols, :]
        for h in range(heads):
            span = slice(h * HEAD_DIM, (h + 1) * HEAD_DIM)
            queries, d_out = q_ref[rows, span], do_ref[rows, span]
            delta = jnp.sum(d_out.astype(jnp.float32) * o_ref[rows, span].astype(jnp.float32), axis=-1, keepdims=True)
            scores = dot(queries, keys, ((1,), (1,))) * SCALE
            probs = jnp.where(live, jnp.exp(scores - lse_ref[rows, h : h + 1]), 0.0)
            d_probs = dot(d_out, values, ((1,), (1,)))
            d_scores = (probs * (d_probs - delta)).astype(jnp.bfloat16)
            dq_ref[rows, span] = (dot(d_scores, keys, ((1,), (0,))) * SCALE).astype(jnp.bfloat16)
            dk_sum[:cols, :] += dot(d_scores, queries, ((0,), (0,)))
            dv_sum[:cols, :] += dot(probs.astype(jnp.bfloat16), d_out, ((0,), (0,)))
    dk_ref[...] = (dk_sum[...] * SCALE).astype(jnp.bfloat16)
    dv_ref[...] = dv_sum[...].astype(jnp.bfloat16)


def attend_back(queries, keys, values, out, d_out, lse, q_seg, k_seg):
    size, width = queries.shape
    heads = width // HEAD_DIM
    like_kv = jax.ShapeDtypeStruct((size, HEAD_DIM), jnp.bfloat16)
    return pl.pallas_call(
        functools.partial(attend_back_kernel, heads, math.gcd(size, 256)),
        out_shape=(jax.ShapeDtypeStruct((size, width), jnp.bfloat16), like_kv, like_kv),
        scratch_shapes=[pltpu.VMEM((size, HEAD_DIM), jnp.float32)] * 2,
        compiler_params=pltpu.CompilerParams(vmem_limit_bytes=48 * MIB),
    )(queries, keys, values, out, d_out, lse, q_seg, k_seg)


def remote(src, dst, send_sem, recv_sem, device):
    return pltpu.make_async_remote_copy(
        src_ref=src, dst_ref=dst, send_sem=send_sem, recv_sem=recv_sem, device_id=device, device_id_type=pl.DeviceIdType.MESH
    )


def greet(devices, extra):
    barrier = pltpu.get_barrier_semaphore()
    count = len(devices)
    for device in devices:
        pl.semaphore_signal(barrier, inc=1, device_id=device, device_id_type=pl.DeviceIdType.MESH)
    for condition, device in extra:

        @pl.when(condition)
        def _():
            pl.semaphore_signal(barrier, inc=1, device_id=device, device_id_type=pl.DeviceIdType.MESH)

        count = count + condition.astype(jnp.int32)
    pl.semaphore_wait(barrier, count)


def add_rows(target, sources, rows, keep=None, step=32):
    @pl.loop(0, rows // step)
    def _(i):
        part = pl.ds(pl.multiple_of(i * step, step), step)
        total = target[part, :].astype(jnp.float32)
        for source in sources:
            total = total + source[part, :].astype(jnp.float32)
        if keep is None:
            target[part, :] = total.astype(jnp.bfloat16)
        else:
            keep[part, :] = total


class Place:
    def __init__(self, line):
        self.line = line
        self.c, self.z = lax.axis_index("ctx"), lax.axis_index("shard")
        self.q, self.core = self.c // 2, self.c % 2
        self.me = self.c * line + self.z
        self.every = 8 * line
        self.cx, self.cy = (self.c + 2 - 4 * (self.q % 2), self.z), (self.c + 4 - 8 * (self.q // 2), self.z)
        self.sibling = (self.c + 1 - 2 * self.core, self.z)
        self.qx, self.qy, self.qd = self.q + 1 - 2 * (self.q % 2), self.q + 2 - 4 * (self.q // 2), 3 - self.q

    def source(self, k):
        if self.line == 1:
            return self.z * 0
        mirrored = self.z >= self.line // 2
        near = jnp.where(mirrored, self.line - 1 - self.z, self.z)
        turn = (k + 1) // 2
        both = near - turn if k % 2 == 1 else near + turn
        at = jnp.where(k <= 2 * near, both, k)
        return jnp.where(mirrored, self.line - 1 - at, at)

    def line_spread(self, copy, k):
        at = self.source(k)
        if k > 0:
            copy(at, 0).wait_recv()
        for way, condition in enumerate(self.line_ways(at)):

            @pl.when(condition)
            def _():
                copy(at, way).start()

    def line_sent(self, copy, k):
        at = self.source(k)
        for way, condition in enumerate(self.line_ways(at)):

            @pl.when(condition)
            def _():
                copy(at, way).wait_send()

    def line_ways(self, at):
        return ((at <= self.z) & (self.z < self.line - 1), (at >= self.z) & (self.z > 0))

    def peer(self, i):
        other = lax.rem(self.me + i, self.every)
        return other, (other // self.line, other % self.line)

    def greet_all(self):
        barrier = pltpu.get_barrier_semaphore()

        @pl.loop(1, self.every)
        def _(i):
            pl.semaphore_signal(barrier, inc=1, device_id=self.peer(i)[1], device_id_type=pl.DeviceIdType.MESH)

        pl.semaphore_wait(barrier, self.every - 1)

    def push_all(self, source, target, send_sems, recv_sems):
        @pl.loop(1, self.every)
        def _(i):
            other, device = self.peer(i)
            remote(source(other), target(self.me), send_sems.at[other], recv_sems.at[self.me], device).start()

    def wait_all(self, source, target, send_sems, recv_sems, sent=True):
        @pl.loop(1, self.every)
        def _(i):
            other, device = self.peer(i)
            copy = remote(source(other), target(other), send_sems.at[other], recv_sems.at[other], device)
            if sent:
                copy.wait_send()
            else:
                copy.wait_recv()


class SliceGather:
    def __init__(self, place, rows, blk, sems):
        self.place, self.rows, self.half = place, rows, blk // 2
        self.z_send, self.z_recv, self.p_send, self.p_recv, self.f_send, self.f_recv = sems
        p, half = place, blk // 2
        self.ways = ((p.cx, p.qx, 0), (p.cy, p.qy, half), (p.cx, p.qx, half), (p.cy, p.qy, 0))
        self.turns = ((p.qx, 0, p.cy), (p.qy, half, p.cx))

    def line_copy(self, at, way):
        ref = self.rows(at, self.place.q, 0, 2 * self.half)
        return remote(ref, ref, self.z_send.at[at, way], self.z_recv.at[at], (self.place.c, self.place.z + 1 - 2 * way))

    def plane_copy(self, at, i, arriving=False):
        device, chip, first = self.ways[i]
        ref = self.rows(at, chip if arriving else self.place.q, first, self.half)
        return remote(ref, ref, self.p_send.at[at, i], self.p_recv.at[at, i], device)

    def onward_copy(self, at, i, arriving=False):
        chip, first, device = self.turns[i]
        ref = self.rows(at, self.place.qd if arriving else chip, first, self.half)
        return remote(ref, ref, self.f_send.at[at, i], self.f_recv.at[at, i], device)

    def a(self, k):
        self.place.line_spread(self.line_copy, k)
        for i in range(4):
            self.plane_copy(self.place.source(k), i).start()

    def b(self, k):
        at = self.place.source(k)
        for i in (0, 1):
            self.plane_copy(at, i, True).wait_recv()
            self.onward_copy(at, i).start()

    def c(self, k):
        at = self.place.source(k)
        for i in (2, 3):
            self.plane_copy(at, i, True).wait_recv()
        for i in (0, 1):
            self.onward_copy(at, i, True).wait_recv()
        for i in range(4):
            self.plane_copy(at, i).wait_send()
        for i in (0, 1):
            self.onward_copy(at, i).wait_send()
        self.place.line_sent(self.line_copy, k)


def slice_gather_sems(line):
    return [pltpu.SemaphoreType.DMA(shape) for shape in ((line, 2), (line,), (line, 4), (line, 4), (line, 2), (line, 2))]


class SliceReduce:
    def __init__(self, place, rows, blk, land, line_land, result, sems):
        self.place, self.rows, self.blk, self.half = place, rows, blk, blk // 2
        self.land, self.line_land, self.result = land, line_land, result
        self.r2_send, self.r2_recv, self.r3_send, self.r3_recv, self.r4_send, self.r4_recv = sems
        p, half = place, blk // 2
        self.seconds = ((0, p.cy), (half, p.cx))
        self.thirds = ((p.cx, p.qx, 0, 0), (p.cy, p.qy, half, blk + half), (p.cx, p.qx, half, half), (p.cy, p.qy, 0, blk))

    def landing(self, at, first, count):
        return self.land.at[at, pl.ds(first, count), :]

    def second(self, at, i):
        first, device = self.seconds[i]
        return remote(
            self.rows(at, self.place.qd, first, self.half), self.landing(at, 2 * self.blk + first, self.half), self.r2_send.at[at, i], self.r2_recv.at[at, i], device
        )

    def third(self, at, i):
        device, chip, first, lands = self.thirds[i]
        return remote(
            self.rows(at, chip, first, self.half), self.landing(at, lands, self.half), self.r3_send.at[at, i], self.r3_recv.at[at, i], device
        )

    def line_copy(self, at, way):
        p = self.place
        slot = jnp.where((way == 1) & (at == p.z - 1), p.line, at)
        return remote(
            self.rows(at, p.q, 0, self.blk), self.line_land.at[slot], self.r4_send.at[at], self.r4_recv.at[slot], (p.c, p.z + 1 - 2 * way)
        )

    def line_arrival(self, at, slot):
        return remote(self.rows(at, self.place.q, 0, self.blk), self.line_land.at[slot], self.r4_send.at[at], self.r4_recv.at[slot], self.place.sibling)

    def a(self, k):
        at = self.place.source(k)
        for i in (0, 1):
            self.second(at, i).start()
        for i in (2, 3):
            self.third(at, i).start()

    def b(self, k):
        at = self.place.source(k)
        for i in (0, 1):
            chip, first = self.thirds[i][1:3]
            self.second(at, i).wait_recv()
            add_rows(self.rows(at, chip, first, self.half), [self.landing(at, 2 * self.blk + first, self.half)], self.half)
            self.third(at, i).start()

    def c(self, k):
        p, blk = self.place, self.blk
        at = p.source(k)
        has_up, has_down = p.z < p.line - 1, p.z > 0
        for i in range(4):
            self.third(at, i).wait_recv()
        mine = self.rows(at, p.q, 0, blk)
        plane = [self.landing(at, 0, blk), self.landing(at, blk, blk)]
        if k > 0:
            joined = ((at > p.z) & has_down) | ((at < p.z) & has_up)

            @pl.when(joined)
            def _():
                self.line_arrival(at, at).wait_recv()
                add_rows(mine, plane + [self.line_land.at[at]], blk)

            @pl.when(jnp.logical_not(joined))
            def _():
                add_rows(mine, plane, blk)

            for way, condition in enumerate((at > p.z, at < p.z)):

                @pl.when(condition)
                def _():
                    self.line_copy(at, way).start()

        else:
            add_rows(mine, plane, blk, self.result)
            for condition, slot in ((has_down, at), (has_up, p.line)):

                @pl.when(condition)
                def _():
                    self.line_arrival(at, slot).wait_recv()
                    add_rows(self.result, [self.line_land.at[slot]], blk, self.result)

    def end(self, k):
        at = self.place.source(k)
        for i in (0, 1):
            self.second(at, i).wait_send()
        for i in range(4):
            self.third(at, i).wait_send()
        if k > 0:
            self.line_copy(at, 0).wait_send()


def slice_reduce_sems(line):
    return [pltpu.SemaphoreType.DMA(shape) for shape in ((line, 2), (line, 2), (line, 4), (line, 4), (line,), (line + 1,))]


def slice_rows(ref, blk):
    def rows(at, chip, first, count):
        return ref.at[pl.ds(pl.multiple_of((at * 4 + chip) * blk + first, blk // 2), count), :]

    return rows


class ColumnSpread:
    def __init__(self, place, source, target, part, send_sems, recv_sems):
        self.place, self.source, self.target, self.part = place, source, target, part
        self.send_sems, self.recv_sems = send_sems, recv_sems

    def copies(self, other, slot):
        rows = self.source.shape[0]
        for j in (0, 1):
            columns = self.source.at[:, pl.ds(pl.multiple_of((j * self.place.every + other) * self.part, self.part), self.part)]
            yield j, columns, self.target.at[pl.ds(pl.multiple_of(slot * rows, rows), rows), pl.ds(j * self.part, self.part)]

    def start(self):
        @pl.loop(1, self.place.every)
        def _(i):
            other, device = self.place.peer(i)
            for j, source, target in self.copies(other, self.place.me):
                remote(source, target, self.send_sems.at[j, other], self.recv_sems.at[j, self.place.me], device).start()

    def own(self, sems):
        return [pltpu.make_async_copy(source, target, sems[j]) for j, source, target in self.copies(self.place.me, self.place.me)]

    def wait(self):
        @pl.loop(1, self.place.every)
        def _(i):
            other, device = self.place.peer(i)
            for j, source, target in self.copies(other, other):
                copy = remote(source, target, self.send_sems.at[j, other], self.recv_sems.at[j, other], device)
                copy.wait_recv()
                copy.wait_send()


def mlp_kernel(
    line, blk, part, normed_ref, d_mlp_ref, gate_up_ref, down_ref, mid_ref, grad_ref, gain_ref,
    mlp_term_ref, d_mid_ref, d_attn_ref, gain_term_ref, gate_up_grad_ref, down_grad_ref,
    act, land, line_land, w_gu, w_down, acc_gu, acc_down, hid, d_gu, sib_gu, sib_down, d_normed,
    w_send, w_recv, g_send, g_recv, own_sem, out_sem, *sems,
):
    place = Place(line)
    core, sibling = place.core, place.sibling
    width = w_down.shape[1]
    slot_rows = 4 * blk
    rows = slice_rows(act.at[0], blk)
    gather = SliceGather(place, rows, blk, sems[:6])
    reduce = SliceReduce(place, rows, blk, land, line_land, d_normed, sems[6:])

    def slot_of(k):
        return pl.ds(pl.multiple_of(place.source(k) * slot_rows, slot_rows), slot_rows)

    own = pltpu.make_async_copy(normed_ref, rows(place.z, place.q, 0, blk), own_sem.at[0])
    d_mlp_in = pltpu.make_async_copy(d_mlp_ref, act.at[1], own_sem.at[1])
    mine = pl.ds(pl.multiple_of(core * 2 * part, 2 * part), 2 * part)
    theirs = pl.ds(pl.multiple_of((1 - core) * 2 * part, 2 * part), 2 * part)
    mine_rows = pl.ds(pl.multiple_of(core * part, part), part)
    their_rows = pl.ds(pl.multiple_of((1 - core) * part, part), part)

    own_weights = [
        pltpu.make_async_copy(gate_up_ref, w_gu.at[:, mine], own_sem.at[2]),
        pltpu.make_async_copy(down_ref, w_down.at[mine_rows, :], own_sem.at[3]),
    ]
    weights_to = [
        remote(gate_up_ref, w_gu.at[:, mine], w_send.at[0], w_recv.at[0], sibling),
        remote(down_ref, w_down.at[mine_rows, :], w_send.at[1], w_recv.at[1], sibling),
    ]
    weights_from = [
        remote(gate_up_ref, w_gu.at[:, theirs], w_send.at[0], w_recv.at[0], sibling),
        remote(down_ref, w_down.at[their_rows, :], w_send.at[1], w_recv.at[1], sibling),
    ]

    def compute(k):
        slot = slot_of(k)

        @pl.loop(0, 2)
        def _(j):
            span = pl.ds(pl.multiple_of(j * part, part), part)
            lower = pl.ds(pl.multiple_of(j * 2 * part, part), part)
            upper = pl.ds(pl.multiple_of(j * 2 * part + part, part), part)
            gate = dot(act[0, slot, :], w_gu[:, lower], ((1,), (0,)))
            above = dot(act[0, slot, :], w_gu[:, upper], ((1,), (0,)))
            d_hidden = dot(act[1, slot, :], w_down[span, :], ((1,), (1,)))
            sigma = jax.nn.sigmoid(gate)
            active = gate * sigma
            hid[:, span] = (active * above).astype(jnp.bfloat16)
            d_gu[:, lower] = (d_hidden * above * sigma * (1.0 + gate * (1.0 - sigma))).astype(jnp.bfloat16)
            d_gu[:, upper] = (d_hidden * active).astype(jnp.bfloat16)

        @pl.loop(0, width // 256)
        def _(j):
            span = pl.ds(pl.multiple_of(j * 256, 256), 256)
            down_term = dot(hid[...], act[1, slot, span], ((0,), (0,)))
            gate_up_term = dot(act[0, slot, span], d_gu[...], ((0,), (0,)))
            if k > 0:
                down_term = down_term + acc_down[:, span]
                gate_up_term = gate_up_term + acc_gu[span, :]
            acc_down[:, span] = down_term
            acc_gu[span, :] = gate_up_term
            act[1, slot, span] = dot(hid[...], w_down[:, span], ((1,), (0,))).astype(jnp.bfloat16)
            act[0, slot, span] = dot(d_gu[...], w_gu[span, :], ((1,), (1,))).astype(jnp.bfloat16)

    def term_out(k):
        return pltpu.make_async_copy(act.at[1, slot_of(k), :], mlp_term_ref.at[slot_of(k), :], out_sem.at[2 + k])

    half_gu, whole_gu = pl.ds(0, 2 * part), pl.ds(2 * part, 2 * part)
    grad_copies = [
        remote(w_gu.at[:, half_gu], sib_gu, g_send.at[0], g_recv.at[0], sibling),
        remote(w_down.at[:part, :], sib_down, g_send.at[1], g_recv.at[1], sibling),
    ]
    down_out = pltpu.make_async_copy(acc_down.at[mine_rows, :], down_grad_ref, out_sem.at[0])

    def exchange_grads():
        @pl.loop(0, width // 256)
        def _(j):
            span = pl.ds(pl.multiple_of(j * 256, 256), 256)
            w_gu[span, half_gu] = acc_gu[span, theirs].astype(jnp.bfloat16)

        w_down[:part, :] = acc_down[their_rows, :].astype(jnp.bfloat16)
        for copy in grad_copies:
            copy.start()

    columns_out = pltpu.make_async_copy(w_gu.at[:, whole_gu], gate_up_grad_ref, out_sem.at[1])

    def finish_grads():
        for copy in grad_copies:
            copy.wait_recv()

        @pl.loop(0, width // 256)
        def _(j):
            span = pl.ds(pl.multiple_of(j * 256, 256), 256)
            w_gu[span, whole_gu] = (acc_gu[span, mine] + sib_gu[span, :].astype(jnp.float32)).astype(jnp.bfloat16)

        columns_out.start()
        acc_down[mine_rows, :] = acc_down[mine_rows, :] + sib_down[...].astype(jnp.float32)
        down_out.start()

    for copy in [own, d_mlp_in] + own_weights:
        copy.start()
    place.greet_all()
    own.wait()
    gather.a(0)
    for copy in weights_to:
        copy.start()
    gather.a(1)
    gather.b(0)
    gather.a(2)
    gather.b(1)
    for copy in [d_mlp_in] + own_weights:
        copy.wait()
    for copy in weights_from:
        copy.wait_recv()
    for copy in weights_to:
        copy.wait_send()
    gather.a(3)
    gather.b(2)
    gather.c(0)
    compute(0)
    term_out(0).start()
    gather.b(3)
    gather.c(1)
    compute(1)
    term_out(1).start()
    reduce.a(1)
    gather.c(2)
    compute(2)
    term_out(2).start()
    reduce.a(2)
    gather.c(3)
    compute(3)
    term_out(3).start()
    reduce.a(3)
    exchange_grads()
    reduce.b(3)
    reduce.b(2)
    finish_grads()
    reduce.a(0)
    reduce.c(3)
    reduce.b(1)
    reduce.c(2)
    reduce.b(0)
    reduce.c(1)
    reduce.c(0)
    backwards = range(line - 1, -1, -1)

    gain_term_ref[...] = jnp.zeros_like(gain_term_ref)

    @pl.loop(0, blk // 32)
    def _(i):
        part = pl.ds(pl.multiple_of(i * 32, 32), 32)
        mid = mid_ref[part, :]
        d_rows, gain_term = norm_backward(d_normed[part, :], mid, rms_scale(mid), gain_ref[1:2, :])
        d_mid = grad_ref[part, :].astype(jnp.float32) + d_rows
        d_mid_ref[part, :] = d_mid
        d_attn_ref[part, :] = (BRANCH * d_mid).astype(jnp.bfloat16)
        gain_term_ref[0:1, :] += gain_term.reshape(1, width)

    for k in backwards:
        reduce.end(k)
        term_out(k).wait()
    for copy in grad_copies:
        copy.wait_send()
    down_out.wait()
    columns_out.wait()


def mlp_exchange(line, normed, d_mlp, gate_up, down, mid, grad, gain):
    blk, width = normed.shape
    part = down.shape[0]
    any_spec, vmem_spec = pl.BlockSpec(memory_space=pl.ANY), pl.BlockSpec(memory_space=pltpu.VMEM)
    bf16, f32, dma = jnp.bfloat16, jnp.float32, pltpu.SemaphoreType.DMA
    return pl.pallas_call(
        functools.partial(mlp_kernel, line, blk, part),
        out_shape=(
            jax.ShapeDtypeStruct(d_mlp.shape, bf16),
            jax.ShapeDtypeStruct((blk, width), f32),
            jax.ShapeDtypeStruct((blk, width), bf16),
            jax.ShapeDtypeStruct((8, width), f32),
            jax.ShapeDtypeStruct(gate_up.shape, bf16),
            jax.ShapeDtypeStruct((part, width), f32),
        ),
        in_specs=[any_spec] * 4 + [vmem_spec] * 3,
        out_specs=(any_spec, vmem_spec, vmem_spec, vmem_spec, any_spec, any_spec),
        scratch_shapes=[
            pltpu.VMEM((2, line * 4 * blk, width), bf16),
            pltpu.VMEM((line, 3 * blk, width), bf16),
            pltpu.VMEM((line + 1, blk, width), bf16),
            pltpu.VMEM((width, 4 * part), bf16),
            pltpu.VMEM((2 * part, width), bf16),
            pltpu.VMEM((width, 4 * part), f32),
            pltpu.VMEM((2 * part, width), f32),
            pltpu.VMEM((4 * blk, 2 * part), bf16),
            pltpu.VMEM((4 * blk, 4 * part), bf16),
            pltpu.VMEM((width, 2 * part), bf16),
            pltpu.VMEM((part, width), bf16),
            pltpu.VMEM((blk, width), f32),
            dma((2,)),
            dma((2,)),
            dma((2,)),
            dma((2,)),
            dma((5,)),
            dma((2 + line,)),
            *slice_gather_sems(line),
            *slice_reduce_sems(line),
        ],
        compiler_params=pltpu.CompilerParams(collective_id=0, has_side_effects=True, vmem_limit_bytes=63 * MIB),
    )(normed, d_mlp, gate_up, down, mid, grad, gain)


def plane_gather(at, buf, blk, sems):
    p_send, p_recv, f_send, f_recv, s_send, s_recv = sems
    half = blk // 2

    def rows(chip, core, first=0, count=half):
        return buf.at[pl.ds(pl.multiple_of((2 * chip + core) * blk + first, half), count), :]

    def same(ref, send, recv, device):
        return remote(ref, ref, send, recv, device)

    way = ((at.cx, at.qx, 0), (at.cy, at.qy, half), (at.cx, at.qx, half), (at.cy, at.qy, 0))

    def sent(i):
        return same(rows(at.q, at.core, way[i][2]), p_send.at[i], p_recv.at[i], way[i][0])

    def arriving(i):
        return same(rows(way[i][1], at.core, way[i][2]), p_send.at[i], p_recv.at[i], way[i][0])

    def onward(i):
        chip, first, device = ((at.qx, 0, at.cy), (at.qy, half, at.cx))[i]
        return same(rows(chip, at.core, first), f_send.at[i], f_recv.at[i], device)

    def passed(i):
        first, device = ((0, at.cy), (half, at.cx))[i]
        return same(rows(at.qd, at.core, first), f_send.at[i], f_recv.at[i], device)

    def across(i, core):
        if i == 0:
            ref = rows(at.q, core, 0, blk)
        elif i < 5:
            ref = rows(way[i - 1][1], core, way[i - 1][2])
        else:
            ref = rows(at.qd, core, (i - 5) * half)
        return same(ref, s_send.at[i], s_recv.at[i], at.sibling)

    def start():
        for i in range(4):
            sent(i).start()
        across(0, at.core).start()

    def turn():
        for i in (0, 1):
            arriving(i).wait_recv()
            onward(i).start()
            across(i + 1, at.core).start()

    def rest():
        for i in (2, 3):
            arriving(i).wait_recv()
            across(i + 1, at.core).start()
        for i in (0, 1):
            passed(i).wait_recv()
            across(i + 5, at.core).start()

    def whole():
        for i in range(7):
            across(i, 1 - at.core).wait_recv()

    def end():
        for i in range(4):
            sent(i).wait_send()
        for i in (0, 1):
            onward(i).wait_send()
        for i in range(7):
            across(i, at.core).wait_send()

    return start, turn, rest, whole, end


GATHER_SEMS = (4, 4, 2, 2, 7, 7)
REDUCE_SEMS = (4, 4, 2, 2, 4, 4)


def plane_reduce(at, term, core_land, land, blk, sems):
    s_send, s_recv, r2_send, r2_recv, r3_send, r3_recv = sems
    half = blk // 2
    chips = (at.qd, at.qx, at.qy, at.q)

    def rows(chip, core, first=0, count=half):
        return term.at[pl.ds(pl.multiple_of((2 * chip + core) * blk + first, half), count), :]

    def landed(first, count):
        return land.at[pl.ds(first, count), :]

    def across(i):
        return remote(rows(chips[i], 1 - at.core, 0, blk), core_land.at[i], s_send.at[i], s_recv.at[i], at.sibling)

    def second(i):
        first, device = ((0, at.cy), (half, at.cx))[i]
        return remote(rows(at.qd, at.core, first), landed(2 * blk + first, half), r2_send.at[i], r2_recv.at[i], device)

    def third(i):
        device, chip, first, lands = (
            (at.cx, at.qx, 0, 0), (at.cy, at.qy, half, blk + half), (at.cx, at.qx, half, half), (at.cy, at.qy, 0, blk)
        )[i]
        return remote(rows(chip, at.core, first), landed(lands, half), r3_send.at[i], r3_recv.at[i], device)

    def add_core(i):
        across(i).wait_recv()
        add_rows(rows(chips[i], at.core, 0, blk), [core_land.at[i]], blk)

    def give(i):
        across(i).start()

    def take(result):
        add_core(0)
        second(0).start()
        second(1).start()
        add_core(1)
        third(2).start()
        add_core(2)
        third(3).start()
        for i, (chip, first) in enumerate(((at.qx, 0), (at.qy, half))):
            second(i).wait_recv()
            add_rows(rows(chip, at.core, first), [landed(2 * blk + first, half)], half)
            third(i).start()
        add_core(3)
        for i in range(4):
            third(i).wait_recv()
        add_rows(rows(at.q, at.core, 0, blk), [landed(0, blk), landed(blk, blk)], blk, result)

    def end():
        for i in range(4):
            across(i).wait_send()
            third(i).wait_send()
        for i in (0, 1):
            second(i).wait_send()

    return give, take, end


def front_kernel(
    line, blk, q_part, kv_part,
    tokens_ref, grad_ref, w_gate_up_ref, gains_ref, w_qkv_ref, w_out_ref, q_seg_ref, k_seg_ref,
    mid_ref, normed_two_ref, qkv_ref, attn_ref, lse_ref, tops_ref, gain_ref, normed_ref, w_qkv_all_ref, w_out_all_ref, d_mlp_all_ref, gate_up_ref,
    buf, term, core_land, land, w_qkv, w_line, w_out, gain_land, top_land, proj, d_mlp,
    *sems,
):
    at = Place(line)
    gather = plane_gather(at, buf, blk, sems[:6])
    reduce = plane_reduce(at, term, core_land, land, blk, sems[6:12])
    line_send, line_recv, qkv_send, qkv_recv, gain_send, gain_recv, top_send, top_recv, out_send, out_recv, own_sem, write_sem = sems[12:24]
    d_mlp_rows = slice_rows(d_mlp_all_ref, blk)
    beside = SliceGather(at, d_mlp_rows, blk, sems[24:30])
    spread = ColumnSpread(at, w_gate_up_ref, gate_up_ref, gate_up_ref.shape[1] // 2, *sems[30:])
    w_rows, width = w_out_ref.shape
    size = 8 * blk
    mine = pl.ds(pl.multiple_of(at.c * blk, blk), blk)

    own = [
        pltpu.make_async_copy(tokens_ref, buf.at[mine, :], own_sem.at[0]),
        pltpu.make_async_copy(gains_ref, gain_land.at[at.me], own_sem.at[1]),
        pltpu.make_async_copy(w_qkv_ref, w_line.at[at.z], own_sem.at[2]),
        pltpu.make_async_copy(w_out_ref, w_out.at[at.z], own_sem.at[3]),
        pltpu.make_async_copy(d_mlp, d_mlp_rows(at.z, at.q, 0, blk), own_sem.at[4]),
        *spread.own([own_sem.at[5], own_sem.at[6]]),
    ]
    for copy in own[:4] + own[5:]:
        copy.start()
    d_mlp[...] = (BRANCH * grad_ref[...].astype(jnp.float32)).astype(jnp.bfloat16)
    own[4].start()
    at.greet_all()
    gain_push = (lambda other: gains_ref, lambda slot: gain_land.at[slot], gain_send, gain_recv)
    top_push = (lambda other: top_land.at[at.me], lambda slot: top_land.at[slot], top_send, top_recv)

    def qkv_line(place, way):
        return remote(w_line.at[place], w_line.at[place], line_send.at[place, way], line_recv.at[place], (at.c, at.z + 1 - 2 * way))

    def out_line(place, way):
        return remote(w_out.at[place], w_out.at[place], out_send.at[place, way], out_recv.at[place], (at.c, at.z + 1 - 2 * way))

    def qkv_copy(i, place, arriving=False):
        other = lax.rem(at.c + i, 8)
        slot = (other if arriving else at.c) * line + place
        return remote(w_line.at[place, other], w_qkv.at[slot], qkv_send.at[place, other], qkv_recv.at[slot], (other, at.z))

    def qkv_step(k):
        at.line_spread(qkv_line, k)

        @pl.loop(1, 8)
        def _(i):
            qkv_copy(i, at.source(k)).start()

        w_qkv[at.c * line + at.source(k)] = w_line[at.source(k), at.c]

    start, turn, rest, whole, end = gather
    own[0].wait()
    start()
    own[2].wait()
    qkv_step(0)
    at.push_all(*gain_push)
    turn()
    qkv_step(1)
    spread.start()
    rest()
    for k in range(2, line - 1):
        qkv_step(k)
    own[1].wait()
    at.wait_all(*gain_push, sent=False)
    for i in range(at.every // 2):
        pair = gain_land[2 * i].astype(jnp.float32) + gain_land[2 * i + 1].astype(jnp.float32)
        gain_ref[:, i * 128 : (i + 1) * 128] = pair[:8, :]
    own[4].wait()
    beside.a(0)
    whole()
    end()
    at.wait_all(*gain_push)

    @pl.loop(0, size // 32)
    def _(i):
        part = pl.ds(pl.multiple_of(i * 32, 32), 32)
        rows = buf[part, :].astype(jnp.float32)
        buf[part, :] = (rows * rms_scale(rows) * gain_ref[0:1, :]).astype(jnp.bfloat16)

    writes = [
        pltpu.make_async_copy(buf, normed_ref, write_sem.at[0]),
        pltpu.make_async_copy(w_qkv, w_qkv_all_ref, write_sem.at[1]),
        pltpu.make_async_copy(w_out, w_out_all_ref, write_sem.at[2]),
    ]
    writes[0].start()
    qkv_step(line - 1)
    own[3].wait()
    at.line_spread(out_line, 0)
    beside.b(0)
    for k in range(line):

        @pl.loop(1, 8)
        def _(i):
            qkv_copy(i, at.source(k), True).wait_recv()

    writes[1].start()

    @pl.loop(0, size // 256)
    def _(i):
        part = pl.ds(pl.multiple_of(i * 256, 256), 256)
        qkv_ref[part, :] = dot(buf[part, :], w_qkv[...].reshape(width, q_part + 2 * kv_part), ((1,), (0,))).astype(jnp.bfloat16)

    at.line_spread(out_line, 1)
    beside.a(1)
    heads = q_part // HEAD_DIM
    block = math.gcd(size, 256)
    tops = [jnp.full((1, 1), NEGATIVE, jnp.float32)] * heads
    for i in range(size // block):
        if i > 0 and i + 1 < line:
            at.line_spread(out_line, i + 1)
        rows, cols = pl.ds(i * block, block), (i + 1) * block
        live = seen_mask(i * block, block, cols, q_seg_ref[rows, :], k_seg_ref[:, :cols])
        keys, values = qkv_ref[:cols, q_part : q_part + kv_part], qkv_ref[:cols, q_part + kv_part :]
        for h in range(heads):
            span = slice(h * HEAD_DIM, (h + 1) * HEAD_DIM)
            scores = dot(qkv_ref[rows, span], keys, ((1,), (1,))) * SCALE
            scores = jnp.where(live, scores, NEGATIVE)
            peak = jnp.max(scores, axis=-1, keepdims=True)
            weights = jnp.exp(scores - peak)
            total = jnp.sum(weights, axis=-1, keepdims=True)
            out = dot(weights.astype(jnp.bfloat16), values, ((1,), (0,)))
            attn_ref[rows, span] = (out / total).astype(jnp.bfloat16)
            lse_ref[rows, h : h + 1] = peak + jnp.log(total)
            tops[h] = jnp.maximum(tops[h], jnp.max(peak, axis=0, keepdims=True))
    lanes = lax.broadcasted_iota(jnp.int32, (8, 128), 1)
    tile = jnp.full((8, 128), NEGATIVE, jnp.float32)
    for h in range(heads):
        tile = jnp.where(lanes == h, tops[h], tile)
    top_land[at.me] = tile
    at.push_all(*top_push)

    for k in range(size // block + 1, line):
        at.line_spread(out_line, k)
    beside.b(1)
    beside.a(2)
    writes[2].start()
    for i, chip in enumerate((at.qd, at.qx, at.qy, at.q)):
        for core in (1 - at.core, at.core):
            part = pl.ds(pl.multiple_of((2 * chip + core) * blk, blk), blk)

            @pl.loop(0, width // 512)
            def _(j):
                span = pl.ds(pl.multiple_of(j * 512, 512), 512)
                matrix = w_out[:, :, span].reshape(line * w_rows, 512)
                term[part, span] = dot(attn_ref[part, :], matrix, ((1,), (0,))).astype(jnp.bfloat16)

        reduce[0](i)
    reduce[1](proj)
    beside.b(2)
    for k in range(3, line):
        beside.a(k)
        beside.b(k)

    own_again = pltpu.make_async_copy(tokens_ref, land.at[pl.ds(0, blk), :], own_sem.at[0])
    own_again.start()
    own_again.wait()

    @pl.loop(0, blk // 32)
    def _(i):
        part = pl.ds(pl.multiple_of(i * 32, 32), 32)
        rows = land[part, :].astype(jnp.float32) + BRANCH * proj[part, :]
        mid_ref[part, :] = rows
        normed_two_ref[part, :] = (rows * rms_scale(rows) * gain_ref[1:2, :]).astype(jnp.bfloat16)

    at.wait_all(*top_push, sent=False)
    tops_ref[...] = top_land[...]
    reduce[2]()
    at.wait_all(*top_push)
    for k in range(line):
        at.line_sent(qkv_line, k)
        at.line_sent(out_line, k)

        @pl.loop(1, 8)
        def _(i):
            qkv_copy(i, at.source(k)).wait_send()

    for k in range(line):
        beside.c(k)
    spread.wait()
    for copy in own[5:]:
        copy.wait()
    for copy in writes:
        copy.wait()


def front(line, tokens, grad, w_gate_up, gains, w_qkv, w_out, q_seg, k_seg):
    blk, width = tokens.shape
    w_rows, cols = w_out.shape[0], w_qkv.shape[2]
    size, every = 8 * blk, 8 * line
    q_part = HEADS * HEAD_DIM // 8
    kv_part = (cols - q_part) // 2
    heads = q_part // HEAD_DIM
    any_spec, vmem_spec = pl.BlockSpec(memory_space=pl.ANY), pl.BlockSpec(memory_space=pltpu.VMEM)
    bf16, f32, dma, out = jnp.bfloat16, jnp.float32, pltpu.SemaphoreType.DMA, jax.ShapeDtypeStruct
    return pl.pallas_call(
        functools.partial(front_kernel, line, blk, q_part, kv_part),
        out_shape=(
            out((blk, width), f32),
            out((blk, width), bf16),
            out((size, cols), bf16),
            out((size, q_part), bf16),
            out((size, heads), f32),
            out((every, 8, 128), f32),
            out((8, width), f32),
            out((size, width), bf16),
            out((every, w_rows, cols), bf16),
            out((line, w_rows, width), bf16),
            out((line * 4 * blk, width), bf16),
            out((width, w_gate_up.shape[1] // every), bf16),
        ),
        in_specs=[any_spec, vmem_spec] + [any_spec] * 4 + [vmem_spec] * 2,
        out_specs=(vmem_spec,) * 7 + (any_spec,) * 5,
        scratch_shapes=[
            pltpu.VMEM((size, width), bf16),
            pltpu.VMEM((size, width), bf16),
            pltpu.VMEM((4, blk, width), bf16),
            pltpu.VMEM((3 * blk, width), bf16),
            pltpu.VMEM((every, w_rows, cols), bf16),
            pltpu.VMEM((line, 8, w_rows, cols), bf16),
            pltpu.VMEM((line, w_rows, width), bf16),
            pltpu.VMEM((every, 16, 128), bf16),
            pltpu.VMEM((every, 8, 128), f32),
            pltpu.VMEM((blk, width), f32),
            pltpu.VMEM((blk, width), bf16),
            *[dma((n,)) for n in GATHER_SEMS + REDUCE_SEMS],
            dma((line, 2)),
            dma((line,)),
            dma((line, 8)),
            *[dma((every,))] * 5,
            dma((line, 2)),
            dma((line,)),
            dma((7,)),
            dma((3,)),
            *slice_gather_sems(line),
            dma((2, every)),
            dma((2, every)),
        ],
        compiler_params=pltpu.CompilerParams(collective_id=1, has_side_effects=True, vmem_limit_bytes=60 * MIB),
    )(tokens, grad, w_gate_up, gains, w_qkv, w_out, q_seg, k_seg)


def back_kernel(
    line, blk, q_part, kv_part,
    d_attn_ref, tokens_ref, mid_ref, d_mid_ref, qkv_ref, attn_ref, lse_ref, gain_ref, gain_term_ref, q_seg_ref, k_seg_ref, normed_ref, w_qkv_ref, w_out_ref, mlp_term_ref, columns_ref,
    mixed_ref, grad_tokens_ref, grad_qkv_ref, grad_out_ref, gain_sum_ref, grad_gate_up_ref,
    buf, term, core_land, land, w_qkv, w_out, normed, d_heads, d_qkv, dk_sum, dv_sum, stage_qkv, stage_out, qkv_land, out_land, gain_stage, gain_land, d_normed, mlp_term, mlp_land, mlp_line_land, mlp_sum, row_land, row_stage,
    *sems,
):
    at = Place(line)
    gather = plane_gather(at, buf, blk, sems[:6])
    reduce = plane_reduce(at, term, core_land, land, blk, sems[6:12])
    qkv_send, qkv_recv, gain_send, gain_recv, out_send, out_recv, own_sem = sems[12:19]
    beside = SliceReduce(at, slice_rows(mlp_term, blk), blk, mlp_land, mlp_line_land, mlp_sum, sems[19:25])
    row_send, row_recv, row_sem = sems[25:]
    w_cols = w_qkv.shape[1]
    part_ff = columns_ref.shape[1] // 2

    def column_rows(other):
        return columns_ref.at[pl.ds(pl.multiple_of(other * w_cols, w_cols), w_cols), :]

    row_push = (column_rows, lambda slot: row_land.at[slot], row_send, row_recv)
    width = buf.shape[1]
    w_rows = w_out.shape[1]
    size = 8 * blk
    mine = pl.ds(pl.multiple_of(at.c * blk, blk), blk)
    own = [
        pltpu.make_async_copy(d_attn_ref, buf.at[mine, :], own_sem.at[0]),
        pltpu.make_async_copy(w_out_ref, w_out, own_sem.at[1]),
        pltpu.make_async_copy(w_qkv_ref, w_qkv, own_sem.at[2]),
        pltpu.make_async_copy(normed_ref, normed, own_sem.at[3]),
        pltpu.make_async_copy(mlp_term_ref, mlp_term, own_sem.at[4]),
        pltpu.make_async_copy(column_rows(at.me), row_land.at[at.me], own_sem.at[5]),
    ]
    for copy in own:
        copy.start()
    at.greet_all()
    own[0].wait()
    start, turn, rest, whole, end = gather
    start()
    turn()
    rest()
    at.push_all(*row_push)
    for copy in own[1:]:
        copy.wait()
    beside.a(line - 1)
    whole()

    @pl.loop(0, size // 256)
    def _(i):
        part = pl.ds(pl.multiple_of(i * 256, 256), 256)
        d_heads[part, :] = dot(buf[part, :], w_out[...].reshape(line * w_rows, width), ((1,), (1,))).astype(jnp.bfloat16)

    if line > 1:
        beside.a(line - 2)

    @pl.loop(0, width // 256)
    def _(i):
        span = pl.ds(pl.multiple_of(i * 256, 256), 256)
        stage_out[:, :, span] = dot(attn_ref[...], buf[:, span], ((0,), (0,))).astype(jnp.bfloat16).reshape(line, w_rows, 256)

    def out_copy(i):
        z = lax.rem(at.z + i, line)
        return remote(stage_out.at[z], out_land.at[at.z], out_send.at[z], out_recv.at[at.z], (at.c, z))

    def out_arrival(i):
        z = lax.rem(at.z + i, line)
        return remote(stage_out.at[z], out_land.at[z], out_send.at[z], out_recv.at[z], (at.c, z))

    for i in range(1, line):
        out_copy(i).start()

    heads = q_part // HEAD_DIM
    block = math.gcd(size, 256)
    dk_sum[...] = jnp.zeros_like(dk_sum)
    dv_sum[...] = jnp.zeros_like(dv_sum)
    for i in range(size // block):
        rows, cols = pl.ds(i * block, block), (i + 1) * block
        live = seen_mask(i * block, block, cols, q_seg_ref[rows, :], k_seg_ref[:, :cols])
        keys, values = qkv_ref[:cols, q_part : q_part + kv_part], qkv_ref[:cols, q_part + kv_part :]
        for h in range(heads):
            span = slice(h * HEAD_DIM, (h + 1) * HEAD_DIM)
            queries, d_out = qkv_ref[rows, span], d_heads[rows, span]
            delta = jnp.sum(d_out.astype(jnp.float32) * attn_ref[rows, span].astype(jnp.float32), axis=-1, keepdims=True)
            scores = dot(queries, keys, ((1,), (1,))) * SCALE
            probs = jnp.where(live, jnp.exp(scores - lse_ref[rows, h : h + 1]), 0.0)
            d_probs = dot(d_out, values, ((1,), (1,)))
            d_scores = (probs * (d_probs - delta)).astype(jnp.bfloat16)
            d_qkv[rows, span] = (dot(d_scores, keys, ((1,), (0,))) * SCALE).astype(jnp.bfloat16)
            dk_sum[:cols, :] += dot(d_scores, queries, ((0,), (0,)))
            dv_sum[:cols, :] += dot(probs.astype(jnp.bfloat16), d_out, ((0,), (0,)))
    d_qkv[:, q_part : q_part + kv_part] = (dk_sum[...] * SCALE).astype(jnp.bfloat16)
    d_qkv[:, q_part + kv_part :] = dv_sum[...].astype(jnp.bfloat16)
    beside.b(line - 1)
    for k in range(line - 3, 0, -1):
        beside.a(k)

    for i, chip in enumerate((at.qd, at.qx, at.qy, at.q)):
        for core in (1 - at.core, at.core):
            part = pl.ds(pl.multiple_of((2 * chip + core) * blk, blk), blk)

            @pl.loop(0, width // 512)
            def _(j):
                span = pl.ds(pl.multiple_of(j * 512, 512), 512)
                matrix = w_qkv[pl.ds(pl.multiple_of(j * (512 // w_rows), 512 // w_rows), 512 // w_rows)].reshape(512, q_part + 2 * kv_part)
                term[part, span] = dot(d_qkv[part, :], matrix, ((1,), (1,))).astype(jnp.bfloat16)

        reduce[0](i)

    @pl.loop(0, width // 256)
    def _(i):
        span = pl.ds(pl.multiple_of(i * 256, 256), 256)
        blocks = pl.ds(pl.multiple_of(i * (256 // w_rows), 256 // w_rows), 256 // w_rows)
        grads = dot(normed[:, span], d_qkv[...], ((0,), (0,))).astype(jnp.bfloat16)
        stage_qkv[blocks] = grads.reshape(256 // w_rows, w_rows, q_part + 2 * kv_part)

    qkv_push = (lambda other: stage_qkv.at[other], lambda slot: qkv_land.at[slot], qkv_send, qkv_recv)
    at.push_all(*qkv_push)
    qkv_land[at.me] = stage_qkv[at.me]
    out_land[at.z] = stage_out[at.z]
    reduce[1](d_normed)
    if line > 2:
        beside.a(0)
    for k in range(line - 2, -1, -1):
        beside.b(k)

    gain_stage[...] = jnp.zeros_like(gain_stage)
    gain_stage[1:2, :] = gain_term_ref[0:1, :]

    @pl.loop(0, blk // 32)
    def _(i):
        part = pl.ds(pl.multiple_of(i * 32, 32), 32)
        rows = tokens_ref[part, :].astype(jnp.float32)
        d_rows, gain_term = norm_backward(d_normed[part, :], rows, rms_scale(rows), gain_ref[0:1, :])
        grad_tokens_ref[part, :] = d_mid_ref[part, :] + d_rows
        gain_stage[0:1, :] += gain_term.reshape(1, width)

    def gain_tile(other):
        return gain_stage.at[:, pl.ds(pl.multiple_of((other // 2) * 128, 128), 128)]

    gain_push = (gain_tile, lambda slot: gain_land.at[slot], gain_send, gain_recv)
    at.push_all(*gain_push)
    gain_land[at.me] = gain_stage[:, pl.ds(pl.multiple_of((at.me // 2) * 128, 128), 128)]

    at.wait_all(*row_push, sent=False)

    @pl.loop(0, at.every)
    def _(j):
        span = pl.ds(pl.multiple_of(j * w_cols, w_cols), w_cols)
        row_stage[span, :] = row_land[j].astype(jnp.float32)
        for i in (0, 1):
            target = grad_gate_up_ref.at[:, pl.ds(pl.multiple_of((i * at.every + j) * part_ff, part_ff), part_ff)]
            pltpu.make_async_copy(row_stage.at[span, pl.ds(i * part_ff, part_ff)], target, row_sem.at[0]).start()

    for k in range(line - 1, -1, -1):
        beside.c(k)
    mixed_ref[...] = (mid_ref[...] + BRANCH * mlp_sum[...]).astype(jnp.bfloat16)
    for i in range(1, line):
        out_arrival(i).wait_recv()
    total = out_land[0].astype(jnp.float32)
    for i in range(1, line):
        total = total + out_land[i].astype(jnp.float32)
    grad_out_ref[...] = total
    at.wait_all(*qkv_push, sent=False)

    @pl.loop(0, 8)
    def _(i):
        total = qkv_land[i * line].astype(jnp.float32)
        for j in range(1, line):
            total = total + qkv_land[i * line + j].astype(jnp.float32)
        grad_qkv_ref[i] = total

    at.wait_all(*gain_push, sent=False)
    gain_sum_ref[...] = jnp.sum(gain_land[...], axis=0)
    end()
    reduce[2]()
    for k in range(line):
        beside.end(k)
    at.wait_all(*row_push)
    pltpu.make_async_copy(grad_gate_up_ref, grad_gate_up_ref, row_sem.at[0]).wait()
    at.wait_all(*qkv_push)
    at.wait_all(*gain_push)
    for i in range(1, line):
        out_copy(i).wait_send()


def back(line, d_attn, tokens, mid, d_mid, qkv, attn_out, lse, gain, gain_term, q_seg, k_seg, normed, w_qkv, w_out, mlp_term, columns):
    blk, width = tokens.shape
    w_rows, cols = w_out.shape[1], w_qkv.shape[2]
    size, every = 8 * blk, 8 * line
    q_part = HEADS * HEAD_DIM // 8
    kv_part = (cols - q_part) // 2
    any_spec, vmem_spec = pl.BlockSpec(memory_space=pl.ANY), pl.BlockSpec(memory_space=pltpu.VMEM)
    bf16, f32, dma, out = jnp.bfloat16, jnp.float32, pltpu.SemaphoreType.DMA, jax.ShapeDtypeStruct
    return pl.pallas_call(
        functools.partial(back_kernel, line, blk, q_part, kv_part),
        out_shape=(out((blk, width), bf16), out((blk, width), f32), out((8, w_rows, cols), f32), out((w_rows, width), f32), out((8, 128), f32), out((w_rows, every * columns.shape[1]), f32)),
        in_specs=[any_spec] + [vmem_spec] * 10 + [any_spec] * 5,
        out_specs=(vmem_spec,) * 5 + (any_spec,),
        scratch_shapes=[
            pltpu.VMEM((size, width), bf16),
            pltpu.VMEM((size, width), bf16),
            pltpu.VMEM((4, blk, width), bf16),
            pltpu.VMEM((3 * blk, width), bf16),
            pltpu.VMEM((every, w_rows, cols), bf16),
            pltpu.VMEM((line, w_rows, width), bf16),
            pltpu.VMEM((size, width), bf16),
            pltpu.VMEM((size, q_part), bf16),
            pltpu.VMEM((size, cols), bf16),
            pltpu.VMEM((size, kv_part), f32),
            pltpu.VMEM((size, kv_part), f32),
            pltpu.VMEM((every, w_rows, cols), bf16),
            pltpu.VMEM((line, w_rows, width), bf16),
            pltpu.VMEM((every, w_rows, cols), bf16),
            pltpu.VMEM((line, w_rows, width), bf16),
            pltpu.VMEM((8, width), f32),
            pltpu.VMEM((every, 8, 128), f32),
            pltpu.VMEM((blk, width), f32),
            pltpu.VMEM((line * 4 * blk, width), bf16),
            pltpu.VMEM((line, 3 * blk, width), bf16),
            pltpu.VMEM((line + 1, blk, width), bf16),
            pltpu.VMEM((blk, width), f32),
            pltpu.VMEM((every, w_rows, columns.shape[1]), bf16),
            pltpu.VMEM(columns.shape, f32),
            *[dma((n,)) for n in GATHER_SEMS + REDUCE_SEMS + (every,) * 4 + (line, line, 6)],
            *slice_reduce_sems(line),
            dma((every,)),
            dma((every,)),
            dma((1,)),
        ],
        compiler_params=pltpu.CompilerParams(collective_id=2, has_side_effects=True, vmem_limit_bytes=63 * MIB),
    )(d_attn, tokens, mid, d_mid, qkv, attn_out, lse, gain, gain_term, q_seg, k_seg, normed, w_qkv, w_out, mlp_term, columns)


def split_heads(w, parts):
    rows = w.shape[0]
    q_width, kv_width = HEADS * HEAD_DIM, KV_HEADS * HEAD_DIM
    copies = max(1, parts // KV_HEADS)
    q = w[:, :q_width].reshape(rows, parts, q_width // parts)
    k = w[:, q_width : q_width + kv_width].reshape(rows, parts // copies, 1, -1)
    v = w[:, q_width + kv_width :].reshape(rows, parts // copies, 1, -1)
    k, v = (jnp.broadcast_to(a, (rows, parts // copies, copies, a.shape[3])).reshape(rows, parts, -1) for a in (k, v))
    return jnp.concatenate([q, k, v], axis=2)


def join_heads(grads, parts):
    rows = grads.shape[0]
    copies = max(1, parts // KV_HEADS)
    q_part = HEADS * HEAD_DIM // parts
    kv_part = (grads.shape[2] - q_part) // 2
    q = grads[:, :, :q_part].reshape(rows, -1)
    k, v = (
        jnp.sum(grads[:, :, at : at + kv_part].reshape(rows, parts // copies, copies, kv_part), axis=2).reshape(rows, -1)
        for at in (q_part, q_part + kv_part)
    )
    return jnp.concatenate([q, k, v], axis=1)


def per_device(n_ctx, n_shard, tokens, lengths, cotangent, w_qkv, w_out, w_gate_up, w_down, gain_attn, gain_mlp):
    count, width = tokens.shape[1:]
    n = n_ctx * n_shard
    w_rows = w_qkv.shape[0]
    ff_part = w_down.shape[0]
    q_part = HEADS * HEAD_DIM // n_ctx
    rows = tokens.reshape(count, width).astype(jnp.float32)
    grad_rows = cotangent.reshape(count, width).astype(jnp.float32)
    size = count * n_ctx
    positions = jnp.arange(size, dtype=jnp.int32)
    seg = segment_ids(positions, lengths[0])
    q_seg, k_seg = seg.reshape(size, 1), seg.reshape(1, size)

    gains = lax.all_gather(jnp.stack([gain_attn, gain_mlp]), EVERY, axis=1, tiled=True).astype(jnp.float32)
    gain_one, gain_two = gains[0], gains[1]

    qkv_cols = lax.all_to_all(split_heads(w_qkv, n_ctx), "ctx", split_axis=1, concat_axis=1, tiled=True)
    qkv_cols = qkv_cols.reshape(w_rows, n_ctx, -1).transpose(1, 0, 2)
    qkv_mine = lax.all_gather(qkv_cols, "shard", axis=1, tiled=True).reshape(width, -1)
    out_mine = lax.all_gather(w_out, "shard", axis=0, tiled=True)
    gate_up_mine = lax.all_to_all(w_gate_up.reshape(w_rows, 2, n, ff_part), EVERY, split_axis=2, concat_axis=0, tiled=True)
    gate_up_mine = gate_up_mine.reshape(width, 2 * ff_part)

    scale_one = rms_scale(rows)
    normed_one = lax.all_gather((rows * scale_one * gain_one).astype(jnp.bfloat16), "ctx", axis=0, tiled=True)
    projected = dot(normed_one, qkv_mine, ((1,), (0,))).astype(jnp.bfloat16)
    kv_part = (projected.shape[1] - q_part) // 2
    queries, keys, values = (
        projected[:, :q_part],
        projected[:, q_part : q_part + kv_part],
        projected[:, q_part + kv_part :],
    )
    attn_out, lse, tops = attend(queries, keys, values, q_seg, k_seg)
    out_term = dot(attn_out, out_mine, ((1,), (0,))).astype(jnp.bfloat16)
    attn_proj = lax.psum_scatter(out_term, "ctx", scatter_dimension=0, tiled=True)
    mid = rows + BRANCH * attn_proj.astype(jnp.float32)
    head_top = lax.all_gather(lax.pmax(tops, "shard"), "ctx", axis=1, tiled=True).reshape(HEADS)
    clip = CLIP_TARGET / jnp.maximum(head_top, CLIP_TARGET)

    scale_two = rms_scale(mid)
    d_mlp = lax.all_gather((BRANCH * grad_rows).astype(jnp.bfloat16), EVERY, axis=0, tiled=True)
    normed_two = lax.all_gather((mid * scale_two * gain_two).astype(jnp.bfloat16), EVERY, axis=0, tiled=True)
    gate_up = dot(normed_two, gate_up_mine, ((1,), (0,)))
    gate, up = gate_up[:, :ff_part], gate_up[:, ff_part:]
    sigma = jax.nn.sigmoid(gate)
    active = gate * sigma
    hidden = (active * up).astype(jnp.bfloat16)
    down_term = dot(hidden, w_down, ((1,), (0,))).astype(jnp.bfloat16)
    d_hidden = dot(d_mlp, w_down, ((1,), (1,)))
    d_gate = d_hidden * up * sigma * (1.0 + gate * (1.0 - sigma))
    d_up = d_hidden * active
    d_gate_up = jnp.concatenate([d_gate, d_up], axis=1).astype(jnp.bfloat16)
    normed_term = dot(d_gate_up, gate_up_mine, ((1,), (1,))).astype(jnp.bfloat16)
    grad_down = dot(hidden, d_mlp, ((0,), (0,)))
    gate_up_grad = dot(normed_two, d_gate_up, ((0,), (0,))).astype(jnp.bfloat16)
    mlp_proj = lax.psum_scatter(down_term, EVERY, scatter_dimension=0, tiled=True)
    mixed = (mid + BRANCH * mlp_proj.astype(jnp.float32)).astype(jnp.bfloat16).reshape(1, count, width)
    d_normed_two = lax.psum_scatter(normed_term, EVERY, scatter_dimension=0, tiled=True).astype(jnp.float32)
    grad_gate_up = lax.all_to_all(gate_up_grad.reshape(n * w_rows, 2, 1, ff_part), EVERY, split_axis=0, concat_axis=2, tiled=True)
    grad_gate_up = grad_gate_up.reshape(w_rows, 2 * n * ff_part).astype(jnp.float32)
    d_mid_norm, gain_two_term = norm_backward(d_normed_two, mid, scale_two, gain_two)
    d_mid = grad_rows + d_mid_norm

    d_attn = lax.all_gather((BRANCH * d_mid).astype(jnp.bfloat16), "ctx", axis=0, tiled=True)
    grad_out = lax.psum_scatter(dot(attn_out, d_attn, ((0,), (0,))), "shard", scatter_dimension=0, tiled=True)
    d_heads = dot(d_attn, out_mine, ((1,), (1,))).astype(jnp.bfloat16)
    d_q, d_k, d_v = attend_back(queries, keys, values, attn_out, d_heads, lse, q_seg, k_seg)
    d_qkv = jnp.concatenate([d_q, d_k, d_v], axis=1)
    qkv_term = dot(d_qkv, qkv_mine, ((1,), (1,))).astype(jnp.bfloat16)
    d_normed_one = lax.psum_scatter(qkv_term, "ctx", scatter_dimension=0, tiled=True).astype(jnp.float32)
    qkv_grad = dot(normed_one, d_qkv, ((0,), (0,))).reshape(n_ctx, n_shard * w_rows, -1)
    qkv_grad = lax.psum_scatter(qkv_grad, "shard", scatter_dimension=1, tiled=True)
    qkv_grad = lax.all_to_all(qkv_grad, "ctx", split_axis=0, concat_axis=0, tiled=True)
    grad_qkv = join_heads(qkv_grad.transpose(1, 0, 2), n_ctx)
    d_rows_norm, gain_one_term = norm_backward(d_normed_one, rows, scale_one, gain_one)
    grad_tokens = (d_mid + d_rows_norm).reshape(1, count, width)
    gain_terms = lax.psum_scatter(jnp.stack([gain_one_term, gain_two_term]), EVERY, scatter_dimension=1, tiled=True)
    return (mixed, grad_tokens, grad_qkv, grad_out, grad_gate_up, grad_down, gain_terms[0], gain_terms[1], clip)


def on_planes(n_shard, tokens, lengths, cotangent, w_qkv, w_out, w_gate_up, w_down, gain_attn, gain_mlp):
    count, width = tokens.shape[1:]
    w_rows = w_qkv.shape[0]
    rows = tokens.reshape(count, width)
    grad = cotangent.reshape(count, width)
    size = count * 8
    seg = segment_ids(jnp.arange(size, dtype=jnp.int32), lengths[0])
    q_seg, k_seg = seg.reshape(size, 1), seg.reshape(1, size)
    side = lax.rem(lax.axis_index("ctx") * n_shard + lax.axis_index("shard"), 2)

    gains = jnp.stack([gain_attn, gain_mlp])
    none = jnp.zeros_like(gains)
    gains = jnp.where(side == 0, jnp.concatenate([gains, none], axis=1), jnp.concatenate([none, gains], axis=1))
    gains = jnp.pad(gains, ((0, 14), (0, 0)))
    mid, normed_two, qkv, attn_out, lse, tops, gain, normed_one, qkv_mine, out_mine, d_mlp, gate_up_mine = front(
        n_shard, rows, grad, w_gate_up, gains, split_heads(w_qkv, 8).transpose(1, 0, 2), w_out, q_seg, k_seg
    )
    heads = HEADS // 8
    head_top = jnp.max(tops[:, 0, :heads].reshape(8, n_shard, heads), axis=1).reshape(HEADS)
    clip = CLIP_TARGET / jnp.maximum(head_top, CLIP_TARGET)

    mlp_term, d_mid, d_attn, gain_term, gate_up_grad, grad_down = mlp_exchange(
        n_shard, normed_two, d_mlp, gate_up_mine, w_down, mid, grad, gain
    )
    mixed, grad_tokens, qkv_grad, grad_out, gain_sum, grad_gate_up = back(
        n_shard, d_attn, rows, mid, d_mid, qkv, attn_out, lse, gain, gain_term, q_seg, k_seg, normed_one, qkv_mine, out_mine, mlp_term, gate_up_grad
    )
    grad_qkv = join_heads(qkv_grad.transpose(1, 0, 2), 8)
    gain_grads = jnp.where(side == 0, gain_sum[:2, :w_rows], gain_sum[:2, w_rows : 2 * w_rows])
    return (mixed.reshape(1, count, width), grad_tokens.reshape(1, count, width), grad_qkv, grad_out, grad_gate_up, grad_down, gain_grads[0], gain_grads[1], clip)


def solution(mesh):
    by_token, by_row = P("shard", "ctx", None), P(EVERY, None)
    n_ctx, n_shard = mesh.shape["ctx"], mesh.shape["shard"]
    program = functools.partial(on_planes, n_shard) if n_ctx == 8 else functools.partial(per_device, n_ctx, n_shard)
    return jax.shard_map(
        program,
        mesh=mesh,
        in_specs=(by_token, P("shard", None), by_token, by_row, by_row, by_row, by_row, P(EVERY), P(EVERY)),
        out_specs=(by_token, by_token, by_row, by_row, by_row, by_row, P(EVERY), P(EVERY), P()),
        check_vma=False,
    )
```

```python
import functools
import math

import jax
import jax.numpy as jnp
from jax import lax
from jax.experimental import pallas as pl
from jax.experimental.pallas import tpu as pltpu
from jax.sharding import PartitionSpec as P

HEADS = 32
KV_HEADS = 8
HEAD_DIM = 64


SCALE = 0.015625
BRANCH = 0.22
EPSILON = 1e-05
CLIP_TARGET = 4.0
NEGATIVE = -1e30
MIB = 1024 * 1024
EVERY = ("ctx", "shard")


def segment_ids(positions, lengths_row):
    bounds = jnp.cumsum(lengths_row)[:-1]
    return jnp.sum((positions[:, None] >= bounds[None, :]).astype(jnp.int32), axis=1)


def rms_scale(rows):
    return lax.rsqrt(jnp.mean(rows * rows, axis=-1, keepdims=True) + EPSILON)


def norm_backward(d_normed, rows, scale, gain):
    unit = rows * scale
    d_unit = d_normed * gain
    gain_term = jnp.sum(d_normed * unit, axis=0)
    d_rows = scale * (d_unit - unit * jnp.mean(d_unit * unit, axis=-1, keepdims=True))
    return (d_rows, gain_term)


def dot(left, right, dims):
    return lax.dot_general(left, right, ((dims[0], dims[1]), ((), ())), preferred_element_type=jnp.float32)


def seen_mask(row0, rows, cols, q_seg, k_seg):
    q_pos = row0 + lax.broadcasted_iota(jnp.int32, (rows, cols), 0)
    k_pos = lax.broadcasted_iota(jnp.int32, (rows, cols), 1)
    return (k_pos <= q_pos) & ((k_seg == 0) | (k_seg == q_seg))


def attend_kernel(heads, block, q_ref, k_ref, v_ref, q_seg_ref, k_seg_ref, o_ref, lse_ref, top_ref):
    size = q_ref.shape[0]
    tops = [jnp.full((1, 1), NEGATIVE, jnp.float32)] * heads
    for i in range(size // block):
        rows, cols = pl.ds(i * block, block), (i + 1) * block
        live = seen_mask(i * block, block, cols, q_seg_ref[rows, :], k_seg_ref[:, :cols])
        keys, values = k_ref[:cols, :], v_ref[:cols, :]
        for h in range(heads):
            span = slice(h * HEAD_DIM, (h + 1) * HEAD_DIM)
            scores = dot(q_ref[rows, span], keys, ((1,), (1,))) * SCALE
            scores = jnp.where(live, scores, NEGATIVE)
            peak = jnp.max(scores, axis=-1, keepdims=True)
            weights = jnp.exp(scores - peak)
            total = jnp.sum(weights, axis=-1, keepdims=True)
            out = dot(weights.astype(jnp.bfloat16), values, ((1,), (0,)))
            o_ref[rows, span] = (out / total).astype(jnp.bfloat16)
            lse_ref[rows, h : h + 1] = peak + jnp.log(total)
            tops[h] = jnp.maximum(tops[h], jnp.max(peak, axis=0, keepdims=True))
    for h in range(heads):
        top_ref[:, h : h + 1] = tops[h]


def attend(queries, keys, values, q_seg, k_seg):
    size, width = queries.shape
    heads = width // HEAD_DIM
    return pl.pallas_call(
        functools.partial(attend_kernel, heads, math.gcd(size, 256)),
        out_shape=(
            jax.ShapeDtypeStruct((size, width), jnp.bfloat16),
            jax.ShapeDtypeStruct((size, heads), jnp.float32),
            jax.ShapeDtypeStruct((1, heads), jnp.float32),
        ),
        compiler_params=pltpu.CompilerParams(vmem_limit_bytes=48 * MIB),
    )(queries, keys, values, q_seg, k_seg)


def attend_back_kernel(
    heads, block, q_ref, k_ref, v_ref, o_ref, do_ref, lse_ref, q_seg_ref, k_seg_ref, dq_ref, dk_ref, dv_ref, dk_sum, dv_sum
):
    size = q_ref.shape[0]
    dk_sum[...] = jnp.zeros_like(dk_sum)
    dv_sum[...] = jnp.zeros_like(dv_sum)
    for i in range(size // block):
        rows, cols = pl.ds(i * block, block), (i + 1) * block
        live = seen_mask(i * block, block, cols, q_seg_ref[rows, :], k_seg_ref[:, :cols])
        keys, values = k_ref[:cols, :], v_ref[:cols, :]
        for h in range(heads):
            span = slice(h * HEAD_DIM, (h + 1) * HEAD_DIM)
            queries, d_out = q_ref[rows, span], do_ref[rows, span]
            delta = jnp.sum(d_out.astype(jnp.float32) * o_ref[rows, span].astype(jnp.float32), axis=-1, keepdims=True)
            scores = dot(queries, keys, ((1,), (1,))) * SCALE
            probs = jnp.where(live, jnp.exp(scores - lse_ref[rows, h : h + 1]), 0.0)
            d_probs = dot(d_out, values, ((1,), (1,)))
            d_scores = (probs * (d_probs - delta)).astype(jnp.bfloat16)
            dq_ref[rows, span] = (dot(d_scores, keys, ((1,), (0,))) * SCALE).astype(jnp.bfloat16)
            dk_sum[:cols, :] += dot(d_scores, queries, ((0,), (0,)))
            dv_sum[:cols, :] += dot(probs.astype(jnp.bfloat16), d_out, ((0,), (0,)))
    dk_ref[...] = (dk_sum[...] * SCALE).astype(jnp.bfloat16)
    dv_ref[...] = dv_sum[...].astype(jnp.bfloat16)


def attend_back(queries, keys, values, out, d_out, lse, q_seg, k_seg):
    size, width = queries.shape
    heads = width // HEAD_DIM
    like_kv = jax.ShapeDtypeStruct((size, HEAD_DIM), jnp.bfloat16)
    return pl.pallas_call(
        functools.partial(attend_back_kernel, heads, math.gcd(size, 256)),
        out_shape=(jax.ShapeDtypeStruct((size, width), jnp.bfloat16), like_kv, like_kv),
        scratch_shapes=[pltpu.VMEM((size, HEAD_DIM), jnp.float32)] * 2,
        compiler_params=pltpu.CompilerParams(vmem_limit_bytes=48 * MIB),
    )(queries, keys, values, out, d_out, lse, q_seg, k_seg)


def remote(src, dst, send_sem, recv_sem, device):
    return pltpu.make_async_remote_copy(
        src_ref=src, dst_ref=dst, send_sem=send_sem, recv_sem=recv_sem, device_id=device, device_id_type=pl.DeviceIdType.MESH
    )


def greet(devices, extra):
    barrier = pltpu.get_barrier_semaphore()
    count = len(devices)
    for device in devices:
        pl.semaphore_signal(barrier, inc=1, device_id=device, device_id_type=pl.DeviceIdType.MESH)
    for condition, device in extra:

        @pl.when(condition)
        def _():
            pl.semaphore_signal(barrier, inc=1, device_id=device, device_id_type=pl.DeviceIdType.MESH)

        count = count + condition.astype(jnp.int32)
    pl.semaphore_wait(barrier, count)


def add_rows(target, sources, rows, keep=None, step=32):
    @pl.loop(0, rows // step)
    def _(i):
        part = pl.ds(pl.multiple_of(i * step, step), step)
        total = target[part, :].astype(jnp.float32)
        for source in sources:
            total = total + source[part, :].astype(jnp.float32)
        if keep is None:
            target[part, :] = total.astype(jnp.bfloat16)
        else:
            keep[part, :] = total


class Place:
    def __init__(self, line):
        self.line = line
        self.c, self.z = lax.axis_index("ctx"), lax.axis_index("shard")
        self.q, self.core = self.c // 2, self.c % 2
        self.me = self.c * line + self.z
        self.every = 8 * line
        self.cx, self.cy = (self.c + 2 - 4 * (self.q % 2), self.z), (self.c + 4 - 8 * (self.q // 2), self.z)
        self.sibling = (self.c + 1 - 2 * self.core, self.z)
        self.qx, self.qy, self.qd = self.q + 1 - 2 * (self.q % 2), self.q + 2 - 4 * (self.q // 2), 3 - self.q

    def source(self, k):
        if self.line == 1:
            return self.z * 0
        mirrored = self.z >= self.line // 2
        near = jnp.where(mirrored, self.line - 1 - self.z, self.z)
        turn = (k + 1) // 2
        both = near - turn if k % 2 == 1 else near + turn
        at = jnp.where(k <= 2 * near, both, k)
        return jnp.where(mirrored, self.line - 1 - at, at)

    def line_spread(self, copy, k):
        at = self.source(k)
        if k > 0:
            copy(at, 0).wait_recv()
        for way, condition in enumerate(self.line_ways(at)):

            @pl.when(condition)
            def _():
                copy(at, way).start()

    def line_sent(self, copy, k):
        at = self.source(k)
        for way, condition in enumerate(self.line_ways(at)):

            @pl.when(condition)
            def _():
                copy(at, way).wait_send()

    def line_ways(self, at):
        return ((at <= self.z) & (self.z < self.line - 1), (at >= self.z) & (self.z > 0))

    def peer(self, i):
        other = lax.rem(self.me + i, self.every)
        return other, (other // self.line, other % self.line)

    def greet_near(self):
        z, last = self.z, self.line - 1
        greet([self.cx, self.cy, self.sibling], [(z < last, (self.c, z + 1)), (z > 0, (self.c, z - 1))])

    def greet_all(self):
        barrier = pltpu.get_barrier_semaphore()

        @pl.loop(1, self.every)
        def _(i):
            pl.semaphore_signal(barrier, inc=1, device_id=self.peer(i)[1], device_id_type=pl.DeviceIdType.MESH)

        pl.semaphore_wait(barrier, self.every - 1)

    def push_all(self, source, target, send_sems, recv_sems, piece=0, pieces=1):
        @pl.loop(max(1, piece * self.every // pieces), (piece + 1) * self.every // pieces)
        def _(i):
            other, device = self.peer(i)
            remote(source(other), target(self.me), send_sems.at[other], recv_sems.at[self.me], device).start()

    def wait_all(self, source, target, send_sems, recv_sems, sent=True):
        @pl.loop(1, self.every)
        def _(i):
            other, device = self.peer(i)
            copy = remote(source(other), target(other), send_sems.at[other], recv_sems.at[other], device)
            if sent:
                copy.wait_send()
            else:
                copy.wait_recv()


class SliceGather:
    def __init__(self, place, rows, blk, sems):
        self.place, self.rows, self.half = place, rows, blk // 2
        self.z_send, self.z_recv, self.p_send, self.p_recv, self.f_send, self.f_recv = sems
        p, half = place, blk // 2
        self.ways = ((p.cx, p.qx, 0), (p.cy, p.qy, half), (p.cx, p.qx, half), (p.cy, p.qy, 0))
        self.turns = ((p.qx, 0, p.cy), (p.qy, half, p.cx))

    def line_copy(self, at, way):
        ref = self.rows(at, self.place.q, 0, 2 * self.half)
        return remote(ref, ref, self.z_send.at[at, way], self.z_recv.at[at], (self.place.c, self.place.z + 1 - 2 * way))

    def plane_copy(self, at, i, arriving=False):
        device, chip, first = self.ways[i]
        ref = self.rows(at, chip if arriving else self.place.q, first, self.half)
        return remote(ref, ref, self.p_send.at[at, i], self.p_recv.at[at, i], device)

    def onward_copy(self, at, i, arriving=False):
        chip, first, device = self.turns[i]
        ref = self.rows(at, self.place.qd if arriving else chip, first, self.half)
        return remote(ref, ref, self.f_send.at[at, i], self.f_recv.at[at, i], device)

    def a(self, k):
        self.place.line_spread(self.line_copy, k)
        for i in range(4):
            self.plane_copy(self.place.source(k), i).start()

    def b(self, k):
        at = self.place.source(k)
        for i in (0, 1):
            self.plane_copy(at, i, True).wait_recv()
            self.onward_copy(at, i).start()

    def c(self, k):
        at = self.place.source(k)
        for i in (2, 3):
            self.plane_copy(at, i, True).wait_recv()
        for i in (0, 1):
            self.onward_copy(at, i, True).wait_recv()
        for i in range(4):
            self.plane_copy(at, i).wait_send()
        for i in (0, 1):
            self.onward_copy(at, i).wait_send()
        self.place.line_sent(self.line_copy, k)


def slice_gather_sems(line):
    return [pltpu.SemaphoreType.DMA(shape) for shape in ((line, 2), (line,), (line, 4), (line, 4), (line, 2), (line, 2))]


class SliceReduce:
    def __init__(self, place, rows, blk, land, line_land, result, sems):
        self.place, self.rows, self.blk, self.half = place, rows, blk, blk // 2
        self.land, self.line_land, self.result = land, line_land, result
        self.r2_send, self.r2_recv, self.r3_send, self.r3_recv, self.r4_send, self.r4_recv = sems
        p, half = place, blk // 2
        self.seconds = ((0, p.cy), (half, p.cx))
        self.thirds = ((p.cx, p.qx, 0, 0), (p.cy, p.qy, half, blk + half), (p.cx, p.qx, half, half), (p.cy, p.qy, 0, blk))

    def landing(self, at, first, count):
        return self.land.at[at, pl.ds(first, count), :]

    def second(self, at, i):
        first, device = self.seconds[i]
        return remote(
            self.rows(at, self.place.qd, first, self.half), self.landing(at, 2 * self.blk + first, self.half), self.r2_send.at[at, i], self.r2_recv.at[at, i], device
        )

    def third(self, at, i):
        device, chip, first, lands = self.thirds[i]
        return remote(
            self.rows(at, chip, first, self.half), self.landing(at, lands, self.half), self.r3_send.at[at, i], self.r3_recv.at[at, i], device
        )

    def line_part(self, at, slot, part):
        rows = pl.ds(part * self.half, self.half)
        return self.rows(at, self.place.q, part * self.half, self.half), self.line_land.at[slot, rows, :]

    def line_copy(self, at, way, part):
        p = self.place
        slot = jnp.where((way == 1) & (at == p.z - 1), p.line, at)
        source, target = self.line_part(at, slot, part)
        return remote(source, target, self.r4_send.at[at, part], self.r4_recv.at[slot, part], (p.c, p.z + 1 - 2 * way))

    def line_arrival(self, at, slot, part):
        source, target = self.line_part(at, slot, part)
        return remote(source, target, self.r4_send.at[at, part], self.r4_recv.at[slot, part], self.place.sibling)

    def a(self, k):
        at = self.place.source(k)
        for i in (0, 1):
            self.second(at, i).start()
        for i in (2, 3):
            self.third(at, i).start()

    def b(self, k):
        at = self.place.source(k)
        for i in (0, 1):
            chip, first = self.thirds[i][1:3]
            self.second(at, i).wait_recv()
            add_rows(self.rows(at, chip, first, self.half), [self.landing(at, 2 * self.blk + first, self.half)], self.half)
            self.third(at, i).start()

    def c(self, k):
        p, blk = self.place, self.blk
        at = p.source(k)
        has_up, has_down = p.z < p.line - 1, p.z > 0
        for i in range(4):
            self.third(at, i).wait_recv()
        half = self.half
        joined = ((at > p.z) & has_down) | ((at < p.z) & has_up)
        for part in (0, 1):
            mine = self.rows(at, p.q, part * half, half)
            plane = [self.landing(at, part * half, half), self.landing(at, blk + part * half, half)]
            if k > 0:

                @pl.when(joined)
                def _():
                    self.line_arrival(at, at, part).wait_recv()
                    add_rows(mine, plane + [self.line_part(at, at, part)[1]], half)

                @pl.when(jnp.logical_not(joined))
                def _():
                    add_rows(mine, plane, half)

                for way, condition in enumerate((at > p.z, at < p.z)):

                    @pl.when(condition)
                    def _():
                        self.line_copy(at, way, part).start()

            else:
                result = self.result.at[pl.ds(part * half, half), :]
                add_rows(mine, plane, half, result)
                for condition, slot in ((has_down, at), (has_up, p.line)):

                    @pl.when(condition)
                    def _():
                        self.line_arrival(at, slot, part).wait_recv()
                        add_rows(result, [self.line_part(at, slot, part)[1]], half, result)

    def end(self, k):
        at = self.place.source(k)
        for i in (0, 1):
            self.second(at, i).wait_send()
        for i in range(4):
            self.third(at, i).wait_send()
        if k > 0:
            for part in (0, 1):
                self.line_copy(at, 0, part).wait_send()


class LineReduce:
    def __init__(self, place, block, land, rows, sems):
        self.place, self.block, self.land, self.rows = place, block, land, rows
        self.send, self.recv = sems

    def copy(self, at, way):
        p = self.place
        slot = jnp.where((way == 1) & (at == p.z - 1), p.line, at)
        return remote(self.block(at), self.land.at[slot], self.send.at[at], self.recv.at[slot], (p.c, p.z + 1 - 2 * way))

    def arrive(self, at, slot):
        p = self.place
        remote(self.block(at), self.land.at[slot], self.send.at[at], self.recv.at[slot], p.sibling).wait_recv()
        add_rows(self.block(at), [self.land.at[slot]], self.rows)

    def each(self, k, joined, after):
        p = self.place
        at = p.source(k)
        for way, toward, behind in ((0, at > p.z, p.z > 0), (1, at < p.z, p.z < p.line - 1)):

            @pl.when(toward & (behind if joined else jnp.logical_not(behind)))
            def _():
                after(at, way)

    def first(self):
        for k in range(self.place.line - 1, 0, -1):
            self.each(k, False, lambda at, way: self.copy(at, way).start())

    def join(self, k):
        def step(at, way):
            self.arrive(at, at)
            self.copy(at, way).start()

        self.each(k, True, step)

    def last(self):
        p = self.place
        for condition, slot in ((p.z > 0, p.z), (p.z < p.line - 1, p.line)):

            @pl.when(condition)
            def _():
                self.arrive(p.z, slot)

    def end(self):
        for k in range(1, self.place.line):
            self.copy(self.place.source(k), 0).wait_send()


def slice_reduce_sems(line):
    return [pltpu.SemaphoreType.DMA(shape) for shape in ((line, 2), (line, 2), (line, 4), (line, 4), (line, 2), (line + 1, 2))]


def slice_rows(ref, blk):
    def rows(at, chip, first, count):
        return ref.at[pl.ds(pl.multiple_of((at * 4 + chip) * blk + first, blk // 2), count), :]

    return rows


class ColumnSpread:
    def __init__(self, place, source, target, part, send_sems, recv_sems):
        self.place, self.source, self.target, self.part = place, source, target, part
        self.send_sems, self.recv_sems = send_sems, recv_sems

    def copies(self, other, slot):
        rows = self.source.shape[0]
        for j in (0, 1):
            columns = self.source.at[:, pl.ds(pl.multiple_of((j * self.place.every + other) * self.part, self.part), self.part)]
            yield j, columns, self.target.at[pl.ds(pl.multiple_of(slot * rows, rows), rows), pl.ds(j * self.part, self.part)]

    def start(self, piece, pieces):
        every = self.place.every

        @pl.loop(max(1, piece * every // pieces), (piece + 1) * every // pieces)
        def _(i):
            other, device = self.place.peer(i)
            for j, source, target in self.copies(other, self.place.me):
                remote(source, target, self.send_sems.at[j, other], self.recv_sems.at[j, self.place.me], device).start()

    def own(self, sems):
        return [pltpu.make_async_copy(source, target, sems[j]) for j, source, target in self.copies(self.place.me, self.place.me)]

    def wait(self):
        @pl.loop(1, self.place.every)
        def _(i):
            other, device = self.place.peer(i)
            for j, source, target in self.copies(other, other):
                copy = remote(source, target, self.send_sems.at[j, other], self.recv_sems.at[j, other], device)
                copy.wait_recv()
                copy.wait_send()


def mlp_kernel(
    line, blk, part, normed_ref, d_mlp_ref, gate_up_ref, down_ref, mid_ref, grad_ref, gain_ref,
    mlp_term_ref, d_mid_ref, d_attn_ref, gain_term_ref, gate_up_grad_ref, down_grad_ref,
    act, land, line_land, w_gu, w_down, acc_gu, acc_down, hid, d_gu, sib_gu, sib_down, d_normed,
    w_send, w_recv, g_send, g_recv, own_sem, out_sem, *sems,
):
    place = Place(line)
    core, sibling = place.core, place.sibling
    width = w_down.shape[1]
    slot_rows = 4 * blk
    rows = slice_rows(act.at[0], blk)
    gather = SliceGather(place, rows, blk, sems[:6])
    reduce = SliceReduce(place, rows, blk, land, line_land, d_normed, sems[6:])

    def slot_of(k):
        return pl.ds(pl.multiple_of(place.source(k) * slot_rows, slot_rows), slot_rows)

    own = pltpu.make_async_copy(normed_ref, rows(place.z, place.q, 0, blk), own_sem.at[0])
    d_mlp_in = pltpu.make_async_copy(d_mlp_ref, act.at[1], own_sem.at[1])
    mine = pl.ds(pl.multiple_of(core * 2 * part, 2 * part), 2 * part)
    theirs = pl.ds(pl.multiple_of((1 - core) * 2 * part, 2 * part), 2 * part)
    mine_rows = pl.ds(pl.multiple_of(core * part, part), part)
    their_rows = pl.ds(pl.multiple_of((1 - core) * part, part), part)

    own_weights = [
        pltpu.make_async_copy(gate_up_ref, w_gu.at[:, mine], own_sem.at[2]),
        pltpu.make_async_copy(down_ref, w_down.at[mine_rows, :], own_sem.at[3]),
    ]
    weights_to = [
        remote(gate_up_ref, w_gu.at[:, mine], w_send.at[0], w_recv.at[0], sibling),
        remote(down_ref, w_down.at[mine_rows, :], w_send.at[1], w_recv.at[1], sibling),
    ]
    weights_from = [
        remote(gate_up_ref, w_gu.at[:, theirs], w_send.at[0], w_recv.at[0], sibling),
        remote(down_ref, w_down.at[their_rows, :], w_send.at[1], w_recv.at[1], sibling),
    ]

    def compute(k):
        slot = slot_of(k)

        @pl.loop(0, 2)
        def _(j):
            span = pl.ds(pl.multiple_of(j * part, part), part)
            lower = pl.ds(pl.multiple_of(j * 2 * part, part), part)
            upper = pl.ds(pl.multiple_of(j * 2 * part + part, part), part)
            gate = dot(act[0, slot, :], w_gu[:, lower], ((1,), (0,)))
            above = dot(act[0, slot, :], w_gu[:, upper], ((1,), (0,)))
            d_hidden = dot(act[1, slot, :], w_down[span, :], ((1,), (1,)))
            sigma = jax.nn.sigmoid(gate)
            active = gate * sigma
            hid[:, span] = (active * above).astype(jnp.bfloat16)
            d_gu[:, lower] = (d_hidden * above * sigma * (1.0 + gate * (1.0 - sigma))).astype(jnp.bfloat16)
            d_gu[:, upper] = (d_hidden * active).astype(jnp.bfloat16)

        @pl.loop(0, width // 256)
        def _(j):
            span = pl.ds(pl.multiple_of(j * 256, 256), 256)
            down_term = dot(hid[...], act[1, slot, span], ((0,), (0,)))
            gate_up_term = dot(act[0, slot, span], d_gu[...], ((0,), (0,)))
            if k > 0:
                down_term = down_term + acc_down[:, span]
                gate_up_term = gate_up_term + acc_gu[span, :]
            acc_down[:, span] = down_term
            acc_gu[span, :] = gate_up_term
            act[1, slot, span] = dot(hid[...], w_down[:, span], ((1,), (0,))).astype(jnp.bfloat16)
            act[0, slot, span] = dot(d_gu[...], w_gu[span, :], ((1,), (1,))).astype(jnp.bfloat16)

    def term_out(k):
        return pltpu.make_async_copy(act.at[1, slot_of(k), :], mlp_term_ref.at[slot_of(k), :], out_sem.at[2 + k])

    half_gu, whole_gu = pl.ds(0, 2 * part), pl.ds(2 * part, 2 * part)
    grad_copies = [
        remote(w_gu.at[:, half_gu], sib_gu, g_send.at[0], g_recv.at[0], sibling),
        remote(w_down.at[:part, :], sib_down, g_send.at[1], g_recv.at[1], sibling),
    ]
    down_out = pltpu.make_async_copy(acc_down.at[mine_rows, :], down_grad_ref, out_sem.at[0])

    def exchange_grads():
        @pl.loop(0, width // 256)
        def _(j):
            span = pl.ds(pl.multiple_of(j * 256, 256), 256)
            w_gu[span, half_gu] = acc_gu[span, theirs].astype(jnp.bfloat16)

        w_down[:part, :] = acc_down[their_rows, :].astype(jnp.bfloat16)
        for copy in grad_copies:
            copy.start()

    columns_out = pltpu.make_async_copy(w_gu.at[:, whole_gu], gate_up_grad_ref, out_sem.at[1])

    def finish_grads():
        for copy in grad_copies:
            copy.wait_recv()

        @pl.loop(0, width // 256)
        def _(j):
            span = pl.ds(pl.multiple_of(j * 256, 256), 256)
            w_gu[span, whole_gu] = (acc_gu[span, mine] + sib_gu[span, :].astype(jnp.float32)).astype(jnp.bfloat16)

        columns_out.start()
        acc_down[mine_rows, :] = acc_down[mine_rows, :] + sib_down[...].astype(jnp.float32)
        down_out.start()

    for copy in [own, d_mlp_in] + own_weights:
        copy.start()
    place.greet_near()
    own.wait()
    gather.a(0)
    for copy in weights_to:
        copy.start()
    gather.a(1)
    gather.b(0)
    gather.a(2)
    gather.b(1)
    for copy in [d_mlp_in] + own_weights:
        copy.wait()
    for copy in weights_from:
        copy.wait_recv()
    for copy in weights_to:
        copy.wait_send()
    gather.a(3)
    gather.b(2)
    gather.c(0)
    compute(0)
    term_out(0).start()
    gather.b(3)
    gather.c(1)
    compute(1)
    term_out(1).start()
    reduce.a(1)
    gather.c(2)
    compute(2)
    term_out(2).start()
    reduce.a(2)
    gather.c(3)
    compute(3)
    term_out(3).start()
    reduce.a(3)
    exchange_grads()
    reduce.b(3)
    reduce.b(2)
    finish_grads()
    reduce.a(0)
    reduce.c(3)
    reduce.b(1)
    reduce.c(2)
    reduce.b(0)
    reduce.c(1)
    reduce.c(0)
    backwards = range(line - 1, -1, -1)

    gain_term_ref[...] = jnp.zeros_like(gain_term_ref)

    @pl.loop(0, blk // 32)
    def _(i):
        part = pl.ds(pl.multiple_of(i * 32, 32), 32)
        mid = mid_ref[part, :]
        d_rows, gain_term = norm_backward(d_normed[part, :], mid, rms_scale(mid), gain_ref[1:2, :])
        d_mid = grad_ref[part, :].astype(jnp.float32) + d_rows
        d_mid_ref[part, :] = d_mid
        d_attn_ref[part, :] = (BRANCH * d_mid).astype(jnp.bfloat16)
        gain_term_ref[0:1, :] += gain_term.reshape(1, width)

    for k in backwards:
        reduce.end(k)
        term_out(k).wait()
    for copy in grad_copies:
        copy.wait_send()
    down_out.wait()
    columns_out.wait()


def mlp_exchange(line, normed, d_mlp, gate_up, down, mid, grad, gain):
    blk, width = normed.shape
    part = down.shape[0]
    any_spec, vmem_spec = pl.BlockSpec(memory_space=pl.ANY), pl.BlockSpec(memory_space=pltpu.VMEM)
    bf16, f32, dma = jnp.bfloat16, jnp.float32, pltpu.SemaphoreType.DMA
    return pl.pallas_call(
        functools.partial(mlp_kernel, line, blk, part),
        out_shape=(
            jax.ShapeDtypeStruct(d_mlp.shape, bf16),
            jax.ShapeDtypeStruct((blk, width), f32),
            jax.ShapeDtypeStruct((blk, width), bf16),
            jax.ShapeDtypeStruct((8, width), f32),
            jax.ShapeDtypeStruct(gate_up.shape, bf16),
            jax.ShapeDtypeStruct((part, width), f32),
        ),
        in_specs=[any_spec] * 4 + [vmem_spec] * 3,
        out_specs=(any_spec, vmem_spec, vmem_spec, vmem_spec, any_spec, any_spec),
        scratch_shapes=[
            pltpu.VMEM((2, line * 4 * blk, width), bf16),
            pltpu.VMEM((line, 3 * blk, width), bf16),
            pltpu.VMEM((line + 1, blk, width), bf16),
            pltpu.VMEM((width, 4 * part), bf16),
            pltpu.VMEM((2 * part, width), bf16),
            pltpu.VMEM((width, 4 * part), f32),
            pltpu.VMEM((2 * part, width), f32),
            pltpu.VMEM((4 * blk, 2 * part), bf16),
            pltpu.VMEM((4 * blk, 4 * part), bf16),
            pltpu.VMEM((width, 2 * part), bf16),
            pltpu.VMEM((part, width), bf16),
            pltpu.VMEM((blk, width), f32),
            dma((2,)),
            dma((2,)),
            dma((2,)),
            dma((2,)),
            dma((5,)),
            dma((2 + line,)),
            *slice_gather_sems(line),
            *slice_reduce_sems(line),
        ],
        compiler_params=pltpu.CompilerParams(collective_id=0, has_side_effects=True, vmem_limit_bytes=63 * MIB),
    )(normed, d_mlp, gate_up, down, mid, grad, gain)


def plane_gather(at, buf, blk, sems):
    p_send, p_recv, f_send, f_recv, s_send, s_recv = sems
    half = blk // 2

    def rows(chip, core, first=0, count=half):
        return buf.at[pl.ds(pl.multiple_of((2 * chip + core) * blk + first, half), count), :]

    def same(ref, send, recv, device):
        return remote(ref, ref, send, recv, device)

    way = ((at.cx, at.qx, 0), (at.cy, at.qy, half), (at.cx, at.qx, half), (at.cy, at.qy, 0))

    def sent(i):
        return same(rows(at.q, at.core, way[i][2]), p_send.at[i], p_recv.at[i], way[i][0])

    def arriving(i):
        return same(rows(way[i][1], at.core, way[i][2]), p_send.at[i], p_recv.at[i], way[i][0])

    def onward(i):
        chip, first, device = ((at.qx, 0, at.cy), (at.qy, half, at.cx))[i]
        return same(rows(chip, at.core, first), f_send.at[i], f_recv.at[i], device)

    def passed(i):
        first, device = ((0, at.cy), (half, at.cx))[i]
        return same(rows(at.qd, at.core, first), f_send.at[i], f_recv.at[i], device)

    def across(i, core):
        if i == 0:
            ref = rows(at.q, core, 0, blk)
        elif i < 5:
            ref = rows(way[i - 1][1], core, way[i - 1][2])
        else:
            ref = rows(at.qd, core, (i - 5) * half)
        return same(ref, s_send.at[i], s_recv.at[i], at.sibling)

    def start():
        for i in range(4):
            sent(i).start()
        across(0, at.core).start()

    def turn():
        for i in (0, 1):
            arriving(i).wait_recv()
            onward(i).start()
            across(i + 1, at.core).start()

    def rest():
        for i in (2, 3):
            arriving(i).wait_recv()
            across(i + 1, at.core).start()
        for i in (0, 1):
            passed(i).wait_recv()
            across(i + 5, at.core).start()

    def whole():
        for i in range(7):
            across(i, 1 - at.core).wait_recv()

    def end():
        for i in range(4):
            sent(i).wait_send()
        for i in (0, 1):
            onward(i).wait_send()
        for i in range(7):
            across(i, at.core).wait_send()

    return start, turn, rest, whole, end


GATHER_SEMS = (4, 4, 2, 2, 7, 7)
REDUCE_SEMS = (4, 4, 2, 2, 4, 4)


def plane_reduce(at, term, core_land, land, blk, sems):
    s_send, s_recv, r2_send, r2_recv, r3_send, r3_recv = sems
    half = blk // 2
    chips = (at.qd, at.qx, at.qy, at.q)

    def rows(chip, core, first=0, count=half):
        return term.at[pl.ds(pl.multiple_of((2 * chip + core) * blk + first, half), count), :]

    def landed(first, count):
        return land.at[pl.ds(first, count), :]

    def across(i):
        return remote(rows(chips[i], 1 - at.core, 0, blk), core_land.at[i], s_send.at[i], s_recv.at[i], at.sibling)

    def second(i):
        first, device = ((0, at.cy), (half, at.cx))[i]
        return remote(rows(at.qd, at.core, first), landed(2 * blk + first, half), r2_send.at[i], r2_recv.at[i], device)

    def third(i):
        device, chip, first, lands = (
            (at.cx, at.qx, 0, 0), (at.cy, at.qy, half, blk + half), (at.cx, at.qx, half, half), (at.cy, at.qy, 0, blk)
        )[i]
        return remote(rows(chip, at.core, first), landed(lands, half), r3_send.at[i], r3_recv.at[i], device)

    def add_core(i):
        across(i).wait_recv()
        add_rows(rows(chips[i], at.core, 0, blk), [core_land.at[i]], blk)

    def give(i):
        across(i).start()

    def take(result):
        add_core(0)
        second(0).start()
        second(1).start()
        add_core(1)
        third(2).start()
        add_core(2)
        third(3).start()
        for i, (chip, first) in enumerate(((at.qx, 0), (at.qy, half))):
            second(i).wait_recv()
            add_rows(rows(chip, at.core, first), [landed(2 * blk + first, half)], half)
            third(i).start()
        add_core(3)
        for i in range(4):
            third(i).wait_recv()
        add_rows(rows(at.q, at.core, 0, blk), [landed(0, blk), landed(blk, blk)], blk, result)

    def end():
        for i in range(4):
            across(i).wait_send()
            third(i).wait_send()
        for i in (0, 1):
            second(i).wait_send()

    return give, take, end


def front_kernel(
    line, blk, q_part, kv_part,
    tokens_ref, grad_ref, w_gate_up_ref, gains_ref, w_qkv_ref, w_out_ref, q_seg_ref, k_seg_ref,
    mid_ref, normed_two_ref, qkv_ref, attn_ref, lse_ref, tops_ref, gain_ref, normed_ref, w_qkv_all_ref, w_out_all_ref, d_mlp_all_ref, gate_up_ref,
    buf, term, core_land, land, w_qkv, w_line, w_out, gain_land, top_land, proj, d_mlp,
    *sems,
):
    at = Place(line)
    gather = plane_gather(at, buf, blk, sems[:6])
    reduce = plane_reduce(at, term, core_land, land, blk, sems[6:12])
    line_send, line_recv, qkv_send, qkv_recv, gain_send, gain_recv, top_send, top_recv, out_send, out_recv, own_sem, write_sem = sems[12:24]
    d_mlp_rows = slice_rows(d_mlp_all_ref, blk)
    beside = SliceGather(at, d_mlp_rows, blk, sems[24:30])
    spread = ColumnSpread(at, w_gate_up_ref, gate_up_ref, gate_up_ref.shape[1] // 2, *sems[30:])
    w_rows, width = w_out_ref.shape
    size = 8 * blk
    mine = pl.ds(pl.multiple_of(at.c * blk, blk), blk)

    own = [
        pltpu.make_async_copy(tokens_ref, buf.at[mine, :], own_sem.at[0]),
        pltpu.make_async_copy(gains_ref, gain_land.at[at.me], own_sem.at[1]),
        pltpu.make_async_copy(w_qkv_ref, w_line.at[at.z], own_sem.at[2]),
        pltpu.make_async_copy(w_out_ref, w_out.at[at.z], own_sem.at[3]),
        pltpu.make_async_copy(d_mlp, d_mlp_rows(at.z, at.q, 0, blk), own_sem.at[4]),
        *spread.own([own_sem.at[5], own_sem.at[6]]),
    ]
    for copy in own[:4] + own[5:]:
        copy.start()
    d_mlp[...] = (BRANCH * grad_ref[...].astype(jnp.float32)).astype(jnp.bfloat16)
    own[4].start()
    at.greet_all()
    gain_push = (lambda other: gains_ref, lambda slot: gain_land.at[slot], gain_send, gain_recv)
    top_push = (lambda other: top_land.at[at.me], lambda slot: top_land.at[slot], top_send, top_recv)

    def qkv_line(place, way):
        return remote(w_line.at[place], w_line.at[place], line_send.at[place, way], line_recv.at[place], (at.c, at.z + 1 - 2 * way))

    def out_line(place, way):
        return remote(w_out.at[place], w_out.at[place], out_send.at[place, way], out_recv.at[place], (at.c, at.z + 1 - 2 * way))

    def qkv_copy(i, place, arriving=False):
        other = lax.rem(at.c + i, 8)
        slot = (other if arriving else at.c) * line + place
        return remote(w_line.at[place, other], w_qkv.at[slot], qkv_send.at[place, other], qkv_recv.at[slot], (other, at.z))

    def qkv_step(k):
        at.line_spread(qkv_line, k)

        @pl.loop(1, 8)
        def _(i):
            qkv_copy(i, at.source(k)).start()

        w_qkv[at.c * line + at.source(k)] = w_line[at.source(k), at.c]

    start, turn, rest, whole, end = gather
    own[0].wait()
    start()
    own[2].wait()
    qkv_step(0)
    at.push_all(*gain_push)
    turn()
    qkv_step(1)
    own[4].wait()
    beside.a(0)
    rest()
    for k in range(2, line - 1):
        qkv_step(k)
    own[1].wait()
    at.wait_all(*gain_push, sent=False)
    for i in range(at.every // 2):
        pair = gain_land[2 * i].astype(jnp.float32) + gain_land[2 * i + 1].astype(jnp.float32)
        gain_ref[:, i * 128 : (i + 1) * 128] = pair[:8, :]
    spread.start(0, 4)
    whole()
    end()
    at.wait_all(*gain_push)

    @pl.loop(0, size // 32)
    def _(i):
        part = pl.ds(pl.multiple_of(i * 32, 32), 32)
        rows = buf[part, :].astype(jnp.float32)
        buf[part, :] = (rows * rms_scale(rows) * gain_ref[0:1, :]).astype(jnp.bfloat16)

    writes = [
        pltpu.make_async_copy(buf, normed_ref, write_sem.at[0]),
        pltpu.make_async_copy(w_qkv, w_qkv_all_ref, write_sem.at[1]),
        pltpu.make_async_copy(w_out, w_out_all_ref, write_sem.at[2]),
    ]
    writes[0].start()
    qkv_step(line - 1)
    own[3].wait()
    at.line_spread(out_line, 0)
    beside.b(0)
    beside.a(1)
    spread.start(1, 4)
    for k in range(line):

        @pl.loop(1, 8)
        def _(i):
            qkv_copy(i, at.source(k), True).wait_recv()

    writes[1].start()

    @pl.loop(0, size // 256)
    def _(i):
        part = pl.ds(pl.multiple_of(i * 256, 256), 256)
        qkv_ref[part, :] = dot(buf[part, :], w_qkv[...].reshape(width, q_part + 2 * kv_part), ((1,), (0,))).astype(jnp.bfloat16)

    at.line_spread(out_line, 1)
    beside.b(1)
    beside.a(2)
    spread.start(2, 4)
    heads = q_part // HEAD_DIM
    block = math.gcd(size, 256)
    tops = [jnp.full((1, 1), NEGATIVE, jnp.float32)] * heads
    for i in range(size // block):
        if i > 0 and i + 1 < line:
            at.line_spread(out_line, i + 1)
        if i == 2:
            beside.b(2)
            beside.a(3)
        rows, cols = pl.ds(i * block, block), (i + 1) * block
        live = seen_mask(i * block, block, cols, q_seg_ref[rows, :], k_seg_ref[:, :cols])
        keys, values = qkv_ref[:cols, q_part : q_part + kv_part], qkv_ref[:cols, q_part + kv_part :]
        for h in range(heads):
            span = slice(h * HEAD_DIM, (h + 1) * HEAD_DIM)
            scores = dot(qkv_ref[rows, span], keys, ((1,), (1,))) * SCALE
            scores = jnp.where(live, scores, NEGATIVE)
            peak = jnp.max(scores, axis=-1, keepdims=True)
            weights = jnp.exp(scores - peak)
            total = jnp.sum(weights, axis=-1, keepdims=True)
            out = dot(weights.astype(jnp.bfloat16), values, ((1,), (0,)))
            attn_ref[rows, span] = (out / total).astype(jnp.bfloat16)
            lse_ref[rows, h : h + 1] = peak + jnp.log(total)
            tops[h] = jnp.maximum(tops[h], jnp.max(peak, axis=0, keepdims=True))
    lanes = lax.broadcasted_iota(jnp.int32, (8, 128), 1)
    tile = jnp.full((8, 128), NEGATIVE, jnp.float32)
    for h in range(heads):
        tile = jnp.where(lanes == h, tops[h], tile)
    top_land[at.me] = tile
    at.push_all(*top_push)

    for k in range(size // block + 1, line):
        at.line_spread(out_line, k)
    beside.b(3)
    spread.start(3, 4)
    writes[2].start()
    for i, chip in enumerate((at.qd, at.qx, at.qy, at.q)):
        for core in (1 - at.core, at.core):
            part = pl.ds(pl.multiple_of((2 * chip + core) * blk, blk), blk)

            @pl.loop(0, width // 512)
            def _(j):
                span = pl.ds(pl.multiple_of(j * 512, 512), 512)
                matrix = w_out[:, :, span].reshape(line * w_rows, 512)
                term[part, span] = dot(attn_ref[part, :], matrix, ((1,), (0,))).astype(jnp.bfloat16)

        reduce[0](i)
    reduce[1](proj)

    own_again = pltpu.make_async_copy(tokens_ref, land.at[pl.ds(0, blk), :], own_sem.at[0])
    own_again.start()
    own_again.wait()

    @pl.loop(0, blk // 32)
    def _(i):
        part = pl.ds(pl.multiple_of(i * 32, 32), 32)
        rows = land[part, :].astype(jnp.float32) + BRANCH * proj[part, :]
        mid_ref[part, :] = rows
        normed_two_ref[part, :] = (rows * rms_scale(rows) * gain_ref[1:2, :]).astype(jnp.bfloat16)

    at.wait_all(*top_push, sent=False)
    tops_ref[...] = top_land[...]
    reduce[2]()
    at.wait_all(*top_push)
    for k in range(line):
        at.line_sent(qkv_line, k)
        at.line_sent(out_line, k)

        @pl.loop(1, 8)
        def _(i):
            qkv_copy(i, at.source(k)).wait_send()

    for k in range(line):
        beside.c(k)
    spread.wait()
    for copy in own[5:]:
        copy.wait()
    for copy in writes:
        copy.wait()


def front(line, tokens, grad, w_gate_up, gains, w_qkv, w_out, q_seg, k_seg):
    blk, width = tokens.shape
    w_rows, cols = w_out.shape[0], w_qkv.shape[2]
    size, every = 8 * blk, 8 * line
    q_part = HEADS * HEAD_DIM // 8
    kv_part = (cols - q_part) // 2
    heads = q_part // HEAD_DIM
    any_spec, vmem_spec = pl.BlockSpec(memory_space=pl.ANY), pl.BlockSpec(memory_space=pltpu.VMEM)
    bf16, f32, dma, out = jnp.bfloat16, jnp.float32, pltpu.SemaphoreType.DMA, jax.ShapeDtypeStruct
    return pl.pallas_call(
        functools.partial(front_kernel, line, blk, q_part, kv_part),
        out_shape=(
            out((blk, width), f32),
            out((blk, width), bf16),
            out((size, cols), bf16),
            out((size, q_part), bf16),
            out((size, heads), f32),
            out((every, 8, 128), f32),
            out((8, width), f32),
            out((size, width), bf16),
            out((every, w_rows, cols), bf16),
            out((line, w_rows, width), bf16),
            out((line * 4 * blk, width), bf16),
            out((width, w_gate_up.shape[1] // every), bf16),
        ),
        in_specs=[any_spec, vmem_spec] + [any_spec] * 4 + [vmem_spec] * 2,
        out_specs=(vmem_spec,) * 7 + (any_spec,) * 5,
        scratch_shapes=[
            pltpu.VMEM((size, width), bf16),
            pltpu.VMEM((size, width), bf16),
            pltpu.VMEM((4, blk, width), bf16),
            pltpu.VMEM((3 * blk, width), bf16),
            pltpu.VMEM((every, w_rows, cols), bf16),
            pltpu.VMEM((line, 8, w_rows, cols), bf16),
            pltpu.VMEM((line, w_rows, width), bf16),
            pltpu.VMEM((every, 16, 128), bf16),
            pltpu.VMEM((every, 8, 128), f32),
            pltpu.VMEM((blk, width), f32),
            pltpu.VMEM((blk, width), bf16),
            *[dma((n,)) for n in GATHER_SEMS + REDUCE_SEMS],
            dma((line, 2)),
            dma((line,)),
            dma((line, 8)),
            *[dma((every,))] * 5,
            dma((line, 2)),
            dma((line,)),
            dma((7,)),
            dma((3,)),
            *slice_gather_sems(line),
            dma((2, every)),
            dma((2, every)),
        ],
        compiler_params=pltpu.CompilerParams(collective_id=1, has_side_effects=True, vmem_limit_bytes=60 * MIB),
    )(tokens, grad, w_gate_up, gains, w_qkv, w_out, q_seg, k_seg)


def back_kernel(
    line, blk, q_part, kv_part,
    d_attn_ref, tokens_ref, mid_ref, d_mid_ref, qkv_ref, attn_ref, lse_ref, gain_ref, gain_term_ref, q_seg_ref, k_seg_ref, normed_ref, w_qkv_ref, w_out_ref, mlp_term_ref, columns_ref,
    mixed_ref, grad_tokens_ref, grad_qkv_ref, grad_out_ref, gain_sum_ref, grad_gate_up_ref,
    buf, term, core_land, land, w_qkv, w_out, normed, d_heads, d_qkv, dk_sum, dv_sum, stage_qkv, stage_out, qkv_land, out_land, gain_stage, gain_land, d_normed, mlp_term, mlp_land, mlp_line_land, mlp_sum, row_land, row_stage, qkv_line_land,
    *sems,
):
    at = Place(line)
    gather = plane_gather(at, buf, blk, sems[:6])
    reduce = plane_reduce(at, term, core_land, land, blk, sems[6:12])
    qkv_send, qkv_recv, gain_send, gain_recv, out_send, out_recv, own_sem = sems[12:19]
    beside = SliceReduce(at, slice_rows(mlp_term, blk), blk, mlp_land, mlp_line_land, mlp_sum, sems[19:25])
    row_send, row_recv, row_sem = sems[25:28]
    w_cols = w_qkv.shape[1]
    part_ff = columns_ref.shape[1] // 2

    def column_rows(other):
        return columns_ref.at[pl.ds(pl.multiple_of(other * w_cols, w_cols), w_cols), :]

    row_push = (column_rows, lambda slot: row_land.at[slot], row_send, row_recv)
    width = buf.shape[1]
    w_rows = w_out.shape[1]
    size = 8 * blk
    mine = pl.ds(pl.multiple_of(at.c * blk, blk), blk)
    own = [
        pltpu.make_async_copy(d_attn_ref, buf.at[mine, :], own_sem.at[0]),
        pltpu.make_async_copy(w_out_ref, w_out, own_sem.at[1]),
        pltpu.make_async_copy(w_qkv_ref, w_qkv, own_sem.at[2]),
        pltpu.make_async_copy(normed_ref, normed, own_sem.at[3]),
        pltpu.make_async_copy(mlp_term_ref, mlp_term, own_sem.at[4]),
        pltpu.make_async_copy(column_rows(at.me), row_land.at[at.me], own_sem.at[5]),
    ]
    for copy in own:
        copy.start()
    at.greet_all()
    own[0].wait()
    start, turn, rest, whole, end = gather
    start()
    turn()
    rest()
    at.push_all(*row_push)
    for copy in own[1:]:
        copy.wait()
    beside.a(line - 1)
    whole()

    @pl.loop(0, size // 256)
    def _(i):
        part = pl.ds(pl.multiple_of(i * 256, 256), 256)
        d_heads[part, :] = dot(buf[part, :], w_out[...].reshape(line * w_rows, width), ((1,), (1,))).astype(jnp.bfloat16)

    if line > 1:
        beside.a(line - 2)

    @pl.loop(0, width // 256)
    def _(i):
        span = pl.ds(pl.multiple_of(i * 256, 256), 256)
        stage_out[:, :, span] = dot(attn_ref[...], buf[:, span], ((0,), (0,))).astype(jnp.bfloat16).reshape(line, w_rows, 256)

    def out_copy(i):
        z = lax.rem(at.z + i, line)
        return remote(stage_out.at[z], out_land.at[at.z], out_send.at[z], out_recv.at[at.z], (at.c, z))

    def out_arrival(i):
        z = lax.rem(at.z + i, line)
        return remote(stage_out.at[z], out_land.at[z], out_send.at[z], out_recv.at[z], (at.c, z))

    for i in range(1, line):
        out_copy(i).start()

    heads = q_part // HEAD_DIM
    block = math.gcd(size, 256)
    dk_sum[...] = jnp.zeros_like(dk_sum)
    dv_sum[...] = jnp.zeros_like(dv_sum)
    for i in range(size // block):
        rows, cols = pl.ds(i * block, block), (i + 1) * block
        live = seen_mask(i * block, block, cols, q_seg_ref[rows, :], k_seg_ref[:, :cols])
        keys, values = qkv_ref[:cols, q_part : q_part + kv_part], qkv_ref[:cols, q_part + kv_part :]
        for h in range(heads):
            span = slice(h * HEAD_DIM, (h + 1) * HEAD_DIM)
            queries, d_out = qkv_ref[rows, span], d_heads[rows, span]
            delta = jnp.sum(d_out.astype(jnp.float32) * attn_ref[rows, span].astype(jnp.float32), axis=-1, keepdims=True)
            scores = dot(queries, keys, ((1,), (1,))) * SCALE
            probs = jnp.where(live, jnp.exp(scores - lse_ref[rows, h : h + 1]), 0.0)
            d_probs = dot(d_out, values, ((1,), (1,)))
            d_scores = (probs * (d_probs - delta)).astype(jnp.bfloat16)
            d_qkv[rows, span] = (dot(d_scores, keys, ((1,), (0,))) * SCALE).astype(jnp.bfloat16)
            dk_sum[:cols, :] += dot(d_scores, queries, ((0,), (0,)))
            dv_sum[:cols, :] += dot(probs.astype(jnp.bfloat16), d_out, ((0,), (0,)))
    d_qkv[:, q_part : q_part + kv_part] = (dk_sum[...] * SCALE).astype(jnp.bfloat16)
    d_qkv[:, q_part + kv_part :] = dv_sum[...].astype(jnp.bfloat16)
    beside.b(line - 1)
    for k in range(line - 3, 0, -1):
        beside.a(k)

    for i, chip in enumerate((at.qd, at.qx, at.qy, at.q)):
        for core in (1 - at.core, at.core):
            part = pl.ds(pl.multiple_of((2 * chip + core) * blk, blk), blk)

            @pl.loop(0, width // 512)
            def _(j):
                span = pl.ds(pl.multiple_of(j * 512, 512), 512)
                matrix = w_qkv[pl.ds(pl.multiple_of(j * (512 // w_rows), 512 // w_rows), 512 // w_rows)].reshape(512, q_part + 2 * kv_part)
                term[part, span] = dot(d_qkv[part, :], matrix, ((1,), (1,))).astype(jnp.bfloat16)

        reduce[0](i)

    chunk = line * w_cols

    @pl.loop(0, 8)
    def _(i):
        grads = dot(normed[:, pl.ds(pl.multiple_of(i * chunk, chunk), chunk)], d_qkv[...], ((0,), (0,))).astype(jnp.bfloat16)
        for place in range(line):
            stage_qkv[pl.ds(pl.multiple_of((place * 8 + i) * w_cols, w_cols), w_cols), :] = grads[place * w_cols : (place + 1) * w_cols, :]

    def qkv_block(place):
        return stage_qkv.at[pl.ds(pl.multiple_of(place * 8 * w_cols, w_cols), 8 * w_cols), :]

    def qkv_rows(i):
        return stage_qkv.at[pl.ds(pl.multiple_of((at.z * 8 + i) * w_cols, w_cols), w_cols), :]

    def qkv_copy(i, arriving=False):
        other = lax.rem(at.c + i, 8)
        slot = other if arriving else at.c
        return remote(qkv_rows(other), qkv_land.at[slot], qkv_send.at[other], qkv_recv.at[slot], (other, at.z))

    sum_qkv = LineReduce(at, qkv_block, qkv_line_land, 8 * w_cols, sems[28:])
    sum_qkv.first()
    out_land[at.z] = stage_out[at.z]
    reduce[1](d_normed)
    if line > 2:
        beside.a(0)
    for k in range(line - 1, 0, -1):
        sum_qkv.join(k)
    for k in range(line - 2, -1, -1):
        beside.b(k)

    gain_stage[...] = jnp.zeros_like(gain_stage)
    gain_stage[1:2, :] = gain_term_ref[0:1, :]

    @pl.loop(0, blk // 32)
    def _(i):
        part = pl.ds(pl.multiple_of(i * 32, 32), 32)
        rows = tokens_ref[part, :].astype(jnp.float32)
        d_rows, gain_term = norm_backward(d_normed[part, :], rows, rms_scale(rows), gain_ref[0:1, :])
        grad_tokens_ref[part, :] = d_mid_ref[part, :] + d_rows
        gain_stage[0:1, :] += gain_term.reshape(1, width)

    def gain_tile(other):
        return gain_stage.at[:, pl.ds(pl.multiple_of((other // 2) * 128, 128), 128)]

    gain_push = (gain_tile, lambda slot: gain_land.at[slot], gain_send, gain_recv)
    at.push_all(*gain_push)
    gain_land[at.me] = gain_stage[:, pl.ds(pl.multiple_of((at.me // 2) * 128, 128), 128)]

    sum_qkv.last()

    @pl.loop(1, 8)
    def _(i):
        qkv_copy(i).start()

    qkv_land[at.c] = stage_qkv[pl.ds(pl.multiple_of((at.z * 8 + at.c) * w_cols, w_cols), w_cols), :]
    at.wait_all(*row_push, sent=False)

    @pl.loop(0, at.every)
    def _(j):
        span = pl.ds(pl.multiple_of(j * w_cols, w_cols), w_cols)
        row_stage[span, :] = row_land[j].astype(jnp.float32)
        for i in (0, 1):
            target = grad_gate_up_ref.at[:, pl.ds(pl.multiple_of((i * at.every + j) * part_ff, part_ff), part_ff)]
            pltpu.make_async_copy(row_stage.at[span, pl.ds(i * part_ff, part_ff)], target, row_sem.at[0]).start()

    for k in range(line - 1, -1, -1):
        beside.c(k)
    mixed_ref[...] = (mid_ref[...] + BRANCH * mlp_sum[...]).astype(jnp.bfloat16)
    for i in range(1, line):
        out_arrival(i).wait_recv()
    total = out_land[0].astype(jnp.float32)
    for i in range(1, line):
        total = total + out_land[i].astype(jnp.float32)
    grad_out_ref[...] = total
    @pl.loop(1, 8)
    def _(i):
        qkv_copy(i, True).wait_recv()

    grad_qkv_ref[...] = qkv_land[...].astype(jnp.float32)
    at.wait_all(*gain_push, sent=False)
    gain_sum_ref[...] = jnp.sum(gain_land[...], axis=0)
    end()
    reduce[2]()
    for k in range(line):
        beside.end(k)
    at.wait_all(*row_push)
    pltpu.make_async_copy(grad_gate_up_ref, grad_gate_up_ref, row_sem.at[0]).wait()
    sum_qkv.end()

    @pl.loop(1, 8)
    def _(i):
        qkv_copy(i).wait_send()

    at.wait_all(*gain_push)
    for i in range(1, line):
        out_copy(i).wait_send()


def back(line, d_attn, tokens, mid, d_mid, qkv, attn_out, lse, gain, gain_term, q_seg, k_seg, normed, w_qkv, w_out, mlp_term, columns):
    blk, width = tokens.shape
    w_rows, cols = w_out.shape[1], w_qkv.shape[2]
    size, every = 8 * blk, 8 * line
    q_part = HEADS * HEAD_DIM // 8
    kv_part = (cols - q_part) // 2
    any_spec, vmem_spec = pl.BlockSpec(memory_space=pl.ANY), pl.BlockSpec(memory_space=pltpu.VMEM)
    bf16, f32, dma, out = jnp.bfloat16, jnp.float32, pltpu.SemaphoreType.DMA, jax.ShapeDtypeStruct
    return pl.pallas_call(
        functools.partial(back_kernel, line, blk, q_part, kv_part),
        out_shape=(out((blk, width), bf16), out((blk, width), f32), out((8, w_rows, cols), f32), out((w_rows, width), f32), out((8, 128), f32), out((w_rows, every * columns.shape[1]), f32)),
        in_specs=[any_spec] + [vmem_spec] * 10 + [any_spec] * 5,
        out_specs=(vmem_spec,) * 5 + (any_spec,),
        scratch_shapes=[
            pltpu.VMEM((size, width), bf16),
            pltpu.VMEM((size, width), bf16),
            pltpu.VMEM((4, blk, width), bf16),
            pltpu.VMEM((3 * blk, width), bf16),
            pltpu.VMEM((every, w_rows, cols), bf16),
            pltpu.VMEM((line, w_rows, width), bf16),
            pltpu.VMEM((size, width), bf16),
            pltpu.VMEM((size, q_part), bf16),
            pltpu.VMEM((size, cols), bf16),
            pltpu.VMEM((size, kv_part), f32),
            pltpu.VMEM((size, kv_part), f32),
            pltpu.VMEM((every * w_rows, cols), bf16),
            pltpu.VMEM((line, w_rows, width), bf16),
            pltpu.VMEM((8, w_rows, cols), bf16),
            pltpu.VMEM((line, w_rows, width), bf16),
            pltpu.VMEM((8, width), f32),
            pltpu.VMEM((every, 8, 128), f32),
            pltpu.VMEM((blk, width), f32),
            pltpu.VMEM((line * 4 * blk, width), bf16),
            pltpu.VMEM((line, 3 * blk, width), bf16),
            pltpu.VMEM((line + 1, blk, width), bf16),
            pltpu.VMEM((blk, width), f32),
            pltpu.VMEM((every, w_rows, columns.shape[1]), bf16),
            pltpu.VMEM(columns.shape, f32),
            pltpu.VMEM((line + 1, 8 * w_rows, cols), bf16),
            *[dma((n,)) for n in GATHER_SEMS + REDUCE_SEMS + (every,) * 4 + (line, line, 6)],
            *slice_reduce_sems(line),
            dma((every,)),
            dma((every,)),
            dma((1,)),
            dma((line,)),
            dma((line + 1,)),
        ],
        compiler_params=pltpu.CompilerParams(collective_id=2, has_side_effects=True, vmem_limit_bytes=63 * MIB),
    )(d_attn, tokens, mid, d_mid, qkv, attn_out, lse, gain, gain_term, q_seg, k_seg, normed, w_qkv, w_out, mlp_term, columns)


def split_heads(w, parts):
    rows = w.shape[0]
    q_width, kv_width = HEADS * HEAD_DIM, KV_HEADS * HEAD_DIM
    copies = max(1, parts // KV_HEADS)
    q = w[:, :q_width].reshape(rows, parts, q_width // parts)
    k = w[:, q_width : q_width + kv_width].reshape(rows, parts // copies, 1, -1)
    v = w[:, q_width + kv_width :].reshape(rows, parts // copies, 1, -1)
    k, v = (jnp.broadcast_to(a, (rows, parts // copies, copies, a.shape[3])).reshape(rows, parts, -1) for a in (k, v))
    return jnp.concatenate([q, k, v], axis=2)


def join_heads(grads, parts):
    rows = grads.shape[0]
    copies = max(1, parts // KV_HEADS)
    q_part = HEADS * HEAD_DIM // parts
    kv_part = (grads.shape[2] - q_part) // 2
    q = grads[:, :, :q_part].reshape(rows, -1)
    k, v = (
        jnp.sum(grads[:, :, at : at + kv_part].reshape(rows, parts // copies, copies, kv_part), axis=2).reshape(rows, -1)
        for at in (q_part, q_part + kv_part)
    )
    return jnp.concatenate([q, k, v], axis=1)


def per_device(n_ctx, n_shard, tokens, lengths, cotangent, w_qkv, w_out, w_gate_up, w_down, gain_attn, gain_mlp):
    count, width = tokens.shape[1:]
    n = n_ctx * n_shard
    w_rows = w_qkv.shape[0]
    ff_part = w_down.shape[0]
    q_part = HEADS * HEAD_DIM // n_ctx
    rows = tokens.reshape(count, width).astype(jnp.float32)
    grad_rows = cotangent.reshape(count, width).astype(jnp.float32)
    size = count * n_ctx
    positions = jnp.arange(size, dtype=jnp.int32)
    seg = segment_ids(positions, lengths[0])
    q_seg, k_seg = seg.reshape(size, 1), seg.reshape(1, size)

    gains = lax.all_gather(jnp.stack([gain_attn, gain_mlp]), EVERY, axis=1, tiled=True).astype(jnp.float32)
    gain_one, gain_two = gains[0], gains[1]

    qkv_cols = lax.all_to_all(split_heads(w_qkv, n_ctx), "ctx", split_axis=1, concat_axis=1, tiled=True)
    qkv_cols = qkv_cols.reshape(w_rows, n_ctx, -1).transpose(1, 0, 2)
    qkv_mine = lax.all_gather(qkv_cols, "shard", axis=1, tiled=True).reshape(width, -1)
    out_mine = lax.all_gather(w_out, "shard", axis=0, tiled=True)
    gate_up_mine = lax.all_to_all(w_gate_up.reshape(w_rows, 2, n, ff_part), EVERY, split_axis=2, concat_axis=0, tiled=True)
    gate_up_mine = gate_up_mine.reshape(width, 2 * ff_part)

    scale_one = rms_scale(rows)
    normed_one = lax.all_gather((rows * scale_one * gain_one).astype(jnp.bfloat16), "ctx", axis=0, tiled=True)
    projected = dot(normed_one, qkv_mine, ((1,), (0,))).astype(jnp.bfloat16)
    kv_part = (projected.shape[1] - q_part) // 2
    queries, keys, values = (
        projected[:, :q_part],
        projected[:, q_part : q_part + kv_part],
        projected[:, q_part + kv_part :],
    )
    attn_out, lse, tops = attend(queries, keys, values, q_seg, k_seg)
    out_term = dot(attn_out, out_mine, ((1,), (0,))).astype(jnp.bfloat16)
    attn_proj = lax.psum_scatter(out_term, "ctx", scatter_dimension=0, tiled=True)
    mid = rows + BRANCH * attn_proj.astype(jnp.float32)
    head_top = lax.all_gather(lax.pmax(tops, "shard"), "ctx", axis=1, tiled=True).reshape(HEADS)
    clip = CLIP_TARGET / jnp.maximum(head_top, CLIP_TARGET)

    scale_two = rms_scale(mid)
    d_mlp = lax.all_gather((BRANCH * grad_rows).astype(jnp.bfloat16), EVERY, axis=0, tiled=True)
    normed_two = lax.all_gather((mid * scale_two * gain_two).astype(jnp.bfloat16), EVERY, axis=0, tiled=True)
    gate_up = dot(normed_two, gate_up_mine, ((1,), (0,)))
    gate, up = gate_up[:, :ff_part], gate_up[:, ff_part:]
    sigma = jax.nn.sigmoid(gate)
    active = gate * sigma
    hidden = (active * up).astype(jnp.bfloat16)
    down_term = dot(hidden, w_down, ((1,), (0,))).astype(jnp.bfloat16)
    d_hidden = dot(d_mlp, w_down, ((1,), (1,)))
    d_gate = d_hidden * up * sigma * (1.0 + gate * (1.0 - sigma))
    d_up = d_hidden * active
    d_gate_up = jnp.concatenate([d_gate, d_up], axis=1).astype(jnp.bfloat16)
    normed_term = dot(d_gate_up, gate_up_mine, ((1,), (1,))).astype(jnp.bfloat16)
    grad_down = dot(hidden, d_mlp, ((0,), (0,)))
    gate_up_grad = dot(normed_two, d_gate_up, ((0,), (0,))).astype(jnp.bfloat16)
    mlp_proj = lax.psum_scatter(down_term, EVERY, scatter_dimension=0, tiled=True)
    mixed = (mid + BRANCH * mlp_proj.astype(jnp.float32)).astype(jnp.bfloat16).reshape(1, count, width)
    d_normed_two = lax.psum_scatter(normed_term, EVERY, scatter_dimension=0, tiled=True).astype(jnp.float32)
    grad_gate_up = lax.all_to_all(gate_up_grad.reshape(n * w_rows, 2, 1, ff_part), EVERY, split_axis=0, concat_axis=2, tiled=True)
    grad_gate_up = grad_gate_up.reshape(w_rows, 2 * n * ff_part).astype(jnp.float32)
    d_mid_norm, gain_two_term = norm_backward(d_normed_two, mid, scale_two, gain_two)
    d_mid = grad_rows + d_mid_norm

    d_attn = lax.all_gather((BRANCH * d_mid).astype(jnp.bfloat16), "ctx", axis=0, tiled=True)
    grad_out = lax.psum_scatter(dot(attn_out, d_attn, ((0,), (0,))), "shard", scatter_dimension=0, tiled=True)
    d_heads = dot(d_attn, out_mine, ((1,), (1,))).astype(jnp.bfloat16)
    d_q, d_k, d_v = attend_back(queries, keys, values, attn_out, d_heads, lse, q_seg, k_seg)
    d_qkv = jnp.concatenate([d_q, d_k, d_v], axis=1)
    qkv_term = dot(d_qkv, qkv_mine, ((1,), (1,))).astype(jnp.bfloat16)
    d_normed_one = lax.psum_scatter(qkv_term, "ctx", scatter_dimension=0, tiled=True).astype(jnp.float32)
    qkv_grad = dot(normed_one, d_qkv, ((0,), (0,))).reshape(n_ctx, n_shard * w_rows, -1)
    qkv_grad = lax.psum_scatter(qkv_grad, "shard", scatter_dimension=1, tiled=True)
    qkv_grad = lax.all_to_all(qkv_grad, "ctx", split_axis=0, concat_axis=0, tiled=True)
    grad_qkv = join_heads(qkv_grad.transpose(1, 0, 2), n_ctx)
    d_rows_norm, gain_one_term = norm_backward(d_normed_one, rows, scale_one, gain_one)
    grad_tokens = (d_mid + d_rows_norm).reshape(1, count, width)
    gain_terms = lax.psum_scatter(jnp.stack([gain_one_term, gain_two_term]), EVERY, scatter_dimension=1, tiled=True)
    return (mixed, grad_tokens, grad_qkv, grad_out, grad_gate_up, grad_down, gain_terms[0], gain_terms[1], clip)


def on_planes(n_shard, tokens, lengths, cotangent, w_qkv, w_out, w_gate_up, w_down, gain_attn, gain_mlp):
    count, width = tokens.shape[1:]
    w_rows = w_qkv.shape[0]
    rows = tokens.reshape(count, width)
    grad = cotangent.reshape(count, width)
    size = count * 8
    seg = segment_ids(jnp.arange(size, dtype=jnp.int32), lengths[0])
    q_seg, k_seg = seg.reshape(size, 1), seg.reshape(1, size)
    side = lax.rem(lax.axis_index("ctx") * n_shard + lax.axis_index("shard"), 2)

    gains = jnp.stack([gain_attn, gain_mlp])
    none = jnp.zeros_like(gains)
    gains = jnp.where(side == 0, jnp.concatenate([gains, none], axis=1), jnp.concatenate([none, gains], axis=1))
    gains = jnp.pad(gains, ((0, 14), (0, 0)))
    mid, normed_two, qkv, attn_out, lse, tops, gain, normed_one, qkv_mine, out_mine, d_mlp, gate_up_mine = front(
        n_shard, rows, grad, w_gate_up, gains, split_heads(w_qkv, 8).transpose(1, 0, 2), w_out, q_seg, k_seg
    )
    heads = HEADS // 8
    head_top = jnp.max(tops[:, 0, :heads].reshape(8, n_shard, heads), axis=1).reshape(HEADS)
    clip = CLIP_TARGET / jnp.maximum(head_top, CLIP_TARGET)

    mlp_term, d_mid, d_attn, gain_term, gate_up_grad, grad_down = mlp_exchange(
        n_shard, normed_two, d_mlp, gate_up_mine, w_down, mid, grad, gain
    )
    mixed, grad_tokens, qkv_grad, grad_out, gain_sum, grad_gate_up = back(
        n_shard, d_attn, rows, mid, d_mid, qkv, attn_out, lse, gain, gain_term, q_seg, k_seg, normed_one, qkv_mine, out_mine, mlp_term, gate_up_grad
    )
    grad_qkv = join_heads(qkv_grad.transpose(1, 0, 2), 8)
    gain_grads = jnp.where(side == 0, gain_sum[:2, :w_rows], gain_sum[:2, w_rows : 2 * w_rows])
    return (mixed.reshape(1, count, width), grad_tokens.reshape(1, count, width), grad_qkv, grad_out, grad_gate_up, grad_down, gain_grads[0], gain_grads[1], clip)


def solution(mesh):
    by_token, by_row = P("shard", "ctx", None), P(EVERY, None)
    n_ctx, n_shard = mesh.shape["ctx"], mesh.shape["shard"]
    program = functools.partial(on_planes, n_shard) if (n_ctx, n_shard) == (8, 4) else functools.partial(per_device, n_ctx, n_shard)
    return jax.shard_map(
        program,
        mesh=mesh,
        in_specs=(by_token, P("shard", None), by_token, by_row, by_row, by_row, by_row, P(EVERY), P(EVERY)),
        out_specs=(by_token, by_token, by_row, by_row, by_row, by_row, P(EVERY), P(EVERY), P()),
        check_vma=False,
    )
```

```python
import functools
import math

import jax
import jax.numpy as jnp
from jax import lax
from jax.experimental import pallas as pl
from jax.experimental.pallas import tpu as pltpu
from jax.sharding import PartitionSpec as P

HEADS = 32
KV_HEADS = 8
HEAD_DIM = 64


SCALE = 0.015625
BRANCH = 0.22
EPSILON = 1e-05
CLIP_TARGET = 4.0
NEGATIVE = -1e30
MIB = 1024 * 1024
EVERY = ("ctx", "shard")


def segment_ids(positions, lengths_row):
    bounds = jnp.cumsum(lengths_row)[:-1]
    return jnp.sum((positions[:, None] >= bounds[None, :]).astype(jnp.int32), axis=1)


def rms_scale(rows):
    return lax.rsqrt(jnp.mean(rows * rows, axis=-1, keepdims=True) + EPSILON)


def norm_backward(d_normed, rows, scale, gain):
    unit = rows * scale
    d_unit = d_normed * gain
    gain_term = jnp.sum(d_normed * unit, axis=0)
    d_rows = scale * (d_unit - unit * jnp.mean(d_unit * unit, axis=-1, keepdims=True))
    return (d_rows, gain_term)


def dot(left, right, dims):
    return lax.dot_general(left, right, ((dims[0], dims[1]), ((), ())), preferred_element_type=jnp.float32)


def segments(lengths_ref, positions):
    bound = jnp.int32(0)
    seg = jnp.zeros(positions.shape, jnp.int32)
    for i in range(lengths_ref.shape[1] - 1):
        bound = bound + lengths_ref[0, i]
        seg = seg + jnp.where(positions >= bound, 1, 0)
    return seg


def block_mask(lengths_ref, row0, rows, cols):
    q_seg = segments(lengths_ref, row0 + lax.broadcasted_iota(jnp.int32, (rows, 1), 0))
    return seen_mask(row0, rows, cols, q_seg, segments(lengths_ref, lax.broadcasted_iota(jnp.int32, (1, cols), 1)))


def seen_mask(row0, rows, cols, q_seg, k_seg):
    q_pos = row0 + lax.broadcasted_iota(jnp.int32, (rows, cols), 0)
    k_pos = lax.broadcasted_iota(jnp.int32, (rows, cols), 1)
    return (k_pos <= q_pos) & ((k_seg == 0) | (k_seg == q_seg))


def attend_kernel(heads, block, q_ref, k_ref, v_ref, q_seg_ref, k_seg_ref, o_ref, lse_ref, top_ref):
    size = q_ref.shape[0]
    tops = [jnp.full((1, 1), NEGATIVE, jnp.float32)] * heads
    for i in range(size // block):
        rows, cols = pl.ds(i * block, block), (i + 1) * block
        live = seen_mask(i * block, block, cols, q_seg_ref[rows, :], k_seg_ref[:, :cols])
        keys, values = k_ref[:cols, :], v_ref[:cols, :]
        for h in range(heads):
            span = slice(h * HEAD_DIM, (h + 1) * HEAD_DIM)
            scores = dot(q_ref[rows, span], keys, ((1,), (1,))) * SCALE
            scores = jnp.where(live, scores, NEGATIVE)
            peak = jnp.max(scores, axis=-1, keepdims=True)
            weights = jnp.exp(scores - peak)
            total = jnp.sum(weights, axis=-1, keepdims=True)
            out = dot(weights.astype(jnp.bfloat16), values, ((1,), (0,)))
            o_ref[rows, span] = (out / total).astype(jnp.bfloat16)
            lse_ref[rows, h : h + 1] = peak + jnp.log(total)
            tops[h] = jnp.maximum(tops[h], jnp.max(peak, axis=0, keepdims=True))
    for h in range(heads):
        top_ref[:, h : h + 1] = tops[h]


def attend(queries, keys, values, q_seg, k_seg):
    size, width = queries.shape
    heads = width // HEAD_DIM
    return pl.pallas_call(
        functools.partial(attend_kernel, heads, math.gcd(size, 256)),
        out_shape=(
            jax.ShapeDtypeStruct((size, width), jnp.bfloat16),
            jax.ShapeDtypeStruct((size, heads), jnp.float32),
            jax.ShapeDtypeStruct((1, heads), jnp.float32),
        ),
        compiler_params=pltpu.CompilerParams(vmem_limit_bytes=48 * MIB),
    )(queries, keys, values, q_seg, k_seg)


def attend_back_kernel(
    heads, block, q_ref, k_ref, v_ref, o_ref, do_ref, lse_ref, q_seg_ref, k_seg_ref, dq_ref, dk_ref, dv_ref, dk_sum, dv_sum
):
    size = q_ref.shape[0]
    dk_sum[...] = jnp.zeros_like(dk_sum)
    dv_sum[...] = jnp.zeros_like(dv_sum)
    for i in range(size // block):
        rows, cols = pl.ds(i * block, block), (i + 1) * block
        live = seen_mask(i * block, block, cols, q_seg_ref[rows, :], k_seg_ref[:, :cols])
        keys, values = k_ref[:cols, :], v_ref[:cols, :]
        for h in range(heads):
            span = slice(h * HEAD_DIM, (h + 1) * HEAD_DIM)
            queries, d_out = q_ref[rows, span], do_ref[rows, span]
            delta = jnp.sum(d_out.astype(jnp.float32) * o_ref[rows, span].astype(jnp.float32), axis=-1, keepdims=True)
            scores = dot(queries, keys, ((1,), (1,))) * SCALE
            probs = jnp.where(live, jnp.exp(scores - lse_ref[rows, h : h + 1]), 0.0)
            d_probs = dot(d_out, values, ((1,), (1,)))
            d_scores = (probs * (d_probs - delta)).astype(jnp.bfloat16)
            dq_ref[rows, span] = (dot(d_scores, keys, ((1,), (0,))) * SCALE).astype(jnp.bfloat16)
            dk_sum[:cols, :] += dot(d_scores, queries, ((0,), (0,)))
            dv_sum[:cols, :] += dot(probs.astype(jnp.bfloat16), d_out, ((0,), (0,)))
    dk_ref[...] = (dk_sum[...] * SCALE).astype(jnp.bfloat16)
    dv_ref[...] = dv_sum[...].astype(jnp.bfloat16)


def attend_back(queries, keys, values, out, d_out, lse, q_seg, k_seg):
    size, width = queries.shape
    heads = width // HEAD_DIM
    like_kv = jax.ShapeDtypeStruct((size, HEAD_DIM), jnp.bfloat16)
    return pl.pallas_call(
        functools.partial(attend_back_kernel, heads, math.gcd(size, 256)),
        out_shape=(jax.ShapeDtypeStruct((size, width), jnp.bfloat16), like_kv, like_kv),
        scratch_shapes=[pltpu.VMEM((size, HEAD_DIM), jnp.float32)] * 2,
        compiler_params=pltpu.CompilerParams(vmem_limit_bytes=48 * MIB),
    )(queries, keys, values, out, d_out, lse, q_seg, k_seg)


def remote(src, dst, send_sem, recv_sem, device):
    return pltpu.make_async_remote_copy(
        src_ref=src, dst_ref=dst, send_sem=send_sem, recv_sem=recv_sem, device_id=device, device_id_type=pl.DeviceIdType.MESH
    )


def greet(devices, extra):
    barrier = pltpu.get_barrier_semaphore()
    count = len(devices)
    for device in devices:
        pl.semaphore_signal(barrier, inc=1, device_id=device, device_id_type=pl.DeviceIdType.MESH)
    for condition, device in extra:

        @pl.when(condition)
        def _():
            pl.semaphore_signal(barrier, inc=1, device_id=device, device_id_type=pl.DeviceIdType.MESH)

        count = count + condition.astype(jnp.int32)
    pl.semaphore_wait(barrier, count)


def add_rows(target, sources, rows, keep=None, step=32):
    @pl.loop(0, rows // step)
    def _(i):
        part = pl.ds(pl.multiple_of(i * step, step), step)
        total = target[part, :].astype(jnp.float32)
        for source in sources:
            total = total + source[part, :].astype(jnp.float32)
        if keep is None:
            target[part, :] = total.astype(jnp.bfloat16)
        else:
            keep[part, :] = total


class Place:
    def __init__(self, line):
        self.line = line
        self.c, self.z = lax.axis_index("ctx"), lax.axis_index("shard")
        self.q, self.core = self.c // 2, self.c % 2
        self.me = self.c * line + self.z
        self.every = 8 * line
        self.cx, self.cy = (self.c + 2 - 4 * (self.q % 2), self.z), (self.c + 4 - 8 * (self.q // 2), self.z)
        self.sibling = (self.c + 1 - 2 * self.core, self.z)
        self.qx, self.qy, self.qd = self.q + 1 - 2 * (self.q % 2), self.q + 2 - 4 * (self.q // 2), 3 - self.q

    def source(self, k):
        if self.line == 1:
            return self.z * 0
        mirrored = self.z >= self.line // 2
        near = jnp.where(mirrored, self.line - 1 - self.z, self.z)
        turn = (k + 1) // 2
        both = near - turn if k % 2 == 1 else near + turn
        at = jnp.where(k <= 2 * near, both, k)
        return jnp.where(mirrored, self.line - 1 - at, at)

    def line_spread(self, copy, k):
        at = self.source(k)
        if k > 0:
            copy(at, 0).wait_recv()
        for way, condition in enumerate(self.line_ways(at)):

            @pl.when(condition)
            def _():
                copy(at, way).start()

    def line_sent(self, copy, k):
        at = self.source(k)
        for way, condition in enumerate(self.line_ways(at)):

            @pl.when(condition)
            def _():
                copy(at, way).wait_send()

    def line_ways(self, at):
        return ((at <= self.z) & (self.z < self.line - 1), (at >= self.z) & (self.z > 0))

    def peer(self, i):
        other = lax.rem(self.me + i, self.every)
        return other, (other // self.line, other % self.line)

    def greet_near(self):
        z, last = self.z, self.line - 1
        greet([self.cx, self.cy, self.sibling], [(z < last, (self.c, z + 1)), (z > 0, (self.c, z - 1))])

    def greet_all(self):
        barrier = pltpu.get_barrier_semaphore()

        @pl.loop(1, self.every)
        def _(i):
            pl.semaphore_signal(barrier, inc=1, device_id=self.peer(i)[1], device_id_type=pl.DeviceIdType.MESH)

        pl.semaphore_wait(barrier, self.every - 1)

    def push_all(self, source, target, send_sems, recv_sems, piece=0, pieces=1):
        @pl.loop(max(1, piece * self.every // pieces), (piece + 1) * self.every // pieces)
        def _(i):
            other, device = self.peer(i)
            remote(source(other), target(self.me), send_sems.at[other], recv_sems.at[self.me], device).start()

    def wait_all(self, source, target, send_sems, recv_sems, sent=True):
        @pl.loop(1, self.every)
        def _(i):
            other, device = self.peer(i)
            copy = remote(source(other), target(other), send_sems.at[other], recv_sems.at[other], device)
            if sent:
                copy.wait_send()
            else:
                copy.wait_recv()


class SliceGather:
    def __init__(self, place, rows, blk, sems):
        self.place, self.rows, self.half = place, rows, blk // 2
        self.z_send, self.z_recv, self.p_send, self.p_recv, self.f_send, self.f_recv = sems
        p, half = place, blk // 2
        self.ways = ((p.cx, p.qx, 0), (p.cy, p.qy, half), (p.cx, p.qx, half), (p.cy, p.qy, 0))
        self.turns = ((p.qx, 0, p.cy), (p.qy, half, p.cx))

    def line_copy(self, at, way):
        ref = self.rows(at, self.place.q, 0, 2 * self.half)
        return remote(ref, ref, self.z_send.at[at, way], self.z_recv.at[at], (self.place.c, self.place.z + 1 - 2 * way))

    def plane_copy(self, at, i, arriving=False):
        device, chip, first = self.ways[i]
        ref = self.rows(at, chip if arriving else self.place.q, first, self.half)
        return remote(ref, ref, self.p_send.at[at, i], self.p_recv.at[at, i], device)

    def onward_copy(self, at, i, arriving=False):
        chip, first, device = self.turns[i]
        ref = self.rows(at, self.place.qd if arriving else chip, first, self.half)
        return remote(ref, ref, self.f_send.at[at, i], self.f_recv.at[at, i], device)

    def a(self, k):
        self.place.line_spread(self.line_copy, k)
        for i in range(4):
            self.plane_copy(self.place.source(k), i).start()

    def b(self, k):
        at = self.place.source(k)
        for i in (0, 1):
            self.plane_copy(at, i, True).wait_recv()
            self.onward_copy(at, i).start()

    def c(self, k):
        at = self.place.source(k)
        for i in (2, 3):
            self.plane_copy(at, i, True).wait_recv()
        for i in (0, 1):
            self.onward_copy(at, i, True).wait_recv()
        for i in range(4):
            self.plane_copy(at, i).wait_send()
        for i in (0, 1):
            self.onward_copy(at, i).wait_send()
        self.place.line_sent(self.line_copy, k)


def slice_gather_sems(line):
    return [pltpu.SemaphoreType.DMA(shape) for shape in ((line, 2), (line,), (line, 4), (line, 4), (line, 2), (line, 2))]


class SliceReduce:
    def __init__(self, place, rows, blk, land, line_land, result, sems):
        self.place, self.rows, self.blk, self.half = place, rows, blk, blk // 2
        self.land, self.line_land, self.result = land, line_land, result
        self.r2_send, self.r2_recv, self.r3_send, self.r3_recv, self.r4_send, self.r4_recv = sems
        p, half = place, blk // 2
        self.seconds = ((0, p.cy), (half, p.cx))
        self.thirds = ((p.cx, p.qx, 0, 0), (p.cy, p.qy, half, blk + half), (p.cx, p.qx, half, half), (p.cy, p.qy, 0, blk))

    def landing(self, at, first, count):
        return self.land.at[at, pl.ds(first, count), :]

    def second(self, at, i):
        first, device = self.seconds[i]
        return remote(
            self.rows(at, self.place.qd, first, self.half), self.landing(at, 2 * self.blk + first, self.half), self.r2_send.at[at, i], self.r2_recv.at[at, i], device
        )

    def third(self, at, i):
        device, chip, first, lands = self.thirds[i]
        return remote(
            self.rows(at, chip, first, self.half), self.landing(at, lands, self.half), self.r3_send.at[at, i], self.r3_recv.at[at, i], device
        )

    def line_part(self, at, slot, part):
        rows = pl.ds(part * self.half, self.half)
        return self.rows(at, self.place.q, part * self.half, self.half), self.line_land.at[slot, rows, :]

    def line_copy(self, at, way, part):
        p = self.place
        slot = jnp.where((way == 1) & (at == p.z - 1), p.line, at)
        source, target = self.line_part(at, slot, part)
        return remote(source, target, self.r4_send.at[at, part], self.r4_recv.at[slot, part], (p.c, p.z + 1 - 2 * way))

    def line_arrival(self, at, slot, part):
        source, target = self.line_part(at, slot, part)
        return remote(source, target, self.r4_send.at[at, part], self.r4_recv.at[slot, part], self.place.sibling)

    def a(self, k):
        at = self.place.source(k)
        for i in (0, 1):
            self.second(at, i).start()
        for i in (2, 3):
            self.third(at, i).start()

    def b(self, k):
        at = self.place.source(k)
        for i in (0, 1):
            chip, first = self.thirds[i][1:3]
            self.second(at, i).wait_recv()
            add_rows(self.rows(at, chip, first, self.half), [self.landing(at, 2 * self.blk + first, self.half)], self.half)
            self.third(at, i).start()

    def c(self, k):
        p, blk = self.place, self.blk
        at = p.source(k)
        has_up, has_down = p.z < p.line - 1, p.z > 0
        for i in range(4):
            self.third(at, i).wait_recv()
        half = self.half
        joined = ((at > p.z) & has_down) | ((at < p.z) & has_up)
        for part in (0, 1):
            mine = self.rows(at, p.q, part * half, half)
            plane = [self.landing(at, part * half, half), self.landing(at, blk + part * half, half)]
            if k > 0:

                @pl.when(joined)
                def _():
                    self.line_arrival(at, at, part).wait_recv()
                    add_rows(mine, plane + [self.line_part(at, at, part)[1]], half)

                @pl.when(jnp.logical_not(joined))
                def _():
                    add_rows(mine, plane, half)

                for way, condition in enumerate((at > p.z, at < p.z)):

                    @pl.when(condition)
                    def _():
                        self.line_copy(at, way, part).start()

            else:
                result = self.result.at[pl.ds(part * half, half), :]
                add_rows(mine, plane, half, result)
                for condition, slot in ((has_down, at), (has_up, p.line)):

                    @pl.when(condition)
                    def _():
                        self.line_arrival(at, slot, part).wait_recv()
                        add_rows(result, [self.line_part(at, slot, part)[1]], half, result)

    def end(self, k):
        at = self.place.source(k)
        for i in (0, 1):
            self.second(at, i).wait_send()
        for i in range(4):
            self.third(at, i).wait_send()
        if k > 0:
            for part in (0, 1):
                self.line_copy(at, 0, part).wait_send()


class LineReduce:
    def __init__(self, place, block, land, rows, sems):
        self.place, self.block, self.land, self.rows = place, block, land, rows
        self.send, self.recv = sems

    def copy(self, at, way):
        p = self.place
        slot = jnp.where((way == 1) & (at == p.z - 1), p.line, at)
        return remote(self.block(at), self.land.at[slot], self.send.at[at], self.recv.at[slot], (p.c, p.z + 1 - 2 * way))

    def arrive(self, at, slot):
        p = self.place
        remote(self.block(at), self.land.at[slot], self.send.at[at], self.recv.at[slot], p.sibling).wait_recv()
        add_rows(self.block(at), [self.land.at[slot]], self.rows)

    def each(self, k, joined, after):
        p = self.place
        at = p.source(k)
        for way, toward, behind in ((0, at > p.z, p.z > 0), (1, at < p.z, p.z < p.line - 1)):

            @pl.when(toward & (behind if joined else jnp.logical_not(behind)))
            def _():
                after(at, way)

    def first(self):
        for k in range(self.place.line - 1, 0, -1):
            self.each(k, False, lambda at, way: self.copy(at, way).start())

    def join(self, k):
        def step(at, way):
            self.arrive(at, at)
            self.copy(at, way).start()

        self.each(k, True, step)

    def last(self):
        p = self.place
        for condition, slot in ((p.z > 0, p.z), (p.z < p.line - 1, p.line)):

            @pl.when(condition)
            def _():
                self.arrive(p.z, slot)

    def end(self):
        for k in range(1, self.place.line):
            self.copy(self.place.source(k), 0).wait_send()


def slice_reduce_sems(line):
    return [pltpu.SemaphoreType.DMA(shape) for shape in ((line, 2), (line, 2), (line, 4), (line, 4), (line, 2), (line + 1, 2))]


def slice_rows(ref, blk):
    def rows(at, chip, first, count):
        return ref.at[pl.ds(pl.multiple_of((at * 4 + chip) * blk + first, blk // 2), count), :]

    return rows


class ColumnSpread:
    def __init__(self, place, source, target, part, send_sems, recv_sems):
        self.place, self.source, self.target, self.part = place, source, target, part
        self.send_sems, self.recv_sems = send_sems, recv_sems

    def copies(self, other, slot):
        rows = self.source.shape[0]
        for j in (0, 1):
            columns = self.source.at[:, pl.ds(pl.multiple_of((j * self.place.every + other) * self.part, self.part), self.part)]
            yield j, columns, self.target.at[pl.ds(pl.multiple_of(slot * rows, rows), rows), pl.ds(j * self.part, self.part)]

    def start(self, piece, pieces):
        every = self.place.every

        @pl.loop(max(1, piece * every // pieces), (piece + 1) * every // pieces)
        def _(i):
            other, device = self.place.peer(i)
            for j, source, target in self.copies(other, self.place.me):
                remote(source, target, self.send_sems.at[j, other], self.recv_sems.at[j, self.place.me], device).start()

    def own(self, sems):
        return [pltpu.make_async_copy(source, target, sems[j]) for j, source, target in self.copies(self.place.me, self.place.me)]

    def wait(self):
        @pl.loop(1, self.place.every)
        def _(i):
            other, device = self.place.peer(i)
            for j, source, target in self.copies(other, other):
                copy = remote(source, target, self.send_sems.at[j, other], self.recv_sems.at[j, other], device)
                copy.wait_recv()
                copy.wait_send()


def mlp_kernel(
    line, blk, part, normed_ref, d_mlp_ref, gate_up_ref, down_ref, mid_ref, grad_ref, gain_ref,
    mlp_term_ref, d_mid_ref, d_attn_ref, gain_term_ref, gate_up_grad_ref, down_grad_ref,
    act, land, line_land, w_gu, w_down, acc_gu, acc_down, hid, d_gu, sib_gu, sib_down, d_normed,
    w_send, w_recv, g_send, g_recv, own_sem, out_sem, *sems,
):
    place = Place(line)
    core, sibling = place.core, place.sibling
    width = w_down.shape[1]
    slot_rows = 4 * blk
    rows = slice_rows(act.at[0], blk)
    gather = SliceGather(place, rows, blk, sems[:6])
    reduce = SliceReduce(place, rows, blk, land, line_land, d_normed, sems[6:])

    def slot_of(k):
        return pl.ds(pl.multiple_of(place.source(k) * slot_rows, slot_rows), slot_rows)

    own = pltpu.make_async_copy(normed_ref, rows(place.z, place.q, 0, blk), own_sem.at[0])
    d_mlp_in = pltpu.make_async_copy(d_mlp_ref, act.at[1], own_sem.at[1])
    mine = pl.ds(pl.multiple_of(core * 2 * part, 2 * part), 2 * part)
    theirs = pl.ds(pl.multiple_of((1 - core) * 2 * part, 2 * part), 2 * part)
    mine_rows = pl.ds(pl.multiple_of(core * part, part), part)
    their_rows = pl.ds(pl.multiple_of((1 - core) * part, part), part)

    own_weights = [
        pltpu.make_async_copy(gate_up_ref, w_gu.at[:, mine], own_sem.at[2]),
        pltpu.make_async_copy(down_ref, w_down.at[mine_rows, :], own_sem.at[3]),
    ]
    weights_to = [
        remote(gate_up_ref, w_gu.at[:, mine], w_send.at[0], w_recv.at[0], sibling),
        remote(down_ref, w_down.at[mine_rows, :], w_send.at[1], w_recv.at[1], sibling),
    ]
    weights_from = [
        remote(gate_up_ref, w_gu.at[:, theirs], w_send.at[0], w_recv.at[0], sibling),
        remote(down_ref, w_down.at[their_rows, :], w_send.at[1], w_recv.at[1], sibling),
    ]

    def compute(k):
        slot = slot_of(k)

        @pl.loop(0, 2)
        def _(j):
            span = pl.ds(pl.multiple_of(j * part, part), part)
            lower = pl.ds(pl.multiple_of(j * 2 * part, part), part)
            upper = pl.ds(pl.multiple_of(j * 2 * part + part, part), part)
            gate = dot(act[0, slot, :], w_gu[:, lower], ((1,), (0,)))
            above = dot(act[0, slot, :], w_gu[:, upper], ((1,), (0,)))
            d_hidden = dot(act[1, slot, :], w_down[span, :], ((1,), (1,)))
            sigma = jax.nn.sigmoid(gate)
            active = gate * sigma
            hid[:, span] = (active * above).astype(jnp.bfloat16)
            d_gu[:, lower] = (d_hidden * above * sigma * (1.0 + gate * (1.0 - sigma))).astype(jnp.bfloat16)
            d_gu[:, upper] = (d_hidden * active).astype(jnp.bfloat16)

        @pl.loop(0, width // 256)
        def _(j):
            span = pl.ds(pl.multiple_of(j * 256, 256), 256)
            down_term = dot(hid[...], act[1, slot, span], ((0,), (0,)))
            gate_up_term = dot(act[0, slot, span], d_gu[...], ((0,), (0,)))
            if k > 0:
                down_term = down_term + acc_down[:, span]
                gate_up_term = gate_up_term + acc_gu[span, :]
            acc_down[:, span] = down_term
            acc_gu[span, :] = gate_up_term
            act[1, slot, span] = dot(hid[...], w_down[:, span], ((1,), (0,))).astype(jnp.bfloat16)
            act[0, slot, span] = dot(d_gu[...], w_gu[span, :], ((1,), (1,))).astype(jnp.bfloat16)

    def term_out(k):
        return pltpu.make_async_copy(act.at[1, slot_of(k), :], mlp_term_ref.at[slot_of(k), :], out_sem.at[2 + k])

    half_gu, whole_gu = pl.ds(0, 2 * part), pl.ds(2 * part, 2 * part)
    grad_copies = [
        remote(w_gu.at[:, half_gu], sib_gu, g_send.at[0], g_recv.at[0], sibling),
        remote(w_down.at[:part, :], sib_down, g_send.at[1], g_recv.at[1], sibling),
    ]
    down_out = pltpu.make_async_copy(acc_down.at[mine_rows, :], down_grad_ref, out_sem.at[0])

    def exchange_grads():
        @pl.loop(0, width // 256)
        def _(j):
            span = pl.ds(pl.multiple_of(j * 256, 256), 256)
            w_gu[span, half_gu] = acc_gu[span, theirs].astype(jnp.bfloat16)

        w_down[:part, :] = acc_down[their_rows, :].astype(jnp.bfloat16)
        for copy in grad_copies:
            copy.start()

    columns_out = pltpu.make_async_copy(w_gu.at[:, whole_gu], gate_up_grad_ref, out_sem.at[1])

    def finish_grads():
        for copy in grad_copies:
            copy.wait_recv()

        @pl.loop(0, width // 256)
        def _(j):
            span = pl.ds(pl.multiple_of(j * 256, 256), 256)
            w_gu[span, whole_gu] = (acc_gu[span, mine] + sib_gu[span, :].astype(jnp.float32)).astype(jnp.bfloat16)

        columns_out.start()
        acc_down[mine_rows, :] = acc_down[mine_rows, :] + sib_down[...].astype(jnp.float32)
        down_out.start()

    for copy in [own, d_mlp_in] + own_weights:
        copy.start()
    place.greet_near()
    own.wait()
    gather.a(0)
    for copy in weights_to:
        copy.start()
    gather.a(1)
    gather.b(0)
    gather.a(2)
    gather.b(1)
    for copy in [d_mlp_in] + own_weights:
        copy.wait()
    for copy in weights_from:
        copy.wait_recv()
    for copy in weights_to:
        copy.wait_send()
    gather.a(3)
    gather.b(2)
    gather.c(0)
    compute(0)
    term_out(0).start()
    gather.b(3)
    gather.c(1)
    compute(1)
    term_out(1).start()
    reduce.a(1)
    gather.c(2)
    compute(2)
    term_out(2).start()
    reduce.a(2)
    gather.c(3)
    compute(3)
    term_out(3).start()
    reduce.a(3)
    exchange_grads()
    reduce.b(3)
    reduce.b(2)
    finish_grads()
    reduce.a(0)
    reduce.c(3)
    reduce.b(1)
    reduce.c(2)
    reduce.b(0)
    reduce.c(1)
    reduce.c(0)
    backwards = range(line - 1, -1, -1)

    gain_term_ref[...] = jnp.zeros_like(gain_term_ref)

    @pl.loop(0, blk // 32)
    def _(i):
        part = pl.ds(pl.multiple_of(i * 32, 32), 32)
        mid = mid_ref[part, :]
        d_rows, gain_term = norm_backward(d_normed[part, :], mid, rms_scale(mid), gain_ref[1:2, :])
        d_mid = grad_ref[part, :].astype(jnp.float32) + d_rows
        d_mid_ref[part, :] = d_mid
        d_attn_ref[part, :] = (BRANCH * d_mid).astype(jnp.bfloat16)
        gain_term_ref[0:1, :] += gain_term.reshape(1, width)

    for k in backwards:
        reduce.end(k)
        term_out(k).wait()
    for copy in grad_copies:
        copy.wait_send()
    down_out.wait()
    columns_out.wait()


def mlp_exchange(line, normed, d_mlp, gate_up, down, mid, grad, gain):
    blk, width = normed.shape
    part = down.shape[0]
    any_spec, vmem_spec = pl.BlockSpec(memory_space=pl.ANY), pl.BlockSpec(memory_space=pltpu.VMEM)
    bf16, f32, dma = jnp.bfloat16, jnp.float32, pltpu.SemaphoreType.DMA
    return pl.pallas_call(
        functools.partial(mlp_kernel, line, blk, part),
        out_shape=(
            jax.ShapeDtypeStruct(d_mlp.shape, bf16),
            jax.ShapeDtypeStruct((blk, width), f32),
            jax.ShapeDtypeStruct((blk, width), bf16),
            jax.ShapeDtypeStruct((8, width), f32),
            jax.ShapeDtypeStruct(gate_up.shape, bf16),
            jax.ShapeDtypeStruct((part, width), f32),
        ),
        in_specs=[any_spec] * 4 + [vmem_spec] * 3,
        out_specs=(any_spec, vmem_spec, vmem_spec, vmem_spec, any_spec, any_spec),
        scratch_shapes=[
            pltpu.VMEM((2, line * 4 * blk, width), bf16),
            pltpu.VMEM((line, 3 * blk, width), bf16),
            pltpu.VMEM((line + 1, blk, width), bf16),
            pltpu.VMEM((width, 4 * part), bf16),
            pltpu.VMEM((2 * part, width), bf16),
            pltpu.VMEM((width, 4 * part), f32),
            pltpu.VMEM((2 * part, width), f32),
            pltpu.VMEM((4 * blk, 2 * part), bf16),
            pltpu.VMEM((4 * blk, 4 * part), bf16),
            pltpu.VMEM((width, 2 * part), bf16),
            pltpu.VMEM((part, width), bf16),
            pltpu.VMEM((blk, width), f32),
            dma((2,)),
            dma((2,)),
            dma((2,)),
            dma((2,)),
            dma((5,)),
            dma((2 + line,)),
            *slice_gather_sems(line),
            *slice_reduce_sems(line),
        ],
        compiler_params=pltpu.CompilerParams(collective_id=0, has_side_effects=True, vmem_limit_bytes=63 * MIB),
    )(normed, d_mlp, gate_up, down, mid, grad, gain)


def plane_gather(at, buf, blk, sems):
    p_send, p_recv, f_send, f_recv, s_send, s_recv = sems
    half = blk // 2

    def rows(chip, core, first=0, count=half):
        return buf.at[pl.ds(pl.multiple_of((2 * chip + core) * blk + first, half), count), :]

    def same(ref, send, recv, device):
        return remote(ref, ref, send, recv, device)

    way = ((at.cx, at.qx, 0), (at.cy, at.qy, half), (at.cx, at.qx, half), (at.cy, at.qy, 0))

    def sent(i):
        return same(rows(at.q, at.core, way[i][2]), p_send.at[i], p_recv.at[i], way[i][0])

    def arriving(i):
        return same(rows(way[i][1], at.core, way[i][2]), p_send.at[i], p_recv.at[i], way[i][0])

    def onward(i):
        chip, first, device = ((at.qx, 0, at.cy), (at.qy, half, at.cx))[i]
        return same(rows(chip, at.core, first), f_send.at[i], f_recv.at[i], device)

    def passed(i):
        first, device = ((0, at.cy), (half, at.cx))[i]
        return same(rows(at.qd, at.core, first), f_send.at[i], f_recv.at[i], device)

    def across(i, core):
        if i == 0:
            ref = rows(at.q, core, 0, blk)
        elif i < 5:
            ref = rows(way[i - 1][1], core, way[i - 1][2])
        else:
            ref = rows(at.qd, core, (i - 5) * half)
        return same(ref, s_send.at[i], s_recv.at[i], at.sibling)

    def start():
        for i in range(4):
            sent(i).start()
        across(0, at.core).start()

    def turn():
        for i in (0, 1):
            arriving(i).wait_recv()
            onward(i).start()
            across(i + 1, at.core).start()

    def rest():
        for i in (2, 3):
            arriving(i).wait_recv()
            across(i + 1, at.core).start()
        for i in (0, 1):
            passed(i).wait_recv()
            across(i + 5, at.core).start()

    def whole():
        for i in range(7):
            across(i, 1 - at.core).wait_recv()

    def end():
        for i in range(4):
            sent(i).wait_send()
        for i in (0, 1):
            onward(i).wait_send()
        for i in range(7):
            across(i, at.core).wait_send()

    return start, turn, rest, whole, end


GATHER_SEMS = (4, 4, 2, 2, 7, 7)
REDUCE_SEMS = (4, 4, 2, 2, 4, 4)


def plane_reduce(at, term, core_land, land, blk, sems):
    s_send, s_recv, r2_send, r2_recv, r3_send, r3_recv = sems
    half = blk // 2
    chips = (at.qd, at.qx, at.qy, at.q)

    def rows(chip, core, first=0, count=half):
        return term.at[pl.ds(pl.multiple_of((2 * chip + core) * blk + first, half), count), :]

    def landed(first, count):
        return land.at[pl.ds(first, count), :]

    def across(i):
        return remote(rows(chips[i], 1 - at.core, 0, blk), core_land.at[i], s_send.at[i], s_recv.at[i], at.sibling)

    def second(i):
        first, device = ((0, at.cy), (half, at.cx))[i]
        return remote(rows(at.qd, at.core, first), landed(2 * blk + first, half), r2_send.at[i], r2_recv.at[i], device)

    def third(i):
        device, chip, first, lands = (
            (at.cx, at.qx, 0, 0), (at.cy, at.qy, half, blk + half), (at.cx, at.qx, half, half), (at.cy, at.qy, 0, blk)
        )[i]
        return remote(rows(chip, at.core, first), landed(lands, half), r3_send.at[i], r3_recv.at[i], device)

    def add_core(i):
        across(i).wait_recv()
        add_rows(rows(chips[i], at.core, 0, blk), [core_land.at[i]], blk)

    def give(i):
        across(i).start()

    def take(result):
        add_core(0)
        second(0).start()
        second(1).start()
        add_core(1)
        third(2).start()
        add_core(2)
        third(3).start()
        for i, (chip, first) in enumerate(((at.qx, 0), (at.qy, half))):
            second(i).wait_recv()
            add_rows(rows(chip, at.core, first), [landed(2 * blk + first, half)], half)
            third(i).start()
        add_core(3)
        for i in range(4):
            third(i).wait_recv()
        add_rows(rows(at.q, at.core, 0, blk), [landed(0, blk), landed(blk, blk)], blk, result)

    def end():
        for i in range(4):
            across(i).wait_send()
            third(i).wait_send()
        for i in (0, 1):
            second(i).wait_send()

    return give, take, end


def front_kernel(
    line, blk, q_part, kv_part,
    tokens_ref, grad_ref, w_gate_up_ref, gains_ref, w_qkv_ref, w_out_ref, lengths_ref,
    mid_ref, normed_two_ref, qkv_ref, attn_ref, lse_ref, tops_ref, gain_ref, normed_ref, w_qkv_all_ref, w_out_all_ref, d_mlp_all_ref, gate_up_ref,
    buf, term, core_land, land, w_qkv, w_line, w_out, gain_land, top_land, proj, d_mlp,
    *sems,
):
    at = Place(line)
    gather = plane_gather(at, buf, blk, sems[:6])
    reduce = plane_reduce(at, term, core_land, land, blk, sems[6:12])
    line_send, line_recv, qkv_send, qkv_recv, gain_send, gain_recv, top_send, top_recv, out_send, out_recv, own_sem, write_sem = sems[12:24]
    d_mlp_rows = slice_rows(d_mlp_all_ref, blk)
    beside = SliceGather(at, d_mlp_rows, blk, sems[24:30])
    spread = ColumnSpread(at, w_gate_up_ref, gate_up_ref, gate_up_ref.shape[1] // 2, *sems[30:])
    w_rows, width = w_out_ref.shape
    size = 8 * blk
    mine = pl.ds(pl.multiple_of(at.c * blk, blk), blk)

    own = [
        pltpu.make_async_copy(tokens_ref, buf.at[mine, :], own_sem.at[0]),
        pltpu.make_async_copy(gains_ref, gain_land.at[at.me], own_sem.at[1]),
        pltpu.make_async_copy(w_qkv_ref, w_line.at[at.z], own_sem.at[2]),
        pltpu.make_async_copy(w_out_ref, w_out.at[at.z], own_sem.at[3]),
        pltpu.make_async_copy(d_mlp, d_mlp_rows(at.z, at.q, 0, blk), own_sem.at[4]),
        *spread.own([own_sem.at[5], own_sem.at[6]]),
    ]
    for copy in own[:4] + own[5:]:
        copy.start()
    d_mlp[...] = (BRANCH * grad_ref[...].astype(jnp.float32)).astype(jnp.bfloat16)
    own[4].start()
    at.greet_all()
    gain_push = (lambda other: gains_ref, lambda slot: gain_land.at[slot], gain_send, gain_recv)
    top_push = (lambda other: top_land.at[at.me], lambda slot: top_land.at[slot], top_send, top_recv)

    def qkv_line(place, way):
        return remote(w_line.at[place], w_line.at[place], line_send.at[place, way], line_recv.at[place], (at.c, at.z + 1 - 2 * way))

    def out_line(place, way):
        return remote(w_out.at[place], w_out.at[place], out_send.at[place, way], out_recv.at[place], (at.c, at.z + 1 - 2 * way))

    def qkv_copy(i, place, arriving=False):
        other = lax.rem(at.c + i, 8)
        slot = (other if arriving else at.c) * line + place
        return remote(w_line.at[place, other], w_qkv.at[slot], qkv_send.at[place, other], qkv_recv.at[slot], (other, at.z))

    def qkv_step(k):
        at.line_spread(qkv_line, k)

        @pl.loop(1, 8)
        def _(i):
            qkv_copy(i, at.source(k)).start()

        w_qkv[at.c * line + at.source(k)] = w_line[at.source(k), at.c]

    start, turn, rest, whole, end = gather
    own[0].wait()
    start()
    own[2].wait()
    qkv_step(0)
    at.push_all(*gain_push)
    turn()
    qkv_step(1)
    own[4].wait()
    beside.a(0)
    rest()
    for k in range(2, line - 1):
        qkv_step(k)
    own[1].wait()
    at.wait_all(*gain_push, sent=False)
    for i in range(at.every // 2):
        pair = gain_land[2 * i].astype(jnp.float32) + gain_land[2 * i + 1].astype(jnp.float32)
        gain_ref[:, i * 128 : (i + 1) * 128] = pair[:8, :]
    spread.start(0, 4)
    whole()
    end()
    at.wait_all(*gain_push)

    @pl.loop(0, size // 32)
    def _(i):
        part = pl.ds(pl.multiple_of(i * 32, 32), 32)
        rows = buf[part, :].astype(jnp.float32)
        buf[part, :] = (rows * rms_scale(rows) * gain_ref[0:1, :]).astype(jnp.bfloat16)

    writes = [
        pltpu.make_async_copy(buf, normed_ref, write_sem.at[0]),
        pltpu.make_async_copy(w_qkv, w_qkv_all_ref, write_sem.at[1]),
        pltpu.make_async_copy(w_out, w_out_all_ref, write_sem.at[2]),
    ]
    writes[0].start()
    qkv_step(line - 1)
    own[3].wait()
    at.line_spread(out_line, 0)
    beside.b(0)
    beside.a(1)
    spread.start(1, 4)
    for k in range(line):

        @pl.loop(1, 8)
        def _(i):
            qkv_copy(i, at.source(k), True).wait_recv()

    writes[1].start()

    @pl.loop(0, size // 256)
    def _(i):
        part = pl.ds(pl.multiple_of(i * 256, 256), 256)
        qkv_ref[part, :] = dot(buf[part, :], w_qkv[...].reshape(width, q_part + 2 * kv_part), ((1,), (0,))).astype(jnp.bfloat16)

    at.line_spread(out_line, 1)
    beside.b(1)
    beside.a(2)
    spread.start(2, 4)
    heads = q_part // HEAD_DIM
    block = math.gcd(size, 256)
    tops = [jnp.full((1, 1), NEGATIVE, jnp.float32)] * heads
    for i in range(size // block):
        if i > 0 and i + 1 < line:
            at.line_spread(out_line, i + 1)
        if i == 2:
            beside.b(2)
            beside.a(3)
        rows, cols = pl.ds(i * block, block), (i + 1) * block
        live = block_mask(lengths_ref, i * block, block, cols)
        keys, values = qkv_ref[:cols, q_part : q_part + kv_part], qkv_ref[:cols, q_part + kv_part :]
        for h in range(heads):
            span = slice(h * HEAD_DIM, (h + 1) * HEAD_DIM)
            scores = dot(qkv_ref[rows, span], keys, ((1,), (1,))) * SCALE
            scores = jnp.where(live, scores, NEGATIVE)
            peak = jnp.max(scores, axis=-1, keepdims=True)
            weights = jnp.exp(scores - peak)
            total = jnp.sum(weights, axis=-1, keepdims=True)
            out = dot(weights.astype(jnp.bfloat16), values, ((1,), (0,)))
            attn_ref[rows, span] = (out / total).astype(jnp.bfloat16)
            lse_ref[rows, h : h + 1] = peak + jnp.log(total)
            tops[h] = jnp.maximum(tops[h], jnp.max(peak, axis=0, keepdims=True))
    lanes = lax.broadcasted_iota(jnp.int32, (8, 128), 1)
    tile = jnp.full((8, 128), NEGATIVE, jnp.float32)
    for h in range(heads):
        tile = jnp.where(lanes == h, tops[h], tile)
    top_land[at.me] = tile
    at.push_all(*top_push)

    for k in range(size // block + 1, line):
        at.line_spread(out_line, k)
    beside.b(3)
    spread.start(3, 4)
    writes[2].start()
    for i, chip in enumerate((at.qd, at.qx, at.qy, at.q)):
        for core in (1 - at.core, at.core):
            part = pl.ds(pl.multiple_of((2 * chip + core) * blk, blk), blk)

            @pl.loop(0, width // 512)
            def _(j):
                span = pl.ds(pl.multiple_of(j * 512, 512), 512)
                matrix = w_out[:, :, span].reshape(line * w_rows, 512)
                term[part, span] = dot(attn_ref[part, :], matrix, ((1,), (0,))).astype(jnp.bfloat16)

        reduce[0](i)
    reduce[1](proj)

    own_again = pltpu.make_async_copy(tokens_ref, land.at[pl.ds(0, blk), :], own_sem.at[0])
    own_again.start()
    own_again.wait()

    @pl.loop(0, blk // 32)
    def _(i):
        part = pl.ds(pl.multiple_of(i * 32, 32), 32)
        rows = land[part, :].astype(jnp.float32) + BRANCH * proj[part, :]
        mid_ref[part, :] = rows
        normed_two_ref[part, :] = (rows * rms_scale(rows) * gain_ref[1:2, :]).astype(jnp.bfloat16)

    at.wait_all(*top_push, sent=False)
    tops_ref[...] = top_land[...]
    reduce[2]()
    at.wait_all(*top_push)
    for k in range(line):
        at.line_sent(qkv_line, k)
        at.line_sent(out_line, k)

        @pl.loop(1, 8)
        def _(i):
            qkv_copy(i, at.source(k)).wait_send()

    for k in range(line):
        beside.c(k)
    spread.wait()
    for copy in own[5:]:
        copy.wait()
    for copy in writes:
        copy.wait()


def front(line, tokens, grad, w_gate_up, gains, w_qkv, w_out, lengths):
    blk, width = tokens.shape
    w_rows, cols = w_out.shape[0], w_qkv.shape[2]
    size, every = 8 * blk, 8 * line
    q_part = HEADS * HEAD_DIM // 8
    kv_part = (cols - q_part) // 2
    heads = q_part // HEAD_DIM
    any_spec, vmem_spec = pl.BlockSpec(memory_space=pl.ANY), pl.BlockSpec(memory_space=pltpu.VMEM)
    bf16, f32, dma, out = jnp.bfloat16, jnp.float32, pltpu.SemaphoreType.DMA, jax.ShapeDtypeStruct
    return pl.pallas_call(
        functools.partial(front_kernel, line, blk, q_part, kv_part),
        out_shape=(
            out((blk, width), f32),
            out((blk, width), bf16),
            out((size, cols), bf16),
            out((size, q_part), bf16),
            out((size, heads), f32),
            out((every, 8, 128), f32),
            out((8, width), f32),
            out((size, width), bf16),
            out((every, w_rows, cols), bf16),
            out((line, w_rows, width), bf16),
            out((line * 4 * blk, width), bf16),
            out((width, w_gate_up.shape[1] // every), bf16),
        ),
        in_specs=[any_spec, vmem_spec] + [any_spec] * 4 + [pl.BlockSpec(memory_space=pltpu.SMEM)],
        out_specs=(vmem_spec,) * 7 + (any_spec,) * 5,
        scratch_shapes=[
            pltpu.VMEM((size, width), bf16),
            pltpu.VMEM((size, width), bf16),
            pltpu.VMEM((4, blk, width), bf16),
            pltpu.VMEM((3 * blk, width), bf16),
            pltpu.VMEM((every, w_rows, cols), bf16),
            pltpu.VMEM((line, 8, w_rows, cols), bf16),
            pltpu.VMEM((line, w_rows, width), bf16),
            pltpu.VMEM((every, 16, 128), bf16),
            pltpu.VMEM((every, 8, 128), f32),
            pltpu.VMEM((blk, width), f32),
            pltpu.VMEM((blk, width), bf16),
            *[dma((n,)) for n in GATHER_SEMS + REDUCE_SEMS],
            dma((line, 2)),
            dma((line,)),
            dma((line, 8)),
            *[dma((every,))] * 5,
            dma((line, 2)),
            dma((line,)),
            dma((7,)),
            dma((3,)),
            *slice_gather_sems(line),
            dma((2, every)),
            dma((2, every)),
        ],
        compiler_params=pltpu.CompilerParams(collective_id=1, has_side_effects=True, vmem_limit_bytes=60 * MIB),
    )(tokens, grad, w_gate_up, gains, w_qkv, w_out, lengths)


def back_kernel(
    line, blk, q_part, kv_part,
    d_attn_ref, tokens_ref, mid_ref, d_mid_ref, qkv_ref, attn_ref, lse_ref, gain_ref, gain_term_ref, lengths_ref, normed_ref, w_qkv_ref, w_out_ref, mlp_term_ref, columns_ref,
    mixed_ref, grad_tokens_ref, grad_qkv_ref, grad_out_ref, gain_sum_ref, grad_gate_up_ref,
    buf, term, core_land, land, w_qkv, w_out, normed, d_heads, d_qkv, dk_sum, dv_sum, stage_qkv, stage_out, qkv_land, out_land, gain_stage, gain_land, d_normed, mlp_term, mlp_land, mlp_line_land, mlp_sum, row_land, row_stage, qkv_line_land,
    *sems,
):
    at = Place(line)
    gather = plane_gather(at, buf, blk, sems[:6])
    reduce = plane_reduce(at, term, core_land, land, blk, sems[6:12])
    qkv_send, qkv_recv, gain_send, gain_recv, out_send, out_recv, own_sem = sems[12:19]
    beside = SliceReduce(at, slice_rows(mlp_term, blk), blk, mlp_land, mlp_line_land, mlp_sum, sems[19:25])
    row_send, row_recv, row_sem = sems[25:28]
    w_cols = w_qkv.shape[1]
    part_ff = columns_ref.shape[1] // 2

    def column_rows(other):
        return columns_ref.at[pl.ds(pl.multiple_of(other * w_cols, w_cols), w_cols), :]

    row_push = (column_rows, lambda slot: row_land.at[slot], row_send, row_recv)
    width = buf.shape[1]
    w_rows = w_out.shape[1]
    size = 8 * blk
    mine = pl.ds(pl.multiple_of(at.c * blk, blk), blk)
    own = [
        pltpu.make_async_copy(d_attn_ref, buf.at[mine, :], own_sem.at[0]),
        pltpu.make_async_copy(w_out_ref, w_out, own_sem.at[1]),
        pltpu.make_async_copy(w_qkv_ref, w_qkv, own_sem.at[2]),
        pltpu.make_async_copy(normed_ref, normed, own_sem.at[3]),
        pltpu.make_async_copy(mlp_term_ref, mlp_term, own_sem.at[4]),
        pltpu.make_async_copy(column_rows(at.me), row_land.at[at.me], own_sem.at[5]),
    ]
    for copy in own:
        copy.start()
    at.greet_all()
    own[0].wait()
    start, turn, rest, whole, end = gather
    start()
    turn()
    rest()
    at.push_all(*row_push)
    for copy in own[1:]:
        copy.wait()
    beside.a(line - 1)
    whole()

    @pl.loop(0, size // 256)
    def _(i):
        part = pl.ds(pl.multiple_of(i * 256, 256), 256)
        d_heads[part, :] = dot(buf[part, :], w_out[...].reshape(line * w_rows, width), ((1,), (1,))).astype(jnp.bfloat16)

    if line > 1:
        beside.a(line - 2)

    @pl.loop(0, width // 256)
    def _(i):
        span = pl.ds(pl.multiple_of(i * 256, 256), 256)
        stage_out[:, :, span] = dot(attn_ref[...], buf[:, span], ((0,), (0,))).astype(jnp.bfloat16).reshape(line, w_rows, 256)

    def out_copy(i):
        z = lax.rem(at.z + i, line)
        return remote(stage_out.at[z], out_land.at[at.z], out_send.at[z], out_recv.at[at.z], (at.c, z))

    def out_arrival(i):
        z = lax.rem(at.z + i, line)
        return remote(stage_out.at[z], out_land.at[z], out_send.at[z], out_recv.at[z], (at.c, z))

    for i in range(1, line):
        out_copy(i).start()

    heads = q_part // HEAD_DIM
    block = math.gcd(size, 256)
    dk_sum[...] = jnp.zeros_like(dk_sum)
    dv_sum[...] = jnp.zeros_like(dv_sum)
    for i in range(size // block):
        rows, cols = pl.ds(i * block, block), (i + 1) * block
        live = block_mask(lengths_ref, i * block, block, cols)
        keys, values = qkv_ref[:cols, q_part : q_part + kv_part], qkv_ref[:cols, q_part + kv_part :]
        for h in range(heads):
            span = slice(h * HEAD_DIM, (h + 1) * HEAD_DIM)
            queries, d_out = qkv_ref[rows, span], d_heads[rows, span]
            delta = jnp.sum(d_out.astype(jnp.float32) * attn_ref[rows, span].astype(jnp.float32), axis=-1, keepdims=True)
            scores = dot(queries, keys, ((1,), (1,))) * SCALE
            probs = jnp.where(live, jnp.exp(scores - lse_ref[rows, h : h + 1]), 0.0)
            d_probs = dot(d_out, values, ((1,), (1,)))
            d_scores = (probs * (d_probs - delta)).astype(jnp.bfloat16)
            d_qkv[rows, span] = (dot(d_scores, keys, ((1,), (0,))) * SCALE).astype(jnp.bfloat16)
            dk_sum[:cols, :] += dot(d_scores, queries, ((0,), (0,)))
            dv_sum[:cols, :] += dot(probs.astype(jnp.bfloat16), d_out, ((0,), (0,)))
    d_qkv[:, q_part : q_part + kv_part] = (dk_sum[...] * SCALE).astype(jnp.bfloat16)
    d_qkv[:, q_part + kv_part :] = dv_sum[...].astype(jnp.bfloat16)
    beside.b(line - 1)
    for k in range(line - 3, 0, -1):
        beside.a(k)

    for i, chip in enumerate((at.qd, at.qx, at.qy, at.q)):
        for core in (1 - at.core, at.core):
            part = pl.ds(pl.multiple_of((2 * chip + core) * blk, blk), blk)

            @pl.loop(0, width // 512)
            def _(j):
                span = pl.ds(pl.multiple_of(j * 512, 512), 512)
                matrix = w_qkv[pl.ds(pl.multiple_of(j * (512 // w_rows), 512 // w_rows), 512 // w_rows)].reshape(512, q_part + 2 * kv_part)
                term[part, span] = dot(d_qkv[part, :], matrix, ((1,), (1,))).astype(jnp.bfloat16)

        reduce[0](i)

    chunk = line * w_cols

    @pl.loop(0, 8)
    def _(i):
        grads = dot(normed[:, pl.ds(pl.multiple_of(i * chunk, chunk), chunk)], d_qkv[...], ((0,), (0,))).astype(jnp.bfloat16)
        for place in range(line):
            stage_qkv[pl.ds(pl.multiple_of((place * 8 + i) * w_cols, w_cols), w_cols), :] = grads[place * w_cols : (place + 1) * w_cols, :]

    def qkv_block(place):
        return stage_qkv.at[pl.ds(pl.multiple_of(place * 8 * w_cols, w_cols), 8 * w_cols), :]

    def qkv_rows(i):
        return stage_qkv.at[pl.ds(pl.multiple_of((at.z * 8 + i) * w_cols, w_cols), w_cols), :]

    def qkv_copy(i, arriving=False):
        other = lax.rem(at.c + i, 8)
        slot = other if arriving else at.c
        return remote(qkv_rows(other), qkv_land.at[slot], qkv_send.at[other], qkv_recv.at[slot], (other, at.z))

    sum_qkv = LineReduce(at, qkv_block, qkv_line_land, 8 * w_cols, sems[28:])
    sum_qkv.first()
    out_land[at.z] = stage_out[at.z]
    reduce[1](d_normed)
    if line > 2:
        beside.a(0)
    for k in range(line - 1, 0, -1):
        sum_qkv.join(k)
    for k in range(line - 2, -1, -1):
        beside.b(k)
    for k in range(line - 1, 1, -1):
        beside.c(k)

    gain_stage[...] = jnp.zeros_like(gain_stage)
    gain_stage[1:2, :] = gain_term_ref[0:1, :]

    @pl.loop(0, blk // 32)
    def _(i):
        part = pl.ds(pl.multiple_of(i * 32, 32), 32)
        rows = tokens_ref[part, :].astype(jnp.float32)
        d_rows, gain_term = norm_backward(d_normed[part, :], rows, rms_scale(rows), gain_ref[0:1, :])
        grad_tokens_ref[part, :] = d_mid_ref[part, :] + d_rows
        gain_stage[0:1, :] += gain_term.reshape(1, width)

    def gain_tile(other):
        return gain_stage.at[:, pl.ds(pl.multiple_of((other // 2) * 128, 128), 128)]

    gain_push = (gain_tile, lambda slot: gain_land.at[slot], gain_send, gain_recv)
    at.push_all(*gain_push)
    gain_land[at.me] = gain_stage[:, pl.ds(pl.multiple_of((at.me // 2) * 128, 128), 128)]

    sum_qkv.last()

    @pl.loop(1, 8)
    def _(i):
        qkv_copy(i).start()

    qkv_land[at.c] = stage_qkv[pl.ds(pl.multiple_of((at.z * 8 + at.c) * w_cols, w_cols), w_cols), :]
    at.wait_all(*row_push, sent=False)

    @pl.loop(0, at.every)
    def _(j):
        span = pl.ds(pl.multiple_of(j * w_cols, w_cols), w_cols)
        row_stage[span, :] = row_land[j].astype(jnp.float32)
        for i in (0, 1):
            target = grad_gate_up_ref.at[:, pl.ds(pl.multiple_of((i * at.every + j) * part_ff, part_ff), part_ff)]
            pltpu.make_async_copy(row_stage.at[span, pl.ds(i * part_ff, part_ff)], target, row_sem.at[0]).start()

    for k in (1, 0):
        beside.c(k)
    mixed_ref[...] = (mid_ref[...] + BRANCH * mlp_sum[...]).astype(jnp.bfloat16)
    for i in range(1, line):
        out_arrival(i).wait_recv()
    total = out_land[0].astype(jnp.float32)
    for i in range(1, line):
        total = total + out_land[i].astype(jnp.float32)
    grad_out_ref[...] = total
    @pl.loop(1, 8)
    def _(i):
        qkv_copy(i, True).wait_recv()

    grad_qkv_ref[...] = qkv_land[...].astype(jnp.float32)
    at.wait_all(*gain_push, sent=False)
    gain_sum_ref[...] = jnp.sum(gain_land[...], axis=0)
    end()
    reduce[2]()
    for k in range(line):
        beside.end(k)
    at.wait_all(*row_push)
    pltpu.make_async_copy(grad_gate_up_ref, grad_gate_up_ref, row_sem.at[0]).wait()
    sum_qkv.end()

    @pl.loop(1, 8)
    def _(i):
        qkv_copy(i).wait_send()

    at.wait_all(*gain_push)
    for i in range(1, line):
        out_copy(i).wait_send()


def back(line, d_attn, tokens, mid, d_mid, qkv, attn_out, lse, gain, gain_term, lengths, normed, w_qkv, w_out, mlp_term, columns):
    blk, width = tokens.shape
    w_rows, cols = w_out.shape[1], w_qkv.shape[2]
    size, every = 8 * blk, 8 * line
    q_part = HEADS * HEAD_DIM // 8
    kv_part = (cols - q_part) // 2
    any_spec, vmem_spec = pl.BlockSpec(memory_space=pl.ANY), pl.BlockSpec(memory_space=pltpu.VMEM)
    bf16, f32, dma, out = jnp.bfloat16, jnp.float32, pltpu.SemaphoreType.DMA, jax.ShapeDtypeStruct
    return pl.pallas_call(
        functools.partial(back_kernel, line, blk, q_part, kv_part),
        out_shape=(out((blk, width), bf16), out((blk, width), f32), out((8, w_rows, cols), f32), out((w_rows, width), f32), out((8, 128), f32), out((w_rows, every * columns.shape[1]), f32)),
        in_specs=[any_spec] + [vmem_spec] * 8 + [pl.BlockSpec(memory_space=pltpu.SMEM)] + [any_spec] * 5,
        out_specs=(vmem_spec,) * 5 + (any_spec,),
        scratch_shapes=[
            pltpu.VMEM((size, width), bf16),
            pltpu.VMEM((size, width), bf16),
            pltpu.VMEM((4, blk, width), bf16),
            pltpu.VMEM((3 * blk, width), bf16),
            pltpu.VMEM((every, w_rows, cols), bf16),
            pltpu.VMEM((line, w_rows, width), bf16),
            pltpu.VMEM((size, width), bf16),
            pltpu.VMEM((size, q_part), bf16),
            pltpu.VMEM((size, cols), bf16),
            pltpu.VMEM((size, kv_part), f32),
            pltpu.VMEM((size, kv_part), f32),
            pltpu.VMEM((every * w_rows, cols), bf16),
            pltpu.VMEM((line, w_rows, width), bf16),
            pltpu.VMEM((8, w_rows, cols), bf16),
            pltpu.VMEM((line, w_rows, width), bf16),
            pltpu.VMEM((8, width), f32),
            pltpu.VMEM((every, 8, 128), f32),
            pltpu.VMEM((blk, width), f32),
            pltpu.VMEM((line * 4 * blk, width), bf16),
            pltpu.VMEM((line, 3 * blk, width), bf16),
            pltpu.VMEM((line + 1, blk, width), bf16),
            pltpu.VMEM((blk, width), f32),
            pltpu.VMEM((every, w_rows, columns.shape[1]), bf16),
            pltpu.VMEM(columns.shape, f32),
            pltpu.VMEM((line + 1, 8 * w_rows, cols), bf16),
            *[dma((n,)) for n in GATHER_SEMS + REDUCE_SEMS + (every,) * 4 + (line, line, 6)],
            *slice_reduce_sems(line),
            dma((every,)),
            dma((every,)),
            dma((1,)),
            dma((line,)),
            dma((line + 1,)),
        ],
        compiler_params=pltpu.CompilerParams(collective_id=2, has_side_effects=True, vmem_limit_bytes=63 * MIB),
    )(d_attn, tokens, mid, d_mid, qkv, attn_out, lse, gain, gain_term, lengths, normed, w_qkv, w_out, mlp_term, columns)


def split_heads(w, parts):
    rows = w.shape[0]
    q_width, kv_width = HEADS * HEAD_DIM, KV_HEADS * HEAD_DIM
    copies = max(1, parts // KV_HEADS)
    q = w[:, :q_width].reshape(rows, parts, q_width // parts)
    k = w[:, q_width : q_width + kv_width].reshape(rows, parts // copies, 1, -1)
    v = w[:, q_width + kv_width :].reshape(rows, parts // copies, 1, -1)
    k, v = (jnp.broadcast_to(a, (rows, parts // copies, copies, a.shape[3])).reshape(rows, parts, -1) for a in (k, v))
    return jnp.concatenate([q, k, v], axis=2)


def join_heads(grads, parts):
    rows = grads.shape[0]
    copies = max(1, parts // KV_HEADS)
    q_part = HEADS * HEAD_DIM // parts
    kv_part = (grads.shape[2] - q_part) // 2
    q = grads[:, :, :q_part].reshape(rows, -1)
    k, v = (
        jnp.sum(grads[:, :, at : at + kv_part].reshape(rows, parts // copies, copies, kv_part), axis=2).reshape(rows, -1)
        for at in (q_part, q_part + kv_part)
    )
    return jnp.concatenate([q, k, v], axis=1)


def per_device(n_ctx, n_shard, tokens, lengths, cotangent, w_qkv, w_out, w_gate_up, w_down, gain_attn, gain_mlp):
    count, width = tokens.shape[1:]
    n = n_ctx * n_shard
    w_rows = w_qkv.shape[0]
    ff_part = w_down.shape[0]
    q_part = HEADS * HEAD_DIM // n_ctx
    rows = tokens.reshape(count, width).astype(jnp.float32)
    grad_rows = cotangent.reshape(count, width).astype(jnp.float32)
    size = count * n_ctx
    positions = jnp.arange(size, dtype=jnp.int32)
    seg = segment_ids(positions, lengths[0])
    q_seg, k_seg = seg.reshape(size, 1), seg.reshape(1, size)

    gains = lax.all_gather(jnp.stack([gain_attn, gain_mlp]), EVERY, axis=1, tiled=True).astype(jnp.float32)
    gain_one, gain_two = gains[0], gains[1]

    qkv_cols = lax.all_to_all(split_heads(w_qkv, n_ctx), "ctx", split_axis=1, concat_axis=1, tiled=True)
    qkv_cols = qkv_cols.reshape(w_rows, n_ctx, -1).transpose(1, 0, 2)
    qkv_mine = lax.all_gather(qkv_cols, "shard", axis=1, tiled=True).reshape(width, -1)
    out_mine = lax.all_gather(w_out, "shard", axis=0, tiled=True)
    gate_up_mine = lax.all_to_all(w_gate_up.reshape(w_rows, 2, n, ff_part), EVERY, split_axis=2, concat_axis=0, tiled=True)
    gate_up_mine = gate_up_mine.reshape(width, 2 * ff_part)

    scale_one = rms_scale(rows)
    normed_one = lax.all_gather((rows * scale_one * gain_one).astype(jnp.bfloat16), "ctx", axis=0, tiled=True)
    projected = dot(normed_one, qkv_mine, ((1,), (0,))).astype(jnp.bfloat16)
    kv_part = (projected.shape[1] - q_part) // 2
    queries, keys, values = (
        projected[:, :q_part],
        projected[:, q_part : q_part + kv_part],
        projected[:, q_part + kv_part :],
    )
    attn_out, lse, tops = attend(queries, keys, values, q_seg, k_seg)
    out_term = dot(attn_out, out_mine, ((1,), (0,))).astype(jnp.bfloat16)
    attn_proj = lax.psum_scatter(out_term, "ctx", scatter_dimension=0, tiled=True)
    mid = rows + BRANCH * attn_proj.astype(jnp.float32)
    head_top = lax.all_gather(lax.pmax(tops, "shard"), "ctx", axis=1, tiled=True).reshape(HEADS)
    clip = CLIP_TARGET / jnp.maximum(head_top, CLIP_TARGET)

    scale_two = rms_scale(mid)
    d_mlp = lax.all_gather((BRANCH * grad_rows).astype(jnp.bfloat16), EVERY, axis=0, tiled=True)
    normed_two = lax.all_gather((mid * scale_two * gain_two).astype(jnp.bfloat16), EVERY, axis=0, tiled=True)
    gate_up = dot(normed_two, gate_up_mine, ((1,), (0,)))
    gate, up = gate_up[:, :ff_part], gate_up[:, ff_part:]
    sigma = jax.nn.sigmoid(gate)
    active = gate * sigma
    hidden = (active * up).astype(jnp.bfloat16)
    down_term = dot(hidden, w_down, ((1,), (0,))).astype(jnp.bfloat16)
    d_hidden = dot(d_mlp, w_down, ((1,), (1,)))
    d_gate = d_hidden * up * sigma * (1.0 + gate * (1.0 - sigma))
    d_up = d_hidden * active
    d_gate_up = jnp.concatenate([d_gate, d_up], axis=1).astype(jnp.bfloat16)
    normed_term = dot(d_gate_up, gate_up_mine, ((1,), (1,))).astype(jnp.bfloat16)
    grad_down = dot(hidden, d_mlp, ((0,), (0,)))
    gate_up_grad = dot(normed_two, d_gate_up, ((0,), (0,))).astype(jnp.bfloat16)
    mlp_proj = lax.psum_scatter(down_term, EVERY, scatter_dimension=0, tiled=True)
    mixed = (mid + BRANCH * mlp_proj.astype(jnp.float32)).astype(jnp.bfloat16).reshape(1, count, width)
    d_normed_two = lax.psum_scatter(normed_term, EVERY, scatter_dimension=0, tiled=True).astype(jnp.float32)
    grad_gate_up = lax.all_to_all(gate_up_grad.reshape(n * w_rows, 2, 1, ff_part), EVERY, split_axis=0, concat_axis=2, tiled=True)
    grad_gate_up = grad_gate_up.reshape(w_rows, 2 * n * ff_part).astype(jnp.float32)
    d_mid_norm, gain_two_term = norm_backward(d_normed_two, mid, scale_two, gain_two)
    d_mid = grad_rows + d_mid_norm

    d_attn = lax.all_gather((BRANCH * d_mid).astype(jnp.bfloat16), "ctx", axis=0, tiled=True)
    grad_out = lax.psum_scatter(dot(attn_out, d_attn, ((0,), (0,))), "shard", scatter_dimension=0, tiled=True)
    d_heads = dot(d_attn, out_mine, ((1,), (1,))).astype(jnp.bfloat16)
    d_q, d_k, d_v = attend_back(queries, keys, values, attn_out, d_heads, lse, q_seg, k_seg)
    d_qkv = jnp.concatenate([d_q, d_k, d_v], axis=1)
    qkv_term = dot(d_qkv, qkv_mine, ((1,), (1,))).astype(jnp.bfloat16)
    d_normed_one = lax.psum_scatter(qkv_term, "ctx", scatter_dimension=0, tiled=True).astype(jnp.float32)
    qkv_grad = dot(normed_one, d_qkv, ((0,), (0,))).reshape(n_ctx, n_shard * w_rows, -1)
    qkv_grad = lax.psum_scatter(qkv_grad, "shard", scatter_dimension=1, tiled=True)
    qkv_grad = lax.all_to_all(qkv_grad, "ctx", split_axis=0, concat_axis=0, tiled=True)
    grad_qkv = join_heads(qkv_grad.transpose(1, 0, 2), n_ctx)
    d_rows_norm, gain_one_term = norm_backward(d_normed_one, rows, scale_one, gain_one)
    grad_tokens = (d_mid + d_rows_norm).reshape(1, count, width)
    gain_terms = lax.psum_scatter(jnp.stack([gain_one_term, gain_two_term]), EVERY, scatter_dimension=1, tiled=True)
    return (mixed, grad_tokens, grad_qkv, grad_out, grad_gate_up, grad_down, gain_terms[0], gain_terms[1], clip)


def on_planes(n_shard, tokens, lengths, cotangent, w_qkv, w_out, w_gate_up, w_down, gain_attn, gain_mlp):
    count, width = tokens.shape[1:]
    w_rows = w_qkv.shape[0]
    rows = tokens.reshape(count, width)
    grad = cotangent.reshape(count, width)
    side = lax.rem(lax.axis_index("ctx") * n_shard + lax.axis_index("shard"), 2)

    gains = jnp.stack([gain_attn, gain_mlp])
    none = jnp.zeros_like(gains)
    gains = jnp.where(side == 0, jnp.concatenate([gains, none], axis=1), jnp.concatenate([none, gains], axis=1))
    gains = jnp.pad(gains, ((0, 14), (0, 0)))
    mid, normed_two, qkv, attn_out, lse, tops, gain, normed_one, qkv_mine, out_mine, d_mlp, gate_up_mine = front(
        n_shard, rows, grad, w_gate_up, gains, split_heads(w_qkv, 8).transpose(1, 0, 2), w_out, lengths
    )
    heads = HEADS // 8
    head_top = jnp.max(tops[:, 0, :heads].reshape(8, n_shard, heads), axis=1).reshape(HEADS)
    clip = CLIP_TARGET / jnp.maximum(head_top, CLIP_TARGET)

    mlp_term, d_mid, d_attn, gain_term, gate_up_grad, grad_down = mlp_exchange(
        n_shard, normed_two, d_mlp, gate_up_mine, w_down, mid, grad, gain
    )
    mixed, grad_tokens, qkv_grad, grad_out, gain_sum, grad_gate_up = back(
        n_shard, d_attn, rows, mid, d_mid, qkv, attn_out, lse, gain, gain_term, lengths, normed_one, qkv_mine, out_mine, mlp_term, gate_up_grad
    )
    grad_qkv = join_heads(qkv_grad.transpose(1, 0, 2), 8)
    gain_grads = jnp.where(side == 0, gain_sum[:2, :w_rows], gain_sum[:2, w_rows : 2 * w_rows])
    return (mixed.reshape(1, count, width), grad_tokens.reshape(1, count, width), grad_qkv, grad_out, grad_gate_up, grad_down, gain_grads[0], gain_grads[1], clip)


def solution(mesh):
    by_token, by_row = P("shard", "ctx", None), P(EVERY, None)
    n_ctx, n_shard = mesh.shape["ctx"], mesh.shape["shard"]
    program = functools.partial(on_planes, n_shard) if (n_ctx, n_shard) == (8, 4) else functools.partial(per_device, n_ctx, n_shard)
    return jax.shard_map(
        program,
        mesh=mesh,
        in_specs=(by_token, P("shard", None), by_token, by_row, by_row, by_row, by_row, P(EVERY), P(EVERY)),
        out_specs=(by_token, by_token, by_row, by_row, by_row, by_row, P(EVERY), P(EVERY), P()),
        check_vma=False,
    )
```

```python
import functools
import math

import jax
import jax.numpy as jnp
from jax import lax
from jax.experimental import pallas as pl
from jax.experimental.pallas import tpu as pltpu
from jax.sharding import PartitionSpec as P

HEADS = 32
KV_HEADS = 8
HEAD_DIM = 64


SCALE = 0.015625
BRANCH = 0.22
EPSILON = 1e-05
CLIP_TARGET = 4.0
NEGATIVE = -1e30
MIB = 1024 * 1024
EVERY = ("ctx", "shard")


def segment_ids(positions, lengths_row):
    bounds = jnp.cumsum(lengths_row)[:-1]
    return jnp.sum((positions[:, None] >= bounds[None, :]).astype(jnp.int32), axis=1)


def rms_scale(rows):
    return lax.rsqrt(jnp.mean(rows * rows, axis=-1, keepdims=True) + EPSILON)


def norm_backward(d_normed, rows, scale, gain):
    unit = rows * scale
    d_unit = d_normed * gain
    gain_term = jnp.sum(d_normed * unit, axis=0)
    d_rows = scale * (d_unit - unit * jnp.mean(d_unit * unit, axis=-1, keepdims=True))
    return (d_rows, gain_term)


def dot(left, right, dims):
    return lax.dot_general(left, right, ((dims[0], dims[1]), ((), ())), preferred_element_type=jnp.float32)


def segments(lengths_ref, positions):
    bound = jnp.int32(0)
    seg = jnp.zeros(positions.shape, jnp.int32)
    for i in range(lengths_ref.shape[1] - 1):
        bound = bound + lengths_ref[0, i]
        seg = seg + jnp.where(positions >= bound, 1, 0)
    return seg


def block_mask(lengths_ref, row0, rows, cols):
    q_seg = segments(lengths_ref, row0 + lax.broadcasted_iota(jnp.int32, (rows, 1), 0))
    return seen_mask(row0, rows, cols, q_seg, segments(lengths_ref, lax.broadcasted_iota(jnp.int32, (1, cols), 1)))


def seen_mask(row0, rows, cols, q_seg, k_seg):
    q_pos = row0 + lax.broadcasted_iota(jnp.int32, (rows, cols), 0)
    k_pos = lax.broadcasted_iota(jnp.int32, (rows, cols), 1)
    return (k_pos <= q_pos) & ((k_seg == 0) | (k_seg == q_seg))


def attend_kernel(heads, block, q_ref, k_ref, v_ref, q_seg_ref, k_seg_ref, o_ref, lse_ref, top_ref):
    size = q_ref.shape[0]
    tops = [jnp.full((1, 1), NEGATIVE, jnp.float32)] * heads
    for i in range(size // block):
        rows, cols = pl.ds(i * block, block), (i + 1) * block
        live = seen_mask(i * block, block, cols, q_seg_ref[rows, :], k_seg_ref[:, :cols])
        keys, values = k_ref[:cols, :], v_ref[:cols, :]
        for h in range(heads):
            span = slice(h * HEAD_DIM, (h + 1) * HEAD_DIM)
            scores = dot(q_ref[rows, span], keys, ((1,), (1,))) * SCALE
            scores = jnp.where(live, scores, NEGATIVE)
            peak = jnp.max(scores, axis=-1, keepdims=True)
            weights = jnp.exp(scores - peak)
            total = jnp.sum(weights, axis=-1, keepdims=True)
            out = dot(weights.astype(jnp.bfloat16), values, ((1,), (0,)))
            o_ref[rows, span] = (out / total).astype(jnp.bfloat16)
            lse_ref[rows, h : h + 1] = peak + jnp.log(total)
            tops[h] = jnp.maximum(tops[h], jnp.max(peak, axis=0, keepdims=True))
    for h in range(heads):
        top_ref[:, h : h + 1] = tops[h]


def attend(queries, keys, values, q_seg, k_seg):
    size, width = queries.shape
    heads = width // HEAD_DIM
    return pl.pallas_call(
        functools.partial(attend_kernel, heads, math.gcd(size, 256)),
        out_shape=(
            jax.ShapeDtypeStruct((size, width), jnp.bfloat16),
            jax.ShapeDtypeStruct((size, heads), jnp.float32),
            jax.ShapeDtypeStruct((1, heads), jnp.float32),
        ),
        compiler_params=pltpu.CompilerParams(vmem_limit_bytes=48 * MIB),
    )(queries, keys, values, q_seg, k_seg)


def attend_back_kernel(
    heads, block, q_ref, k_ref, v_ref, o_ref, do_ref, lse_ref, q_seg_ref, k_seg_ref, dq_ref, dk_ref, dv_ref, dk_sum, dv_sum
):
    size = q_ref.shape[0]
    dk_sum[...] = jnp.zeros_like(dk_sum)
    dv_sum[...] = jnp.zeros_like(dv_sum)
    for i in range(size // block):
        rows, cols = pl.ds(i * block, block), (i + 1) * block
        live = seen_mask(i * block, block, cols, q_seg_ref[rows, :], k_seg_ref[:, :cols])
        keys, values = k_ref[:cols, :], v_ref[:cols, :]
        for h in range(heads):
            span = slice(h * HEAD_DIM, (h + 1) * HEAD_DIM)
            queries, d_out = q_ref[rows, span], do_ref[rows, span]
            delta = jnp.sum(d_out.astype(jnp.float32) * o_ref[rows, span].astype(jnp.float32), axis=-1, keepdims=True)
            scores = dot(queries, keys, ((1,), (1,))) * SCALE
            probs = jnp.where(live, jnp.exp(scores - lse_ref[rows, h : h + 1]), 0.0)
            d_probs = dot(d_out, values, ((1,), (1,)))
            d_scores = (probs * (d_probs - delta)).astype(jnp.bfloat16)
            dq_ref[rows, span] = (dot(d_scores, keys, ((1,), (0,))) * SCALE).astype(jnp.bfloat16)
            dk_sum[:cols, :] += dot(d_scores, queries, ((0,), (0,)))
            dv_sum[:cols, :] += dot(probs.astype(jnp.bfloat16), d_out, ((0,), (0,)))
    dk_ref[...] = (dk_sum[...] * SCALE).astype(jnp.bfloat16)
    dv_ref[...] = dv_sum[...].astype(jnp.bfloat16)


def attend_back(queries, keys, values, out, d_out, lse, q_seg, k_seg):
    size, width = queries.shape
    heads = width // HEAD_DIM
    like_kv = jax.ShapeDtypeStruct((size, HEAD_DIM), jnp.bfloat16)
    return pl.pallas_call(
        functools.partial(attend_back_kernel, heads, math.gcd(size, 256)),
        out_shape=(jax.ShapeDtypeStruct((size, width), jnp.bfloat16), like_kv, like_kv),
        scratch_shapes=[pltpu.VMEM((size, HEAD_DIM), jnp.float32)] * 2,
        compiler_params=pltpu.CompilerParams(vmem_limit_bytes=48 * MIB),
    )(queries, keys, values, out, d_out, lse, q_seg, k_seg)


def remote(src, dst, send_sem, recv_sem, device):
    return pltpu.make_async_remote_copy(
        src_ref=src, dst_ref=dst, send_sem=send_sem, recv_sem=recv_sem, device_id=device, device_id_type=pl.DeviceIdType.MESH
    )


def greet(devices, extra):
    barrier = pltpu.get_barrier_semaphore()
    count = len(devices)
    for device in devices:
        pl.semaphore_signal(barrier, inc=1, device_id=device, device_id_type=pl.DeviceIdType.MESH)
    for condition, device in extra:

        @pl.when(condition)
        def _():
            pl.semaphore_signal(barrier, inc=1, device_id=device, device_id_type=pl.DeviceIdType.MESH)

        count = count + condition.astype(jnp.int32)
    pl.semaphore_wait(barrier, count)


def add_rows(target, sources, rows, keep=None, step=32):
    @pl.loop(0, rows // step)
    def _(i):
        part = pl.ds(pl.multiple_of(i * step, step), step)
        total = target[part, :].astype(jnp.float32)
        for source in sources:
            total = total + source[part, :].astype(jnp.float32)
        if keep is None:
            target[part, :] = total.astype(jnp.bfloat16)
        else:
            keep[part, :] = total


class Place:
    def __init__(self, line):
        self.line = line
        self.c, self.z = lax.axis_index("ctx"), lax.axis_index("shard")
        self.q, self.core = self.c // 2, self.c % 2
        self.me = self.c * line + self.z
        self.every = 8 * line
        self.cx, self.cy = (self.c + 2 - 4 * (self.q % 2), self.z), (self.c + 4 - 8 * (self.q // 2), self.z)
        self.sibling = (self.c + 1 - 2 * self.core, self.z)
        self.qx, self.qy, self.qd = self.q + 1 - 2 * (self.q % 2), self.q + 2 - 4 * (self.q // 2), 3 - self.q

    def source(self, k):
        if self.line == 1:
            return self.z * 0
        mirrored = self.z >= self.line // 2
        near = jnp.where(mirrored, self.line - 1 - self.z, self.z)
        turn = (k + 1) // 2
        both = near - turn if k % 2 == 1 else near + turn
        at = jnp.where(k <= 2 * near, both, k)
        return jnp.where(mirrored, self.line - 1 - at, at)

    def line_spread(self, copy, k):
        at = self.source(k)
        if k > 0:
            copy(at, 0).wait_recv()
        for way, condition in enumerate(self.line_ways(at)):

            @pl.when(condition)
            def _():
                copy(at, way).start()

    def line_sent(self, copy, k):
        at = self.source(k)
        for way, condition in enumerate(self.line_ways(at)):

            @pl.when(condition)
            def _():
                copy(at, way).wait_send()

    def line_ways(self, at):
        return ((at <= self.z) & (self.z < self.line - 1), (at >= self.z) & (self.z > 0))

    def peer(self, i):
        other = lax.rem(self.me + i, self.every)
        return other, (other // self.line, other % self.line)

    def greet_near(self):
        z, last = self.z, self.line - 1
        greet([self.cx, self.cy, self.sibling], [(z < last, (self.c, z + 1)), (z > 0, (self.c, z - 1))])

    def greet_all(self):
        barrier = pltpu.get_barrier_semaphore()

        @pl.loop(1, self.every)
        def _(i):
            pl.semaphore_signal(barrier, inc=1, device_id=self.peer(i)[1], device_id_type=pl.DeviceIdType.MESH)

        pl.semaphore_wait(barrier, self.every - 1)

    def push_all(self, source, target, send_sems, recv_sems, piece=0, pieces=1):
        @pl.loop(max(1, piece * self.every // pieces), (piece + 1) * self.every // pieces)
        def _(i):
            other, device = self.peer(i)
            remote(source(other), target(self.me), send_sems.at[other], recv_sems.at[self.me], device).start()

    def wait_all(self, source, target, send_sems, recv_sems, sent=True):
        @pl.loop(1, self.every)
        def _(i):
            other, device = self.peer(i)
            copy = remote(source(other), target(other), send_sems.at[other], recv_sems.at[other], device)
            if sent:
                copy.wait_send()
            else:
                copy.wait_recv()


class SliceGather:
    def __init__(self, place, rows, blk, sems):
        self.place, self.rows, self.half = place, rows, blk // 2
        self.z_send, self.z_recv, self.p_send, self.p_recv, self.f_send, self.f_recv = sems
        p, half = place, blk // 2
        self.ways = ((p.cx, p.qx, 0), (p.cy, p.qy, half), (p.cx, p.qx, half), (p.cy, p.qy, 0))
        self.turns = ((p.qx, 0, p.cy), (p.qy, half, p.cx))

    def line_copy(self, at, way):
        ref = self.rows(at, self.place.q, 0, 2 * self.half)
        return remote(ref, ref, self.z_send.at[at, way], self.z_recv.at[at], (self.place.c, self.place.z + 1 - 2 * way))

    def plane_copy(self, at, i, arriving=False):
        device, chip, first = self.ways[i]
        ref = self.rows(at, chip if arriving else self.place.q, first, self.half)
        return remote(ref, ref, self.p_send.at[at, i], self.p_recv.at[at, i], device)

    def onward_copy(self, at, i, arriving=False):
        chip, first, device = self.turns[i]
        ref = self.rows(at, self.place.qd if arriving else chip, first, self.half)
        return remote(ref, ref, self.f_send.at[at, i], self.f_recv.at[at, i], device)

    def a(self, k):
        self.place.line_spread(self.line_copy, k)
        for i in range(4):
            self.plane_copy(self.place.source(k), i).start()

    def b(self, k):
        at = self.place.source(k)
        for i in (0, 1):
            self.plane_copy(at, i, True).wait_recv()
            self.onward_copy(at, i).start()

    def c(self, k):
        at = self.place.source(k)
        for i in (2, 3):
            self.plane_copy(at, i, True).wait_recv()
        for i in (0, 1):
            self.onward_copy(at, i, True).wait_recv()
        for i in range(4):
            self.plane_copy(at, i).wait_send()
        for i in (0, 1):
            self.onward_copy(at, i).wait_send()
        self.place.line_sent(self.line_copy, k)


def slice_gather_sems(line):
    return [pltpu.SemaphoreType.DMA(shape) for shape in ((line, 2), (line,), (line, 4), (line, 4), (line, 2), (line, 2))]


class SliceReduce:
    def __init__(self, place, rows, blk, land, line_land, result, sems):
        self.place, self.rows, self.blk, self.half = place, rows, blk, blk // 2
        self.land, self.line_land, self.result = land, line_land, result
        self.r2_send, self.r2_recv, self.r3_send, self.r3_recv, self.r4_send, self.r4_recv = sems
        p, half = place, blk // 2
        self.seconds = ((0, p.cy), (half, p.cx))
        self.thirds = ((p.cx, p.qx, 0, 0), (p.cy, p.qy, half, blk + half), (p.cx, p.qx, half, half), (p.cy, p.qy, 0, blk))

    def landing(self, at, first, count):
        return self.land.at[at, pl.ds(first, count), :]

    def second(self, at, i):
        first, device = self.seconds[i]
        return remote(
            self.rows(at, self.place.qd, first, self.half), self.landing(at, 2 * self.blk + first, self.half), self.r2_send.at[at, i], self.r2_recv.at[at, i], device
        )

    def third(self, at, i):
        device, chip, first, lands = self.thirds[i]
        return remote(
            self.rows(at, chip, first, self.half), self.landing(at, lands, self.half), self.r3_send.at[at, i], self.r3_recv.at[at, i], device
        )

    def line_part(self, at, slot, part):
        rows = pl.ds(part * self.half, self.half)
        return self.rows(at, self.place.q, part * self.half, self.half), self.line_land.at[slot, rows, :]

    def line_copy(self, at, way, part):
        p = self.place
        slot = jnp.where((way == 1) & (at == p.z - 1), p.line, at)
        source, target = self.line_part(at, slot, part)
        return remote(source, target, self.r4_send.at[at, part], self.r4_recv.at[slot, part], (p.c, p.z + 1 - 2 * way))

    def line_arrival(self, at, slot, part):
        source, target = self.line_part(at, slot, part)
        return remote(source, target, self.r4_send.at[at, part], self.r4_recv.at[slot, part], self.place.sibling)

    def a(self, k):
        at = self.place.source(k)
        for i in (0, 1):
            self.second(at, i).start()
        for i in (2, 3):
            self.third(at, i).start()

    def b(self, k):
        at = self.place.source(k)
        for i in (0, 1):
            chip, first = self.thirds[i][1:3]
            self.second(at, i).wait_recv()
            add_rows(self.rows(at, chip, first, self.half), [self.landing(at, 2 * self.blk + first, self.half)], self.half)
            self.third(at, i).start()

    def c(self, k):
        p, blk = self.place, self.blk
        at = p.source(k)
        has_up, has_down = p.z < p.line - 1, p.z > 0
        for i in range(4):
            self.third(at, i).wait_recv()
        half = self.half
        joined = ((at > p.z) & has_down) | ((at < p.z) & has_up)
        for part in (0, 1):
            mine = self.rows(at, p.q, part * half, half)
            plane = [self.landing(at, part * half, half), self.landing(at, blk + part * half, half)]
            if k > 0:

                @pl.when(joined)
                def _():
                    self.line_arrival(at, at, part).wait_recv()
                    add_rows(mine, plane + [self.line_part(at, at, part)[1]], half)

                @pl.when(jnp.logical_not(joined))
                def _():
                    add_rows(mine, plane, half)

                for way, condition in enumerate((at > p.z, at < p.z)):

                    @pl.when(condition)
                    def _():
                        self.line_copy(at, way, part).start()

            else:
                result = self.result.at[pl.ds(part * half, half), :]
                add_rows(mine, plane, half, result)
                for condition, slot in ((has_down, at), (has_up, p.line)):

                    @pl.when(condition)
                    def _():
                        self.line_arrival(at, slot, part).wait_recv()
                        add_rows(result, [self.line_part(at, slot, part)[1]], half, result)

    def end(self, k):
        at = self.place.source(k)
        for i in (0, 1):
            self.second(at, i).wait_send()
        for i in range(4):
            self.third(at, i).wait_send()
        if k > 0:
            for part in (0, 1):
                self.line_copy(at, 0, part).wait_send()


class LineReduce:
    def __init__(self, place, block, land, rows, sems):
        self.place, self.block, self.land, self.rows = place, block, land, rows
        self.send, self.recv = sems

    def copy(self, at, way):
        p = self.place
        slot = jnp.where((way == 1) & (at == p.z - 1), p.line, at)
        return remote(self.block(at), self.land.at[slot], self.send.at[at], self.recv.at[slot], (p.c, p.z + 1 - 2 * way))

    def arrive(self, at, slot):
        p = self.place
        remote(self.block(at), self.land.at[slot], self.send.at[at], self.recv.at[slot], p.sibling).wait_recv()
        add_rows(self.block(at), [self.land.at[slot]], self.rows)

    def each(self, k, joined, after):
        p = self.place
        at = p.source(k)
        for way, toward, behind in ((0, at > p.z, p.z > 0), (1, at < p.z, p.z < p.line - 1)):

            @pl.when(toward & (behind if joined else jnp.logical_not(behind)))
            def _():
                after(at, way)

    def first(self):
        for k in range(self.place.line - 1, 0, -1):
            self.each(k, False, lambda at, way: self.copy(at, way).start())

    def join(self, k):
        def step(at, way):
            self.arrive(at, at)
            self.copy(at, way).start()

        self.each(k, True, step)

    def last(self):
        p = self.place
        for condition, slot in ((p.z > 0, p.z), (p.z < p.line - 1, p.line)):

            @pl.when(condition)
            def _():
                self.arrive(p.z, slot)

    def end(self):
        for k in range(1, self.place.line):
            self.copy(self.place.source(k), 0).wait_send()


def slice_reduce_sems(line):
    return [pltpu.SemaphoreType.DMA(shape) for shape in ((line, 2), (line, 2), (line, 4), (line, 4), (line, 2), (line + 1, 2))]


def slice_rows(ref, blk):
    def rows(at, chip, first, count):
        return ref.at[pl.ds(pl.multiple_of((at * 4 + chip) * blk + first, blk // 2), count), :]

    return rows


class ColumnSpread:
    def __init__(self, place, source, target, part, send_sems, recv_sems):
        self.place, self.source, self.target, self.part = place, source, target, part
        self.send_sems, self.recv_sems = send_sems, recv_sems

    def copies(self, other, slot):
        rows = self.source.shape[0]
        for j in (0, 1):
            columns = self.source.at[:, pl.ds(pl.multiple_of((j * self.place.every + other) * self.part, self.part), self.part)]
            yield j, columns, self.target.at[pl.ds(pl.multiple_of(slot * rows, rows), rows), pl.ds(j * self.part, self.part)]

    def start(self, piece, pieces):
        every = self.place.every

        @pl.loop(max(1, piece * every // pieces), (piece + 1) * every // pieces)
        def _(i):
            other, device = self.place.peer(i)
            for j, source, target in self.copies(other, self.place.me):
                remote(source, target, self.send_sems.at[j, other], self.recv_sems.at[j, self.place.me], device).start()

    def own(self, sems):
        return [pltpu.make_async_copy(source, target, sems[j]) for j, source, target in self.copies(self.place.me, self.place.me)]

    def wait(self):
        @pl.loop(1, self.place.every)
        def _(i):
            other, device = self.place.peer(i)
            for j, source, target in self.copies(other, other):
                copy = remote(source, target, self.send_sems.at[j, other], self.recv_sems.at[j, other], device)
                copy.wait_recv()
                copy.wait_send()


def mlp_kernel(
    line, blk, part, normed_ref, d_mlp_ref, gate_up_ref, down_ref, mid_ref, grad_ref, gain_ref,
    mlp_term_ref, d_mid_ref, d_attn_ref, gain_term_ref, gate_up_grad_ref, down_grad_ref,
    act, land, line_land, w_gu, w_down, acc_gu, acc_down, hid, d_gu, sib_gu, sib_down, d_normed,
    w_send, w_recv, g_send, g_recv, own_sem, out_sem, *sems,
):
    place = Place(line)
    core, sibling = place.core, place.sibling
    width = w_down.shape[1]
    slot_rows = 4 * blk
    rows = slice_rows(act.at[0], blk)
    gather = SliceGather(place, rows, blk, sems[:6])
    reduce = SliceReduce(place, rows, blk, land, line_land, d_normed, sems[6:])

    def slot_of(k):
        return pl.ds(pl.multiple_of(place.source(k) * slot_rows, slot_rows), slot_rows)

    own = pltpu.make_async_copy(normed_ref, rows(place.z, place.q, 0, blk), own_sem.at[0])
    d_mlp_in = pltpu.make_async_copy(d_mlp_ref, act.at[1], own_sem.at[1])
    mine = pl.ds(pl.multiple_of(core * 2 * part, 2 * part), 2 * part)
    theirs = pl.ds(pl.multiple_of((1 - core) * 2 * part, 2 * part), 2 * part)
    mine_rows = pl.ds(pl.multiple_of(core * part, part), part)
    their_rows = pl.ds(pl.multiple_of((1 - core) * part, part), part)

    own_weights = [
        pltpu.make_async_copy(gate_up_ref, w_gu.at[:, mine], own_sem.at[2]),
        pltpu.make_async_copy(down_ref, w_down.at[mine_rows, :], own_sem.at[3]),
    ]
    weights_to = [
        remote(gate_up_ref, w_gu.at[:, mine], w_send.at[0], w_recv.at[0], sibling),
        remote(down_ref, w_down.at[mine_rows, :], w_send.at[1], w_recv.at[1], sibling),
    ]
    weights_from = [
        remote(gate_up_ref, w_gu.at[:, theirs], w_send.at[0], w_recv.at[0], sibling),
        remote(down_ref, w_down.at[their_rows, :], w_send.at[1], w_recv.at[1], sibling),
    ]

    def compute(k):
        slot = slot_of(k)

        @pl.loop(0, 2)
        def _(j):
            span = pl.ds(pl.multiple_of(j * part, part), part)
            lower = pl.ds(pl.multiple_of(j * 2 * part, part), part)
            upper = pl.ds(pl.multiple_of(j * 2 * part + part, part), part)
            gate = dot(act[0, slot, :], w_gu[:, lower], ((1,), (0,)))
            above = dot(act[0, slot, :], w_gu[:, upper], ((1,), (0,)))
            d_hidden = dot(act[1, slot, :], w_down[span, :], ((1,), (1,)))
            sigma = jax.nn.sigmoid(gate)
            active = gate * sigma
            hid[:, span] = (active * above).astype(jnp.bfloat16)
            d_gu[:, lower] = (d_hidden * above * sigma * (1.0 + gate * (1.0 - sigma))).astype(jnp.bfloat16)
            d_gu[:, upper] = (d_hidden * active).astype(jnp.bfloat16)

        @pl.loop(0, width // 256)
        def _(j):
            span = pl.ds(pl.multiple_of(j * 256, 256), 256)
            down_term = dot(hid[...], act[1, slot, span], ((0,), (0,)))
            gate_up_term = dot(act[0, slot, span], d_gu[...], ((0,), (0,)))
            if k > 0:
                down_term = down_term + acc_down[:, span]
                gate_up_term = gate_up_term + acc_gu[span, :]
            acc_down[:, span] = down_term
            acc_gu[span, :] = gate_up_term
            act[1, slot, span] = dot(hid[...], w_down[:, span], ((1,), (0,))).astype(jnp.bfloat16)
            act[0, slot, span] = dot(d_gu[...], w_gu[span, :], ((1,), (1,))).astype(jnp.bfloat16)

    def term_out(k):
        return pltpu.make_async_copy(act.at[1, slot_of(k), :], mlp_term_ref.at[slot_of(k), :], out_sem.at[2 + k])

    half_gu, whole_gu = pl.ds(0, 2 * part), pl.ds(2 * part, 2 * part)
    grad_copies = [
        remote(w_gu.at[:, half_gu], sib_gu, g_send.at[0], g_recv.at[0], sibling),
        remote(w_down.at[:part, :], sib_down, g_send.at[1], g_recv.at[1], sibling),
    ]
    down_out = pltpu.make_async_copy(acc_down.at[mine_rows, :], down_grad_ref, out_sem.at[0])

    def exchange_grads():
        @pl.loop(0, width // 256)
        def _(j):
            span = pl.ds(pl.multiple_of(j * 256, 256), 256)
            w_gu[span, half_gu] = acc_gu[span, theirs].astype(jnp.bfloat16)

        w_down[:part, :] = acc_down[their_rows, :].astype(jnp.bfloat16)
        for copy in grad_copies:
            copy.start()

    columns_out = pltpu.make_async_copy(w_gu.at[:, whole_gu], gate_up_grad_ref, out_sem.at[1])

    def finish_grads():
        for copy in grad_copies:
            copy.wait_recv()

        @pl.loop(0, width // 256)
        def _(j):
            span = pl.ds(pl.multiple_of(j * 256, 256), 256)
            w_gu[span, whole_gu] = (acc_gu[span, mine] + sib_gu[span, :].astype(jnp.float32)).astype(jnp.bfloat16)

        columns_out.start()
        acc_down[mine_rows, :] = acc_down[mine_rows, :] + sib_down[...].astype(jnp.float32)
        down_out.start()

    for copy in [own, d_mlp_in] + own_weights:
        copy.start()
    place.greet_near()
    own.wait()
    gather.a(0)
    for copy in weights_to:
        copy.start()
    gather.a(1)
    gather.b(0)
    gather.a(2)
    gather.b(1)
    for copy in [d_mlp_in] + own_weights:
        copy.wait()
    for copy in weights_from:
        copy.wait_recv()
    for copy in weights_to:
        copy.wait_send()
    gather.a(3)
    gather.b(2)
    gather.c(0)
    compute(0)
    term_out(0).start()
    gather.b(3)
    gather.c(1)
    compute(1)
    term_out(1).start()
    reduce.a(1)
    gather.c(2)
    compute(2)
    term_out(2).start()
    reduce.a(2)
    gather.c(3)
    compute(3)
    term_out(3).start()
    reduce.a(3)
    exchange_grads()
    reduce.b(3)
    reduce.b(2)
    finish_grads()
    reduce.a(0)
    reduce.c(3)
    reduce.b(1)
    reduce.c(2)
    reduce.b(0)
    reduce.c(1)
    reduce.c(0)
    backwards = range(line - 1, -1, -1)

    gain_term_ref[...] = jnp.zeros_like(gain_term_ref)

    @pl.loop(0, blk // 32)
    def _(i):
        part = pl.ds(pl.multiple_of(i * 32, 32), 32)
        mid = mid_ref[part, :]
        d_rows, gain_term = norm_backward(d_normed[part, :], mid, rms_scale(mid), gain_ref[1:2, :])
        d_mid = grad_ref[part, :].astype(jnp.float32) + d_rows
        d_mid_ref[part, :] = d_mid
        d_attn_ref[part, :] = (BRANCH * d_mid).astype(jnp.bfloat16)
        gain_term_ref[0:1, :] += gain_term.reshape(1, width)

    for k in backwards:
        reduce.end(k)
        term_out(k).wait()
    for copy in grad_copies:
        copy.wait_send()
    down_out.wait()
    columns_out.wait()


def mlp_exchange(line, normed, d_mlp, gate_up, down, mid, grad, gain):
    blk, width = normed.shape
    part = down.shape[0]
    any_spec, vmem_spec = pl.BlockSpec(memory_space=pl.ANY), pl.BlockSpec(memory_space=pltpu.VMEM)
    bf16, f32, dma = jnp.bfloat16, jnp.float32, pltpu.SemaphoreType.DMA
    return pl.pallas_call(
        functools.partial(mlp_kernel, line, blk, part),
        out_shape=(
            jax.ShapeDtypeStruct(d_mlp.shape, bf16),
            jax.ShapeDtypeStruct((blk, width), f32),
            jax.ShapeDtypeStruct((blk, width), bf16),
            jax.ShapeDtypeStruct((8, width), f32),
            jax.ShapeDtypeStruct(gate_up.shape, bf16),
            jax.ShapeDtypeStruct((part, width), f32),
        ),
        in_specs=[any_spec] * 4 + [vmem_spec] * 3,
        out_specs=(any_spec, vmem_spec, vmem_spec, vmem_spec, any_spec, any_spec),
        scratch_shapes=[
            pltpu.VMEM((2, line * 4 * blk, width), bf16),
            pltpu.VMEM((line, 3 * blk, width), bf16),
            pltpu.VMEM((line + 1, blk, width), bf16),
            pltpu.VMEM((width, 4 * part), bf16),
            pltpu.VMEM((2 * part, width), bf16),
            pltpu.VMEM((width, 4 * part), f32),
            pltpu.VMEM((2 * part, width), f32),
            pltpu.VMEM((4 * blk, 2 * part), bf16),
            pltpu.VMEM((4 * blk, 4 * part), bf16),
            pltpu.VMEM((width, 2 * part), bf16),
            pltpu.VMEM((part, width), bf16),
            pltpu.VMEM((blk, width), f32),
            dma((2,)),
            dma((2,)),
            dma((2,)),
            dma((2,)),
            dma((5,)),
            dma((2 + line,)),
            *slice_gather_sems(line),
            *slice_reduce_sems(line),
        ],
        compiler_params=pltpu.CompilerParams(collective_id=0, has_side_effects=True, vmem_limit_bytes=63 * MIB),
    )(normed, d_mlp, gate_up, down, mid, grad, gain)


def plane_gather(at, buf, blk, sems):
    p_send, p_recv, f_send, f_recv, s_send, s_recv = sems
    half = blk // 2

    def rows(chip, core, first=0, count=half):
        return buf.at[pl.ds(pl.multiple_of((2 * chip + core) * blk + first, half), count), :]

    def same(ref, send, recv, device):
        return remote(ref, ref, send, recv, device)

    way = ((at.cx, at.qx, 0), (at.cy, at.qy, half), (at.cx, at.qx, half), (at.cy, at.qy, 0))

    def sent(i):
        return same(rows(at.q, at.core, way[i][2]), p_send.at[i], p_recv.at[i], way[i][0])

    def arriving(i):
        return same(rows(way[i][1], at.core, way[i][2]), p_send.at[i], p_recv.at[i], way[i][0])

    def onward(i):
        chip, first, device = ((at.qx, 0, at.cy), (at.qy, half, at.cx))[i]
        return same(rows(chip, at.core, first), f_send.at[i], f_recv.at[i], device)

    def passed(i):
        first, device = ((0, at.cy), (half, at.cx))[i]
        return same(rows(at.qd, at.core, first), f_send.at[i], f_recv.at[i], device)

    def across(i, core):
        if i == 0:
            ref = rows(at.q, core, 0, blk)
        elif i < 5:
            ref = rows(way[i - 1][1], core, way[i - 1][2])
        else:
            ref = rows(at.qd, core, (i - 5) * half)
        return same(ref, s_send.at[i], s_recv.at[i], at.sibling)

    def start():
        for i in range(4):
            sent(i).start()
        across(0, at.core).start()

    def turn():
        for i in (0, 1):
            arriving(i).wait_recv()
            onward(i).start()
            across(i + 1, at.core).start()

    def rest():
        for i in (2, 3):
            arriving(i).wait_recv()
            across(i + 1, at.core).start()
        for i in (0, 1):
            passed(i).wait_recv()
            across(i + 5, at.core).start()

    def whole():
        for i in range(7):
            across(i, 1 - at.core).wait_recv()

    def end():
        for i in range(4):
            sent(i).wait_send()
        for i in (0, 1):
            onward(i).wait_send()
        for i in range(7):
            across(i, at.core).wait_send()

    return start, turn, rest, whole, end


GATHER_SEMS = (4, 4, 2, 2, 7, 7)
REDUCE_SEMS = (4, 4, 2, 2, 4, 4)


def plane_reduce(at, term, core_land, land, blk, sems):
    s_send, s_recv, r2_send, r2_recv, r3_send, r3_recv = sems
    half = blk // 2
    chips = (at.qd, at.qx, at.qy, at.q)

    def rows(chip, core, first=0, count=half):
        return term.at[pl.ds(pl.multiple_of((2 * chip + core) * blk + first, half), count), :]

    def landed(first, count):
        return land.at[pl.ds(first, count), :]

    def across(i):
        return remote(rows(chips[i], 1 - at.core, 0, blk), core_land.at[i], s_send.at[i], s_recv.at[i], at.sibling)

    def second(i):
        first, device = ((0, at.cy), (half, at.cx))[i]
        return remote(rows(at.qd, at.core, first), landed(2 * blk + first, half), r2_send.at[i], r2_recv.at[i], device)

    def third(i):
        device, chip, first, lands = (
            (at.cx, at.qx, 0, 0), (at.cy, at.qy, half, blk + half), (at.cx, at.qx, half, half), (at.cy, at.qy, 0, blk)
        )[i]
        return remote(rows(chip, at.core, first), landed(lands, half), r3_send.at[i], r3_recv.at[i], device)

    def add_core(i):
        across(i).wait_recv()
        add_rows(rows(chips[i], at.core, 0, blk), [core_land.at[i]], blk)

    def give(i):
        across(i).start()

    def take(result):
        add_core(0)
        second(0).start()
        second(1).start()
        add_core(1)
        third(2).start()
        add_core(2)
        third(3).start()
        for i, (chip, first) in enumerate(((at.qx, 0), (at.qy, half))):
            second(i).wait_recv()
            add_rows(rows(chip, at.core, first), [landed(2 * blk + first, half)], half)
            third(i).start()
        add_core(3)
        for i in range(4):
            third(i).wait_recv()
        add_rows(rows(at.q, at.core, 0, blk), [landed(0, blk), landed(blk, blk)], blk, result)

    def end():
        for i in range(4):
            across(i).wait_send()
            third(i).wait_send()
        for i in (0, 1):
            second(i).wait_send()

    return give, take, end


def front_kernel(
    line, blk, q_part, kv_part,
    tokens_ref, grad_ref, w_gate_up_ref, gains_ref, w_qkv_ref, w_out_ref, lengths_ref,
    mid_ref, normed_two_ref, qkv_ref, attn_ref, lse_ref, tops_ref, gain_ref, normed_ref, w_qkv_all_ref, w_out_all_ref, d_mlp_all_ref, gate_up_ref,
    buf, term, core_land, land, w_qkv, w_line, w_out, gain_land, top_land, proj, d_mlp,
    *sems,
):
    at = Place(line)
    gather = plane_gather(at, buf, blk, sems[:6])
    reduce = plane_reduce(at, term, core_land, land, blk, sems[6:12])
    line_send, line_recv, qkv_send, qkv_recv, gain_send, gain_recv, top_send, top_recv, out_send, out_recv, own_sem, write_sem = sems[12:24]
    d_mlp_rows = slice_rows(d_mlp_all_ref, blk)
    beside = SliceGather(at, d_mlp_rows, blk, sems[24:30])
    spread = ColumnSpread(at, w_gate_up_ref, gate_up_ref, gate_up_ref.shape[1] // 2, *sems[30:])
    w_rows, width = w_out_ref.shape
    size = 8 * blk
    mine = pl.ds(pl.multiple_of(at.c * blk, blk), blk)

    own = [
        pltpu.make_async_copy(tokens_ref, buf.at[mine, :], own_sem.at[0]),
        pltpu.make_async_copy(gains_ref, gain_land.at[at.me], own_sem.at[1]),
        pltpu.make_async_copy(w_qkv_ref, w_line.at[at.z], own_sem.at[2]),
        pltpu.make_async_copy(w_out_ref, w_out.at[at.z], own_sem.at[3]),
        pltpu.make_async_copy(d_mlp, d_mlp_rows(at.z, at.q, 0, blk), own_sem.at[4]),
        *spread.own([own_sem.at[5], own_sem.at[6]]),
    ]
    for copy in own[:4] + own[5:]:
        copy.start()
    d_mlp[...] = (BRANCH * grad_ref[...].astype(jnp.float32)).astype(jnp.bfloat16)
    own[4].start()
    at.greet_all()
    gain_push = (lambda other: gains_ref, lambda slot: gain_land.at[slot], gain_send, gain_recv)
    top_push = (lambda other: top_land.at[at.me], lambda slot: top_land.at[slot], top_send, top_recv)

    def qkv_line(place, way):
        return remote(w_line.at[place], w_line.at[place], line_send.at[place, way], line_recv.at[place], (at.c, at.z + 1 - 2 * way))

    def out_line(place, way):
        return remote(w_out.at[place], w_out.at[place], out_send.at[place, way], out_recv.at[place], (at.c, at.z + 1 - 2 * way))

    def qkv_copy(i, place, arriving=False):
        other = lax.rem(at.c + i, 8)
        slot = (other if arriving else at.c) * line + place
        return remote(w_line.at[place, other], w_qkv.at[slot], qkv_send.at[place, other], qkv_recv.at[slot], (other, at.z))

    def qkv_step(k):
        at.line_spread(qkv_line, k)

        @pl.loop(1, 8)
        def _(i):
            qkv_copy(i, at.source(k)).start()

        w_qkv[at.c * line + at.source(k)] = w_line[at.source(k), at.c]

    inner = (at.z > 0) & (at.z < line - 1)
    outer = jnp.logical_not(inner)
    start, turn, rest, whole, end = gather
    own[0].wait()
    start()
    own[2].wait()
    qkv_step(0)
    at.push_all(*gain_push)
    turn()
    qkv_step(1)
    own[4].wait()
    beside.a(0)
    rest()
    for k in range(2, line - 1):
        qkv_step(k)
    own[1].wait()
    at.wait_all(*gain_push, sent=False)
    for i in range(at.every // 2):
        pair = gain_land[2 * i].astype(jnp.float32) + gain_land[2 * i + 1].astype(jnp.float32)
        gain_ref[:, i * 128 : (i + 1) * 128] = pair[:8, :]
    spread.start(0, 4)
    whole()
    end()
    at.wait_all(*gain_push)

    @pl.loop(0, size // 32)
    def _(i):
        part = pl.ds(pl.multiple_of(i * 32, 32), 32)
        rows = buf[part, :].astype(jnp.float32)
        buf[part, :] = (rows * rms_scale(rows) * gain_ref[0:1, :]).astype(jnp.bfloat16)

    writes = [
        pltpu.make_async_copy(buf, normed_ref, write_sem.at[0]),
        pltpu.make_async_copy(w_qkv, w_qkv_all_ref, write_sem.at[1]),
        pltpu.make_async_copy(w_out, w_out_all_ref, write_sem.at[2]),
    ]
    writes[0].start()
    qkv_step(line - 1)
    own[3].wait()
    at.line_spread(out_line, 0)
    beside.b(0)
    beside.a(1)
    pl.when(inner)(lambda: beside.a(2))
    spread.start(1, 4)
    for k in range(line):

        @pl.loop(1, 8)
        def _(i):
            qkv_copy(i, at.source(k), True).wait_recv()

    writes[1].start()

    @pl.loop(0, size // 256)
    def _(i):
        part = pl.ds(pl.multiple_of(i * 256, 256), 256)
        qkv_ref[part, :] = dot(buf[part, :], w_qkv[...].reshape(width, q_part + 2 * kv_part), ((1,), (0,))).astype(jnp.bfloat16)

    at.line_spread(out_line, 1)
    beside.b(1)
    pl.when(outer)(lambda: beside.a(2))
    pl.when(inner)(lambda: beside.a(3))
    spread.start(2, 4)
    heads = q_part // HEAD_DIM
    block = math.gcd(size, 256)
    tops = [jnp.full((1, 1), NEGATIVE, jnp.float32)] * heads
    for i in range(size // block):
        if i > 0 and i + 1 < line:
            at.line_spread(out_line, i + 1)
        if i == 2:
            beside.b(2)
        rows, cols = pl.ds(i * block, block), (i + 1) * block
        live = block_mask(lengths_ref, i * block, block, cols)
        keys, values = qkv_ref[:cols, q_part : q_part + kv_part], qkv_ref[:cols, q_part + kv_part :]
        for h in range(heads):
            span = slice(h * HEAD_DIM, (h + 1) * HEAD_DIM)
            scores = dot(qkv_ref[rows, span], keys, ((1,), (1,))) * SCALE
            scores = jnp.where(live, scores, NEGATIVE)
            peak = jnp.max(scores, axis=-1, keepdims=True)
            weights = jnp.exp(scores - peak)
            total = jnp.sum(weights, axis=-1, keepdims=True)
            out = dot(weights.astype(jnp.bfloat16), values, ((1,), (0,)))
            attn_ref[rows, span] = (out / total).astype(jnp.bfloat16)
            lse_ref[rows, h : h + 1] = peak + jnp.log(total)
            tops[h] = jnp.maximum(tops[h], jnp.max(peak, axis=0, keepdims=True))
    lanes = lax.broadcasted_iota(jnp.int32, (8, 128), 1)
    tile = jnp.full((8, 128), NEGATIVE, jnp.float32)
    for h in range(heads):
        tile = jnp.where(lanes == h, tops[h], tile)
    top_land[at.me] = tile
    at.push_all(*top_push)

    for k in range(size // block + 1, line):
        at.line_spread(out_line, k)
    pl.when(outer)(lambda: beside.a(3))
    pl.when(inner)(lambda: beside.b(3))
    spread.start(3, 4)
    writes[2].start()
    for i, chip in enumerate((at.qd, at.qx, at.qy, at.q)):
        for core in (1 - at.core, at.core):
            part = pl.ds(pl.multiple_of((2 * chip + core) * blk, blk), blk)

            @pl.loop(0, width // 512)
            def _(j):
                span = pl.ds(pl.multiple_of(j * 512, 512), 512)
                matrix = w_out[:, :, span].reshape(line * w_rows, 512)
                term[part, span] = dot(attn_ref[part, :], matrix, ((1,), (0,))).astype(jnp.bfloat16)

        reduce[0](i)
    reduce[1](proj)
    pl.when(outer)(lambda: beside.b(3))

    own_again = pltpu.make_async_copy(tokens_ref, land.at[pl.ds(0, blk), :], own_sem.at[0])
    own_again.start()
    own_again.wait()

    @pl.loop(0, blk // 32)
    def _(i):
        part = pl.ds(pl.multiple_of(i * 32, 32), 32)
        rows = land[part, :].astype(jnp.float32) + BRANCH * proj[part, :]
        mid_ref[part, :] = rows
        normed_two_ref[part, :] = (rows * rms_scale(rows) * gain_ref[1:2, :]).astype(jnp.bfloat16)

    at.wait_all(*top_push, sent=False)
    tops_ref[...] = top_land[...]
    reduce[2]()
    at.wait_all(*top_push)
    for k in range(line):
        at.line_sent(qkv_line, k)
        at.line_sent(out_line, k)

        @pl.loop(1, 8)
        def _(i):
            qkv_copy(i, at.source(k)).wait_send()

    for k in range(line):
        beside.c(k)
    spread.wait()
    for copy in own[5:]:
        copy.wait()
    for copy in writes:
        copy.wait()


def front(line, tokens, grad, w_gate_up, gains, w_qkv, w_out, lengths):
    blk, width = tokens.shape
    w_rows, cols = w_out.shape[0], w_qkv.shape[2]
    size, every = 8 * blk, 8 * line
    q_part = HEADS * HEAD_DIM // 8
    kv_part = (cols - q_part) // 2
    heads = q_part // HEAD_DIM
    any_spec, vmem_spec = pl.BlockSpec(memory_space=pl.ANY), pl.BlockSpec(memory_space=pltpu.VMEM)
    bf16, f32, dma, out = jnp.bfloat16, jnp.float32, pltpu.SemaphoreType.DMA, jax.ShapeDtypeStruct
    return pl.pallas_call(
        functools.partial(front_kernel, line, blk, q_part, kv_part),
        out_shape=(
            out((blk, width), f32),
            out((blk, width), bf16),
            out((size, cols), bf16),
            out((size, q_part), bf16),
            out((size, heads), f32),
            out((every, 8, 128), f32),
            out((8, width), f32),
            out((size, width), bf16),
            out((every, w_rows, cols), bf16),
            out((line, w_rows, width), bf16),
            out((line * 4 * blk, width), bf16),
            out((width, w_gate_up.shape[1] // every), bf16),
        ),
        in_specs=[any_spec, vmem_spec] + [any_spec] * 4 + [pl.BlockSpec(memory_space=pltpu.SMEM)],
        out_specs=(vmem_spec,) * 7 + (any_spec,) * 5,
        scratch_shapes=[
            pltpu.VMEM((size, width), bf16),
            pltpu.VMEM((size, width), bf16),
            pltpu.VMEM((4, blk, width), bf16),
            pltpu.VMEM((3 * blk, width), bf16),
            pltpu.VMEM((every, w_rows, cols), bf16),
            pltpu.VMEM((line, 8, w_rows, cols), bf16),
            pltpu.VMEM((line, w_rows, width), bf16),
            pltpu.VMEM((every, 16, 128), bf16),
            pltpu.VMEM((every, 8, 128), f32),
            pltpu.VMEM((blk, width), f32),
            pltpu.VMEM((blk, width), bf16),
            *[dma((n,)) for n in GATHER_SEMS + REDUCE_SEMS],
            dma((line, 2)),
            dma((line,)),
            dma((line, 8)),
            *[dma((every,))] * 5,
            dma((line, 2)),
            dma((line,)),
            dma((7,)),
            dma((3,)),
            *slice_gather_sems(line),
            dma((2, every)),
            dma((2, every)),
        ],
        compiler_params=pltpu.CompilerParams(collective_id=1, has_side_effects=True, vmem_limit_bytes=60 * MIB),
    )(tokens, grad, w_gate_up, gains, w_qkv, w_out, lengths)


def back_kernel(
    line, blk, q_part, kv_part,
    d_attn_ref, tokens_ref, mid_ref, d_mid_ref, qkv_ref, attn_ref, lse_ref, gain_ref, gain_term_ref, lengths_ref, normed_ref, w_qkv_ref, w_out_ref, mlp_term_ref, columns_ref,
    mixed_ref, grad_tokens_ref, grad_qkv_ref, grad_out_ref, gain_sum_ref, grad_gate_up_ref,
    buf, term, core_land, land, w_qkv, w_out, normed, d_heads, d_qkv, dk_sum, dv_sum, stage_qkv, stage_out, qkv_land, out_land, gain_stage, gain_land, d_normed, mlp_term, mlp_land, mlp_line_land, mlp_sum, row_land, row_stage, qkv_line_land,
    *sems,
):
    at = Place(line)
    gather = plane_gather(at, buf, blk, sems[:6])
    reduce = plane_reduce(at, term, core_land, land, blk, sems[6:12])
    qkv_send, qkv_recv, gain_send, gain_recv, out_send, out_recv, own_sem = sems[12:19]
    beside = SliceReduce(at, slice_rows(mlp_term, blk), blk, mlp_land, mlp_line_land, mlp_sum, sems[19:25])
    row_send, row_recv, row_sem = sems[25:28]
    w_cols = w_qkv.shape[1]
    part_ff = columns_ref.shape[1] // 2

    def column_rows(other):
        return columns_ref.at[pl.ds(pl.multiple_of(other * w_cols, w_cols), w_cols), :]

    row_push = (column_rows, lambda slot: row_land.at[slot], row_send, row_recv)
    width = buf.shape[1]
    w_rows = w_out.shape[1]
    size = 8 * blk
    mine = pl.ds(pl.multiple_of(at.c * blk, blk), blk)
    own = [
        pltpu.make_async_copy(d_attn_ref, buf.at[mine, :], own_sem.at[0]),
        pltpu.make_async_copy(w_out_ref, w_out, own_sem.at[1]),
        pltpu.make_async_copy(w_qkv_ref, w_qkv, own_sem.at[2]),
        pltpu.make_async_copy(normed_ref, normed, own_sem.at[3]),
        pltpu.make_async_copy(mlp_term_ref, mlp_term, own_sem.at[4]),
        pltpu.make_async_copy(column_rows(at.me), row_land.at[at.me], own_sem.at[5]),
    ]
    for copy in own:
        copy.start()
    at.greet_all()
    own[0].wait()
    start, turn, rest, whole, end = gather
    start()
    turn()
    rest()
    at.push_all(*row_push)
    for copy in own[1:]:
        copy.wait()
    beside.a(line - 1)
    whole()

    @pl.loop(0, size // 256)
    def _(i):
        part = pl.ds(pl.multiple_of(i * 256, 256), 256)
        d_heads[part, :] = dot(buf[part, :], w_out[...].reshape(line * w_rows, width), ((1,), (1,))).astype(jnp.bfloat16)

    if line > 1:
        beside.a(line - 2)

    @pl.loop(0, width // 256)
    def _(i):
        span = pl.ds(pl.multiple_of(i * 256, 256), 256)
        stage_out[:, :, span] = dot(attn_ref[...], buf[:, span], ((0,), (0,))).astype(jnp.bfloat16).reshape(line, w_rows, 256)

    def out_copy(i):
        z = lax.rem(at.z + i, line)
        return remote(stage_out.at[z], out_land.at[at.z], out_send.at[z], out_recv.at[at.z], (at.c, z))

    def out_arrival(i):
        z = lax.rem(at.z + i, line)
        return remote(stage_out.at[z], out_land.at[z], out_send.at[z], out_recv.at[z], (at.c, z))

    for i in range(1, line):
        out_copy(i).start()

    heads = q_part // HEAD_DIM
    block = math.gcd(size, 256)
    dk_sum[...] = jnp.zeros_like(dk_sum)
    dv_sum[...] = jnp.zeros_like(dv_sum)
    for i in range(size // block):
        rows, cols = pl.ds(i * block, block), (i + 1) * block
        live = block_mask(lengths_ref, i * block, block, cols)
        keys, values = qkv_ref[:cols, q_part : q_part + kv_part], qkv_ref[:cols, q_part + kv_part :]
        for h in range(heads):
            span = slice(h * HEAD_DIM, (h + 1) * HEAD_DIM)
            queries, d_out = qkv_ref[rows, span], d_heads[rows, span]
            delta = jnp.sum(d_out.astype(jnp.float32) * attn_ref[rows, span].astype(jnp.float32), axis=-1, keepdims=True)
            scores = dot(queries, keys, ((1,), (1,))) * SCALE
            probs = jnp.where(live, jnp.exp(scores - lse_ref[rows, h : h + 1]), 0.0)
            d_probs = dot(d_out, values, ((1,), (1,)))
            d_scores = (probs * (d_probs - delta)).astype(jnp.bfloat16)
            d_qkv[rows, span] = (dot(d_scores, keys, ((1,), (0,))) * SCALE).astype(jnp.bfloat16)
            dk_sum[:cols, :] += dot(d_scores, queries, ((0,), (0,)))
            dv_sum[:cols, :] += dot(probs.astype(jnp.bfloat16), d_out, ((0,), (0,)))
    d_qkv[:, q_part : q_part + kv_part] = (dk_sum[...] * SCALE).astype(jnp.bfloat16)
    d_qkv[:, q_part + kv_part :] = dv_sum[...].astype(jnp.bfloat16)
    beside.b(line - 1)
    for k in range(line - 3, 0, -1):
        beside.a(k)

    for i, chip in enumerate((at.qd, at.qx, at.qy, at.q)):
        for core in (1 - at.core, at.core):
            part = pl.ds(pl.multiple_of((2 * chip + core) * blk, blk), blk)

            @pl.loop(0, width // 512)
            def _(j):
                span = pl.ds(pl.multiple_of(j * 512, 512), 512)
                matrix = w_qkv[pl.ds(pl.multiple_of(j * (512 // w_rows), 512 // w_rows), 512 // w_rows)].reshape(512, q_part + 2 * kv_part)
                term[part, span] = dot(d_qkv[part, :], matrix, ((1,), (1,))).astype(jnp.bfloat16)

        reduce[0](i)

    chunk = line * w_cols

    @pl.loop(0, 8)
    def _(i):
        grads = dot(normed[:, pl.ds(pl.multiple_of(i * chunk, chunk), chunk)], d_qkv[...], ((0,), (0,))).astype(jnp.bfloat16)
        for place in range(line):
            stage_qkv[pl.ds(pl.multiple_of((place * 8 + i) * w_cols, w_cols), w_cols), :] = grads[place * w_cols : (place + 1) * w_cols, :]

    def qkv_block(place):
        return stage_qkv.at[pl.ds(pl.multiple_of(place * 8 * w_cols, w_cols), 8 * w_cols), :]

    def qkv_rows(i):
        return stage_qkv.at[pl.ds(pl.multiple_of((at.z * 8 + i) * w_cols, w_cols), w_cols), :]

    def qkv_copy(i, arriving=False):
        other = lax.rem(at.c + i, 8)
        slot = other if arriving else at.c
        return remote(qkv_rows(other), qkv_land.at[slot], qkv_send.at[other], qkv_recv.at[slot], (other, at.z))

    sum_qkv = LineReduce(at, qkv_block, qkv_line_land, 8 * w_cols, sems[28:])
    sum_qkv.first()
    out_land[at.z] = stage_out[at.z]
    reduce[1](d_normed)
    if line > 2:
        beside.a(0)
    for k in range(line - 1, 0, -1):
        sum_qkv.join(k)
    for k in range(line - 2, -1, -1):
        beside.b(k)
    for k in range(line - 1, 1, -1):
        beside.c(k)

    gain_stage[...] = jnp.zeros_like(gain_stage)
    gain_stage[1:2, :] = gain_term_ref[0:1, :]

    @pl.loop(0, blk // 32)
    def _(i):
        part = pl.ds(pl.multiple_of(i * 32, 32), 32)
        rows = tokens_ref[part, :].astype(jnp.float32)
        d_rows, gain_term = norm_backward(d_normed[part, :], rows, rms_scale(rows), gain_ref[0:1, :])
        grad_tokens_ref[part, :] = d_mid_ref[part, :] + d_rows
        gain_stage[0:1, :] += gain_term.reshape(1, width)

    def gain_tile(other):
        return gain_stage.at[:, pl.ds(pl.multiple_of((other // 2) * 128, 128), 128)]

    gain_push = (gain_tile, lambda slot: gain_land.at[slot], gain_send, gain_recv)
    at.push_all(*gain_push)
    gain_land[at.me] = gain_stage[:, pl.ds(pl.multiple_of((at.me // 2) * 128, 128), 128)]

    sum_qkv.last()

    @pl.loop(1, 8)
    def _(i):
        qkv_copy(i).start()

    qkv_land[at.c] = stage_qkv[pl.ds(pl.multiple_of((at.z * 8 + at.c) * w_cols, w_cols), w_cols), :]
    at.wait_all(*row_push, sent=False)

    @pl.loop(0, at.every)
    def _(j):
        span = pl.ds(pl.multiple_of(j * w_cols, w_cols), w_cols)
        row_stage[span, :] = row_land[j].astype(jnp.float32)
        for i in (0, 1):
            target = grad_gate_up_ref.at[:, pl.ds(pl.multiple_of((i * at.every + j) * part_ff, part_ff), part_ff)]
            pltpu.make_async_copy(row_stage.at[span, pl.ds(i * part_ff, part_ff)], target, row_sem.at[0]).start()

    for k in (1, 0):
        beside.c(k)
    mixed_ref[...] = (mid_ref[...] + BRANCH * mlp_sum[...]).astype(jnp.bfloat16)
    for i in range(1, line):
        out_arrival(i).wait_recv()
    total = out_land[0].astype(jnp.float32)
    for i in range(1, line):
        total = total + out_land[i].astype(jnp.float32)
    grad_out_ref[...] = total
    @pl.loop(1, 8)
    def _(i):
        qkv_copy(i, True).wait_recv()

    grad_qkv_ref[...] = qkv_land[...].astype(jnp.float32)
    at.wait_all(*gain_push, sent=False)
    gain_sum_ref[...] = jnp.sum(gain_land[...], axis=0)
    end()
    reduce[2]()
    for k in range(line):
        beside.end(k)
    at.wait_all(*row_push)
    pltpu.make_async_copy(grad_gate_up_ref, grad_gate_up_ref, row_sem.at[0]).wait()
    sum_qkv.end()

    @pl.loop(1, 8)
    def _(i):
        qkv_copy(i).wait_send()

    at.wait_all(*gain_push)
    for i in range(1, line):
        out_copy(i).wait_send()


def back(line, d_attn, tokens, mid, d_mid, qkv, attn_out, lse, gain, gain_term, lengths, normed, w_qkv, w_out, mlp_term, columns):
    blk, width = tokens.shape
    w_rows, cols = w_out.shape[1], w_qkv.shape[2]
    size, every = 8 * blk, 8 * line
    q_part = HEADS * HEAD_DIM // 8
    kv_part = (cols - q_part) // 2
    any_spec, vmem_spec = pl.BlockSpec(memory_space=pl.ANY), pl.BlockSpec(memory_space=pltpu.VMEM)
    bf16, f32, dma, out = jnp.bfloat16, jnp.float32, pltpu.SemaphoreType.DMA, jax.ShapeDtypeStruct
    return pl.pallas_call(
        functools.partial(back_kernel, line, blk, q_part, kv_part),
        out_shape=(out((blk, width), bf16), out((blk, width), f32), out((8, w_rows, cols), f32), out((w_rows, width), f32), out((8, 128), f32), out((w_rows, every * columns.shape[1]), f32)),
        in_specs=[any_spec] + [vmem_spec] * 8 + [pl.BlockSpec(memory_space=pltpu.SMEM)] + [any_spec] * 5,
        out_specs=(vmem_spec,) * 5 + (any_spec,),
        scratch_shapes=[
            pltpu.VMEM((size, width), bf16),
            pltpu.VMEM((size, width), bf16),
            pltpu.VMEM((4, blk, width), bf16),
            pltpu.VMEM((3 * blk, width), bf16),
            pltpu.VMEM((every, w_rows, cols), bf16),
            pltpu.VMEM((line, w_rows, width), bf16),
            pltpu.VMEM((size, width), bf16),
            pltpu.VMEM((size, q_part), bf16),
            pltpu.VMEM((size, cols), bf16),
            pltpu.VMEM((size, kv_part), f32),
            pltpu.VMEM((size, kv_part), f32),
            pltpu.VMEM((every * w_rows, cols), bf16),
            pltpu.VMEM((line, w_rows, width), bf16),
            pltpu.VMEM((8, w_rows, cols), bf16),
            pltpu.VMEM((line, w_rows, width), bf16),
            pltpu.VMEM((8, width), f32),
            pltpu.VMEM((every, 8, 128), f32),
            pltpu.VMEM((blk, width), f32),
            pltpu.VMEM((line * 4 * blk, width), bf16),
            pltpu.VMEM((line, 3 * blk, width), bf16),
            pltpu.VMEM((line + 1, blk, width), bf16),
            pltpu.VMEM((blk, width), f32),
            pltpu.VMEM((every, w_rows, columns.shape[1]), bf16),
            pltpu.VMEM(columns.shape, f32),
            pltpu.VMEM((line + 1, 8 * w_rows, cols), bf16),
            *[dma((n,)) for n in GATHER_SEMS + REDUCE_SEMS + (every,) * 4 + (line, line, 6)],
            *slice_reduce_sems(line),
            dma((every,)),
            dma((every,)),
            dma((1,)),
            dma((line,)),
            dma((line + 1,)),
        ],
        compiler_params=pltpu.CompilerParams(collective_id=2, has_side_effects=True, vmem_limit_bytes=63 * MIB),
    )(d_attn, tokens, mid, d_mid, qkv, attn_out, lse, gain, gain_term, lengths, normed, w_qkv, w_out, mlp_term, columns)


def split_heads(w, parts):
    rows = w.shape[0]
    q_width, kv_width = HEADS * HEAD_DIM, KV_HEADS * HEAD_DIM
    copies = max(1, parts // KV_HEADS)
    q = w[:, :q_width].reshape(rows, parts, q_width // parts)
    k = w[:, q_width : q_width + kv_width].reshape(rows, parts // copies, 1, -1)
    v = w[:, q_width + kv_width :].reshape(rows, parts // copies, 1, -1)
    k, v = (jnp.broadcast_to(a, (rows, parts // copies, copies, a.shape[3])).reshape(rows, parts, -1) for a in (k, v))
    return jnp.concatenate([q, k, v], axis=2)


def join_heads(grads, parts):
    rows = grads.shape[0]
    copies = max(1, parts // KV_HEADS)
    q_part = HEADS * HEAD_DIM // parts
    kv_part = (grads.shape[2] - q_part) // 2
    q = grads[:, :, :q_part].reshape(rows, -1)
    k, v = (
        jnp.sum(grads[:, :, at : at + kv_part].reshape(rows, parts // copies, copies, kv_part), axis=2).reshape(rows, -1)
        for at in (q_part, q_part + kv_part)
    )
    return jnp.concatenate([q, k, v], axis=1)


def per_device(n_ctx, n_shard, tokens, lengths, cotangent, w_qkv, w_out, w_gate_up, w_down, gain_attn, gain_mlp):
    count, width = tokens.shape[1:]
    n = n_ctx * n_shard
    w_rows = w_qkv.shape[0]
    ff_part = w_down.shape[0]
    q_part = HEADS * HEAD_DIM // n_ctx
    rows = tokens.reshape(count, width).astype(jnp.float32)
    grad_rows = cotangent.reshape(count, width).astype(jnp.float32)
    size = count * n_ctx
    positions = jnp.arange(size, dtype=jnp.int32)
    seg = segment_ids(positions, lengths[0])
    q_seg, k_seg = seg.reshape(size, 1), seg.reshape(1, size)

    gains = lax.all_gather(jnp.stack([gain_attn, gain_mlp]), EVERY, axis=1, tiled=True).astype(jnp.float32)
    gain_one, gain_two = gains[0], gains[1]

    qkv_cols = lax.all_to_all(split_heads(w_qkv, n_ctx), "ctx", split_axis=1, concat_axis=1, tiled=True)
    qkv_cols = qkv_cols.reshape(w_rows, n_ctx, -1).transpose(1, 0, 2)
    qkv_mine = lax.all_gather(qkv_cols, "shard", axis=1, tiled=True).reshape(width, -1)
    out_mine = lax.all_gather(w_out, "shard", axis=0, tiled=True)
    gate_up_mine = lax.all_to_all(w_gate_up.reshape(w_rows, 2, n, ff_part), EVERY, split_axis=2, concat_axis=0, tiled=True)
    gate_up_mine = gate_up_mine.reshape(width, 2 * ff_part)

    scale_one = rms_scale(rows)
    normed_one = lax.all_gather((rows * scale_one * gain_one).astype(jnp.bfloat16), "ctx", axis=0, tiled=True)
    projected = dot(normed_one, qkv_mine, ((1,), (0,))).astype(jnp.bfloat16)
    kv_part = (projected.shape[1] - q_part) // 2
    queries, keys, values = (
        projected[:, :q_part],
        projected[:, q_part : q_part + kv_part],
        projected[:, q_part + kv_part :],
    )
    attn_out, lse, tops = attend(queries, keys, values, q_seg, k_seg)
    out_term = dot(attn_out, out_mine, ((1,), (0,))).astype(jnp.bfloat16)
    attn_proj = lax.psum_scatter(out_term, "ctx", scatter_dimension=0, tiled=True)
    mid = rows + BRANCH * attn_proj.astype(jnp.float32)
    head_top = lax.all_gather(lax.pmax(tops, "shard"), "ctx", axis=1, tiled=True).reshape(HEADS)
    clip = CLIP_TARGET / jnp.maximum(head_top, CLIP_TARGET)

    scale_two = rms_scale(mid)
    d_mlp = lax.all_gather((BRANCH * grad_rows).astype(jnp.bfloat16), EVERY, axis=0, tiled=True)
    normed_two = lax.all_gather((mid * scale_two * gain_two).astype(jnp.bfloat16), EVERY, axis=0, tiled=True)
    gate_up = dot(normed_two, gate_up_mine, ((1,), (0,)))
    gate, up = gate_up[:, :ff_part], gate_up[:, ff_part:]
    sigma = jax.nn.sigmoid(gate)
    active = gate * sigma
    hidden = (active * up).astype(jnp.bfloat16)
    down_term = dot(hidden, w_down, ((1,), (0,))).astype(jnp.bfloat16)
    d_hidden = dot(d_mlp, w_down, ((1,), (1,)))
    d_gate = d_hidden * up * sigma * (1.0 + gate * (1.0 - sigma))
    d_up = d_hidden * active
    d_gate_up = jnp.concatenate([d_gate, d_up], axis=1).astype(jnp.bfloat16)
    normed_term = dot(d_gate_up, gate_up_mine, ((1,), (1,))).astype(jnp.bfloat16)
    grad_down = dot(hidden, d_mlp, ((0,), (0,)))
    gate_up_grad = dot(normed_two, d_gate_up, ((0,), (0,))).astype(jnp.bfloat16)
    mlp_proj = lax.psum_scatter(down_term, EVERY, scatter_dimension=0, tiled=True)
    mixed = (mid + BRANCH * mlp_proj.astype(jnp.float32)).astype(jnp.bfloat16).reshape(1, count, width)
    d_normed_two = lax.psum_scatter(normed_term, EVERY, scatter_dimension=0, tiled=True).astype(jnp.float32)
    grad_gate_up = lax.all_to_all(gate_up_grad.reshape(n * w_rows, 2, 1, ff_part), EVERY, split_axis=0, concat_axis=2, tiled=True)
    grad_gate_up = grad_gate_up.reshape(w_rows, 2 * n * ff_part).astype(jnp.float32)
    d_mid_norm, gain_two_term = norm_backward(d_normed_two, mid, scale_two, gain_two)
    d_mid = grad_rows + d_mid_norm

    d_attn = lax.all_gather((BRANCH * d_mid).astype(jnp.bfloat16), "ctx", axis=0, tiled=True)
    grad_out = lax.psum_scatter(dot(attn_out, d_attn, ((0,), (0,))), "shard", scatter_dimension=0, tiled=True)
    d_heads = dot(d_attn, out_mine, ((1,), (1,))).astype(jnp.bfloat16)
    d_q, d_k, d_v = attend_back(queries, keys, values, attn_out, d_heads, lse, q_seg, k_seg)
    d_qkv = jnp.concatenate([d_q, d_k, d_v], axis=1)
    qkv_term = dot(d_qkv, qkv_mine, ((1,), (1,))).astype(jnp.bfloat16)
    d_normed_one = lax.psum_scatter(qkv_term, "ctx", scatter_dimension=0, tiled=True).astype(jnp.float32)
    qkv_grad = dot(normed_one, d_qkv, ((0,), (0,))).reshape(n_ctx, n_shard * w_rows, -1)
    qkv_grad = lax.psum_scatter(qkv_grad, "shard", scatter_dimension=1, tiled=True)
    qkv_grad = lax.all_to_all(qkv_grad, "ctx", split_axis=0, concat_axis=0, tiled=True)
    grad_qkv = join_heads(qkv_grad.transpose(1, 0, 2), n_ctx)
    d_rows_norm, gain_one_term = norm_backward(d_normed_one, rows, scale_one, gain_one)
    grad_tokens = (d_mid + d_rows_norm).reshape(1, count, width)
    gain_terms = lax.psum_scatter(jnp.stack([gain_one_term, gain_two_term]), EVERY, scatter_dimension=1, tiled=True)
    return (mixed, grad_tokens, grad_qkv, grad_out, grad_gate_up, grad_down, gain_terms[0], gain_terms[1], clip)


def on_planes(n_shard, tokens, lengths, cotangent, w_qkv, w_out, w_gate_up, w_down, gain_attn, gain_mlp):
    count, width = tokens.shape[1:]
    w_rows = w_qkv.shape[0]
    rows = tokens.reshape(count, width)
    grad = cotangent.reshape(count, width)
    side = lax.rem(lax.axis_index("ctx") * n_shard + lax.axis_index("shard"), 2)

    gains = jnp.stack([gain_attn, gain_mlp])
    none = jnp.zeros_like(gains)
    gains = jnp.where(side == 0, jnp.concatenate([gains, none], axis=1), jnp.concatenate([none, gains], axis=1))
    gains = jnp.pad(gains, ((0, 14), (0, 0)))
    mid, normed_two, qkv, attn_out, lse, tops, gain, normed_one, qkv_mine, out_mine, d_mlp, gate_up_mine = front(
        n_shard, rows, grad, w_gate_up, gains, split_heads(w_qkv, 8).transpose(1, 0, 2), w_out, lengths
    )
    heads = HEADS // 8
    head_top = jnp.max(tops[:, 0, :heads].reshape(8, n_shard, heads), axis=1).reshape(HEADS)
    clip = CLIP_TARGET / jnp.maximum(head_top, CLIP_TARGET)

    mlp_term, d_mid, d_attn, gain_term, gate_up_grad, grad_down = mlp_exchange(
        n_shard, normed_two, d_mlp, gate_up_mine, w_down, mid, grad, gain
    )
    mixed, grad_tokens, qkv_grad, grad_out, gain_sum, grad_gate_up = back(
        n_shard, d_attn, rows, mid, d_mid, qkv, attn_out, lse, gain, gain_term, lengths, normed_one, qkv_mine, out_mine, mlp_term, gate_up_grad
    )
    grad_qkv = join_heads(qkv_grad.transpose(1, 0, 2), 8)
    gain_grads = jnp.where(side == 0, gain_sum[:2, :w_rows], gain_sum[:2, w_rows : 2 * w_rows])
    return (mixed.reshape(1, count, width), grad_tokens.reshape(1, count, width), grad_qkv, grad_out, grad_gate_up, grad_down, gain_grads[0], gain_grads[1], clip)


def solution(mesh):
    by_token, by_row = P("shard", "ctx", None), P(EVERY, None)
    n_ctx, n_shard = mesh.shape["ctx"], mesh.shape["shard"]
    program = functools.partial(on_planes, n_shard) if (n_ctx, n_shard) == (8, 4) else functools.partial(per_device, n_ctx, n_shard)
    return jax.shard_map(
        program,
        mesh=mesh,
        in_specs=(by_token, P("shard", None), by_token, by_row, by_row, by_row, by_row, P(EVERY), P(EVERY)),
        out_specs=(by_token, by_token, by_row, by_row, by_row, by_row, P(EVERY), P(EVERY), P()),
        check_vma=False,
    )
```

```python
import functools
import math

import jax
import jax.numpy as jnp
from jax import lax
from jax.experimental import pallas as pl
from jax.experimental.pallas import tpu as pltpu
from jax.sharding import PartitionSpec as P

HEADS = 32
KV_HEADS = 8
HEAD_DIM = 64


SCALE = 0.015625
BRANCH = 0.22
EPSILON = 1e-05
CLIP_TARGET = 4.0
NEGATIVE = -1e30
MIB = 1024 * 1024
EVERY = ("ctx", "shard")


def segment_ids(positions, lengths_row):
    bounds = jnp.cumsum(lengths_row)[:-1]
    return jnp.sum((positions[:, None] >= bounds[None, :]).astype(jnp.int32), axis=1)


def rms_scale(rows):
    return lax.rsqrt(jnp.mean(rows * rows, axis=-1, keepdims=True) + EPSILON)


def norm_backward(d_normed, rows, scale, gain):
    unit = rows * scale
    d_unit = d_normed * gain
    gain_term = jnp.sum(d_normed * unit, axis=0)
    d_rows = scale * (d_unit - unit * jnp.mean(d_unit * unit, axis=-1, keepdims=True))
    return (d_rows, gain_term)


def dot(left, right, dims):
    return lax.dot_general(left, right, ((dims[0], dims[1]), ((), ())), preferred_element_type=jnp.float32)


def segments(lengths_ref, positions):
    bound = jnp.int32(0)
    seg = jnp.zeros(positions.shape, jnp.int32)
    for i in range(lengths_ref.shape[1] - 1):
        bound = bound + lengths_ref[0, i]
        seg = seg + jnp.where(positions >= bound, 1, 0)
    return seg


def block_mask(lengths_ref, row0, rows, cols):
    q_seg = segments(lengths_ref, row0 + lax.broadcasted_iota(jnp.int32, (rows, 1), 0))
    return seen_mask(row0, rows, cols, q_seg, segments(lengths_ref, lax.broadcasted_iota(jnp.int32, (1, cols), 1)))


def seen_mask(row0, rows, cols, q_seg, k_seg):
    q_pos = row0 + lax.broadcasted_iota(jnp.int32, (rows, cols), 0)
    k_pos = lax.broadcasted_iota(jnp.int32, (rows, cols), 1)
    return (k_pos <= q_pos) & ((k_seg == 0) | (k_seg == q_seg))


def attend_kernel(heads, block, q_ref, k_ref, v_ref, q_seg_ref, k_seg_ref, o_ref, lse_ref, top_ref):
    size = q_ref.shape[0]
    tops = [jnp.full((1, 1), NEGATIVE, jnp.float32)] * heads
    for i in range(size // block):
        rows, cols = pl.ds(i * block, block), (i + 1) * block
        live = seen_mask(i * block, block, cols, q_seg_ref[rows, :], k_seg_ref[:, :cols])
        keys, values = k_ref[:cols, :], v_ref[:cols, :]
        for h in range(heads):
            span = slice(h * HEAD_DIM, (h + 1) * HEAD_DIM)
            scores = dot(q_ref[rows, span], keys, ((1,), (1,))) * SCALE
            scores = jnp.where(live, scores, NEGATIVE)
            peak = jnp.max(scores, axis=-1, keepdims=True)
            weights = jnp.exp(scores - peak)
            total = jnp.sum(weights, axis=-1, keepdims=True)
            out = dot(weights.astype(jnp.bfloat16), values, ((1,), (0,)))
            o_ref[rows, span] = (out / total).astype(jnp.bfloat16)
            lse_ref[rows, h : h + 1] = peak + jnp.log(total)
            tops[h] = jnp.maximum(tops[h], jnp.max(peak, axis=0, keepdims=True))
    for h in range(heads):
        top_ref[:, h : h + 1] = tops[h]


def attend(queries, keys, values, q_seg, k_seg):
    size, width = queries.shape
    heads = width // HEAD_DIM
    return pl.pallas_call(
        functools.partial(attend_kernel, heads, math.gcd(size, 256)),
        out_shape=(
            jax.ShapeDtypeStruct((size, width), jnp.bfloat16),
            jax.ShapeDtypeStruct((size, heads), jnp.float32),
            jax.ShapeDtypeStruct((1, heads), jnp.float32),
        ),
        compiler_params=pltpu.CompilerParams(vmem_limit_bytes=48 * MIB),
    )(queries, keys, values, q_seg, k_seg)


def attend_back_kernel(
    heads, block, q_ref, k_ref, v_ref, o_ref, do_ref, lse_ref, q_seg_ref, k_seg_ref, dq_ref, dk_ref, dv_ref, dk_sum, dv_sum
):
    size = q_ref.shape[0]
    dk_sum[...] = jnp.zeros_like(dk_sum)
    dv_sum[...] = jnp.zeros_like(dv_sum)
    for i in range(size // block):
        rows, cols = pl.ds(i * block, block), (i + 1) * block
        live = seen_mask(i * block, block, cols, q_seg_ref[rows, :], k_seg_ref[:, :cols])
        keys, values = k_ref[:cols, :], v_ref[:cols, :]
        for h in range(heads):
            span = slice(h * HEAD_DIM, (h + 1) * HEAD_DIM)
            queries, d_out = q_ref[rows, span], do_ref[rows, span]
            delta = jnp.sum(d_out.astype(jnp.float32) * o_ref[rows, span].astype(jnp.float32), axis=-1, keepdims=True)
            scores = dot(queries, keys, ((1,), (1,))) * SCALE
            probs = jnp.where(live, jnp.exp(scores - lse_ref[rows, h : h + 1]), 0.0)
            d_probs = dot(d_out, values, ((1,), (1,)))
            d_scores = (probs * (d_probs - delta)).astype(jnp.bfloat16)
            dq_ref[rows, span] = (dot(d_scores, keys, ((1,), (0,))) * SCALE).astype(jnp.bfloat16)
            dk_sum[:cols, :] += dot(d_scores, queries, ((0,), (0,)))
            dv_sum[:cols, :] += dot(probs.astype(jnp.bfloat16), d_out, ((0,), (0,)))
    dk_ref[...] = (dk_sum[...] * SCALE).astype(jnp.bfloat16)
    dv_ref[...] = dv_sum[...].astype(jnp.bfloat16)


def attend_back(queries, keys, values, out, d_out, lse, q_seg, k_seg):
    size, width = queries.shape
    heads = width // HEAD_DIM
    like_kv = jax.ShapeDtypeStruct((size, HEAD_DIM), jnp.bfloat16)
    return pl.pallas_call(
        functools.partial(attend_back_kernel, heads, math.gcd(size, 256)),
        out_shape=(jax.ShapeDtypeStruct((size, width), jnp.bfloat16), like_kv, like_kv),
        scratch_shapes=[pltpu.VMEM((size, HEAD_DIM), jnp.float32)] * 2,
        compiler_params=pltpu.CompilerParams(vmem_limit_bytes=48 * MIB),
    )(queries, keys, values, out, d_out, lse, q_seg, k_seg)


def remote(src, dst, send_sem, recv_sem, device):
    return pltpu.make_async_remote_copy(
        src_ref=src, dst_ref=dst, send_sem=send_sem, recv_sem=recv_sem, device_id=device, device_id_type=pl.DeviceIdType.MESH
    )


def greet(devices, extra):
    barrier = pltpu.get_barrier_semaphore()
    count = len(devices)
    for device in devices:
        pl.semaphore_signal(barrier, inc=1, device_id=device, device_id_type=pl.DeviceIdType.MESH)
    for condition, device in extra:

        @pl.when(condition)
        def _():
            pl.semaphore_signal(barrier, inc=1, device_id=device, device_id_type=pl.DeviceIdType.MESH)

        count = count + condition.astype(jnp.int32)
    pl.semaphore_wait(barrier, count)


def add_rows(target, sources, rows, keep=None, step=32):
    @pl.loop(0, rows // step)
    def _(i):
        part = pl.ds(pl.multiple_of(i * step, step), step)
        total = target[part, :].astype(jnp.float32)
        for source in sources:
            total = total + source[part, :].astype(jnp.float32)
        if keep is None:
            target[part, :] = total.astype(jnp.bfloat16)
        else:
            keep[part, :] = total


class Place:
    def __init__(self, line):
        self.line = line
        self.c, self.z = lax.axis_index("ctx"), lax.axis_index("shard")
        self.q, self.core = self.c // 2, self.c % 2
        self.me = self.c * line + self.z
        self.every = 8 * line
        self.cx, self.cy = (self.c + 2 - 4 * (self.q % 2), self.z), (self.c + 4 - 8 * (self.q // 2), self.z)
        self.sibling = (self.c + 1 - 2 * self.core, self.z)
        self.qx, self.qy, self.qd = self.q + 1 - 2 * (self.q % 2), self.q + 2 - 4 * (self.q // 2), 3 - self.q

    def source(self, k):
        if self.line == 1:
            return self.z * 0
        mirrored = self.z >= self.line // 2
        near = jnp.where(mirrored, self.line - 1 - self.z, self.z)
        turn = (k + 1) // 2
        both = near - turn if k % 2 == 1 else near + turn
        at = jnp.where(k <= 2 * near, both, k)
        return jnp.where(mirrored, self.line - 1 - at, at)

    def line_spread(self, copy, k):
        at = self.source(k)
        if k > 0:
            copy(at, 0).wait_recv()
        for way, condition in enumerate(self.line_ways(at)):

            @pl.when(condition)
            def _():
                copy(at, way).start()

    def line_sent(self, copy, k):
        at = self.source(k)
        for way, condition in enumerate(self.line_ways(at)):

            @pl.when(condition)
            def _():
                copy(at, way).wait_send()

    def line_ways(self, at):
        return ((at <= self.z) & (self.z < self.line - 1), (at >= self.z) & (self.z > 0))

    def peer(self, i):
        other = lax.rem(self.me + i, self.every)
        return other, (other // self.line, other % self.line)

    def greet_near(self):
        z, last = self.z, self.line - 1
        greet([self.cx, self.cy, self.sibling], [(z < last, (self.c, z + 1)), (z > 0, (self.c, z - 1))])

    def greet_all(self):
        barrier = pltpu.get_barrier_semaphore()

        @pl.loop(1, self.every)
        def _(i):
            pl.semaphore_signal(barrier, inc=1, device_id=self.peer(i)[1], device_id_type=pl.DeviceIdType.MESH)

        pl.semaphore_wait(barrier, self.every - 1)

    def push_all(self, source, target, send_sems, recv_sems, piece=0, pieces=1):
        @pl.loop(max(1, piece * self.every // pieces), (piece + 1) * self.every // pieces)
        def _(i):
            other, device = self.peer(i)
            remote(source(other), target(self.me), send_sems.at[other], recv_sems.at[self.me], device).start()

    def wait_all(self, source, target, send_sems, recv_sems, sent=True):
        @pl.loop(1, self.every)
        def _(i):
            other, device = self.peer(i)
            copy = remote(source(other), target(other), send_sems.at[other], recv_sems.at[other], device)
            if sent:
                copy.wait_send()
            else:
                copy.wait_recv()


class SliceGather:
    def __init__(self, place, rows, blk, sems):
        self.place, self.rows, self.half = place, rows, blk // 2
        self.z_send, self.z_recv, self.p_send, self.p_recv, self.f_send, self.f_recv = sems
        p, half = place, blk // 2
        self.ways = ((p.cx, p.qx, 0), (p.cy, p.qy, half), (p.cx, p.qx, half), (p.cy, p.qy, 0))
        self.turns = ((p.qx, 0, p.cy), (p.qy, half, p.cx))

    def line_copy(self, at, way):
        ref = self.rows(at, self.place.q, 0, 2 * self.half)
        return remote(ref, ref, self.z_send.at[at, way], self.z_recv.at[at], (self.place.c, self.place.z + 1 - 2 * way))

    def plane_copy(self, at, i, arriving=False):
        device, chip, first = self.ways[i]
        ref = self.rows(at, chip if arriving else self.place.q, first, self.half)
        return remote(ref, ref, self.p_send.at[at, i], self.p_recv.at[at, i], device)

    def onward_copy(self, at, i, arriving=False):
        chip, first, device = self.turns[i]
        ref = self.rows(at, self.place.qd if arriving else chip, first, self.half)
        return remote(ref, ref, self.f_send.at[at, i], self.f_recv.at[at, i], device)

    def a(self, k):
        self.place.line_spread(self.line_copy, k)
        for i in range(4):
            self.plane_copy(self.place.source(k), i).start()

    def b(self, k):
        at = self.place.source(k)
        for i in (0, 1):
            self.plane_copy(at, i, True).wait_recv()
            self.onward_copy(at, i).start()

    def c(self, k):
        at = self.place.source(k)
        for i in (2, 3):
            self.plane_copy(at, i, True).wait_recv()
        for i in (0, 1):
            self.onward_copy(at, i, True).wait_recv()
        for i in range(4):
            self.plane_copy(at, i).wait_send()
        for i in (0, 1):
            self.onward_copy(at, i).wait_send()
        self.place.line_sent(self.line_copy, k)


def slice_gather_sems(line):
    return [pltpu.SemaphoreType.DMA(shape) for shape in ((line, 2), (line,), (line, 4), (line, 4), (line, 2), (line, 2))]


class SliceReduce:
    def __init__(self, place, rows, blk, land, line_land, result, sems):
        self.place, self.rows, self.blk, self.half = place, rows, blk, blk // 2
        self.land, self.line_land, self.result = land, line_land, result
        self.r2_send, self.r2_recv, self.r3_send, self.r3_recv, self.r4_send, self.r4_recv = sems
        p, half = place, blk // 2
        self.seconds = ((0, p.cy), (half, p.cx))
        self.thirds = ((p.cx, p.qx, 0, 0), (p.cy, p.qy, half, blk + half), (p.cx, p.qx, half, half), (p.cy, p.qy, 0, blk))

    def landing(self, at, first, count):
        return self.land.at[at, pl.ds(first, count), :]

    def second(self, at, i):
        first, device = self.seconds[i]
        return remote(
            self.rows(at, self.place.qd, first, self.half), self.landing(at, 2 * self.blk + first, self.half), self.r2_send.at[at, i], self.r2_recv.at[at, i], device
        )

    def third(self, at, i):
        device, chip, first, lands = self.thirds[i]
        return remote(
            self.rows(at, chip, first, self.half), self.landing(at, lands, self.half), self.r3_send.at[at, i], self.r3_recv.at[at, i], device
        )

    def line_part(self, at, slot, part):
        rows = pl.ds(part * self.half, self.half)
        return self.rows(at, self.place.q, part * self.half, self.half), self.line_land.at[slot, rows, :]

    def line_copy(self, at, way, part):
        p = self.place
        slot = jnp.where((way == 1) & (at == p.z - 1), p.line, at)
        source, target = self.line_part(at, slot, part)
        return remote(source, target, self.r4_send.at[at, part], self.r4_recv.at[slot, part], (p.c, p.z + 1 - 2 * way))

    def line_arrival(self, at, slot, part):
        source, target = self.line_part(at, slot, part)
        return remote(source, target, self.r4_send.at[at, part], self.r4_recv.at[slot, part], self.place.sibling)

    def a(self, k):
        at = self.place.source(k)
        for i in (0, 1):
            self.second(at, i).start()
        for i in (2, 3):
            self.third(at, i).start()

    def b(self, k):
        at = self.place.source(k)
        for i in (0, 1):
            chip, first = self.thirds[i][1:3]
            self.second(at, i).wait_recv()
            add_rows(self.rows(at, chip, first, self.half), [self.landing(at, 2 * self.blk + first, self.half)], self.half)
            self.third(at, i).start()

    def c(self, k):
        p, blk = self.place, self.blk
        at = p.source(k)
        has_up, has_down = p.z < p.line - 1, p.z > 0
        for i in range(4):
            self.third(at, i).wait_recv()
        half = self.half
        joined = ((at > p.z) & has_down) | ((at < p.z) & has_up)
        for part in (0, 1):
            mine = self.rows(at, p.q, part * half, half)
            plane = [self.landing(at, part * half, half), self.landing(at, blk + part * half, half)]
            if k > 0:

                @pl.when(joined)
                def _():
                    self.line_arrival(at, at, part).wait_recv()
                    add_rows(mine, plane + [self.line_part(at, at, part)[1]], half)

                @pl.when(jnp.logical_not(joined))
                def _():
                    add_rows(mine, plane, half)

                for way, condition in enumerate((at > p.z, at < p.z)):

                    @pl.when(condition)
                    def _():
                        self.line_copy(at, way, part).start()

            else:
                result = self.result.at[pl.ds(part * half, half), :]
                add_rows(mine, plane, half, result)
                for condition, slot in ((has_down, at), (has_up, p.line)):

                    @pl.when(condition)
                    def _():
                        self.line_arrival(at, slot, part).wait_recv()
                        add_rows(result, [self.line_part(at, slot, part)[1]], half, result)

    def end(self, k):
        at = self.place.source(k)
        for i in (0, 1):
            self.second(at, i).wait_send()
        for i in range(4):
            self.third(at, i).wait_send()
        if k > 0:
            for part in (0, 1):
                self.line_copy(at, 0, part).wait_send()


class LineReduce:
    def __init__(self, place, block, land, rows, sems):
        self.place, self.block, self.land, self.rows = place, block, land, rows
        self.send, self.recv = sems

    def copy(self, at, way):
        p = self.place
        slot = jnp.where((way == 1) & (at == p.z - 1), p.line, at)
        return remote(self.block(at), self.land.at[slot], self.send.at[at], self.recv.at[slot], (p.c, p.z + 1 - 2 * way))

    def arrive(self, at, slot):
        p = self.place
        remote(self.block(at), self.land.at[slot], self.send.at[at], self.recv.at[slot], p.sibling).wait_recv()
        add_rows(self.block(at), [self.land.at[slot]], self.rows)

    def each(self, k, joined, after):
        p = self.place
        at = p.source(k)
        for way, toward, behind in ((0, at > p.z, p.z > 0), (1, at < p.z, p.z < p.line - 1)):

            @pl.when(toward & (behind if joined else jnp.logical_not(behind)))
            def _():
                after(at, way)

    def first(self):
        for k in range(self.place.line - 1, 0, -1):
            self.each(k, False, lambda at, way: self.copy(at, way).start())

    def join(self, k):
        def step(at, way):
            self.arrive(at, at)
            self.copy(at, way).start()

        self.each(k, True, step)

    def last(self):
        p = self.place
        for condition, slot in ((p.z > 0, p.z), (p.z < p.line - 1, p.line)):

            @pl.when(condition)
            def _():
                self.arrive(p.z, slot)

    def end(self):
        for k in range(1, self.place.line):
            self.copy(self.place.source(k), 0).wait_send()


def slice_reduce_sems(line):
    return [pltpu.SemaphoreType.DMA(shape) for shape in ((line, 2), (line, 2), (line, 4), (line, 4), (line, 2), (line + 1, 2))]


def slice_rows(ref, blk):
    def rows(at, chip, first, count):
        return ref.at[pl.ds(pl.multiple_of((at * 4 + chip) * blk + first, blk // 2), count), :]

    return rows


class ColumnSpread:
    def __init__(self, place, source, target, part, send_sems, recv_sems):
        self.place, self.source, self.target, self.part = place, source, target, part
        self.send_sems, self.recv_sems = send_sems, recv_sems

    def copies(self, other, slot):
        rows = self.source.shape[0]
        for j in (0, 1):
            columns = self.source.at[:, pl.ds(pl.multiple_of((j * self.place.every + other) * self.part, self.part), self.part)]
            yield j, columns, self.target.at[pl.ds(pl.multiple_of(slot * rows, rows), rows), pl.ds(j * self.part, self.part)]

    def start(self, piece, pieces):
        every = self.place.every

        @pl.loop(max(1, piece * every // pieces), (piece + 1) * every // pieces)
        def _(i):
            other, device = self.place.peer(i)
            for j, source, target in self.copies(other, self.place.me):
                remote(source, target, self.send_sems.at[j, other], self.recv_sems.at[j, self.place.me], device).start()

    def own(self, sems):
        return [pltpu.make_async_copy(source, target, sems[j]) for j, source, target in self.copies(self.place.me, self.place.me)]

    def wait(self):
        @pl.loop(1, self.place.every)
        def _(i):
            other, device = self.place.peer(i)
            for j, source, target in self.copies(other, other):
                copy = remote(source, target, self.send_sems.at[j, other], self.recv_sems.at[j, other], device)
                copy.wait_recv()
                copy.wait_send()


def mlp_kernel(
    line, blk, part, normed_ref, d_mlp_ref, gate_up_ref, down_ref, mid_ref, grad_ref, gain_ref,
    mlp_term_ref, d_mid_ref, d_attn_ref, gain_term_ref, gate_up_grad_ref, down_grad_ref,
    act, land, line_land, w_gu, w_down, acc_gu, acc_down, hid, d_gu, sib_gu, sib_down, d_normed,
    w_send, w_recv, g_send, g_recv, own_sem, out_sem, *sems,
):
    place = Place(line)
    core, sibling = place.core, place.sibling
    width = w_down.shape[1]
    slot_rows = 4 * blk
    rows = slice_rows(act.at[0], blk)
    gather = SliceGather(place, rows, blk, sems[:6])
    reduce = SliceReduce(place, rows, blk, land, line_land, d_normed, sems[6:])

    def slot_of(k):
        return pl.ds(pl.multiple_of(place.source(k) * slot_rows, slot_rows), slot_rows)

    own = pltpu.make_async_copy(normed_ref, rows(place.z, place.q, 0, blk), own_sem.at[0])
    d_mlp_in = pltpu.make_async_copy(d_mlp_ref, act.at[1], own_sem.at[1])
    mine = pl.ds(pl.multiple_of(core * 2 * part, 2 * part), 2 * part)
    theirs = pl.ds(pl.multiple_of((1 - core) * 2 * part, 2 * part), 2 * part)
    mine_rows = pl.ds(pl.multiple_of(core * part, part), part)
    their_rows = pl.ds(pl.multiple_of((1 - core) * part, part), part)

    own_weights = [
        pltpu.make_async_copy(gate_up_ref, w_gu.at[:, mine], own_sem.at[2]),
        pltpu.make_async_copy(down_ref, w_down.at[mine_rows, :], own_sem.at[3]),
    ]
    weights_to = [
        remote(gate_up_ref, w_gu.at[:, mine], w_send.at[0], w_recv.at[0], sibling),
        remote(down_ref, w_down.at[mine_rows, :], w_send.at[1], w_recv.at[1], sibling),
    ]
    weights_from = [
        remote(gate_up_ref, w_gu.at[:, theirs], w_send.at[0], w_recv.at[0], sibling),
        remote(down_ref, w_down.at[their_rows, :], w_send.at[1], w_recv.at[1], sibling),
    ]

    def compute(k):
        slot = slot_of(k)

        @pl.loop(0, 2)
        def _(j):
            span = pl.ds(pl.multiple_of(j * part, part), part)
            lower = pl.ds(pl.multiple_of(j * 2 * part, part), part)
            upper = pl.ds(pl.multiple_of(j * 2 * part + part, part), part)
            gate = dot(act[0, slot, :], w_gu[:, lower], ((1,), (0,)))
            above = dot(act[0, slot, :], w_gu[:, upper], ((1,), (0,)))
            d_hidden = dot(act[1, slot, :], w_down[span, :], ((1,), (1,)))
            sigma = jax.nn.sigmoid(gate)
            active = gate * sigma
            hid[:, span] = (active * above).astype(jnp.bfloat16)
            d_gu[:, lower] = (d_hidden * above * sigma * (1.0 + gate * (1.0 - sigma))).astype(jnp.bfloat16)
            d_gu[:, upper] = (d_hidden * active).astype(jnp.bfloat16)

        @pl.loop(0, width // 256)
        def _(j):
            span = pl.ds(pl.multiple_of(j * 256, 256), 256)
            down_term = dot(hid[...], act[1, slot, span], ((0,), (0,)))
            gate_up_term = dot(act[0, slot, span], d_gu[...], ((0,), (0,)))
            if k > 0:
                down_term = down_term + acc_down[:, span]
                gate_up_term = gate_up_term + acc_gu[span, :]
            acc_down[:, span] = down_term
            acc_gu[span, :] = gate_up_term
            act[1, slot, span] = dot(hid[...], w_down[:, span], ((1,), (0,))).astype(jnp.bfloat16)
            act[0, slot, span] = dot(d_gu[...], w_gu[span, :], ((1,), (1,))).astype(jnp.bfloat16)

    def term_out(k):
        return pltpu.make_async_copy(act.at[1, slot_of(k), :], mlp_term_ref.at[slot_of(k), :], out_sem.at[2 + k])

    half_gu, whole_gu = pl.ds(0, 2 * part), pl.ds(2 * part, 2 * part)
    grad_copies = [
        remote(w_gu.at[:, half_gu], sib_gu, g_send.at[0], g_recv.at[0], sibling),
        remote(w_down.at[:part, :], sib_down, g_send.at[1], g_recv.at[1], sibling),
    ]
    down_out = pltpu.make_async_copy(acc_down.at[mine_rows, :], down_grad_ref, out_sem.at[0])

    def exchange_grads():
        @pl.loop(0, width // 256)
        def _(j):
            span = pl.ds(pl.multiple_of(j * 256, 256), 256)
            w_gu[span, half_gu] = acc_gu[span, theirs].astype(jnp.bfloat16)

        w_down[:part, :] = acc_down[their_rows, :].astype(jnp.bfloat16)
        for copy in grad_copies:
            copy.start()

    columns_out = pltpu.make_async_copy(w_gu.at[:, whole_gu], gate_up_grad_ref, out_sem.at[1])

    def finish_grads():
        for copy in grad_copies:
            copy.wait_recv()

        @pl.loop(0, width // 256)
        def _(j):
            span = pl.ds(pl.multiple_of(j * 256, 256), 256)
            w_gu[span, whole_gu] = (acc_gu[span, mine] + sib_gu[span, :].astype(jnp.float32)).astype(jnp.bfloat16)

        columns_out.start()
        acc_down[mine_rows, :] = acc_down[mine_rows, :] + sib_down[...].astype(jnp.float32)
        down_out.start()

    for copy in [own, d_mlp_in] + own_weights:
        copy.start()
    place.greet_near()
    own.wait()
    gather.a(0)
    for copy in weights_to:
        copy.start()
    gather.a(1)
    gather.b(0)
    gather.a(2)
    gather.b(1)
    for copy in [d_mlp_in] + own_weights:
        copy.wait()
    for copy in weights_from:
        copy.wait_recv()
    for copy in weights_to:
        copy.wait_send()
    gather.a(3)
    gather.b(2)
    gather.c(0)
    compute(0)
    term_out(0).start()
    gather.b(3)
    gather.c(1)
    compute(1)
    term_out(1).start()
    reduce.a(1)
    gather.c(2)
    compute(2)
    term_out(2).start()
    reduce.a(2)
    gather.c(3)
    compute(3)
    term_out(3).start()
    reduce.a(3)
    exchange_grads()
    reduce.b(3)
    reduce.b(2)
    finish_grads()
    reduce.a(0)
    reduce.c(3)
    reduce.b(1)
    reduce.c(2)
    reduce.b(0)
    reduce.c(1)
    reduce.c(0)
    backwards = range(line - 1, -1, -1)

    gain_term_ref[...] = jnp.zeros_like(gain_term_ref)

    @pl.loop(0, blk // 32)
    def _(i):
        part = pl.ds(pl.multiple_of(i * 32, 32), 32)
        mid = mid_ref[part, :]
        d_rows, gain_term = norm_backward(d_normed[part, :], mid, rms_scale(mid), gain_ref[1:2, :])
        d_mid = grad_ref[part, :].astype(jnp.float32) + d_rows
        d_mid_ref[part, :] = d_mid
        d_attn_ref[part, :] = (BRANCH * d_mid).astype(jnp.bfloat16)
        gain_term_ref[0:1, :] += gain_term.reshape(1, width)

    for k in backwards:
        reduce.end(k)
        term_out(k).wait()
    for copy in grad_copies:
        copy.wait_send()
    down_out.wait()
    columns_out.wait()


def mlp_exchange(line, normed, d_mlp, gate_up, down, mid, grad, gain):
    blk, width = normed.shape
    part = down.shape[0]
    any_spec, vmem_spec = pl.BlockSpec(memory_space=pl.ANY), pl.BlockSpec(memory_space=pltpu.VMEM)
    bf16, f32, dma = jnp.bfloat16, jnp.float32, pltpu.SemaphoreType.DMA
    return pl.pallas_call(
        functools.partial(mlp_kernel, line, blk, part),
        out_shape=(
            jax.ShapeDtypeStruct(d_mlp.shape, bf16),
            jax.ShapeDtypeStruct((blk, width), f32),
            jax.ShapeDtypeStruct((blk, width), bf16),
            jax.ShapeDtypeStruct((8, width), f32),
            jax.ShapeDtypeStruct(gate_up.shape, bf16),
            jax.ShapeDtypeStruct((part, width), f32),
        ),
        in_specs=[any_spec] * 4 + [vmem_spec] * 3,
        out_specs=(any_spec, vmem_spec, vmem_spec, vmem_spec, any_spec, any_spec),
        scratch_shapes=[
            pltpu.VMEM((2, line * 4 * blk, width), bf16),
            pltpu.VMEM((line, 3 * blk, width), bf16),
            pltpu.VMEM((line + 1, blk, width), bf16),
            pltpu.VMEM((width, 4 * part), bf16),
            pltpu.VMEM((2 * part, width), bf16),
            pltpu.VMEM((width, 4 * part), f32),
            pltpu.VMEM((2 * part, width), f32),
            pltpu.VMEM((4 * blk, 2 * part), bf16),
            pltpu.VMEM((4 * blk, 4 * part), bf16),
            pltpu.VMEM((width, 2 * part), bf16),
            pltpu.VMEM((part, width), bf16),
            pltpu.VMEM((blk, width), f32),
            dma((2,)),
            dma((2,)),
            dma((2,)),
            dma((2,)),
            dma((5,)),
            dma((2 + line,)),
            *slice_gather_sems(line),
            *slice_reduce_sems(line),
        ],
        compiler_params=pltpu.CompilerParams(collective_id=0, has_side_effects=True, vmem_limit_bytes=63 * MIB),
    )(normed, d_mlp, gate_up, down, mid, grad, gain)


def plane_gather(at, buf, blk, sems):
    p_send, p_recv, f_send, f_recv, s_send, s_recv = sems
    half = blk // 2

    def rows(chip, core, first=0, count=half):
        return buf.at[pl.ds(pl.multiple_of((2 * chip + core) * blk + first, half), count), :]

    def same(ref, send, recv, device):
        return remote(ref, ref, send, recv, device)

    way = ((at.cx, at.qx, 0), (at.cy, at.qy, half), (at.cx, at.qx, half), (at.cy, at.qy, 0))

    def sent(i):
        return same(rows(at.q, at.core, way[i][2]), p_send.at[i], p_recv.at[i], way[i][0])

    def arriving(i):
        return same(rows(way[i][1], at.core, way[i][2]), p_send.at[i], p_recv.at[i], way[i][0])

    def onward(i):
        chip, first, device = ((at.qx, 0, at.cy), (at.qy, half, at.cx))[i]
        return same(rows(chip, at.core, first), f_send.at[i], f_recv.at[i], device)

    def passed(i):
        first, device = ((0, at.cy), (half, at.cx))[i]
        return same(rows(at.qd, at.core, first), f_send.at[i], f_recv.at[i], device)

    def across(i, core):
        if i == 0:
            ref = rows(at.q, core, 0, blk)
        elif i < 5:
            ref = rows(way[i - 1][1], core, way[i - 1][2])
        else:
            ref = rows(at.qd, core, (i - 5) * half)
        return same(ref, s_send.at[i], s_recv.at[i], at.sibling)

    def start():
        for i in range(4):
            sent(i).start()
        across(0, at.core).start()

    def turn():
        for i in (0, 1):
            arriving(i).wait_recv()
            onward(i).start()
            across(i + 1, at.core).start()

    def rest():
        for i in (2, 3):
            arriving(i).wait_recv()
            across(i + 1, at.core).start()
        for i in (0, 1):
            passed(i).wait_recv()
            across(i + 5, at.core).start()

    def whole():
        for i in range(7):
            across(i, 1 - at.core).wait_recv()

    def end():
        for i in range(4):
            sent(i).wait_send()
        for i in (0, 1):
            onward(i).wait_send()
        for i in range(7):
            across(i, at.core).wait_send()

    return start, turn, rest, whole, end


GATHER_SEMS = (4, 4, 2, 2, 7, 7)
REDUCE_SEMS = (4, 4, 2, 2, 4, 4)


def plane_reduce(at, term, core_land, land, blk, sems):
    s_send, s_recv, r2_send, r2_recv, r3_send, r3_recv = sems
    half = blk // 2
    chips = (at.qd, at.qx, at.qy, at.q)

    def rows(chip, core, first=0, count=half):
        return term.at[pl.ds(pl.multiple_of((2 * chip + core) * blk + first, half), count), :]

    def landed(first, count):
        return land.at[pl.ds(first, count), :]

    def across(i):
        return remote(rows(chips[i], 1 - at.core, 0, blk), core_land.at[i], s_send.at[i], s_recv.at[i], at.sibling)

    def second(i):
        first, device = ((0, at.cy), (half, at.cx))[i]
        return remote(rows(at.qd, at.core, first), landed(2 * blk + first, half), r2_send.at[i], r2_recv.at[i], device)

    def third(i):
        device, chip, first, lands = (
            (at.cx, at.qx, 0, 0), (at.cy, at.qy, half, blk + half), (at.cx, at.qx, half, half), (at.cy, at.qy, 0, blk)
        )[i]
        return remote(rows(chip, at.core, first), landed(lands, half), r3_send.at[i], r3_recv.at[i], device)

    def add_core(i):
        across(i).wait_recv()
        add_rows(rows(chips[i], at.core, 0, blk), [core_land.at[i]], blk)

    def give(i):
        across(i).start()

    def take(result):
        add_core(0)
        second(0).start()
        second(1).start()
        add_core(1)
        third(2).start()
        add_core(2)
        third(3).start()
        for i, (chip, first) in enumerate(((at.qx, 0), (at.qy, half))):
            second(i).wait_recv()
            add_rows(rows(chip, at.core, first), [landed(2 * blk + first, half)], half)
            third(i).start()
        add_core(3)
        for i in range(4):
            third(i).wait_recv()
        add_rows(rows(at.q, at.core, 0, blk), [landed(0, blk), landed(blk, blk)], blk, result)

    def end():
        for i in range(4):
            across(i).wait_send()
            third(i).wait_send()
        for i in (0, 1):
            second(i).wait_send()

    return give, take, end


def front_kernel(
    line, blk, q_part, kv_part,
    tokens_ref, grad_ref, w_gate_up_ref, gains_ref, w_qkv_ref, w_out_ref, lengths_ref,
    mid_ref, normed_two_ref, qkv_ref, attn_ref, lse_ref, tops_ref, gain_ref, normed_ref, w_qkv_all_ref, w_out_all_ref, d_mlp_all_ref, gate_up_ref,
    buf, term, core_land, land, w_qkv, w_line, w_out, gain_land, top_land, proj, d_mlp,
    *sems,
):
    at = Place(line)
    gather = plane_gather(at, buf, blk, sems[:6])
    reduce = plane_reduce(at, term, core_land, land, blk, sems[6:12])
    line_send, line_recv, qkv_send, qkv_recv, gain_send, gain_recv, top_send, top_recv, out_send, out_recv, own_sem, write_sem = sems[12:24]
    d_mlp_rows = slice_rows(d_mlp_all_ref, blk)
    beside = SliceGather(at, d_mlp_rows, blk, sems[24:30])
    spread = ColumnSpread(at, w_gate_up_ref, gate_up_ref, gate_up_ref.shape[1] // 2, *sems[30:])
    w_rows, width = w_out_ref.shape
    size = 8 * blk
    mine = pl.ds(pl.multiple_of(at.c * blk, blk), blk)

    own = [
        pltpu.make_async_copy(tokens_ref, buf.at[mine, :], own_sem.at[0]),
        pltpu.make_async_copy(gains_ref, gain_land.at[at.me], own_sem.at[1]),
        pltpu.make_async_copy(w_qkv_ref, w_line.at[at.z], own_sem.at[2]),
        pltpu.make_async_copy(w_out_ref, w_out.at[at.z], own_sem.at[3]),
        pltpu.make_async_copy(d_mlp, d_mlp_rows(at.z, at.q, 0, blk), own_sem.at[4]),
        *spread.own([own_sem.at[5], own_sem.at[6]]),
    ]
    for copy in own[:4] + own[5:]:
        copy.start()
    d_mlp[...] = (BRANCH * grad_ref[...].astype(jnp.float32)).astype(jnp.bfloat16)
    own[4].start()
    at.greet_all()
    gain_push = (lambda other: gains_ref, lambda slot: gain_land.at[slot], gain_send, gain_recv)
    top_push = (lambda other: top_land.at[at.me], lambda slot: top_land.at[slot], top_send, top_recv)

    def qkv_line(place, way):
        return remote(w_line.at[place], w_line.at[place], line_send.at[place, way], line_recv.at[place], (at.c, at.z + 1 - 2 * way))

    def out_line(place, way):
        return remote(w_out.at[place], w_out.at[place], out_send.at[place, way], out_recv.at[place], (at.c, at.z + 1 - 2 * way))

    def qkv_copy(i, place, arriving=False):
        other = lax.rem(at.c + i, 8)
        slot = (other if arriving else at.c) * line + place
        return remote(w_line.at[place, other], w_qkv.at[slot], qkv_send.at[place, other], qkv_recv.at[slot], (other, at.z))

    def qkv_step(k):
        at.line_spread(qkv_line, k)

        @pl.loop(1, 8)
        def _(i):
            qkv_copy(i, at.source(k)).start()

        w_qkv[at.c * line + at.source(k)] = w_line[at.source(k), at.c]

    inner = (at.z > 0) & (at.z < line - 1)
    outer = jnp.logical_not(inner)
    start, turn, rest, whole, end = gather
    own[0].wait()
    start()
    own[2].wait()
    qkv_step(0)
    at.push_all(*gain_push)
    turn()
    qkv_step(1)
    own[4].wait()
    beside.a(0)
    rest()
    for k in range(2, line - 1):
        qkv_step(k)
    own[1].wait()
    at.wait_all(*gain_push, sent=False)
    for i in range(at.every // 2):
        pair = gain_land[2 * i].astype(jnp.float32) + gain_land[2 * i + 1].astype(jnp.float32)
        gain_ref[:, i * 128 : (i + 1) * 128] = pair[:8, :]
    spread.start(0, 4)
    whole()
    end()
    at.wait_all(*gain_push)

    @pl.loop(0, size // 32)
    def _(i):
        part = pl.ds(pl.multiple_of(i * 32, 32), 32)
        rows = buf[part, :].astype(jnp.float32)
        buf[part, :] = (rows * rms_scale(rows) * gain_ref[0:1, :]).astype(jnp.bfloat16)

    writes = [
        pltpu.make_async_copy(buf, normed_ref, write_sem.at[0]),
        pltpu.make_async_copy(w_qkv, w_qkv_all_ref, write_sem.at[1]),
        pltpu.make_async_copy(w_out, w_out_all_ref, write_sem.at[2]),
    ]
    writes[0].start()
    qkv_step(line - 1)
    own[3].wait()
    at.line_spread(out_line, 0)
    beside.b(0)
    beside.a(1)
    pl.when(inner)(lambda: beside.a(2))
    spread.start(1, 4)
    for k in range(line):

        @pl.loop(1, 8)
        def _(i):
            qkv_copy(i, at.source(k), True).wait_recv()

    writes[1].start()

    @pl.loop(0, size // 256)
    def _(i):
        part = pl.ds(pl.multiple_of(i * 256, 256), 256)
        qkv_ref[part, :] = dot(buf[part, :], w_qkv[...].reshape(width, q_part + 2 * kv_part), ((1,), (0,))).astype(jnp.bfloat16)

    at.line_spread(out_line, 1)
    beside.b(1)
    pl.when(outer)(lambda: beside.a(2))
    pl.when(inner)(lambda: beside.a(3))
    spread.start(2, 4)
    heads = q_part // HEAD_DIM
    block = math.gcd(size, 256)
    tops = [jnp.full((1, 1), NEGATIVE, jnp.float32)] * heads
    for i in range(size // block):
        if i > 0 and i + 1 < line:
            at.line_spread(out_line, i + 1)
        if i == 2:
            beside.b(2)
        rows, cols = pl.ds(i * block, block), (i + 1) * block
        live = block_mask(lengths_ref, i * block, block, cols)
        keys, values = qkv_ref[:cols, q_part : q_part + kv_part], qkv_ref[:cols, q_part + kv_part :]
        for h in range(heads):
            span = slice(h * HEAD_DIM, (h + 1) * HEAD_DIM)
            scores = dot(qkv_ref[rows, span], keys, ((1,), (1,))) * SCALE
            scores = jnp.where(live, scores, NEGATIVE)
            peak = jnp.max(scores, axis=-1, keepdims=True)
            weights = jnp.exp(scores - peak)
            total = jnp.sum(weights, axis=-1, keepdims=True)
            out = dot(weights.astype(jnp.bfloat16), values, ((1,), (0,)))
            attn_ref[rows, span] = (out / total).astype(jnp.bfloat16)
            lse_ref[rows, h : h + 1] = peak + jnp.log(total)
            tops[h] = jnp.maximum(tops[h], jnp.max(peak, axis=0, keepdims=True))
    lanes = lax.broadcasted_iota(jnp.int32, (8, 128), 1)
    tile = jnp.full((8, 128), NEGATIVE, jnp.float32)
    for h in range(heads):
        tile = jnp.where(lanes == h, tops[h], tile)
    top_land[at.me] = tile
    at.push_all(*top_push)

    for k in range(size // block + 1, line):
        at.line_spread(out_line, k)
    pl.when(outer)(lambda: beside.a(3))
    pl.when(inner)(lambda: beside.b(3))
    spread.start(3, 4)
    writes[2].start()
    for i, chip in enumerate((at.qd, at.qx, at.qy, at.q)):
        for core in (1 - at.core, at.core):
            part = pl.ds(pl.multiple_of((2 * chip + core) * blk, blk), blk)

            @pl.loop(0, width // 512)
            def _(j):
                span = pl.ds(pl.multiple_of(j * 512, 512), 512)
                matrix = w_out[:, :, span].reshape(line * w_rows, 512)
                term[part, span] = dot(attn_ref[part, :], matrix, ((1,), (0,))).astype(jnp.bfloat16)

        reduce[0](i)
    reduce[1](proj)
    pl.when(outer)(lambda: beside.b(3))

    own_again = pltpu.make_async_copy(tokens_ref, land.at[pl.ds(0, blk), :], own_sem.at[0])
    own_again.start()
    own_again.wait()

    @pl.loop(0, blk // 32)
    def _(i):
        part = pl.ds(pl.multiple_of(i * 32, 32), 32)
        rows = land[part, :].astype(jnp.float32) + BRANCH * proj[part, :]
        mid_ref[part, :] = rows
        normed_two_ref[part, :] = (rows * rms_scale(rows) * gain_ref[1:2, :]).astype(jnp.bfloat16)

    at.wait_all(*top_push, sent=False)
    tops_ref[...] = top_land[...]
    reduce[2]()
    at.wait_all(*top_push)
    for k in range(line):
        at.line_sent(qkv_line, k)
        at.line_sent(out_line, k)

        @pl.loop(1, 8)
        def _(i):
            qkv_copy(i, at.source(k)).wait_send()

    for k in range(line):
        beside.c(k)
    spread.wait()
    for copy in own[5:]:
        copy.wait()
    for copy in writes:
        copy.wait()


def front(line, tokens, grad, w_gate_up, gains, w_qkv, w_out, lengths):
    blk, width = tokens.shape
    w_rows, cols = w_out.shape[0], w_qkv.shape[2]
    size, every = 8 * blk, 8 * line
    q_part = HEADS * HEAD_DIM // 8
    kv_part = (cols - q_part) // 2
    heads = q_part // HEAD_DIM
    any_spec, vmem_spec = pl.BlockSpec(memory_space=pl.ANY), pl.BlockSpec(memory_space=pltpu.VMEM)
    bf16, f32, dma, out = jnp.bfloat16, jnp.float32, pltpu.SemaphoreType.DMA, jax.ShapeDtypeStruct
    return pl.pallas_call(
        functools.partial(front_kernel, line, blk, q_part, kv_part),
        out_shape=(
            out((blk, width), f32),
            out((blk, width), bf16),
            out((size, cols), bf16),
            out((size, q_part), bf16),
            out((size, heads), f32),
            out((every, 8, 128), f32),
            out((8, width), f32),
            out((size, width), bf16),
            out((every, w_rows, cols), bf16),
            out((line, w_rows, width), bf16),
            out((line * 4 * blk, width), bf16),
            out((width, w_gate_up.shape[1] // every), bf16),
        ),
        in_specs=[any_spec, vmem_spec] + [any_spec] * 4 + [pl.BlockSpec(memory_space=pltpu.SMEM)],
        out_specs=(vmem_spec,) * 7 + (any_spec,) * 5,
        scratch_shapes=[
            pltpu.VMEM((size, width), bf16),
            pltpu.VMEM((size, width), bf16),
            pltpu.VMEM((4, blk, width), bf16),
            pltpu.VMEM((3 * blk, width), bf16),
            pltpu.VMEM((every, w_rows, cols), bf16),
            pltpu.VMEM((line, 8, w_rows, cols), bf16),
            pltpu.VMEM((line, w_rows, width), bf16),
            pltpu.VMEM((every, 16, 128), bf16),
            pltpu.VMEM((every, 8, 128), f32),
            pltpu.VMEM((blk, width), f32),
            pltpu.VMEM((blk, width), bf16),
            *[dma((n,)) for n in GATHER_SEMS + REDUCE_SEMS],
            dma((line, 2)),
            dma((line,)),
            dma((line, 8)),
            *[dma((every,))] * 5,
            dma((line, 2)),
            dma((line,)),
            dma((7,)),
            dma((3,)),
            *slice_gather_sems(line),
            dma((2, every)),
            dma((2, every)),
        ],
        compiler_params=pltpu.CompilerParams(collective_id=1, has_side_effects=True, vmem_limit_bytes=60 * MIB),
    )(tokens, grad, w_gate_up, gains, w_qkv, w_out, lengths)


def back_kernel(
    line, blk, q_part, kv_part,
    d_attn_ref, tokens_ref, mid_ref, d_mid_ref, qkv_ref, attn_ref, lse_ref, gain_ref, gain_term_ref, lengths_ref, normed_ref, w_qkv_ref, w_out_ref, mlp_term_ref, columns_ref,
    mixed_ref, grad_tokens_ref, grad_qkv_ref, grad_out_ref, gain_sum_ref, grad_gate_up_ref,
    buf, term, core_land, land, w_qkv, w_out, normed, d_heads, d_qkv, dk_sum, dv_sum, stage_qkv, stage_out, qkv_land, out_land, gain_stage, gain_land, d_normed, mlp_term, mlp_land, mlp_line_land, mlp_sum, row_land, row_stage, qkv_line_land,
    *sems,
):
    at = Place(line)
    gather = plane_gather(at, buf, blk, sems[:6])
    reduce = plane_reduce(at, term, core_land, land, blk, sems[6:12])
    qkv_send, qkv_recv, gain_send, gain_recv, out_send, out_recv, own_sem = sems[12:19]
    beside = SliceReduce(at, slice_rows(mlp_term, blk), blk, mlp_land, mlp_line_land, mlp_sum, sems[19:25])
    row_send, row_recv, row_sem = sems[25:28]
    w_cols = w_qkv.shape[1]
    part_ff = columns_ref.shape[1] // 2

    def column_rows(other):
        return columns_ref.at[pl.ds(pl.multiple_of(other * w_cols, w_cols), w_cols), :]

    row_push = (column_rows, lambda slot: row_land.at[slot], row_send, row_recv)
    width = buf.shape[1]
    w_rows = w_out.shape[1]
    size = 8 * blk
    mine = pl.ds(pl.multiple_of(at.c * blk, blk), blk)
    own = [
        pltpu.make_async_copy(d_attn_ref, buf.at[mine, :], own_sem.at[0]),
        pltpu.make_async_copy(w_out_ref, w_out, own_sem.at[1]),
        pltpu.make_async_copy(w_qkv_ref, w_qkv, own_sem.at[2]),
        pltpu.make_async_copy(normed_ref, normed, own_sem.at[3]),
        pltpu.make_async_copy(mlp_term_ref, mlp_term, own_sem.at[4]),
        pltpu.make_async_copy(column_rows(at.me), row_land.at[at.me], own_sem.at[5]),
    ]
    for copy in own:
        copy.start()
    at.greet_all()
    own[0].wait()
    start, turn, rest, whole, end = gather
    start()
    turn()
    rest()
    at.push_all(*row_push)
    for copy in own[1:]:
        copy.wait()
    beside.a(line - 1)
    whole()

    @pl.loop(0, size // 256)
    def _(i):
        part = pl.ds(pl.multiple_of(i * 256, 256), 256)
        d_heads[part, :] = dot(buf[part, :], w_out[...].reshape(line * w_rows, width), ((1,), (1,))).astype(jnp.bfloat16)

    if line > 1:
        beside.a(line - 2)

    @pl.loop(0, width // 256)
    def _(i):
        span = pl.ds(pl.multiple_of(i * 256, 256), 256)
        stage_out[:, :, span] = dot(attn_ref[...], buf[:, span], ((0,), (0,))).astype(jnp.bfloat16).reshape(line, w_rows, 256)

    def out_copy(i):
        z = lax.rem(at.z + i, line)
        return remote(stage_out.at[z], out_land.at[at.z], out_send.at[z], out_recv.at[at.z], (at.c, z))

    def out_arrival(i):
        z = lax.rem(at.z + i, line)
        return remote(stage_out.at[z], out_land.at[z], out_send.at[z], out_recv.at[z], (at.c, z))

    for i in range(1, line):
        out_copy(i).start()

    heads = q_part // HEAD_DIM
    block = math.gcd(size, 256)
    dk_sum[...] = jnp.zeros_like(dk_sum)
    dv_sum[...] = jnp.zeros_like(dv_sum)
    for i in range(size // block):
        rows, cols = pl.ds(i * block, block), (i + 1) * block
        live = block_mask(lengths_ref, i * block, block, cols)
        keys, values = qkv_ref[:cols, q_part : q_part + kv_part], qkv_ref[:cols, q_part + kv_part :]
        for h in range(heads):
            span = slice(h * HEAD_DIM, (h + 1) * HEAD_DIM)
            queries, d_out = qkv_ref[rows, span], d_heads[rows, span]
            delta = jnp.sum(d_out.astype(jnp.float32) * attn_ref[rows, span].astype(jnp.float32), axis=-1, keepdims=True)
            scores = dot(queries, keys, ((1,), (1,))) * SCALE
            probs = jnp.where(live, jnp.exp(scores - lse_ref[rows, h : h + 1]), 0.0)
            d_probs = dot(d_out, values, ((1,), (1,)))
            d_scores = (probs * (d_probs - delta)).astype(jnp.bfloat16)
            d_qkv[rows, span] = (dot(d_scores, keys, ((1,), (0,))) * SCALE).astype(jnp.bfloat16)
            dk_sum[:cols, :] += dot(d_scores, queries, ((0,), (0,)))
            dv_sum[:cols, :] += dot(probs.astype(jnp.bfloat16), d_out, ((0,), (0,)))
    d_qkv[:, q_part : q_part + kv_part] = (dk_sum[...] * SCALE).astype(jnp.bfloat16)
    d_qkv[:, q_part + kv_part :] = dv_sum[...].astype(jnp.bfloat16)
    beside.b(line - 1)
    for k in range(line - 3, 0, -1):
        beside.a(k)

    for i, chip in enumerate((at.qd, at.qx, at.qy, at.q)):
        for core in (1 - at.core, at.core):
            part = pl.ds(pl.multiple_of((2 * chip + core) * blk, blk), blk)

            @pl.loop(0, width // 512)
            def _(j):
                span = pl.ds(pl.multiple_of(j * 512, 512), 512)
                matrix = w_qkv[pl.ds(pl.multiple_of(j * (512 // w_rows), 512 // w_rows), 512 // w_rows)].reshape(512, q_part + 2 * kv_part)
                term[part, span] = dot(d_qkv[part, :], matrix, ((1,), (1,))).astype(jnp.bfloat16)

        reduce[0](i)

    chunk = line * w_cols

    @pl.loop(0, 8)
    def _(i):
        grads = dot(normed[:, pl.ds(pl.multiple_of(i * chunk, chunk), chunk)], d_qkv[...], ((0,), (0,))).astype(jnp.bfloat16)
        for place in range(line):
            stage_qkv[pl.ds(pl.multiple_of((place * 8 + i) * w_cols, w_cols), w_cols), :] = grads[place * w_cols : (place + 1) * w_cols, :]

    def qkv_block(place):
        return stage_qkv.at[pl.ds(pl.multiple_of(place * 8 * w_cols, w_cols), 8 * w_cols), :]

    def qkv_rows(i):
        return stage_qkv.at[pl.ds(pl.multiple_of((at.z * 8 + i) * w_cols, w_cols), w_cols), :]

    def qkv_copy(i, arriving=False):
        other = lax.rem(at.c + i, 8)
        slot = other if arriving else at.c
        return remote(qkv_rows(other), qkv_land.at[slot], qkv_send.at[other], qkv_recv.at[slot], (other, at.z))

    sum_qkv = LineReduce(at, qkv_block, qkv_line_land, 8 * w_cols, sems[28:])
    sum_qkv.first()
    out_land[at.z] = stage_out[at.z]
    reduce[1](d_normed)
    if line > 2:
        beside.a(0)
    for k in range(line - 1, 0, -1):
        sum_qkv.join(k)
    for k in range(line - 2, -1, -1):
        beside.b(k)
    for k in range(line - 1, 0, -1):
        beside.c(k)

    gain_stage[...] = jnp.zeros_like(gain_stage)
    gain_stage[1:2, :] = gain_term_ref[0:1, :]

    @pl.loop(0, blk // 32)
    def _(i):
        part = pl.ds(pl.multiple_of(i * 32, 32), 32)
        rows = tokens_ref[part, :].astype(jnp.float32)
        d_rows, gain_term = norm_backward(d_normed[part, :], rows, rms_scale(rows), gain_ref[0:1, :])
        grad_tokens_ref[part, :] = d_mid_ref[part, :] + d_rows
        gain_stage[0:1, :] += gain_term.reshape(1, width)

    def gain_tile(other):
        return gain_stage.at[:, pl.ds(pl.multiple_of((other // 2) * 128, 128), 128)]

    gain_push = (gain_tile, lambda slot: gain_land.at[slot], gain_send, gain_recv)
    at.push_all(*gain_push)
    gain_land[at.me] = gain_stage[:, pl.ds(pl.multiple_of((at.me // 2) * 128, 128), 128)]

    sum_qkv.last()

    @pl.loop(1, 8)
    def _(i):
        qkv_copy(i).start()

    qkv_land[at.c] = stage_qkv[pl.ds(pl.multiple_of((at.z * 8 + at.c) * w_cols, w_cols), w_cols), :]
    at.wait_all(*row_push, sent=False)

    @pl.loop(0, at.every)
    def _(j):
        span = pl.ds(pl.multiple_of(j * w_cols, w_cols), w_cols)
        row_stage[span, :] = row_land[j].astype(jnp.float32)
        for i in (0, 1):
            target = grad_gate_up_ref.at[:, pl.ds(pl.multiple_of((i * at.every + j) * part_ff, part_ff), part_ff)]
            pltpu.make_async_copy(row_stage.at[span, pl.ds(i * part_ff, part_ff)], target, row_sem.at[0]).start()

    beside.c(0)
    mixed_ref[...] = (mid_ref[...] + BRANCH * mlp_sum[...]).astype(jnp.bfloat16)
    for i in range(1, line):
        out_arrival(i).wait_recv()
    total = out_land[0].astype(jnp.float32)
    for i in range(1, line):
        total = total + out_land[i].astype(jnp.float32)
    grad_out_ref[...] = total
    @pl.loop(1, 8)
    def _(i):
        qkv_copy(i, True).wait_recv()

    for i in range(8):
        grads = qkv_land[i].astype(jnp.float32)
        grad_qkv_ref[:, i * q_part : (i + 1) * q_part] = grads[:, :q_part]
        for j in (0, 1):
            first = 8 * q_part + (8 * j + i) * kv_part
            grad_qkv_ref[:, first : first + kv_part] = grads[:, q_part + j * kv_part : q_part + (j + 1) * kv_part]
    at.wait_all(*gain_push, sent=False)
    gain_sum_ref[...] = jnp.sum(gain_land[...], axis=0)
    end()
    reduce[2]()
    for k in range(line):
        beside.end(k)
    at.wait_all(*row_push)
    pltpu.make_async_copy(grad_gate_up_ref, grad_gate_up_ref, row_sem.at[0]).wait()
    sum_qkv.end()

    @pl.loop(1, 8)
    def _(i):
        qkv_copy(i).wait_send()

    at.wait_all(*gain_push)
    for i in range(1, line):
        out_copy(i).wait_send()


def back(line, d_attn, tokens, mid, d_mid, qkv, attn_out, lse, gain, gain_term, lengths, normed, w_qkv, w_out, mlp_term, columns):
    blk, width = tokens.shape
    w_rows, cols = w_out.shape[1], w_qkv.shape[2]
    size, every = 8 * blk, 8 * line
    q_part = HEADS * HEAD_DIM // 8
    kv_part = (cols - q_part) // 2
    any_spec, vmem_spec = pl.BlockSpec(memory_space=pl.ANY), pl.BlockSpec(memory_space=pltpu.VMEM)
    bf16, f32, dma, out = jnp.bfloat16, jnp.float32, pltpu.SemaphoreType.DMA, jax.ShapeDtypeStruct
    return pl.pallas_call(
        functools.partial(back_kernel, line, blk, q_part, kv_part),
        out_shape=(out((blk, width), bf16), out((blk, width), f32), out((w_rows, 8 * cols), f32), out((w_rows, width), f32), out((8, 128), f32), out((w_rows, every * columns.shape[1]), f32)),
        in_specs=[any_spec] + [vmem_spec] * 8 + [pl.BlockSpec(memory_space=pltpu.SMEM)] + [any_spec] * 5,
        out_specs=(vmem_spec,) * 5 + (any_spec,),
        scratch_shapes=[
            pltpu.VMEM((size, width), bf16),
            pltpu.VMEM((size, width), bf16),
            pltpu.VMEM((4, blk, width), bf16),
            pltpu.VMEM((3 * blk, width), bf16),
            pltpu.VMEM((every, w_rows, cols), bf16),
            pltpu.VMEM((line, w_rows, width), bf16),
            pltpu.VMEM((size, width), bf16),
            pltpu.VMEM((size, q_part), bf16),
            pltpu.VMEM((size, cols), bf16),
            pltpu.VMEM((size, kv_part), f32),
            pltpu.VMEM((size, kv_part), f32),
            pltpu.VMEM((every * w_rows, cols), bf16),
            pltpu.VMEM((line, w_rows, width), bf16),
            pltpu.VMEM((8, w_rows, cols), bf16),
            pltpu.VMEM((line, w_rows, width), bf16),
            pltpu.VMEM((8, width), f32),
            pltpu.VMEM((every, 8, 128), f32),
            pltpu.VMEM((blk, width), f32),
            pltpu.VMEM((line * 4 * blk, width), bf16),
            pltpu.VMEM((line, 3 * blk, width), bf16),
            pltpu.VMEM((line + 1, blk, width), bf16),
            pltpu.VMEM((blk, width), f32),
            pltpu.VMEM((every, w_rows, columns.shape[1]), bf16),
            pltpu.VMEM(columns.shape, f32),
            pltpu.VMEM((line + 1, 8 * w_rows, cols), bf16),
            *[dma((n,)) for n in GATHER_SEMS + REDUCE_SEMS + (every,) * 4 + (line, line, 6)],
            *slice_reduce_sems(line),
            dma((every,)),
            dma((every,)),
            dma((1,)),
            dma((line,)),
            dma((line + 1,)),
        ],
        compiler_params=pltpu.CompilerParams(collective_id=2, has_side_effects=True, vmem_limit_bytes=63 * MIB),
    )(d_attn, tokens, mid, d_mid, qkv, attn_out, lse, gain, gain_term, lengths, normed, w_qkv, w_out, mlp_term, columns)


def split_heads(w, parts):
    rows = w.shape[0]
    q_width, kv_width = HEADS * HEAD_DIM, KV_HEADS * HEAD_DIM
    copies = max(1, parts // KV_HEADS)
    q = w[:, :q_width].reshape(rows, parts, q_width // parts)
    k = w[:, q_width : q_width + kv_width].reshape(rows, parts // copies, 1, -1)
    v = w[:, q_width + kv_width :].reshape(rows, parts // copies, 1, -1)
    k, v = (jnp.broadcast_to(a, (rows, parts // copies, copies, a.shape[3])).reshape(rows, parts, -1) for a in (k, v))
    return jnp.concatenate([q, k, v], axis=2)


def join_heads(grads, parts):
    rows = grads.shape[0]
    copies = max(1, parts // KV_HEADS)
    q_part = HEADS * HEAD_DIM // parts
    kv_part = (grads.shape[2] - q_part) // 2
    q = grads[:, :, :q_part].reshape(rows, -1)
    k, v = (
        jnp.sum(grads[:, :, at : at + kv_part].reshape(rows, parts // copies, copies, kv_part), axis=2).reshape(rows, -1)
        for at in (q_part, q_part + kv_part)
    )
    return jnp.concatenate([q, k, v], axis=1)


def per_device(n_ctx, n_shard, tokens, lengths, cotangent, w_qkv, w_out, w_gate_up, w_down, gain_attn, gain_mlp):
    count, width = tokens.shape[1:]
    n = n_ctx * n_shard
    w_rows = w_qkv.shape[0]
    ff_part = w_down.shape[0]
    q_part = HEADS * HEAD_DIM // n_ctx
    rows = tokens.reshape(count, width).astype(jnp.float32)
    grad_rows = cotangent.reshape(count, width).astype(jnp.float32)
    size = count * n_ctx
    positions = jnp.arange(size, dtype=jnp.int32)
    seg = segment_ids(positions, lengths[0])
    q_seg, k_seg = seg.reshape(size, 1), seg.reshape(1, size)

    gains = lax.all_gather(jnp.stack([gain_attn, gain_mlp]), EVERY, axis=1, tiled=True).astype(jnp.float32)
    gain_one, gain_two = gains[0], gains[1]

    qkv_cols = lax.all_to_all(split_heads(w_qkv, n_ctx), "ctx", split_axis=1, concat_axis=1, tiled=True)
    qkv_cols = qkv_cols.reshape(w_rows, n_ctx, -1).transpose(1, 0, 2)
    qkv_mine = lax.all_gather(qkv_cols, "shard", axis=1, tiled=True).reshape(width, -1)
    out_mine = lax.all_gather(w_out, "shard", axis=0, tiled=True)
    gate_up_mine = lax.all_to_all(w_gate_up.reshape(w_rows, 2, n, ff_part), EVERY, split_axis=2, concat_axis=0, tiled=True)
    gate_up_mine = gate_up_mine.reshape(width, 2 * ff_part)

    scale_one = rms_scale(rows)
    normed_one = lax.all_gather((rows * scale_one * gain_one).astype(jnp.bfloat16), "ctx", axis=0, tiled=True)
    projected = dot(normed_one, qkv_mine, ((1,), (0,))).astype(jnp.bfloat16)
    kv_part = (projected.shape[1] - q_part) // 2
    queries, keys, values = (
        projected[:, :q_part],
        projected[:, q_part : q_part + kv_part],
        projected[:, q_part + kv_part :],
    )
    attn_out, lse, tops = attend(queries, keys, values, q_seg, k_seg)
    out_term = dot(attn_out, out_mine, ((1,), (0,))).astype(jnp.bfloat16)
    attn_proj = lax.psum_scatter(out_term, "ctx", scatter_dimension=0, tiled=True)
    mid = rows + BRANCH * attn_proj.astype(jnp.float32)
    head_top = lax.all_gather(lax.pmax(tops, "shard"), "ctx", axis=1, tiled=True).reshape(HEADS)
    clip = CLIP_TARGET / jnp.maximum(head_top, CLIP_TARGET)

    scale_two = rms_scale(mid)
    d_mlp = lax.all_gather((BRANCH * grad_rows).astype(jnp.bfloat16), EVERY, axis=0, tiled=True)
    normed_two = lax.all_gather((mid * scale_two * gain_two).astype(jnp.bfloat16), EVERY, axis=0, tiled=True)
    gate_up = dot(normed_two, gate_up_mine, ((1,), (0,)))
    gate, up = gate_up[:, :ff_part], gate_up[:, ff_part:]
    sigma = jax.nn.sigmoid(gate)
    active = gate * sigma
    hidden = (active * up).astype(jnp.bfloat16)
    down_term = dot(hidden, w_down, ((1,), (0,))).astype(jnp.bfloat16)
    d_hidden = dot(d_mlp, w_down, ((1,), (1,)))
    d_gate = d_hidden * up * sigma * (1.0 + gate * (1.0 - sigma))
    d_up = d_hidden * active
    d_gate_up = jnp.concatenate([d_gate, d_up], axis=1).astype(jnp.bfloat16)
    normed_term = dot(d_gate_up, gate_up_mine, ((1,), (1,))).astype(jnp.bfloat16)
    grad_down = dot(hidden, d_mlp, ((0,), (0,)))
    gate_up_grad = dot(normed_two, d_gate_up, ((0,), (0,))).astype(jnp.bfloat16)
    mlp_proj = lax.psum_scatter(down_term, EVERY, scatter_dimension=0, tiled=True)
    mixed = (mid + BRANCH * mlp_proj.astype(jnp.float32)).astype(jnp.bfloat16).reshape(1, count, width)
    d_normed_two = lax.psum_scatter(normed_term, EVERY, scatter_dimension=0, tiled=True).astype(jnp.float32)
    grad_gate_up = lax.all_to_all(gate_up_grad.reshape(n * w_rows, 2, 1, ff_part), EVERY, split_axis=0, concat_axis=2, tiled=True)
    grad_gate_up = grad_gate_up.reshape(w_rows, 2 * n * ff_part).astype(jnp.float32)
    d_mid_norm, gain_two_term = norm_backward(d_normed_two, mid, scale_two, gain_two)
    d_mid = grad_rows + d_mid_norm

    d_attn = lax.all_gather((BRANCH * d_mid).astype(jnp.bfloat16), "ctx", axis=0, tiled=True)
    grad_out = lax.psum_scatter(dot(attn_out, d_attn, ((0,), (0,))), "shard", scatter_dimension=0, tiled=True)
    d_heads = dot(d_attn, out_mine, ((1,), (1,))).astype(jnp.bfloat16)
    d_q, d_k, d_v = attend_back(queries, keys, values, attn_out, d_heads, lse, q_seg, k_seg)
    d_qkv = jnp.concatenate([d_q, d_k, d_v], axis=1)
    qkv_term = dot(d_qkv, qkv_mine, ((1,), (1,))).astype(jnp.bfloat16)
    d_normed_one = lax.psum_scatter(qkv_term, "ctx", scatter_dimension=0, tiled=True).astype(jnp.float32)
    qkv_grad = dot(normed_one, d_qkv, ((0,), (0,))).reshape(n_ctx, n_shard * w_rows, -1)
    qkv_grad = lax.psum_scatter(qkv_grad, "shard", scatter_dimension=1, tiled=True)
    qkv_grad = lax.all_to_all(qkv_grad, "ctx", split_axis=0, concat_axis=0, tiled=True)
    grad_qkv = join_heads(qkv_grad.transpose(1, 0, 2), n_ctx)
    d_rows_norm, gain_one_term = norm_backward(d_normed_one, rows, scale_one, gain_one)
    grad_tokens = (d_mid + d_rows_norm).reshape(1, count, width)
    gain_terms = lax.psum_scatter(jnp.stack([gain_one_term, gain_two_term]), EVERY, scatter_dimension=1, tiled=True)
    return (mixed, grad_tokens, grad_qkv, grad_out, grad_gate_up, grad_down, gain_terms[0], gain_terms[1], clip)


def on_planes(n_shard, tokens, lengths, cotangent, w_qkv, w_out, w_gate_up, w_down, gain_attn, gain_mlp):
    count, width = tokens.shape[1:]
    w_rows = w_qkv.shape[0]
    rows = tokens.reshape(count, width)
    grad = cotangent.reshape(count, width)
    side = lax.rem(lax.axis_index("ctx") * n_shard + lax.axis_index("shard"), 2)

    gains = jnp.stack([gain_attn, gain_mlp])
    none = jnp.zeros_like(gains)
    gains = jnp.where(side == 0, jnp.concatenate([gains, none], axis=1), jnp.concatenate([none, gains], axis=1))
    gains = jnp.pad(gains, ((0, 14), (0, 0)))
    mid, normed_two, qkv, attn_out, lse, tops, gain, normed_one, qkv_mine, out_mine, d_mlp, gate_up_mine = front(
        n_shard, rows, grad, w_gate_up, gains, split_heads(w_qkv, 8).transpose(1, 0, 2), w_out, lengths
    )
    heads = HEADS // 8
    head_top = jnp.max(tops[:, 0, :heads].reshape(8, n_shard, heads), axis=1).reshape(HEADS)
    clip = CLIP_TARGET / jnp.maximum(head_top, CLIP_TARGET)

    mlp_term, d_mid, d_attn, gain_term, gate_up_grad, grad_down = mlp_exchange(
        n_shard, normed_two, d_mlp, gate_up_mine, w_down, mid, grad, gain
    )
    mixed, grad_tokens, grad_qkv, grad_out, gain_sum, grad_gate_up = back(
        n_shard, d_attn, rows, mid, d_mid, qkv, attn_out, lse, gain, gain_term, lengths, normed_one, qkv_mine, out_mine, mlp_term, gate_up_grad
    )
    gain_grads = jnp.where(side == 0, gain_sum[:2, :w_rows], gain_sum[:2, w_rows : 2 * w_rows])
    return (mixed.reshape(1, count, width), grad_tokens.reshape(1, count, width), grad_qkv, grad_out, grad_gate_up, grad_down, gain_grads[0], gain_grads[1], clip)


def solution(mesh):
    by_token, by_row = P("shard", "ctx", None), P(EVERY, None)
    n_ctx, n_shard = mesh.shape["ctx"], mesh.shape["shard"]
    program = functools.partial(on_planes, n_shard) if (n_ctx, n_shard) == (8, 4) else functools.partial(per_device, n_ctx, n_shard)
    return jax.shard_map(
        program,
        mesh=mesh,
        in_specs=(by_token, P("shard", None), by_token, by_row, by_row, by_row, by_row, P(EVERY), P(EVERY)),
        out_specs=(by_token, by_token, by_row, by_row, by_row, by_row, P(EVERY), P(EVERY), P()),
        check_vma=False,
    )
```
